32 devices in a mesh: narrow: 2 (over core), wide: 16 (over z, y, x).
Axes of the slice: x: 2, y: 2, z: 4, core: 2. Of those that a mesh axis runs over, the one named last changes fastest.
Arguments:
- inputs: bfloat16 [64, 512, 768], P(('narrow', 'wide')), may hold values from -6 to 6
- documents: int32 [64, 512], P(('narrow', 'wide')), may hold values from 0 to 5, never falling along the last dimension, each value on 1 to 256 neighbouring positions
- mixing: bfloat16 [12, 512, 512], P(None, 'narrow'), may hold values from -9 to 9
- value_weight: bfloat16 [768, 768], P(None, 'narrow'), may hold values from -0.21875 to 0.21875
- output_weight: bfloat16 [768, 768], P('narrow'), may hold values from -0.875 to 0.875
- mixer_gain: bfloat16 [768], P('narrow'), may hold values from 0.099609375 to 1.8984375
- mixer_shift: bfloat16 [768], P('narrow'), may hold values from -3 to 3
- dense_gain: bfloat16 [768], P('narrow'), may hold values from 0.099609375 to 1.8984375
- dense_shift: bfloat16 [768], P('narrow'), may hold values from -3 to 3
- hidden_weight: bfloat16 [768, 3072], P('narrow', 'wide'), may hold values from -0.21875 to 0.21875
- hidden_bias: bfloat16 [3072], P('narrow'), may hold values from -3 to 3
- down_weight: bfloat16 [3072, 768], P('wide', 'narrow'), may hold values from -0.21875 to 0.21875
- down_bias: bfloat16 [768], P('narrow'), may hold values from -3 to 3
- cotangent: bfloat16 [64, 512, 768], P(('narrow', 'wide')), may hold values from -6 to 6
Outputs:
- result: bfloat16 [64, 512, 768], P(('narrow', 'wide'))
- inputs_gradient: bfloat16 [64, 512, 768], P(('narrow', 'wide'))
- mixing_gradient: float32 [12, 512, 512], P(None, 'narrow')
- value_gradient: float32 [768, 768], P(None, 'narrow')
- output_gradient: float32 [768, 768], P('narrow')
- mixer_gain_gradient: float32 [768], P('narrow')
- mixer_shift_gradient: float32 [768], P('narrow')
- dense_gain_gradient: float32 [768], P('narrow')
- dense_shift_gradient: float32 [768], P('narrow')
- hidden_gradient: float32 [768, 3072], P('narrow', 'wide')
- hidden_bias_gradient: float32 [3072], P('narrow')
- down_gradient: float32 [3072, 768], P('wide', 'narrow')
- down_bias_gradient: float32 [768], P('narrow')
The draws below stay inside these ranges and needn't reach their ends.
Inputs may be any that keep to these rules, and one draw needn't show every extreme that they name: `documents`: document numbers never fall along a row; each document holds 1 to 256 tokens and one holds exactly 256.
All inputs are finite; a program needn't handle non-finite values.
Results may differ from the reference program's by a relative error of at most 0.02.
Values may be sent and summed in bfloat16 or wider, within the bound.
A program may use at most 256 MiB of HBM per device.

```python
import math
import jax
import jax.numpy as jnp
import numpy as np
from jax import lax

D = 768
HEADS = 12
HEAD = 64
FF = 3072
SEQ = 512
DOCS = 6
ROWS = 64


def levels(stream_key, dims, pieces, low, high):
    def one(dim, blocks):
        heights = jax.random.uniform(jax.random.fold_in(jax.random.fold_in(stream_key, 6), dim), (blocks,), jnp.float32, low / len(pieces), high / len(pieces))
        return jnp.repeat(jnp.exp(heights), dims[dim] // blocks).reshape((-1,) + (1,) * (len(dims) - dim - 1))

    factor_of = one(*pieces[0])
    for cut in pieces[1:]:
        factor_of = factor_of * one(*cut)
    return factor_of


def split_up(count, total, limit, slope):
    weights = [(1 << 20) // math.isqrt(rank ** slope) + 1 for rank in range(2, count + 1)]
    surplus, holding = total - limit - (count - 1), [1] * (count - 1)
    while surplus > 0:
        free = [i for i in range(count - 1) if holding[i] < limit]
        whole, budget = sum([weights[i] for i in free]), surplus
        for i in free:
            addition = min(limit - holding[i], max(1, budget * weights[i] // whole), surplus)
            holding[i] = holding[i] + addition
            surplus = surplus - addition
    return np.array([limit] + holding)


def ragged_sizes(own_key, amount, total, reach, lean):
    if amount == 2:
        one = jax.random.randint(own_key, (), max(1, total - reach), min(reach, total - 1) + 1)
        return jnp.stack([one, total - one])
    sizes = jnp.asarray(split_up(amount, total, reach, lean), jnp.int32)
    pairs = (amount - 1) // 2
    donor, receiver = sizes[1:1 + 2 * pairs:2], sizes[2:2 + 2 * pairs:2]
    margin = jnp.minimum(donor - 1, reach - receiver)
    passed = jax.random.randint(jax.random.fold_in(own_key, 1), (pairs,), 0, 1 << 20) % (margin + 1)
    sizes = sizes.at[1:1 + 2 * pairs:2].set(donor - passed).at[2:2 + 2 * pairs:2].set(receiver + passed)
    return sizes[jax.random.permutation(jax.random.fold_in(own_key, 2), amount)]


def gaussian(own_key, dims, scale, reach, split=(), held_as=jnp.bfloat16):
    drawn = jax.random.normal(own_key, dims, jnp.float32) * scale
    if len(split) > 0:
        drawn = levels(own_key, dims, split, -0.22, 0.18) * drawn
    return jnp.clip(drawn, min=-reach, max=reach).astype(held_as)


def setup_inputs(seed: int = 0) -> dict:
    keys = jax.random.split(jax.random.key(seed), 15)
    return {
        "inputs": gaussian(keys[0], (ROWS, SEQ, D), 1.0, 6.0, ((0, 32),)),
        "documents": jax.vmap(lambda own: jnp.searchsorted(jnp.cumsum(ragged_sizes(own, DOCS, SEQ, SEQ // 2, 1)), jnp.arange(SEQ), side="right"))(jax.random.split(keys[1], ROWS)).reshape((ROWS, SEQ)).astype(jnp.int32),
        "mixing": gaussian(keys[2], (HEADS, SEQ, SEQ), 1.5, 9.0, ((1, 2),)),
        "value_weight": gaussian(keys[3], (D, D), D ** -0.5, 0.21875, ((1, 2),)),
        "output_weight": gaussian(keys[4], (D, D), (D // 16) ** -0.5, 0.875, ((0, 2),)),
        "mixer_gain": jnp.clip(1.0 + 0.18 * jax.random.normal(keys[5], (D,), jnp.float32), 0.099609375, 1.8984375).astype(jnp.bfloat16),
        "mixer_shift": gaussian(keys[6], (D,), 0.5, 3.0, ((0, 2),)),
        "dense_gain": jnp.clip(1.0 + 0.18 * jax.random.normal(keys[7], (D,), jnp.float32), 0.099609375, 1.8984375).astype(jnp.bfloat16),
        "dense_shift": gaussian(keys[8], (D,), 0.5, 3.0, ((0, 2),)),
        "hidden_weight": gaussian(keys[9], (D, FF), D ** -0.5, 0.21875, ((0, 2), (1, 16))),
        "hidden_bias": gaussian(keys[10], (FF,), 0.5, 3.0, ((0, 2),)),
        "down_weight": gaussian(keys[11], (FF, D), (FF // 4) ** -0.5, 0.21875, ((0, 16), (1, 2))),
        "down_bias": gaussian(keys[12], (D,), 0.5, 3.0, ((0, 2),)),
        "cotangent": gaussian(keys[13], (ROWS, SEQ, D), 1.0, 6.0, ((0, 32),)),
    }


epsilon = 1e-05
highest = lax.Precision.HIGHEST

@jax.custom_vjp
def low(v):
    return lax.optimization_barrier(v.astype(jnp.bfloat16)).astype(jnp.float32)

@jax.custom_vjp
def low_back(v):
    return v

def low_keep(v):
    return (low(v), None)

def low_pass(kept, grad):
    return (grad,)

def back_keep(v):
    return (v, None)

def back_low(kept, grad):
    return (low(grad),)
low.defvjp(low_keep, low_pass)
low_back.defvjp(back_keep, back_low)

def widen(array):
    return array.astype(jnp.float32)

def norm_rows(matrix, norm_gain, norm_shift):
    average = lax.optimization_barrier(jnp.mean(matrix, axis=-1, keepdims=True))
    center = matrix - average
    spread = lax.optimization_barrier(jnp.mean(center * center, axis=-1, keepdims=True))
    return center * lax.rsqrt(spread + epsilon) * norm_gain + norm_shift

def forward(block_inputs, block_docs, mixing, value_weight, output_weight, mixer_gain, mixer_shift, dense_gain, dense_shift, hidden_weight, hidden_bias, down_weight, down_bias):
    normed = low(norm_rows(block_inputs, mixer_gain, mixer_shift))
    values = low(low_back(jnp.einsum('gsd,de->gse', normed, value_weight, precision=highest)))

    def one_row(bundle):
        row_values, row_docs = bundle
        same_doc = row_docs[:, None] == row_docs[None, :]
        scores = jnp.where(same_doc[None, :, :], mixing, -1e+30)
        row_top = lax.optimization_barrier(jnp.max(scores, axis=-1, keepdims=True))
        raised = jnp.exp(scores - row_top)
        chances = low(raised / lax.optimization_barrier(jnp.sum(raised, axis=-1, keepdims=True)))
        per_head = row_values.reshape(SEQ, HEADS, HEAD)
        blended = jnp.einsum('hij,jhd->ihd', chances, per_head, precision=highest)
        return blended.reshape(SEQ, D)
    blended = lax.map(jax.checkpoint(one_row), (values, block_docs))
    blended = low(low_back(blended))
    attended = low_back(jnp.einsum('gsd,de->gse', blended, output_weight, precision=highest))
    middle = block_inputs + attended
    normed_two = low(norm_rows(middle, dense_gain, dense_shift))
    hidden = low_back(jnp.einsum('gsd,df->gsf', normed_two, hidden_weight, precision=highest) + hidden_bias)
    active = low(jax.nn.gelu(hidden))
    return middle + jnp.einsum('gsf,fd->gsd', active, down_weight, precision=highest) + down_bias

def reference(inputs, documents, mixing, value_weight, output_weight, mixer_gain, mixer_shift, dense_gain, dense_shift, hidden_weight, hidden_bias, down_weight, down_bias, cotangent):
    weights = tuple((widen(array) for array in (mixing, value_weight, output_weight, mixer_gain, mixer_shift, dense_gain, dense_shift, hidden_weight, hidden_bias, down_weight, down_bias)))
    group_rows = math.gcd(ROWS, max(1, 4096 // SEQ))
    group_count = ROWS // group_rows
    inputs_all = widen(inputs).reshape(group_count, group_rows, SEQ, D)
    slopes_all = widen(cotangent).reshape(group_count, group_rows, SEQ, D)
    docs_all = documents.reshape(group_count, group_rows, SEQ)

    def accumulate(running, bundle):
        block_inputs, block_docs, block_slope = bundle

        def forward_block(block_values, *params):
            return forward(block_values, block_docs, *params)
        outputs, pullback = jax.vjp(forward_block, block_inputs, *weights)
        gradients = pullback(block_slope)
        running = jax.tree.map(jnp.add, running, tuple(gradients[1:]))
        return (running, (outputs, gradients[0]))
    initial = tuple((jnp.zeros_like(array) for array in weights))
    running, (outputs, input_slopes) = lax.scan(accumulate, initial, (inputs_all, docs_all, slopes_all))
    result = outputs.reshape(ROWS, SEQ, D).astype(jnp.bfloat16)
    inputs_gradient = input_slopes.reshape(ROWS, SEQ, D).astype(jnp.bfloat16)
    return (result, inputs_gradient, running[0], running[1], running[2], running[3], running[4], running[5], running[6], running[7], running[8], running[9], running[10])
```

```python
import functools

import jax
import jax.numpy as jnp
from jax import lax
from jax.experimental import pallas as pl
from jax.experimental.pallas import tpu as pltpu
from jax.sharding import PartitionSpec as P

D = 768
HEADS = 12
HEAD = 64
SEQ = 512
FF = 3072
HALF = D // 2
CHUNK = 192
GROUP = 4 * CHUNK
epsilon = 1e-05

MESH = pl.DeviceIdType.MESH
f32 = jnp.float32
bf16 = jnp.bfloat16


def place():
    core = lax.axis_index("narrow")
    wide = lax.axis_index("wide")
    return core, lax.rem(wide, 2), lax.rem(lax.div(wide, 2), 2), lax.div(wide, 4)


def seat(core, x, y, z):
    return (core, z * 4 + y * 2 + x)


def remote(src, dst, send_sem, recv_sem, device):
    return pltpu.make_async_remote_copy(
        src_ref=src,
        dst_ref=dst,
        send_sem=send_sem,
        recv_sem=recv_sem,
        device_id=device,
        device_id_type=MESH,
    )


def greet(core, x, y, z):
    barrier = pltpu.get_barrier_semaphore()
    for device in (seat(1 - core, x, y, z), seat(core, 1 - x, y, z), seat(core, x, 1 - y, z)):
        pl.semaphore_signal(barrier, inc=1, device_id=device, device_id_type=MESH)

    @pl.when(z < 3)
    def _():
        pl.semaphore_signal(
            barrier, inc=1, device_id=seat(core, x, y, z + 1), device_id_type=MESH
        )

    @pl.when(z > 0)
    def _():
        pl.semaphore_signal(
            barrier, inc=1, device_id=seat(core, x, y, z - 1), device_id_type=MESH
        )

    above, below = jnp.where(z < 3, 1, 0), jnp.where(z > 0, 1, 0)
    pl.semaphore_wait(barrier, 3 + above + below)


def halves(core):
    mine = pl.ds(pl.multiple_of(core * HALF, 128), HALF)
    other = pl.ds(pl.multiple_of((1 - core) * HALF, 128), HALF)
    return mine, other


def line_order(z, step):
    table = ((0, 1, 2, 3), (1, 0, 2, 3), (2, 3, 1, 0), (3, 2, 1, 0))
    return jnp.where(
        z == 0,
        table[0][step],
        jnp.where(z == 1, table[1][step], jnp.where(z == 2, table[2][step], table[3][step])),
    )


def unit_of(rows):
    center = rows - jnp.mean(rows, axis=-1, keepdims=True)
    reciprocal = lax.rsqrt(jnp.mean(center * center, axis=-1, keepdims=True) + epsilon)
    return center * reciprocal, reciprocal


def dot_nn(left, right):
    return lax.dot_general(left, right, (((1,), (0,)), ((), ())), preferred_element_type=f32)


def dot_nt(left, right):
    return lax.dot_general(left, right, (((1,), (1,)), ((), ())), preferred_element_type=f32)


def dot_tn(left, right):
    return lax.dot_general(left, right, (((0,), (0,)), ((), ())), preferred_element_type=f32)


def lane_ids(rows):
    return lax.broadcasted_iota(jnp.int32, (rows, 128), 1)


def fill_mask(docs_ref, mask, rows):
    for r in range(rows):
        flat = docs_ref[r : r + 1, :].astype(f32)
        for i in range(0, SEQ, 128):
            tall = jnp.broadcast_to(flat[:, i : i + 128], (128, 128)).T
            for j in range(0, SEQ, 128):
                wide = jnp.broadcast_to(flat[:, j : j + 128], (128, 128))
                mask[r, i : i + 128, j : j + 128] = jnp.where(tall == wide, 1.0, 0.0).astype(bf16)


def forward_kernel(
    x_ref, docs_ref, mixing_ref, value_ref, output_ref, shard_ref, vector_ref,
    full_ref, raised_out, value_out, output_out, vector_out, normed_out, values_out, blended_out,
    share_out, middle_out,
    raised, value_full, output_full, mask, vector_full, normed, values, blended, share, middle,
    recv, core_recv, sent_x, sent_y, sent_up, sent_down, sent_core,
    early_send, early_recv, local_sem, out_sem,
):
    core, x, y, z = place()
    mine, other = halves(core)
    near_x, near_y = seat(core, 1 - x, y, z), seat(core, x, 1 - y, z)
    above, below = seat(core, x, y, z + 1), seat(core, x, y, z - 1)
    twin = seat(1 - core, x, y, z)
    tokens = x_ref.shape[0]

    def chunk_of(k, y_of, x_of):
        return k * 4 + y_of * 2 + x_of

    def slot(m, chunk, lanes):
        rows = pl.ds(pl.multiple_of(chunk * CHUNK, CHUNK), CHUNK)
        return full_ref.at[m, rows, lanes]

    own = chunk_of(z, y, x)

    def send(m, chunk, sems, device):
        src = slot(m, chunk, mine)
        return remote(src, src, sems.at[m, chunk], recv.at[m, chunk], device)

    def send_own(m, sems, device):
        return remote(shard_ref.at[m], slot(m, own, mine), sems.at[m, own], recv.at[m, own], device)

    def send_twin(m, chunk):
        src = slot(m, chunk, mine)
        return remote(src, src, sent_core.at[m, chunk], core_recv.at[m, chunk], twin)

    def arrived(m, chunk):
        send(m, chunk, sent_x, near_x).wait_recv()

    heads_part = HEADS // 4
    my_rows = pl.ds(pl.multiple_of(core * (SEQ // 2), SEQ // 2), SEQ // 2)

    def mixing_part(p):
        heads = pl.ds(p * heads_part, heads_part)
        return mixing_ref.at[heads], raised.at[heads, my_rows]

    early = [
        (vector_ref, vector_full.at[:, mine]),
        (value_ref, value_full.at[:, mine]),
        mixing_part(0), mixing_part(1), mixing_part(2), mixing_part(3),
        (output_ref, output_full.at[mine, :]),
    ]
    greet(core, x, y, z)
    early_sends = [
        remote(src, dst, early_send.at[n], early_recv.at[n], twin)
        for n, (src, dst) in enumerate(early)
    ]
    early_local = [
        pltpu.make_async_copy(src, dst, local_sem.at[n]) for n, (src, dst) in enumerate(early)
    ]
    own_local = [
        pltpu.make_async_copy(shard_ref.at[m], slot(m, own, mine), local_sem.at[7 + m])
        for m in range(2)
    ]
    for m in range(2):
        own_local[m].start()
    send_own(0, sent_x, near_x).start()
    send_own(1, sent_y, near_y).start()

    @pl.when(z < 3)
    def _():
        for m in range(2):
            send_own(m, sent_up, above).start()

    @pl.when(z > 0)
    def _():
        for m in range(2):
            send_own(m, sent_down, below).start()

    send_own(1, sent_x, near_x).start()
    send_own(0, sent_y, near_y).start()
    for copy in early_sends:
        copy.start()
    for copy in early_local:
        copy.start()
    for m in range(2):
        own_local[m].wait()
        send_twin(m, own).start()

    def early_ready(n):
        early_local[n].wait()
        early_sends[n].wait_recv()

    def line_event(step):
        k = line_order(z, step)
        chunk = chunk_of(k, y, x)
        for m in range(2):
            arrived(m, chunk)

            @pl.when(jnp.logical_and(k < z, z < 3))
            def _():
                send(m, chunk, sent_up, above).start()

            @pl.when(jnp.logical_and(k > z, z > 0))
            def _():
                send(m, chunk, sent_down, below).start()

            if m == 0:
                send(0, chunk, sent_x, near_x).start()
            else:
                send(1, chunk, sent_y, near_y).start()
        send(1, chunk, sent_x, near_x).start()
        send(0, chunk, sent_y, near_y).start()
        for m in range(2):
            send_twin(m, chunk).start()

    def cross_event(step):
        k = line_order(z, step)
        across_x, across_y = chunk_of(k, y, 1 - x), chunk_of(k, 1 - y, x)
        arrived(0, across_x)
        send(0, across_x, sent_y, near_y).start()
        arrived(1, across_y)
        send(1, across_y, sent_x, near_x).start()
        send_twin(0, across_x).start()
        send_twin(1, across_y).start()

    def rest_event(step):
        k = line_order(z, step)
        across_x, across_y = chunk_of(k, y, 1 - x), chunk_of(k, 1 - y, x)
        arrived(1, across_x)
        send_twin(1, across_x).start()
        arrived(0, across_y)
        send_twin(0, across_y).start()

    def last_event(step):
        k = line_order(z, step)
        corner = chunk_of(k, 1 - y, 1 - x)
        for m in range(2):
            arrived(m, corner)
            send_twin(m, corner).start()

    def out_copy(n, src, dst):
        return pltpu.make_async_copy(src, dst, out_sem.at[n])

    block = 256
    early_ready(0)
    gain, shift = vector_full[0:1, :], vector_full[1:2, :]
    early_ready(1)

    def first_norm(b, _):
        rows = pl.ds(pl.multiple_of(b * block, block), block)
        unit, _r = unit_of(x_ref[rows, :].astype(f32))
        low = (unit * gain + shift).astype(bf16)
        normed[rows, :] = low
        values[rows, :] = dot_nn(low, value_full[...]).astype(bf16)
        return 0

    lax.fori_loop(0, tokens // block, first_norm, 0)
    out_normed = out_copy(0, normed, normed_out)
    out_normed.start()
    out_values = out_copy(1, values, values_out)
    out_values.start()
    out_value = out_copy(2, value_full, value_out)
    out_value.start()
    cross_event(0)
    fill_mask(docs_ref, mask, tokens // SEQ)

    def mix_pair(p, _):
        lanes = pl.ds(pl.multiple_of(p * 128, 128), 128)
        left_half = lane_ids(SEQ) < HEAD
        for i in range(0, SEQ, block):
            for half in range(2):
                h = 2 * p + half
                raised[h, i : i + block] = jnp.exp(raised[h, i : i + block].astype(f32)).astype(bf16)
        for r in range(tokens // SEQ):
            rows = pl.ds(r * SEQ, SEQ)
            pair = values[rows, lanes]
            ones = jnp.ones_like(pair)
            first = jnp.where(left_half, pair, ones)
            second = jnp.where(left_half, ones, pair)
            for i in range(0, SEQ, block):
                keep = mask[r, i : i + block]
                one = dot_nn(raised[2 * p, i : i + block] * keep, first)
                two = dot_nn(raised[2 * p + 1, i : i + block] * keep, second)
                low_lanes = left_half[:block]
                part = 1.0 / pltpu.roll(jnp.where(low_lanes, two, one), HEAD, 1)
                done = pl.ds(r * SEQ + i, block)
                share[done, lanes] = part
                blended[done, lanes] = (jnp.where(low_lanes, one, two) * part).astype(bf16)
        return 0

    for n in (2, 3):
        early_ready(n)
    lax.fori_loop(0, 3, mix_pair, 0)
    line_event(1)
    rest_event(0)
    for n in (4, 5):
        early_ready(n)
    lax.fori_loop(3, 6, mix_pair, 0)
    last_event(0)
    cross_event(1)
    outs = [
        out_copy(3, blended, blended_out), out_copy(4, share, share_out),
        out_copy(5, raised, raised_out), out_copy(6, vector_full, vector_out),
    ]
    for copy in outs:
        copy.start()
    early_ready(6)

    def project(b, _):
        rows = pl.ds(pl.multiple_of(b * block, block), block)
        middle[rows, :] = x_ref[rows, :].astype(f32) + dot_nn(blended[rows, :], output_full[...])
        return 0

    lax.fori_loop(0, tokens // block, project, 0)
    outs.append(out_copy(7, middle, middle_out))
    outs.append(out_copy(8, output_full, output_out))
    outs[-1].start()
    outs[-2].start()
    line_event(2)
    rest_event(1)
    last_event(1)
    cross_event(2)
    line_event(3)
    rest_event(2)
    last_event(2)
    cross_event(3)
    rest_event(3)
    last_event(3)

    for copy in outs + [out_normed, out_values, out_value]:
        copy.wait()
    for copy in early_sends:
        copy.wait_send()

    def settle(chunk, _):
        for m in range(2):
            copy = send_twin(m, chunk)
            copy.wait_recv()
            copy.wait_send()
        return 0

    lax.fori_loop(0, 16, settle, 0)

    def settle_line(k, _):
        line = chunk_of(k, y, x)
        for m in range(2):
            send(m, line, sent_x, near_x).wait_send()
            send(m, line, sent_y, near_y).wait_send()

            @pl.when(jnp.logical_and(k <= z, z < 3))
            def _():
                send(m, line, sent_up, above).wait_send()

            @pl.when(jnp.logical_and(k >= z, z > 0))
            def _():
                send(m, line, sent_down, below).wait_send()

        send(0, chunk_of(k, y, 1 - x), sent_y, near_y).wait_send()
        send(1, chunk_of(k, 1 - y, x), sent_x, near_x).wait_send()
        return 0

    lax.fori_loop(0, 4, settle_line, 0)


def forward_call(x, documents, mixing, value_weight, output_weight, shard, vectors):
    tokens = x.shape[0]
    rows = tokens // SEQ
    any_spec = pl.BlockSpec(memory_space=pl.ANY)
    vmem = pl.BlockSpec(memory_space=pltpu.VMEM)
    shape = jax.ShapeDtypeStruct
    dma = pltpu.SemaphoreType.DMA
    return pl.pallas_call(
        forward_kernel,
        out_shape=(
            shape((2, FF, D), bf16), shape((HEADS, SEQ, SEQ), bf16), shape((D, D), bf16),
            shape((D, D), bf16), shape((16, D), f32), shape((tokens, D), bf16),
            shape((tokens, D), bf16), shape((tokens, D), bf16), shape((tokens, D), f32),
            shape((tokens, D), f32),
        ),
        in_specs=[vmem, vmem] + [any_spec] * 5,
        out_specs=[any_spec] * 10,
        scratch_shapes=[
            pltpu.VMEM((HEADS, SEQ, SEQ), bf16), pltpu.VMEM((D, D), bf16), pltpu.VMEM((D, D), bf16),
            pltpu.VMEM((rows, SEQ, SEQ), bf16), pltpu.VMEM((16, D), f32),
            pltpu.VMEM((tokens, D), bf16), pltpu.VMEM((tokens, D), bf16),
            pltpu.VMEM((tokens, D), bf16), pltpu.VMEM((tokens, D), f32),
            pltpu.VMEM((tokens, D), f32),
            dma((2, 16)), dma((2, 16)), dma((2, 16)), dma((2, 16)), dma((2, 16)), dma((2, 16)),
            dma((2, 16)), dma((8,)), dma((8,)), dma((9,)), dma((9,)),
        ],
        compiler_params=pltpu.CompilerParams(
            collective_id=0, has_side_effects=True, vmem_limit_bytes=60 << 20
        ),
    )(x, documents, mixing, value_weight, output_weight, shard, vectors)


def contract_rows(left_side, right_side):
    return dot_tn(left_side, right_side)


def norm_back(slope_rows, unit_rows, reciprocal, norm_gain):
    tilted = slope_rows * norm_gain
    centered_slope = tilted - jnp.mean(tilted, axis=-1, keepdims=True)
    centered_slope = centered_slope - unit_rows * jnp.mean(
        tilted * unit_rows, axis=-1, keepdims=True
    )
    return (
        centered_slope * reciprocal,
        jnp.sum(slope_rows * unit_rows, axis=0),
        jnp.sum(slope_rows, axis=0),
    )


def local(
    inputs, documents, mixing, value_weight, output_weight, mixer_gain, mixer_shift, dense_gain,
    dense_shift, hidden_weight, hidden_bias, down_weight, down_bias, cotangent,
):
    row_count = inputs.shape[0]
    tokens = row_count * SEQ
    shard = jnp.stack([hidden_weight.T, down_weight])
    small = jnp.stack([mixer_gain, mixer_shift, dense_gain, dense_shift, down_bias])
    vectors = jnp.concatenate(
        [small, hidden_bias.reshape(4, HALF), jnp.zeros((7, HALF), bf16)]
    ).astype(f32)
    (
        full, raised, value_full, output_full, vector_full, normed_low, values, blended, share, middle,
    ) = forward_call(
        inputs.reshape(tokens, D), documents, mixing, value_weight, output_weight, shard, vectors
    )
    gain_first, shift_first, gain_second, shift_second, bias_down = (vector_full[n] for n in range(5))
    bias_hidden = vector_full[5:9].reshape(4, 2, HALF).swapaxes(0, 1).reshape(FF)
    hidden_t, down_full = full[0], full[1]
    stream = inputs.reshape(tokens, D).astype(f32)
    unit_first, recip_first = unit_of(stream)
    unit_second, recip_second = unit_of(middle)
    normed_two_low = (unit_second * gain_second + shift_second).astype(bf16)
    hidden = dot_nt(normed_two_low, hidden_t) + bias_hidden
    activated, gelu_pull = jax.vjp(jax.nn.gelu, hidden)
    active = activated.astype(jnp.bfloat16)
    result = middle + dot_nn(active, down_full) + bias_down
    slope_low = cotangent.reshape(tokens, D)
    slope_wide = slope_low.astype(jnp.float32)
    down_bias_sum = jnp.sum(slope_wide, axis=0)
    down_grad = contract_rows(active, slope_low)
    active_slope = dot_nt(slope_low, down_full)
    hidden_slope = gelu_pull(active_slope)[0].astype(bf16)
    hidden_bias_sum = jnp.sum(hidden_slope.astype(jnp.float32), axis=0)
    hidden_grad = contract_rows(normed_two_low, hidden_slope)
    normed_two_slope = dot_nn(hidden_slope, hidden_t)
    back_second, gain_second_sum, shift_second_sum = norm_back(
        normed_two_slope, unit_second, recip_second, gain_second
    )
    middle_slope = slope_wide + back_second
    attended_slope = middle_slope.astype(jnp.bfloat16)
    output_grad = contract_rows(blended, attended_slope)
    blended_slope = dot_nt(attended_slope, output_full).astype(jnp.bfloat16)
    value_rows = values.reshape(row_count, SEQ, D)

    def mix_back(running, bundle):
        row_values, row_docs, row_slope = bundle
        same = row_docs[:, None] == row_docs[None, :]
        chances = jnp.where(same[None], raised.astype(f32), 0.0)
        chances = chances / jnp.sum(chances, axis=-1, keepdims=True)
        per_head = row_values.reshape(SEQ, HEADS, HEAD)
        head_slope = row_slope.reshape(SEQ, HEADS, HEAD)
        chance_slope = jnp.einsum(
            "ihd,jhd->hij", head_slope, per_head, preferred_element_type=jnp.float32
        )
        score_slope = chances * (
            chance_slope - jnp.sum(chances * chance_slope, axis=-1, keepdims=True)
        )
        value_part = jnp.einsum(
            "hij,ihd->jhd",
            chances.astype(jnp.bfloat16),
            head_slope,
            preferred_element_type=jnp.float32,
        )
        return (running + score_slope, value_part.reshape(SEQ, D).astype(jnp.bfloat16))

    mixing_start = jnp.zeros((HEADS, SEQ, SEQ), jnp.float32)
    mixing_grad, value_slopes = lax.scan(
        mix_back, mixing_start, (value_rows, documents, blended_slope.reshape(row_count, SEQ, D))
    )
    value_slope = value_slopes.reshape(tokens, D)
    value_grad = contract_rows(normed_low, value_slope)
    normed_slope = dot_nt(value_slope, value_full)
    back_first, gain_first_sum, shift_first_sum = norm_back(
        normed_slope, unit_first, recip_first, gain_first
    )
    inputs_slope = (middle_slope + back_first).astype(jnp.bfloat16)

    def scatter(array, axis_name, axis):
        return lax.psum_scatter(
            array.astype(bf16), axis_name, scatter_dimension=axis, tiled=True
        ).astype(f32)

    hidden_share = scatter(scatter(hidden_grad, "wide", 1), "narrow", 0)
    down_share = scatter(scatter(down_grad, "wide", 0), "narrow", 1)
    sums = (
        (mixing_grad, 1), (value_grad, 1), (output_grad, 0), (gain_first_sum, 0),
        (shift_first_sum, 0), (gain_second_sum, 0), (shift_second_sum, 0), (hidden_bias_sum, 0),
        (down_bias_sum, 0),
    )
    totals = [
        lax.psum(scatter(one, "narrow", axis).astype(bf16), "wide").astype(f32)
        for one, axis in sums
    ]
    return (
        result.reshape(row_count, SEQ, D).astype(jnp.bfloat16),
        inputs_slope.reshape(row_count, SEQ, D),
        *totals[:7], hidden_share, totals[7], down_share, totals[8],
    )


def normalize(matrix, norm_gain, norm_shift):
    average = jnp.mean(matrix, axis=-1, keepdims=True)
    center = matrix - average
    reciprocal = lax.rsqrt(jnp.mean(center * center, axis=-1, keepdims=True) + epsilon)
    unit_rows = center * reciprocal
    return (unit_rows * norm_gain + norm_shift, unit_rows, reciprocal)


def plain_norm_back(slope_rows, unit_rows, reciprocal, norm_gain):
    tilted = slope_rows * norm_gain
    centered_slope = tilted - jnp.mean(tilted, axis=-1, keepdims=True)
    centered_slope = centered_slope - unit_rows * jnp.mean(
        tilted * unit_rows, axis=-1, keepdims=True
    )
    return (
        centered_slope * reciprocal,
        jnp.sum(slope_rows * unit_rows, axis=0),
        jnp.sum(slope_rows, axis=0),
    )


def plain_contract(left_side, right_side):
    return lax.dot_general(
        left_side, right_side, (((0,), (0,)), ((), ())), preferred_element_type=jnp.float32
    )


def times_transpose(left_side, right_side):
    return lax.dot_general(
        left_side, right_side, (((1,), (1,)), ((), ())), preferred_element_type=jnp.float32
    )


def row_chances(mixing_full, row_docs):
    same_doc = row_docs[:, None] == row_docs[None, :]
    scores = jnp.where(same_doc[None, :, :], mixing_full.astype(jnp.float32), -1e30)
    row_top = jnp.max(scores, axis=-1, keepdims=True)
    raised = jnp.exp(scores - row_top)
    return raised / jnp.sum(raised, axis=-1, keepdims=True)


def plain(
    inputs,
    documents,
    mixing,
    value_weight,
    output_weight,
    mixer_gain,
    mixer_shift,
    dense_gain,
    dense_shift,
    hidden_weight,
    hidden_bias,
    down_weight,
    down_bias,
    cotangent,
):
    gathered = (
        lax.all_gather(mixing, "narrow", axis=1, tiled=True),
        lax.all_gather(value_weight, "narrow", axis=1, tiled=True),
        lax.all_gather(output_weight, "narrow", axis=0, tiled=True),
        lax.all_gather(mixer_gain, "narrow", axis=0, tiled=True),
        lax.all_gather(mixer_shift, "narrow", axis=0, tiled=True),
        lax.all_gather(dense_gain, "narrow", axis=0, tiled=True),
        lax.all_gather(dense_shift, "narrow", axis=0, tiled=True),
        lax.all_gather(hidden_bias, "narrow", axis=0, tiled=True),
        lax.all_gather(down_bias, "narrow", axis=0, tiled=True),
    )
    mixing_full, value_full, output_full = (gathered[0], gathered[1], gathered[2])
    gain_first = gathered[3].astype(jnp.float32)
    shift_first = gathered[4].astype(jnp.float32)
    gain_second = gathered[5].astype(jnp.float32)
    shift_second = gathered[6].astype(jnp.float32)
    bias_hidden = gathered[7].astype(jnp.float32)
    bias_down = gathered[8].astype(jnp.float32)
    halfway = (
        lax.all_gather(hidden_weight, "narrow", axis=0, tiled=True),
        lax.all_gather(down_weight, "narrow", axis=1, tiled=True),
    )
    hidden_full, down_full = (
        lax.all_gather(halfway[0], "wide", axis=1, tiled=True),
        lax.all_gather(halfway[1], "wide", axis=0, tiled=True),
    )
    row_count = inputs.shape[0]
    stream = inputs.reshape(row_count * SEQ, D).astype(jnp.float32)
    normed, unit_first, recip_first = normalize(stream, gain_first, shift_first)
    normed_low = normed.astype(jnp.bfloat16)
    values = jnp.dot(normed_low, value_full, preferred_element_type=jnp.float32).astype(
        jnp.bfloat16
    )
    value_rows = values.reshape(row_count, SEQ, D)

    def mix_one(bundle):
        row_values, row_docs = bundle
        chances_low = row_chances(mixing_full, row_docs).astype(jnp.bfloat16)
        per_head = row_values.reshape(SEQ, HEADS, HEAD)
        blended_row = jnp.einsum(
            "hij,jhd->ihd", chances_low, per_head, preferred_element_type=jnp.float32
        )
        return blended_row.reshape(SEQ, D).astype(jnp.bfloat16)

    blended = lax.map(mix_one, (value_rows, documents)).reshape(row_count * SEQ, D)
    middle = stream + jnp.dot(blended, output_full, preferred_element_type=jnp.float32)
    normed_two, unit_second, recip_second = normalize(middle, gain_second, shift_second)
    normed_two_low = normed_two.astype(jnp.bfloat16)
    hidden = jnp.dot(normed_two_low, hidden_full, preferred_element_type=jnp.float32) + bias_hidden
    activated, gelu_pull = jax.vjp(jax.nn.gelu, hidden)
    active = activated.astype(jnp.bfloat16)
    result = middle + jnp.dot(active, down_full, preferred_element_type=jnp.float32) + bias_down
    slope_low = cotangent.reshape(row_count * SEQ, D)
    slope_wide = slope_low.astype(jnp.float32)
    down_bias_sum = jnp.sum(slope_wide, axis=0)
    down_grad = plain_contract(active, slope_low)
    active_slope = times_transpose(slope_low, down_full)
    hidden_slope_wide = gelu_pull(active_slope)[0]
    hidden_slope = hidden_slope_wide.astype(jnp.bfloat16)
    hidden_bias_sum = jnp.sum(hidden_slope.astype(jnp.float32), axis=0)
    hidden_grad = plain_contract(normed_two_low, hidden_slope)
    normed_two_slope = times_transpose(hidden_slope, hidden_full)
    back_second, gain_second_sum, shift_second_sum = plain_norm_back(
        normed_two_slope, unit_second, recip_second, gain_second
    )
    middle_slope = slope_wide + back_second
    attended_slope = middle_slope.astype(jnp.bfloat16)
    output_grad = plain_contract(blended, attended_slope)
    blended_slope = times_transpose(attended_slope, output_full).astype(jnp.bfloat16)

    def mix_back(running, bundle):
        row_values, row_docs, row_slope = bundle
        chances = row_chances(mixing_full, row_docs)
        per_head = row_values.reshape(SEQ, HEADS, HEAD)
        head_slope = row_slope.reshape(SEQ, HEADS, HEAD)
        chance_slope = jnp.einsum(
            "ihd,jhd->hij", head_slope, per_head, preferred_element_type=jnp.float32
        )
        score_slope = chances * (
            chance_slope - jnp.sum(chances * chance_slope, axis=-1, keepdims=True)
        )
        value_part = jnp.einsum(
            "hij,ihd->jhd",
            chances.astype(jnp.bfloat16),
            head_slope,
            preferred_element_type=jnp.float32,
        )
        return (running + score_slope, value_part.reshape(SEQ, D).astype(jnp.bfloat16))

    mixing_start = jnp.zeros((HEADS, SEQ, SEQ), jnp.float32)
    mixing_grad, value_slopes = lax.scan(
        mix_back, mixing_start, (value_rows, documents, blended_slope.reshape(row_count, SEQ, D))
    )
    value_slope = value_slopes.reshape(row_count * SEQ, D)
    value_grad = plain_contract(normed_low, value_slope)
    normed_slope = times_transpose(value_slope, value_full)
    back_first, gain_first_sum, shift_first_sum = plain_norm_back(
        normed_slope, unit_first, recip_first, gain_first
    )
    inputs_slope = (middle_slope + back_first).astype(jnp.bfloat16)
    sums_half = (
        lax.psum_scatter(
            hidden_grad.astype(jnp.bfloat16), "wide", scatter_dimension=1, tiled=True
        ).astype(jnp.float32),
        lax.psum_scatter(
            down_grad.astype(jnp.bfloat16), "wide", scatter_dimension=0, tiled=True
        ).astype(jnp.float32),
    )
    hidden_share, down_share = (
        lax.psum_scatter(
            sums_half[0].astype(jnp.bfloat16), "narrow", scatter_dimension=0, tiled=True
        ).astype(jnp.float32),
        lax.psum_scatter(
            sums_half[1].astype(jnp.bfloat16), "narrow", scatter_dimension=1, tiled=True
        ).astype(jnp.float32),
    )
    shares = (
        lax.psum_scatter(
            mixing_grad.astype(jnp.bfloat16), "narrow", scatter_dimension=1, tiled=True
        ).astype(jnp.float32),
        lax.psum_scatter(
            value_grad.astype(jnp.bfloat16), "narrow", scatter_dimension=1, tiled=True
        ).astype(jnp.float32),
        lax.psum_scatter(
            output_grad.astype(jnp.bfloat16), "narrow", scatter_dimension=0, tiled=True
        ).astype(jnp.float32),
        lax.psum_scatter(
            gain_first_sum.astype(jnp.bfloat16), "narrow", scatter_dimension=0, tiled=True
        ).astype(jnp.float32),
        lax.psum_scatter(
            shift_first_sum.astype(jnp.bfloat16), "narrow", scatter_dimension=0, tiled=True
        ).astype(jnp.float32),
        lax.psum_scatter(
            gain_second_sum.astype(jnp.bfloat16), "narrow", scatter_dimension=0, tiled=True
        ).astype(jnp.float32),
        lax.psum_scatter(
            shift_second_sum.astype(jnp.bfloat16), "narrow", scatter_dimension=0, tiled=True
        ).astype(jnp.float32),
        lax.psum_scatter(
            hidden_bias_sum.astype(jnp.bfloat16), "narrow", scatter_dimension=0, tiled=True
        ).astype(jnp.float32),
        lax.psum_scatter(
            down_bias_sum.astype(jnp.bfloat16), "narrow", scatter_dimension=0, tiled=True
        ).astype(jnp.float32),
    )
    totals = (
        lax.psum(shares[0].astype(jnp.bfloat16), "wide").astype(jnp.float32),
        lax.psum(shares[1].astype(jnp.bfloat16), "wide").astype(jnp.float32),
        lax.psum(shares[2].astype(jnp.bfloat16), "wide").astype(jnp.float32),
        lax.psum(shares[3].astype(jnp.bfloat16), "wide").astype(jnp.float32),
        lax.psum(shares[4].astype(jnp.bfloat16), "wide").astype(jnp.float32),
        lax.psum(shares[5].astype(jnp.bfloat16), "wide").astype(jnp.float32),
        lax.psum(shares[6].astype(jnp.bfloat16), "wide").astype(jnp.float32),
        lax.psum(shares[7].astype(jnp.bfloat16), "wide").astype(jnp.float32),
        lax.psum(shares[8].astype(jnp.bfloat16), "wide").astype(jnp.float32),
    )
    return (
        result.reshape(row_count, SEQ, D).astype(jnp.bfloat16),
        inputs_slope.reshape(row_count, SEQ, D),
        totals[0],
        totals[1],
        totals[2],
        totals[3],
        totals[4],
        totals[5],
        totals[6],
        hidden_share,
        totals[7],
        down_share,
        totals[8],
    )


def solution(mesh):
    inner = local if dict(mesh.shape) == {"narrow": 2, "wide": 16} else plain
    return jax.shard_map(
        inner,
        mesh=mesh,
        in_specs=(
            P(("narrow", "wide"), None, None),
            P(("narrow", "wide"), None),
            P(None, "narrow", None),
            P(None, "narrow"),
            P("narrow", None),
            P("narrow"),
            P("narrow"),
            P("narrow"),
            P("narrow"),
            P("narrow", "wide"),
            P("narrow"),
            P("wide", "narrow"),
            P("narrow"),
            P(("narrow", "wide"), None, None),
        ),
        out_specs=(
            P(("narrow", "wide"), None, None),
            P(("narrow", "wide"), None, None),
            P(None, "narrow", None),
            P(None, "narrow"),
            P("narrow", None),
            P("narrow"),
            P("narrow"),
            P("narrow"),
            P("narrow"),
            P("narrow", "wide"),
            P("narrow"),
            P("wide", "narrow"),
            P("narrow"),
        ),
        check_vma=False,
    )
```

```python
import functools

import jax
import jax.numpy as jnp
from jax import lax
from jax.experimental import pallas as pl
from jax.experimental.pallas import tpu as pltpu
from jax.sharding import PartitionSpec as P

D = 768
HEADS = 12
HEAD = 64
SEQ = 512
FF = 3072
HALF = D // 2
CHUNK = 192
GROUP = 4 * CHUNK
epsilon = 1e-05

MESH = pl.DeviceIdType.MESH
f32 = jnp.float32
bf16 = jnp.bfloat16


def place():
    core = lax.axis_index("narrow")
    wide = lax.axis_index("wide")
    return core, lax.rem(wide, 2), lax.rem(lax.div(wide, 2), 2), lax.div(wide, 4)


def seat(core, x, y, z):
    return (core, z * 4 + y * 2 + x)


def remote(src, dst, send_sem, recv_sem, device):
    return pltpu.make_async_remote_copy(
        src_ref=src,
        dst_ref=dst,
        send_sem=send_sem,
        recv_sem=recv_sem,
        device_id=device,
        device_id_type=MESH,
    )


def greet(core, x, y, z):
    barrier = pltpu.get_barrier_semaphore()
    for device in (seat(1 - core, x, y, z), seat(core, 1 - x, y, z), seat(core, x, 1 - y, z)):
        pl.semaphore_signal(barrier, inc=1, device_id=device, device_id_type=MESH)

    @pl.when(z < 3)
    def _():
        pl.semaphore_signal(
            barrier, inc=1, device_id=seat(core, x, y, z + 1), device_id_type=MESH
        )

    @pl.when(z > 0)
    def _():
        pl.semaphore_signal(
            barrier, inc=1, device_id=seat(core, x, y, z - 1), device_id_type=MESH
        )

    above, below = jnp.where(z < 3, 1, 0), jnp.where(z > 0, 1, 0)
    pl.semaphore_wait(barrier, 3 + above + below)


def halves(core):
    mine = pl.ds(pl.multiple_of(core * HALF, 128), HALF)
    other = pl.ds(pl.multiple_of((1 - core) * HALF, 128), HALF)
    return mine, other


def line_order(z, step):
    table = ((0, 1, 2, 3), (1, 0, 2, 3), (2, 3, 1, 0), (3, 2, 1, 0))
    return jnp.where(
        z == 0,
        table[0][step],
        jnp.where(z == 1, table[1][step], jnp.where(z == 2, table[2][step], table[3][step])),
    )


def unit_of(rows):
    center = rows - jnp.mean(rows, axis=-1, keepdims=True)
    reciprocal = lax.rsqrt(jnp.mean(center * center, axis=-1, keepdims=True) + epsilon)
    return center * reciprocal, reciprocal


def dot_nn(left, right):
    return lax.dot_general(left, right, (((1,), (0,)), ((), ())), preferred_element_type=f32)


def dot_nt(left, right):
    return lax.dot_general(left, right, (((1,), (1,)), ((), ())), preferred_element_type=f32)


def dot_tn(left, right):
    return lax.dot_general(left, right, (((0,), (0,)), ((), ())), preferred_element_type=f32)


def lane_ids(rows):
    return lax.broadcasted_iota(jnp.int32, (rows, 128), 1)


def fill_mask(docs_ref, mask, rows):
    for r in range(rows):
        flat = docs_ref[r : r + 1, :].astype(f32)
        for i in range(0, SEQ, 128):
            tall = jnp.broadcast_to(flat[:, i : i + 128], (128, 128)).T
            for j in range(0, SEQ, 128):
                wide = jnp.broadcast_to(flat[:, j : j + 128], (128, 128))
                mask[r, i : i + 128, j : j + 128] = jnp.where(tall == wide, 1.0, 0.0).astype(bf16)


def forward_kernel(
    x_ref, docs_ref, mixing_ref, value_ref, output_ref, shard_ref, vector_ref,
    full_ref, raised_out, value_out, output_out, vector_out, normed_out, values_out, blended_out,
    share_out, middle_out,
    raised, value_full, output_full, mask, vector_full, normed, values, blended, share, middle,
    recv, core_recv, sent_x, sent_y, sent_up, sent_down, sent_core,
    early_send, early_recv, local_sem, out_sem,
):
    core, x, y, z = place()
    mine, other = halves(core)
    near_x, near_y = seat(core, 1 - x, y, z), seat(core, x, 1 - y, z)
    above, below = seat(core, x, y, z + 1), seat(core, x, y, z - 1)
    twin = seat(1 - core, x, y, z)
    tokens = x_ref.shape[0]

    def chunk_of(k, y_of, x_of):
        return k * 4 + y_of * 2 + x_of

    def slot(m, chunk, lanes):
        rows = pl.ds(pl.multiple_of(chunk * CHUNK, CHUNK), CHUNK)
        return full_ref.at[m, rows, lanes]

    own = chunk_of(z, y, x)

    def send(m, chunk, sems, device):
        src = slot(m, chunk, mine)
        return remote(src, src, sems.at[m, chunk], recv.at[m, chunk], device)

    def send_own(m, sems, device):
        return remote(shard_ref.at[m], slot(m, own, mine), sems.at[m, own], recv.at[m, own], device)

    def send_twin(m, chunk):
        src = slot(m, chunk, mine)
        return remote(src, src, sent_core.at[m, chunk], core_recv.at[m, chunk], twin)

    def arrived(m, chunk):
        send(m, chunk, sent_x, near_x).wait_recv()

    heads_part = HEADS // 4
    my_rows = pl.ds(pl.multiple_of(core * (SEQ // 2), SEQ // 2), SEQ // 2)

    def mixing_part(p):
        heads = pl.ds(p * heads_part, heads_part)
        return mixing_ref.at[heads], raised.at[heads, my_rows]

    early = [
        (vector_ref, vector_full.at[:, mine]),
        (value_ref, value_full.at[:, mine]),
        mixing_part(0), mixing_part(1), mixing_part(2), mixing_part(3),
        (output_ref, output_full.at[mine, :]),
    ]
    greet(core, x, y, z)
    early_sends = [
        remote(src, dst, early_send.at[n], early_recv.at[n], twin)
        for n, (src, dst) in enumerate(early)
    ]
    early_local = [
        pltpu.make_async_copy(src, dst, local_sem.at[n]) for n, (src, dst) in enumerate(early)
    ]
    own_local = [
        pltpu.make_async_copy(shard_ref.at[m], slot(m, own, mine), local_sem.at[7 + m])
        for m in range(2)
    ]
    for m in range(2):
        own_local[m].start()
    send_own(0, sent_x, near_x).start()
    send_own(1, sent_y, near_y).start()

    @pl.when(z < 3)
    def _():
        for m in range(2):
            send_own(m, sent_up, above).start()

    @pl.when(z > 0)
    def _():
        for m in range(2):
            send_own(m, sent_down, below).start()

    send_own(1, sent_x, near_x).start()
    send_own(0, sent_y, near_y).start()
    for copy in early_sends:
        copy.start()
    for copy in early_local:
        copy.start()
    for m in range(2):
        own_local[m].wait()
        send_twin(m, own).start()

    def early_ready(n):
        early_local[n].wait()
        early_sends[n].wait_recv()

    def line_event(step):
        k = line_order(z, step)
        chunk = chunk_of(k, y, x)
        for m in range(2):
            arrived(m, chunk)

            @pl.when(jnp.logical_and(k < z, z < 3))
            def _():
                send(m, chunk, sent_up, above).start()

            @pl.when(jnp.logical_and(k > z, z > 0))
            def _():
                send(m, chunk, sent_down, below).start()

            if m == 0:
                send(0, chunk, sent_x, near_x).start()
            else:
                send(1, chunk, sent_y, near_y).start()
        send(1, chunk, sent_x, near_x).start()
        send(0, chunk, sent_y, near_y).start()
        for m in range(2):
            send_twin(m, chunk).start()

    def cross_event(step):
        k = line_order(z, step)
        across_x, across_y = chunk_of(k, y, 1 - x), chunk_of(k, 1 - y, x)
        arrived(0, across_x)
        send(0, across_x, sent_y, near_y).start()
        arrived(1, across_y)
        send(1, across_y, sent_x, near_x).start()
        send_twin(0, across_x).start()
        send_twin(1, across_y).start()

    def rest_event(step):
        k = line_order(z, step)
        across_x, across_y = chunk_of(k, y, 1 - x), chunk_of(k, 1 - y, x)
        arrived(1, across_x)
        send_twin(1, across_x).start()
        arrived(0, across_y)
        send_twin(0, across_y).start()

    def last_event(step):
        k = line_order(z, step)
        corner = chunk_of(k, 1 - y, 1 - x)
        for m in range(2):
            arrived(m, corner)
            send_twin(m, corner).start()

    def out_copy(n, src, dst):
        return pltpu.make_async_copy(src, dst, out_sem.at[n])

    block = 256
    early_ready(0)
    gain, shift = vector_full[0:1, :], vector_full[1:2, :]
    early_ready(1)

    def first_norm(b, _):
        rows = pl.ds(pl.multiple_of(b * block, block), block)
        unit, _r = unit_of(x_ref[rows, :].astype(f32))
        low = (unit * gain + shift).astype(bf16)
        normed[rows, :] = low
        values[rows, :] = dot_nn(low, value_full[...]).astype(bf16)
        return 0

    lax.fori_loop(0, tokens // block, first_norm, 0)
    out_normed = out_copy(0, normed, normed_out)
    out_normed.start()
    out_values = out_copy(1, values, values_out)
    out_values.start()
    out_value = out_copy(2, value_full, value_out)
    out_value.start()
    cross_event(0)
    fill_mask(docs_ref, mask, tokens // SEQ)

    def mix_pair(p, _):
        lanes = pl.ds(pl.multiple_of(p * 128, 128), 128)
        left_half = lane_ids(SEQ) < HEAD
        for i in range(0, SEQ, block):
            for half in range(2):
                h = 2 * p + half
                raised[h, i : i + block] = jnp.exp(raised[h, i : i + block].astype(f32)).astype(bf16)
        for r in range(tokens // SEQ):
            rows = pl.ds(r * SEQ, SEQ)
            pair = values[rows, lanes]
            ones = jnp.ones_like(pair)
            first = jnp.where(left_half, pair, ones)
            second = jnp.where(left_half, ones, pair)
            for i in range(0, SEQ, block):
                keep = mask[r, i : i + block]
                one = dot_nn(raised[2 * p, i : i + block] * keep, first)
                two = dot_nn(raised[2 * p + 1, i : i + block] * keep, second)
                low_lanes = left_half[:block]
                part = 1.0 / pltpu.roll(jnp.where(low_lanes, two, one), HEAD, 1)
                done = pl.ds(r * SEQ + i, block)
                share[done, lanes] = part
                blended[done, lanes] = (jnp.where(low_lanes, one, two) * part).astype(bf16)
        return 0

    for n in (2, 3):
        early_ready(n)
    lax.fori_loop(0, 3, mix_pair, 0)
    line_event(1)
    rest_event(0)
    for n in (4, 5):
        early_ready(n)
    lax.fori_loop(3, 6, mix_pair, 0)
    last_event(0)
    cross_event(1)
    outs = [
        out_copy(3, blended, blended_out), out_copy(4, share, share_out),
        out_copy(5, raised, raised_out), out_copy(6, vector_full, vector_out),
    ]
    for copy in outs:
        copy.start()
    early_ready(6)

    def project(b, _):
        rows = pl.ds(pl.multiple_of(b * block, block), block)
        middle[rows, :] = x_ref[rows, :].astype(f32) + dot_nn(blended[rows, :], output_full[...])
        return 0

    lax.fori_loop(0, tokens // block, project, 0)
    outs.append(out_copy(7, middle, middle_out))
    outs.append(out_copy(8, output_full, output_out))
    outs[-1].start()
    outs[-2].start()
    line_event(2)
    rest_event(1)
    last_event(1)
    cross_event(2)
    line_event(3)
    rest_event(2)
    last_event(2)
    cross_event(3)
    rest_event(3)
    last_event(3)

    for copy in outs + [out_normed, out_values, out_value]:
        copy.wait()
    for copy in early_sends:
        copy.wait_send()

    def settle(chunk, _):
        for m in range(2):
            copy = send_twin(m, chunk)
            copy.wait_recv()
            copy.wait_send()
        return 0

    lax.fori_loop(0, 16, settle, 0)

    def settle_line(k, _):
        line = chunk_of(k, y, x)
        for m in range(2):
            send(m, line, sent_x, near_x).wait_send()
            send(m, line, sent_y, near_y).wait_send()

            @pl.when(jnp.logical_and(k <= z, z < 3))
            def _():
                send(m, line, sent_up, above).wait_send()

            @pl.when(jnp.logical_and(k >= z, z > 0))
            def _():
                send(m, line, sent_down, below).wait_send()

        send(0, chunk_of(k, y, 1 - x), sent_y, near_y).wait_send()
        send(1, chunk_of(k, 1 - y, x), sent_x, near_x).wait_send()
        return 0

    lax.fori_loop(0, 4, settle_line, 0)


def forward_call(x, documents, mixing, value_weight, output_weight, shard, vectors):
    tokens = x.shape[0]
    rows = tokens // SEQ
    any_spec = pl.BlockSpec(memory_space=pl.ANY)
    vmem = pl.BlockSpec(memory_space=pltpu.VMEM)
    shape = jax.ShapeDtypeStruct
    dma = pltpu.SemaphoreType.DMA
    return pl.pallas_call(
        forward_kernel,
        out_shape=(
            shape((2, FF, D), bf16), shape((HEADS, SEQ, SEQ), bf16), shape((D, D), bf16),
            shape((D, D), bf16), shape((16, D), f32), shape((tokens, D), bf16),
            shape((tokens, D), bf16), shape((tokens, D), bf16), shape((tokens, D), f32),
            shape((tokens, D), f32),
        ),
        in_specs=[vmem, vmem] + [any_spec] * 5,
        out_specs=[any_spec] * 10,
        scratch_shapes=[
            pltpu.VMEM((HEADS, SEQ, SEQ), bf16), pltpu.VMEM((D, D), bf16), pltpu.VMEM((D, D), bf16),
            pltpu.VMEM((rows, SEQ, SEQ), bf16), pltpu.VMEM((16, D), f32),
            pltpu.VMEM((tokens, D), bf16), pltpu.VMEM((tokens, D), bf16),
            pltpu.VMEM((tokens, D), bf16), pltpu.VMEM((tokens, D), f32),
            pltpu.VMEM((tokens, D), f32),
            dma((2, 16)), dma((2, 16)), dma((2, 16)), dma((2, 16)), dma((2, 16)), dma((2, 16)),
            dma((2, 16)), dma((8,)), dma((8,)), dma((9,)), dma((9,)),
        ],
        compiler_params=pltpu.CompilerParams(
            collective_id=0, has_side_effects=True, vmem_limit_bytes=60 << 20
        ),
    )(x, documents, mixing, value_weight, output_weight, shard, vectors)


def gelu_and_slope(v):
    scale = 0.7978845608028654
    square = v * v
    t = jnp.tanh(scale * v * (1.0 + 0.044715 * square))
    rise = 0.5 * (1.0 + t)
    slope = rise + 0.5 * scale * v * (1.0 - t * t) * (1.0 + 3.0 * 0.044715 * square)
    return v * rise, slope


def norm_slope(slope, unit, reciprocal, gain):
    tilted = slope * gain
    centered = tilted - jnp.mean(tilted, axis=-1, keepdims=True)
    centered = centered - unit * jnp.mean(tilted * unit, axis=-1, keepdims=True)
    return centered * reciprocal


def dense_kernel(
    middle_ref, cotangent_ref, blended_ref, output_ref, vector_ref, full_ref,
    result_out, slope_out, blended_slope_out, output_grad_out, sums_out, hidden_out, down_out,
    normed, total, slope, active, hidden_slope, weight, grads, to_twin, from_twin, part,
    first_y, first_x, second_x, second_y, line_in, sums,
    weight_sem, twin_sent, twin_recv, first_y_sent, first_y_recv, first_x_sent, first_x_recv,
    second_x_sent, second_x_recv, second_y_sent, second_y_recv, up_sent, down_sent, line_recv, out_sem,
):
    core, x, y, z = place()
    mine, other = halves(core)
    near_x, near_y = seat(core, 1 - x, y, z), seat(core, x, 1 - y, z)
    above, below = seat(core, x, y, z + 1), seat(core, x, y, z - 1)
    twin = seat(1 - core, x, y, z)
    tokens = middle_ref.shape[0]
    block = 256
    order = (0, 3, 1, 2)

    def load(i):
        rows = pl.ds(order[i] * GROUP, GROUP)
        return pltpu.make_async_copy(full_ref.at[:, rows], weight.at[i % 2], weight_sem.at[i % 2])

    load(0).start()
    greet(core, x, y, z)

    def twin_copy(i, m):
        k = order[i]
        return remote(
            to_twin.at[i % 2, m], from_twin.at[k, m], twin_sent.at[k, m], twin_recv.at[k, m], twin
        )

    def first_copy(k, m):
        if m == 0:
            return remote(
                part.at[k, 0, 1 - y], first_y.at[k], first_y_sent.at[k], first_y_recv.at[k], near_y
            )
        return remote(
            part.at[k, 1, :, 1 - x], first_x.at[k], first_x_sent.at[k], first_x_recv.at[k], near_x
        )

    def second_copy(k, m):
        if m == 0:
            return remote(
                part.at[k, 0, y, 1 - x], second_x.at[k], second_x_sent.at[k], second_x_recv.at[k], near_x
            )
        return remote(
            part.at[k, 1, 1 - y, x], second_y.at[k], second_y_sent.at[k], second_y_recv.at[k], near_y
        )

    def line_copy(k, m, up):
        src = part.at[k, m, y, x]
        if up:
            return remote(src, line_in.at[0, k, m], up_sent.at[k, m], line_recv.at[0, k, m], above)
        return remote(src, line_in.at[1, k, m], down_sent.at[k, m], line_recv.at[1, k, m], below)

    def add_in(k, m, y_of, x_of, got):
        part[k, m, y_of, x_of] = (part[k, m, y_of, x_of].astype(f32) + got.astype(f32)).astype(bf16)

    def twin_event(i):
        for m in range(2):
            if i >= 2:
                twin_copy(i - 2, m).wait_send()
            to_twin[i % 2, m] = grads[m, :, other].astype(bf16)
            twin_copy(i, m).start()

    def sum_event(i):
        k = order[i]
        for m in range(2):
            twin_copy(i, m).wait_recv()
            both = grads[m, :, mine] + from_twin[k, m].astype(f32)
            part[k, m] = both.astype(bf16).reshape(2, 2, CHUNK, HALF)
            first_copy(k, m).start()

    def second_event(i):
        k = order[i]
        first_copy(k, 0).wait_recv()
        add_in(k, 0, y, 1 - x, first_y[k, 1 - x])
        second_copy(k, 0).start()
        first_copy(k, 1).wait_recv()
        add_in(k, 1, 1 - y, x, first_x[k, 1 - y])
        second_copy(k, 1).start()
        add_in(k, 0, y, x, first_y[k, x])
        add_in(k, 1, y, x, first_x[k, y])

    def line_event(i):
        k = order[i]
        second_copy(k, 0).wait_recv()
        add_in(k, 0, y, x, second_x[k])
        second_copy(k, 1).wait_recv()
        add_in(k, 1, y, x, second_y[k])
        hop_event(i, 0)

    def hop_event(i, hop):
        k = order[i]
        if hop < k:

            @pl.when(z == hop)
            def _():
                for m in range(2):
                    if hop > 0:
                        line_copy(k, m, True).wait_recv()
                        add_in(k, m, y, x, line_in[0, k, m])
                    line_copy(k, m, True).start()

        if hop < 3 - k:

            @pl.when(z == 3 - hop)
            def _():
                for m in range(2):
                    if hop > 0:
                        line_copy(k, m, False).wait_recv()
                        add_in(k, m, y, x, line_in[1, k, m])
                    line_copy(k, m, False).start()

        if hop == max(k, 3 - k):

            @pl.when(z == k)
            def _():
                for m, out in enumerate((hidden_out, down_out)):
                    both = part[k, m, y, x].astype(f32)
                    if k > 0:
                        line_copy(k, m, True).wait_recv()
                        both = both + line_in[0, k, m].astype(f32)
                    if k < 3:
                        line_copy(k, m, False).wait_recv()
                        both = both + line_in[1, k, m].astype(f32)
                    out[...] = both

    gain, shift, down_bias = vector_ref[2:3, :], vector_ref[3:4, :], vector_ref[4:5, :]

    def rows_of(b):
        return pl.ds(pl.multiple_of(b * block, block), block)

    def second_norm(b, _):
        rows = rows_of(b)
        unit, _r = unit_of(middle_ref[rows, :])
        normed[rows, :] = (unit * gain + shift).astype(bf16)
        return 0

    lax.fori_loop(0, tokens // block, second_norm, 0)
    sums[...] = jnp.zeros_like(sums)

    def dense_block(i, bias, b, _):
        k = order[i]
        rows = rows_of(b)
        low, cot = normed[rows, :], cotangent_ref[rows, :]
        hidden = dot_nt(low, weight[i % 2, 0]) + bias
        pulled = dot_nt(cot, weight[i % 2, 1])
        act, pull = gelu_and_slope(hidden)
        act = act.astype(bf16)
        turned = (pulled * pull).astype(bf16)
        active[rows, :] = act
        hidden_slope[rows, :] = turned
        sums[3 + k : 4 + k, :] += jnp.sum(turned.astype(f32), axis=0, keepdims=True)
        down = dot_nn(act, weight[i % 2, 1])
        back = dot_nn(turned, weight[i % 2, 0])
        if i == 0:
            total[rows, :] = middle_ref[rows, :] + down_bias + down
            slope[rows, :] = back
            sums[0:1, :] += jnp.sum(cot.astype(f32), axis=0, keepdims=True)
        else:
            total[rows, :] += down
            slope[rows, :] += back
        return 0

    def grad_rows(m, b, _):
        lanes = rows_of(b)
        left, right = (hidden_slope, normed) if m == 0 else (active, cotangent_ref)
        grads[m, lanes, :] = dot_tn(left[:, lanes], right[...])
        return 0

    for i in range(4):
        bias_rows = 5 + 2 * (order[i] % 2)
        lanes = slice((order[i] // 2) * HALF, (order[i] // 2 + 1) * HALF)
        bias = jnp.concatenate(
            [vector_ref[bias_rows : bias_rows + 1, lanes], vector_ref[bias_rows + 1 : bias_rows + 2, lanes]],
            axis=1,
        )
        load(i).wait()
        if i < 3:
            load(i + 1).start()
        lax.fori_loop(0, 2, functools.partial(dense_block, i, bias), 0)
        if i >= 1:
            sum_event(i - 1)
        if i >= 2:
            line_event(i - 2)
        if i >= 3:
            hop_event(i - 3, 2)
        lax.fori_loop(2, 4, functools.partial(dense_block, i, bias), 0)
        for m in range(2):
            lax.fori_loop(0, GROUP // block, functools.partial(grad_rows, m), 0)
        twin_event(i)
        if i >= 1:
            second_event(i - 1)
        if i >= 2:
            hop_event(i - 2, 1)
        if i >= 3:
            hop_event(i - 3, 3)

    def finish(b, _):
        rows = rows_of(b)
        unit, reciprocal = unit_of(middle_ref[rows, :])
        raw = slope[rows, :]
        sums[1:2, :] += jnp.sum(raw * unit, axis=0, keepdims=True)
        sums[2:3, :] += jnp.sum(raw, axis=0, keepdims=True)
        moved = cotangent_ref[rows, :].astype(f32) + norm_slope(raw, unit, reciprocal, gain)
        slope[rows, :] = moved
        low = moved.astype(bf16)
        active[rows, :] = low
        hidden_slope[rows, :] = dot_nt(low, output_ref[...]).astype(bf16)
        result_out[rows, :] = total[rows, :].astype(bf16)
        return 0

    lax.fori_loop(0, 2, finish, 0)
    sum_event(3)
    line_event(2)
    hop_event(1, 2)
    lax.fori_loop(2, 4, finish, 0)
    outs = [
        pltpu.make_async_copy(slope, slope_out, out_sem.at[0]),
        pltpu.make_async_copy(hidden_slope, blended_slope_out, out_sem.at[1]),
        pltpu.make_async_copy(grads.at[0], output_grad_out, out_sem.at[2]),
    ]
    outs[0].start()
    outs[1].start()

    def project_grad(b, _):
        lanes = rows_of(b)
        grads[0, lanes, :] = dot_tn(blended_ref[:, lanes], active[...])
        return 0

    lax.fori_loop(0, D // block, project_grad, 0)
    outs[2].start()
    sums_out[...] = sums[...]
    second_event(3)
    hop_event(2, 1)
    hop_event(1, 3)
    line_event(3)
    hop_event(2, 2)
    hop_event(3, 1)
    hop_event(3, 2)
    for copy in outs:
        copy.wait()
    for i in range(4):
        k = order[i]
        for m in range(2):
            if i >= 2:
                twin_copy(i, m).wait_send()
            first_copy(k, m).wait_send()
            second_copy(k, m).wait_send()
            if k > 0:

                @pl.when(z < k)
                def _():
                    line_copy(k, m, True).wait_send()

            if k < 3:

                @pl.when(z > k)
                def _():
                    line_copy(k, m, False).wait_send()


def dense_call(middle, cotangent, blended, output_full, vectors, full):
    tokens = middle.shape[0]
    any_spec = pl.BlockSpec(memory_space=pl.ANY)
    vmem = pl.BlockSpec(memory_space=pltpu.VMEM)
    shape = jax.ShapeDtypeStruct
    dma = pltpu.SemaphoreType.DMA
    piece = (CHUNK, HALF)
    return pl.pallas_call(
        dense_kernel,
        out_shape=(
            shape((tokens, D), bf16), shape((tokens, D), f32), shape((tokens, D), bf16),
            shape((D, D), f32), shape((8, D), f32), shape(piece, f32), shape(piece, f32),
        ),
        in_specs=[vmem] * 5 + [any_spec],
        out_specs=[vmem, any_spec, any_spec, any_spec, vmem, vmem, vmem],
        scratch_shapes=[
            pltpu.VMEM((tokens, D), bf16), pltpu.VMEM((tokens, D), f32), pltpu.VMEM((tokens, D), f32),
            pltpu.VMEM((tokens, GROUP), bf16), pltpu.VMEM((tokens, GROUP), bf16),
            pltpu.VMEM((2, 2, GROUP, D), bf16), pltpu.VMEM((2, GROUP, D), f32),
            pltpu.VMEM((2, 2, GROUP, HALF), bf16), pltpu.VMEM((4, 2, GROUP, HALF), bf16),
            pltpu.VMEM((4, 2, 2, 2) + piece, bf16),
            pltpu.VMEM((4, 2) + piece, bf16), pltpu.VMEM((4, 2) + piece, bf16),
            pltpu.VMEM((4,) + piece, bf16), pltpu.VMEM((4,) + piece, bf16),
            pltpu.VMEM((2, 4, 2) + piece, bf16), pltpu.VMEM((8, D), f32),
            dma((2,)), dma((4, 2)), dma((4, 2)), dma((4,)), dma((4,)), dma((4,)), dma((4,)),
            dma((4,)), dma((4,)), dma((4,)), dma((4,)), dma((4, 2)), dma((4, 2)), dma((2, 4, 2)),
            dma((3,)),
        ],
        compiler_params=pltpu.CompilerParams(
            collective_id=1, has_side_effects=True, vmem_limit_bytes=60 << 20
        ),
    )(middle, cotangent, blended, output_full, vectors, full)


def contract_rows(left_side, right_side):
    return dot_tn(left_side, right_side)


def norm_back(slope_rows, unit_rows, reciprocal, norm_gain):
    tilted = slope_rows * norm_gain
    centered_slope = tilted - jnp.mean(tilted, axis=-1, keepdims=True)
    centered_slope = centered_slope - unit_rows * jnp.mean(
        tilted * unit_rows, axis=-1, keepdims=True
    )
    return (
        centered_slope * reciprocal,
        jnp.sum(slope_rows * unit_rows, axis=0),
        jnp.sum(slope_rows, axis=0),
    )


def local(
    inputs, documents, mixing, value_weight, output_weight, mixer_gain, mixer_shift, dense_gain,
    dense_shift, hidden_weight, hidden_bias, down_weight, down_bias, cotangent,
):
    row_count = inputs.shape[0]
    tokens = row_count * SEQ
    shard = jnp.stack([hidden_weight.T, down_weight])
    small = jnp.stack([mixer_gain, mixer_shift, dense_gain, dense_shift, down_bias])
    vectors = jnp.concatenate(
        [small, hidden_bias.reshape(4, HALF), jnp.zeros((7, HALF), bf16)]
    ).astype(f32)
    (
        full, raised, value_full, output_full, vector_full, normed_low, values, blended, share, middle,
    ) = forward_call(
        inputs.reshape(tokens, D), documents, mixing, value_weight, output_weight, shard, vectors
    )
    gain_first = vector_full[0]
    stream = inputs.reshape(tokens, D).astype(f32)
    unit_first, recip_first = unit_of(stream)
    (
        result, middle_slope, blended_slope, output_grad, sums_two, hidden_share, down_share,
    ) = dense_call(middle, cotangent.reshape(tokens, D), blended, output_full, vector_full, full)
    hidden_share = hidden_share.T
    down_bias_sum, gain_second_sum, shift_second_sum = (sums_two[n] for n in range(3))
    hidden_bias_sum = sums_two[3:7].reshape(FF)
    value_rows = values.reshape(row_count, SEQ, D)

    def mix_back(running, bundle):
        row_values, row_docs, row_slope = bundle
        same = row_docs[:, None] == row_docs[None, :]
        chances = jnp.where(same[None], raised.astype(f32), 0.0)
        chances = chances / jnp.sum(chances, axis=-1, keepdims=True)
        per_head = row_values.reshape(SEQ, HEADS, HEAD)
        head_slope = row_slope.reshape(SEQ, HEADS, HEAD)
        chance_slope = jnp.einsum(
            "ihd,jhd->hij", head_slope, per_head, preferred_element_type=jnp.float32
        )
        score_slope = chances * (
            chance_slope - jnp.sum(chances * chance_slope, axis=-1, keepdims=True)
        )
        value_part = jnp.einsum(
            "hij,ihd->jhd",
            chances.astype(jnp.bfloat16),
            head_slope,
            preferred_element_type=jnp.float32,
        )
        return (running + score_slope, value_part.reshape(SEQ, D).astype(jnp.bfloat16))

    mixing_start = jnp.zeros((HEADS, SEQ, SEQ), jnp.float32)
    mixing_grad, value_slopes = lax.scan(
        mix_back, mixing_start, (value_rows, documents, blended_slope.reshape(row_count, SEQ, D))
    )
    value_slope = value_slopes.reshape(tokens, D)
    value_grad = contract_rows(normed_low, value_slope)
    normed_slope = dot_nt(value_slope, value_full)
    back_first, gain_first_sum, shift_first_sum = norm_back(
        normed_slope, unit_first, recip_first, gain_first
    )
    inputs_slope = (middle_slope + back_first).astype(jnp.bfloat16)

    def scatter(array, axis_name, axis):
        return lax.psum_scatter(
            array.astype(bf16), axis_name, scatter_dimension=axis, tiled=True
        ).astype(f32)

    sums = (
        (mixing_grad, 1), (value_grad, 1), (output_grad, 0), (gain_first_sum, 0),
        (shift_first_sum, 0), (gain_second_sum, 0), (shift_second_sum, 0), (hidden_bias_sum, 0),
        (down_bias_sum, 0),
    )
    totals = [
        lax.psum(scatter(one, "narrow", axis).astype(bf16), "wide").astype(f32)
        for one, axis in sums
    ]
    return (
        result.reshape(row_count, SEQ, D),
        inputs_slope.reshape(row_count, SEQ, D),
        *totals[:7], hidden_share, totals[7], down_share, totals[8],
    )


def normalize(matrix, norm_gain, norm_shift):
    average = jnp.mean(matrix, axis=-1, keepdims=True)
    center = matrix - average
    reciprocal = lax.rsqrt(jnp.mean(center * center, axis=-1, keepdims=True) + epsilon)
    unit_rows = center * reciprocal
    return (unit_rows * norm_gain + norm_shift, unit_rows, reciprocal)


def plain_norm_back(slope_rows, unit_rows, reciprocal, norm_gain):
    tilted = slope_rows * norm_gain
    centered_slope = tilted - jnp.mean(tilted, axis=-1, keepdims=True)
    centered_slope = centered_slope - unit_rows * jnp.mean(
        tilted * unit_rows, axis=-1, keepdims=True
    )
    return (
        centered_slope * reciprocal,
        jnp.sum(slope_rows * unit_rows, axis=0),
        jnp.sum(slope_rows, axis=0),
    )


def plain_contract(left_side, right_side):
    return lax.dot_general(
        left_side, right_side, (((0,), (0,)), ((), ())), preferred_element_type=jnp.float32
    )


def times_transpose(left_side, right_side):
    return lax.dot_general(
        left_side, right_side, (((1,), (1,)), ((), ())), preferred_element_type=jnp.float32
    )


def row_chances(mixing_full, row_docs):
    same_doc = row_docs[:, None] == row_docs[None, :]
    scores = jnp.where(same_doc[None, :, :], mixing_full.astype(jnp.float32), -1e30)
    row_top = jnp.max(scores, axis=-1, keepdims=True)
    raised = jnp.exp(scores - row_top)
    return raised / jnp.sum(raised, axis=-1, keepdims=True)


def plain(
    inputs,
    documents,
    mixing,
    value_weight,
    output_weight,
    mixer_gain,
    mixer_shift,
    dense_gain,
    dense_shift,
    hidden_weight,
    hidden_bias,
    down_weight,
    down_bias,
    cotangent,
):
    gathered = (
        lax.all_gather(mixing, "narrow", axis=1, tiled=True),
        lax.all_gather(value_weight, "narrow", axis=1, tiled=True),
        lax.all_gather(output_weight, "narrow", axis=0, tiled=True),
        lax.all_gather(mixer_gain, "narrow", axis=0, tiled=True),
        lax.all_gather(mixer_shift, "narrow", axis=0, tiled=True),
        lax.all_gather(dense_gain, "narrow", axis=0, tiled=True),
        lax.all_gather(dense_shift, "narrow", axis=0, tiled=True),
        lax.all_gather(hidden_bias, "narrow", axis=0, tiled=True),
        lax.all_gather(down_bias, "narrow", axis=0, tiled=True),
    )
    mixing_full, value_full, output_full = (gathered[0], gathered[1], gathered[2])
    gain_first = gathered[3].astype(jnp.float32)
    shift_first = gathered[4].astype(jnp.float32)
    gain_second = gathered[5].astype(jnp.float32)
    shift_second = gathered[6].astype(jnp.float32)
    bias_hidden = gathered[7].astype(jnp.float32)
    bias_down = gathered[8].astype(jnp.float32)
    halfway = (
        lax.all_gather(hidden_weight, "narrow", axis=0, tiled=True),
        lax.all_gather(down_weight, "narrow", axis=1, tiled=True),
    )
    hidden_full, down_full = (
        lax.all_gather(halfway[0], "wide", axis=1, tiled=True),
        lax.all_gather(halfway[1], "wide", axis=0, tiled=True),
    )
    row_count = inputs.shape[0]
    stream = inputs.reshape(row_count * SEQ, D).astype(jnp.float32)
    normed, unit_first, recip_first = normalize(stream, gain_first, shift_first)
    normed_low = normed.astype(jnp.bfloat16)
    values = jnp.dot(normed_low, value_full, preferred_element_type=jnp.float32).astype(
        jnp.bfloat16
    )
    value_rows = values.reshape(row_count, SEQ, D)

    def mix_one(bundle):
        row_values, row_docs = bundle
        chances_low = row_chances(mixing_full, row_docs).astype(jnp.bfloat16)
        per_head = row_values.reshape(SEQ, HEADS, HEAD)
        blended_row = jnp.einsum(
            "hij,jhd->ihd", chances_low, per_head, preferred_element_type=jnp.float32
        )
        return blended_row.reshape(SEQ, D).astype(jnp.bfloat16)

    blended = lax.map(mix_one, (value_rows, documents)).reshape(row_count * SEQ, D)
    middle = stream + jnp.dot(blended, output_full, preferred_element_type=jnp.float32)
    normed_two, unit_second, recip_second = normalize(middle, gain_second, shift_second)
    normed_two_low = normed_two.astype(jnp.bfloat16)
    hidden = jnp.dot(normed_two_low, hidden_full, preferred_element_type=jnp.float32) + bias_hidden
    activated, gelu_pull = jax.vjp(jax.nn.gelu, hidden)
    active = activated.astype(jnp.bfloat16)
    result = middle + jnp.dot(active, down_full, preferred_element_type=jnp.float32) + bias_down
    slope_low = cotangent.reshape(row_count * SEQ, D)
    slope_wide = slope_low.astype(jnp.float32)
    down_bias_sum = jnp.sum(slope_wide, axis=0)
    down_grad = plain_contract(active, slope_low)
    active_slope = times_transpose(slope_low, down_full)
    hidden_slope_wide = gelu_pull(active_slope)[0]
    hidden_slope = hidden_slope_wide.astype(jnp.bfloat16)
    hidden_bias_sum = jnp.sum(hidden_slope.astype(jnp.float32), axis=0)
    hidden_grad = plain_contract(normed_two_low, hidden_slope)
    normed_two_slope = times_transpose(hidden_slope, hidden_full)
    back_second, gain_second_sum, shift_second_sum = plain_norm_back(
        normed_two_slope, unit_second, recip_second, gain_second
    )
    middle_slope = slope_wide + back_second
    attended_slope = middle_slope.astype(jnp.bfloat16)
    output_grad = plain_contract(blended, attended_slope)
    blended_slope = times_transpose(attended_slope, output_full).astype(jnp.bfloat16)

    def mix_back(running, bundle):
        row_values, row_docs, row_slope = bundle
        chances = row_chances(mixing_full, row_docs)
        per_head = row_values.reshape(SEQ, HEADS, HEAD)
        head_slope = row_slope.reshape(SEQ, HEADS, HEAD)
        chance_slope = jnp.einsum(
            "ihd,jhd->hij", head_slope, per_head, preferred_element_type=jnp.float32
        )
        score_slope = chances * (
            chance_slope - jnp.sum(chances * chance_slope, axis=-1, keepdims=True)
        )
        value_part = jnp.einsum(
            "hij,ihd->jhd",
            chances.astype(jnp.bfloat16),
            head_slope,
            preferred_element_type=jnp.float32,
        )
        return (running + score_slope, value_part.reshape(SEQ, D).astype(jnp.bfloat16))

    mixing_start = jnp.zeros((HEADS, SEQ, SEQ), jnp.float32)
    mixing_grad, value_slopes = lax.scan(
        mix_back, mixing_start, (value_rows, documents, blended_slope.reshape(row_count, SEQ, D))
    )
    value_slope = value_slopes.reshape(row_count * SEQ, D)
    value_grad = plain_contract(normed_low, value_slope)
    normed_slope = times_transpose(value_slope, value_full)
    back_first, gain_first_sum, shift_first_sum = plain_norm_back(
        normed_slope, unit_first, recip_first, gain_first
    )
    inputs_slope = (middle_slope + back_first).astype(jnp.bfloat16)
    sums_half = (
        lax.psum_scatter(
            hidden_grad.astype(jnp.bfloat16), "wide", scatter_dimension=1, tiled=True
        ).astype(jnp.float32),
        lax.psum_scatter(
            down_grad.astype(jnp.bfloat16), "wide", scatter_dimension=0, tiled=True
        ).astype(jnp.float32),
    )
    hidden_share, down_share = (
        lax.psum_scatter(
            sums_half[0].astype(jnp.bfloat16), "narrow", scatter_dimension=0, tiled=True
        ).astype(jnp.float32),
        lax.psum_scatter(
            sums_half[1].astype(jnp.bfloat16), "narrow", scatter_dimension=1, tiled=True
        ).astype(jnp.float32),
    )
    shares = (
        lax.psum_scatter(
            mixing_grad.astype(jnp.bfloat16), "narrow", scatter_dimension=1, tiled=True
        ).astype(jnp.float32),
        lax.psum_scatter(
            value_grad.astype(jnp.bfloat16), "narrow", scatter_dimension=1, tiled=True
        ).astype(jnp.float32),
        lax.psum_scatter(
            output_grad.astype(jnp.bfloat16), "narrow", scatter_dimension=0, tiled=True
        ).astype(jnp.float32),
        lax.psum_scatter(
            gain_first_sum.astype(jnp.bfloat16), "narrow", scatter_dimension=0, tiled=True
        ).astype(jnp.float32),
        lax.psum_scatter(
            shift_first_sum.astype(jnp.bfloat16), "narrow", scatter_dimension=0, tiled=True
        ).astype(jnp.float32),
        lax.psum_scatter(
            gain_second_sum.astype(jnp.bfloat16), "narrow", scatter_dimension=0, tiled=True
        ).astype(jnp.float32),
        lax.psum_scatter(
            shift_second_sum.astype(jnp.bfloat16), "narrow", scatter_dimension=0, tiled=True
        ).astype(jnp.float32),
        lax.psum_scatter(
            hidden_bias_sum.astype(jnp.bfloat16), "narrow", scatter_dimension=0, tiled=True
        ).astype(jnp.float32),
        lax.psum_scatter(
            down_bias_sum.astype(jnp.bfloat16), "narrow", scatter_dimension=0, tiled=True
        ).astype(jnp.float32),
    )
    totals = (
        lax.psum(shares[0].astype(jnp.bfloat16), "wide").astype(jnp.float32),
        lax.psum(shares[1].astype(jnp.bfloat16), "wide").astype(jnp.float32),
        lax.psum(shares[2].astype(jnp.bfloat16), "wide").astype(jnp.float32),
        lax.psum(shares[3].astype(jnp.bfloat16), "wide").astype(jnp.float32),
        lax.psum(shares[4].astype(jnp.bfloat16), "wide").astype(jnp.float32),
        lax.psum(shares[5].astype(jnp.bfloat16), "wide").astype(jnp.float32),
        lax.psum(shares[6].astype(jnp.bfloat16), "wide").astype(jnp.float32),
        lax.psum(shares[7].astype(jnp.bfloat16), "wide").astype(jnp.float32),
        lax.psum(shares[8].astype(jnp.bfloat16), "wide").astype(jnp.float32),
    )
    return (
        result.reshape(row_count, SEQ, D).astype(jnp.bfloat16),
        inputs_slope.reshape(row_count, SEQ, D),
        totals[0],
        totals[1],
        totals[2],
        totals[3],
        totals[4],
        totals[5],
        totals[6],
        hidden_share,
        totals[7],
        down_share,
        totals[8],
    )


def solution(mesh):
    inner = local if dict(mesh.shape) == {"narrow": 2, "wide": 16} else plain
    return jax.shard_map(
        inner,
        mesh=mesh,
        in_specs=(
            P(("narrow", "wide"), None, None),
            P(("narrow", "wide"), None),
            P(None, "narrow", None),
            P(None, "narrow"),
            P("narrow", None),
            P("narrow"),
            P("narrow"),
            P("narrow"),
            P("narrow"),
            P("narrow", "wide"),
            P("narrow"),
            P("wide", "narrow"),
            P("narrow"),
            P(("narrow", "wide"), None, None),
        ),
        out_specs=(
            P(("narrow", "wide"), None, None),
            P(("narrow", "wide"), None, None),
            P(None, "narrow", None),
            P(None, "narrow"),
            P("narrow", None),
            P("narrow"),
            P("narrow"),
            P("narrow"),
            P("narrow"),
            P("narrow", "wide"),
            P("narrow"),
            P("wide", "narrow"),
            P("narrow"),
        ),
        check_vma=False,
    )
```

```python
import functools

import jax
import jax.numpy as jnp
from jax import lax
from jax.experimental import pallas as pl
from jax.experimental.pallas import tpu as pltpu
from jax.sharding import PartitionSpec as P

D = 768
HEADS = 12
HEAD = 64
SEQ = 512
FF = 3072
HALF = D // 2
CHUNK = 192
GROUP = 4 * CHUNK
epsilon = 1e-05

MESH = pl.DeviceIdType.MESH
f32 = jnp.float32
bf16 = jnp.bfloat16


def place():
    core = lax.axis_index("narrow")
    wide = lax.axis_index("wide")
    return core, lax.rem(wide, 2), lax.rem(lax.div(wide, 2), 2), lax.div(wide, 4)


def seat(core, x, y, z):
    return (core, z * 4 + y * 2 + x)


def remote(src, dst, send_sem, recv_sem, device):
    return pltpu.make_async_remote_copy(
        src_ref=src,
        dst_ref=dst,
        send_sem=send_sem,
        recv_sem=recv_sem,
        device_id=device,
        device_id_type=MESH,
    )


def greet(core, x, y, z, more=()):
    barrier = pltpu.get_barrier_semaphore()
    near = (seat(1 - core, x, y, z), seat(core, 1 - x, y, z), seat(core, x, 1 - y, z)) + more
    for device in near:
        pl.semaphore_signal(barrier, inc=1, device_id=device, device_id_type=MESH)

    @pl.when(z < 3)
    def _():
        pl.semaphore_signal(
            barrier, inc=1, device_id=seat(core, x, y, z + 1), device_id_type=MESH
        )

    @pl.when(z > 0)
    def _():
        pl.semaphore_signal(
            barrier, inc=1, device_id=seat(core, x, y, z - 1), device_id_type=MESH
        )

    above, below = jnp.where(z < 3, 1, 0), jnp.where(z > 0, 1, 0)
    pl.semaphore_wait(barrier, len(near) + above + below)


def halves(core):
    mine = pl.ds(pl.multiple_of(core * HALF, 128), HALF)
    other = pl.ds(pl.multiple_of((1 - core) * HALF, 128), HALF)
    return mine, other


def line_order(z, step):
    table = ((0, 1, 2, 3), (1, 0, 2, 3), (2, 3, 1, 0), (3, 2, 1, 0))
    return jnp.where(
        z == 0,
        table[0][step],
        jnp.where(z == 1, table[1][step], jnp.where(z == 2, table[2][step], table[3][step])),
    )


def unit_of(rows):
    center = rows - jnp.mean(rows, axis=-1, keepdims=True)
    reciprocal = lax.rsqrt(jnp.mean(center * center, axis=-1, keepdims=True) + epsilon)
    return center * reciprocal, reciprocal


def dot_nn(left, right):
    return lax.dot_general(left, right, (((1,), (0,)), ((), ())), preferred_element_type=f32)


def dot_nt(left, right):
    return lax.dot_general(left, right, (((1,), (1,)), ((), ())), preferred_element_type=f32)


def dot_tn(left, right):
    return lax.dot_general(left, right, (((0,), (0,)), ((), ())), preferred_element_type=f32)


def lane_ids(rows):
    return lax.broadcasted_iota(jnp.int32, (rows, 128), 1)


def fill_mask(docs_ref, mask, rows):
    for r in range(rows):
        flat = docs_ref[r : r + 1, :].astype(f32)
        for i in range(0, SEQ, 128):
            tall = jnp.broadcast_to(flat[:, i : i + 128], (128, 128)).T
            for j in range(0, SEQ, 128):
                wide = jnp.broadcast_to(flat[:, j : j + 128], (128, 128))
                mask[r, i : i + 128, j : j + 128] = jnp.where(tall == wide, 1.0, 0.0).astype(bf16)


def forward_kernel(
    x_ref, docs_ref, mixing_ref, value_ref, output_ref, shard_ref, vector_ref,
    full_ref, raised_out, value_out, output_out, vector_out, normed_out, values_out, blended_out,
    share_out, middle_out,
    raised, value_full, output_full, mask, vector_full, normed, values, blended, share, middle,
    recv, core_recv, sent_x, sent_y, sent_up, sent_down, sent_core,
    early_send, early_recv, local_sem, out_sem,
):
    core, x, y, z = place()
    mine, other = halves(core)
    near_x, near_y = seat(core, 1 - x, y, z), seat(core, x, 1 - y, z)
    above, below = seat(core, x, y, z + 1), seat(core, x, y, z - 1)
    twin = seat(1 - core, x, y, z)
    tokens = x_ref.shape[0]

    def chunk_of(k, y_of, x_of):
        return k * 4 + y_of * 2 + x_of

    def slot(m, chunk, lanes):
        rows = pl.ds(pl.multiple_of(chunk * CHUNK, CHUNK), CHUNK)
        return full_ref.at[m, rows, lanes]

    own = chunk_of(z, y, x)

    def send(m, chunk, sems, device):
        src = slot(m, chunk, mine)
        return remote(src, src, sems.at[m, chunk], recv.at[m, chunk], device)

    def send_own(m, sems, device):
        return remote(shard_ref.at[m], slot(m, own, mine), sems.at[m, own], recv.at[m, own], device)

    def send_twin(m, chunk):
        src = slot(m, chunk, mine)
        return remote(src, src, sent_core.at[m, chunk], core_recv.at[m, chunk], twin)

    def arrived(m, chunk):
        send(m, chunk, sent_x, near_x).wait_recv()

    heads_part = HEADS // 4
    my_rows = pl.ds(pl.multiple_of(core * (SEQ // 2), SEQ // 2), SEQ // 2)

    def mixing_part(p):
        heads = pl.ds(p * heads_part, heads_part)
        return mixing_ref.at[heads], raised.at[heads, my_rows]

    early = [
        (vector_ref, vector_full.at[:, mine]),
        (value_ref, value_full.at[:, mine]),
        mixing_part(0), mixing_part(1), mixing_part(2), mixing_part(3),
        (output_ref, output_full.at[mine, :]),
    ]
    greet(core, x, y, z)
    early_sends = [
        remote(src, dst, early_send.at[n], early_recv.at[n], twin)
        for n, (src, dst) in enumerate(early)
    ]
    early_local = [
        pltpu.make_async_copy(src, dst, local_sem.at[n]) for n, (src, dst) in enumerate(early)
    ]
    own_local = [
        pltpu.make_async_copy(shard_ref.at[m], slot(m, own, mine), local_sem.at[7 + m])
        for m in range(2)
    ]
    for m in range(2):
        own_local[m].start()
    send_own(0, sent_x, near_x).start()
    send_own(1, sent_y, near_y).start()

    @pl.when(z < 3)
    def _():
        for m in range(2):
            send_own(m, sent_up, above).start()

    @pl.when(z > 0)
    def _():
        for m in range(2):
            send_own(m, sent_down, below).start()

    send_own(1, sent_x, near_x).start()
    send_own(0, sent_y, near_y).start()
    for copy in early_sends:
        copy.start()
    for copy in early_local:
        copy.start()
    for m in range(2):
        own_local[m].wait()
        send_twin(m, own).start()

    def early_ready(n):
        early_local[n].wait()
        early_sends[n].wait_recv()

    def line_event(step):
        k = line_order(z, step)
        chunk = chunk_of(k, y, x)
        for m in range(2):
            arrived(m, chunk)

            @pl.when(jnp.logical_and(k < z, z < 3))
            def _():
                send(m, chunk, sent_up, above).start()

            @pl.when(jnp.logical_and(k > z, z > 0))
            def _():
                send(m, chunk, sent_down, below).start()

            if m == 0:
                send(0, chunk, sent_x, near_x).start()
            else:
                send(1, chunk, sent_y, near_y).start()
        send(1, chunk, sent_x, near_x).start()
        send(0, chunk, sent_y, near_y).start()
        for m in range(2):
            send_twin(m, chunk).start()

    def cross_event(step):
        k = line_order(z, step)
        across_x, across_y = chunk_of(k, y, 1 - x), chunk_of(k, 1 - y, x)
        arrived(0, across_x)
        send(0, across_x, sent_y, near_y).start()
        arrived(1, across_y)
        send(1, across_y, sent_x, near_x).start()
        send_twin(0, across_x).start()
        send_twin(1, across_y).start()

    def rest_event(step):
        k = line_order(z, step)
        across_x, across_y = chunk_of(k, y, 1 - x), chunk_of(k, 1 - y, x)
        arrived(1, across_x)
        send_twin(1, across_x).start()
        arrived(0, across_y)
        send_twin(0, across_y).start()

    def last_event(step):
        k = line_order(z, step)
        corner = chunk_of(k, 1 - y, 1 - x)
        for m in range(2):
            arrived(m, corner)
            send_twin(m, corner).start()

    def out_copy(n, src, dst):
        return pltpu.make_async_copy(src, dst, out_sem.at[n])

    block = 256
    early_ready(0)
    gain, shift = vector_full[0:1, :], vector_full[1:2, :]
    early_ready(1)

    def first_norm(b, _):
        rows = pl.ds(pl.multiple_of(b * block, block), block)
        unit, _r = unit_of(x_ref[rows, :].astype(f32))
        low = (unit * gain + shift).astype(bf16)
        normed[rows, :] = low
        values[rows, :] = dot_nn(low, value_full[...]).astype(bf16)
        return 0

    lax.fori_loop(0, tokens // block, first_norm, 0)
    out_normed = out_copy(0, normed, normed_out)
    out_normed.start()
    out_values = out_copy(1, values, values_out)
    out_values.start()
    out_value = out_copy(2, value_full, value_out)
    out_value.start()
    cross_event(0)
    fill_mask(docs_ref, mask, tokens // SEQ)

    def mix_pair(p, _):
        lanes = pl.ds(pl.multiple_of(p * 128, 128), 128)
        left_half = lane_ids(SEQ) < HEAD
        for i in range(0, SEQ, block):
            for half in range(2):
                h = 2 * p + half
                raised[h, i : i + block] = jnp.exp(raised[h, i : i + block].astype(f32)).astype(bf16)
        for r in range(tokens // SEQ):
            rows = pl.ds(r * SEQ, SEQ)
            pair = values[rows, lanes]
            ones = jnp.ones_like(pair)
            first = jnp.where(left_half, pair, ones)
            second = jnp.where(left_half, ones, pair)
            for i in range(0, SEQ, block):
                keep = mask[r, i : i + block]
                one = dot_nn(raised[2 * p, i : i + block] * keep, first)
                two = dot_nn(raised[2 * p + 1, i : i + block] * keep, second)
                low_lanes = left_half[:block]
                part = 1.0 / pltpu.roll(jnp.where(low_lanes, two, one), HEAD, 1)
                done = pl.ds(r * SEQ + i, block)
                share[done, lanes] = part
                blended[done, lanes] = (jnp.where(low_lanes, one, two) * part).astype(bf16)
        return 0

    for n in (2, 3):
        early_ready(n)
    lax.fori_loop(0, 3, mix_pair, 0)
    line_event(1)
    rest_event(0)
    for n in (4, 5):
        early_ready(n)
    lax.fori_loop(3, 6, mix_pair, 0)
    last_event(0)
    cross_event(1)
    outs = [
        out_copy(3, blended, blended_out), out_copy(4, share, share_out),
        out_copy(5, raised, raised_out), out_copy(6, vector_full, vector_out),
    ]
    for copy in outs:
        copy.start()
    early_ready(6)

    def project(b, _):
        rows = pl.ds(pl.multiple_of(b * block, block), block)
        middle[rows, :] = x_ref[rows, :].astype(f32) + dot_nn(blended[rows, :], output_full[...])
        return 0

    lax.fori_loop(0, tokens // block, project, 0)
    outs.append(out_copy(7, middle, middle_out))
    outs.append(out_copy(8, output_full, output_out))
    outs[-1].start()
    outs[-2].start()
    line_event(2)
    rest_event(1)
    last_event(1)
    cross_event(2)
    line_event(3)
    rest_event(2)
    last_event(2)
    cross_event(3)
    rest_event(3)
    last_event(3)

    for copy in outs + [out_normed, out_values, out_value]:
        copy.wait()
    for copy in early_sends:
        copy.wait_send()

    def settle(chunk, _):
        for m in range(2):
            copy = send_twin(m, chunk)
            copy.wait_recv()
            copy.wait_send()
        return 0

    lax.fori_loop(0, 16, settle, 0)

    def settle_line(k, _):
        line = chunk_of(k, y, x)
        for m in range(2):
            send(m, line, sent_x, near_x).wait_send()
            send(m, line, sent_y, near_y).wait_send()

            @pl.when(jnp.logical_and(k <= z, z < 3))
            def _():
                send(m, line, sent_up, above).wait_send()

            @pl.when(jnp.logical_and(k >= z, z > 0))
            def _():
                send(m, line, sent_down, below).wait_send()

        send(0, chunk_of(k, y, 1 - x), sent_y, near_y).wait_send()
        send(1, chunk_of(k, 1 - y, x), sent_x, near_x).wait_send()
        return 0

    lax.fori_loop(0, 4, settle_line, 0)


def forward_call(x, documents, mixing, value_weight, output_weight, shard, vectors):
    tokens = x.shape[0]
    rows = tokens // SEQ
    any_spec = pl.BlockSpec(memory_space=pl.ANY)
    vmem = pl.BlockSpec(memory_space=pltpu.VMEM)
    shape = jax.ShapeDtypeStruct
    dma = pltpu.SemaphoreType.DMA
    return pl.pallas_call(
        forward_kernel,
        out_shape=(
            shape((2, FF, D), bf16), shape((HEADS, SEQ, SEQ), bf16), shape((D, D), bf16),
            shape((D, D), bf16), shape((16, D), f32), shape((tokens, D), bf16),
            shape((tokens, D), bf16), shape((tokens, D), bf16), shape((tokens, D), f32),
            shape((tokens, D), f32),
        ),
        in_specs=[vmem, vmem] + [any_spec] * 5,
        out_specs=[any_spec] * 10,
        scratch_shapes=[
            pltpu.VMEM((HEADS, SEQ, SEQ), bf16), pltpu.VMEM((D, D), bf16), pltpu.VMEM((D, D), bf16),
            pltpu.VMEM((rows, SEQ, SEQ), bf16), pltpu.VMEM((16, D), f32),
            pltpu.VMEM((tokens, D), bf16), pltpu.VMEM((tokens, D), bf16),
            pltpu.VMEM((tokens, D), bf16), pltpu.VMEM((tokens, D), f32),
            pltpu.VMEM((tokens, D), f32),
            dma((2, 16)), dma((2, 16)), dma((2, 16)), dma((2, 16)), dma((2, 16)), dma((2, 16)),
            dma((2, 16)), dma((8,)), dma((8,)), dma((9,)), dma((9,)),
        ],
        compiler_params=pltpu.CompilerParams(
            collective_id=0, has_side_effects=True, vmem_limit_bytes=60 << 20
        ),
    )(x, documents, mixing, value_weight, output_weight, shard, vectors)


def gelu_and_slope(v):
    scale = 0.7978845608028654
    square = v * v
    t = jnp.tanh(scale * v * (1.0 + 0.044715 * square))
    rise = 0.5 * (1.0 + t)
    slope = rise + 0.5 * scale * v * (1.0 - t * t) * (1.0 + 3.0 * 0.044715 * square)
    return v * rise, slope


def norm_slope(slope, unit, reciprocal, gain):
    tilted = slope * gain
    centered = tilted - jnp.mean(tilted, axis=-1, keepdims=True)
    centered = centered - unit * jnp.mean(tilted * unit, axis=-1, keepdims=True)
    return centered * reciprocal


def dense_kernel(
    middle_ref, cotangent_ref, blended_ref, output_ref, vector_ref, full_ref,
    result_out, slope_out, blended_slope_out, output_grad_out, sums_out, hidden_out, down_out,
    normed, total, slope, active, hidden_slope, weight, grads, to_twin, from_twin, part,
    first_y, first_x, second_x, second_y, line_in, sums,
    weight_sem, twin_sent, twin_recv, first_y_sent, first_y_recv, first_x_sent, first_x_recv,
    second_x_sent, second_x_recv, second_y_sent, second_y_recv, up_sent, down_sent, line_recv, out_sem,
):
    core, x, y, z = place()
    mine, other = halves(core)
    near_x, near_y = seat(core, 1 - x, y, z), seat(core, x, 1 - y, z)
    above, below = seat(core, x, y, z + 1), seat(core, x, y, z - 1)
    twin = seat(1 - core, x, y, z)
    tokens = middle_ref.shape[0]
    block = 256
    order = (0, 3, 1, 2)

    def load(i):
        rows = pl.ds(order[i] * GROUP, GROUP)
        return pltpu.make_async_copy(full_ref.at[:, rows], weight.at[i % 2], weight_sem.at[i % 2])

    load(0).start()
    greet(core, x, y, z)

    def twin_copy(i, m):
        k = order[i]
        return remote(
            to_twin.at[i % 2, m], from_twin.at[k, m], twin_sent.at[k, m], twin_recv.at[k, m], twin
        )

    def first_copy(k, m):
        if m == 0:
            return remote(
                part.at[k, 0, 1 - y], first_y.at[k], first_y_sent.at[k], first_y_recv.at[k], near_y
            )
        return remote(
            part.at[k, 1, :, 1 - x], first_x.at[k], first_x_sent.at[k], first_x_recv.at[k], near_x
        )

    def second_copy(k, m):
        if m == 0:
            return remote(
                part.at[k, 0, y, 1 - x], second_x.at[k], second_x_sent.at[k], second_x_recv.at[k], near_x
            )
        return remote(
            part.at[k, 1, 1 - y, x], second_y.at[k], second_y_sent.at[k], second_y_recv.at[k], near_y
        )

    def line_copy(k, m, up):
        src = part.at[k, m, y, x]
        if up:
            return remote(src, line_in.at[0, k, m], up_sent.at[k, m], line_recv.at[0, k, m], above)
        return remote(src, line_in.at[1, k, m], down_sent.at[k, m], line_recv.at[1, k, m], below)

    def add_in(k, m, y_of, x_of, got):
        part[k, m, y_of, x_of] = (part[k, m, y_of, x_of].astype(f32) + got.astype(f32)).astype(bf16)

    def twin_event(i):
        for m in range(2):
            if i >= 2:
                twin_copy(i - 2, m).wait_send()
            to_twin[i % 2, m] = grads[m, :, other].astype(bf16)
            twin_copy(i, m).start()

    def sum_event(i):
        k = order[i]
        for m in range(2):
            twin_copy(i, m).wait_recv()
            both = grads[m, :, mine] + from_twin[k, m].astype(f32)
            part[k, m] = both.astype(bf16).reshape(2, 2, CHUNK, HALF)
            first_copy(k, m).start()

    def second_event(i):
        k = order[i]
        first_copy(k, 0).wait_recv()
        add_in(k, 0, y, 1 - x, first_y[k, 1 - x])
        second_copy(k, 0).start()
        first_copy(k, 1).wait_recv()
        add_in(k, 1, 1 - y, x, first_x[k, 1 - y])
        second_copy(k, 1).start()
        add_in(k, 0, y, x, first_y[k, x])
        add_in(k, 1, y, x, first_x[k, y])

    def line_event(i):
        k = order[i]
        second_copy(k, 0).wait_recv()
        add_in(k, 0, y, x, second_x[k])
        second_copy(k, 1).wait_recv()
        add_in(k, 1, y, x, second_y[k])
        hop_event(i, 0)

    def hop_event(i, hop):
        k = order[i]
        if hop < k:

            @pl.when(z == hop)
            def _():
                for m in range(2):
                    if hop > 0:
                        line_copy(k, m, True).wait_recv()
                        add_in(k, m, y, x, line_in[0, k, m])
                    line_copy(k, m, True).start()

        if hop < 3 - k:

            @pl.when(z == 3 - hop)
            def _():
                for m in range(2):
                    if hop > 0:
                        line_copy(k, m, False).wait_recv()
                        add_in(k, m, y, x, line_in[1, k, m])
                    line_copy(k, m, False).start()

        if hop == max(k, 3 - k):

            @pl.when(z == k)
            def _():
                for m, out in enumerate((hidden_out, down_out)):
                    both = part[k, m, y, x].astype(f32)
                    if k > 0:
                        line_copy(k, m, True).wait_recv()
                        both = both + line_in[0, k, m].astype(f32)
                    if k < 3:
                        line_copy(k, m, False).wait_recv()
                        both = both + line_in[1, k, m].astype(f32)
                    out[...] = both

    gain, shift, down_bias = vector_ref[2:3, :], vector_ref[3:4, :], vector_ref[4:5, :]

    def rows_of(b):
        return pl.ds(pl.multiple_of(b * block, block), block)

    def second_norm(b, _):
        rows = rows_of(b)
        unit, _r = unit_of(middle_ref[rows, :])
        normed[rows, :] = (unit * gain + shift).astype(bf16)
        return 0

    lax.fori_loop(0, tokens // block, second_norm, 0)
    sums[...] = jnp.zeros_like(sums)

    def dense_block(i, bias, b, _):
        k = order[i]
        rows = rows_of(b)
        low, cot = normed[rows, :], cotangent_ref[rows, :]
        hidden = dot_nt(low, weight[i % 2, 0]) + bias
        pulled = dot_nt(cot, weight[i % 2, 1])
        act, pull = gelu_and_slope(hidden)
        act = act.astype(bf16)
        turned = (pulled * pull).astype(bf16)
        active[rows, :] = act
        hidden_slope[rows, :] = turned
        sums[3 + k : 4 + k, :] += jnp.sum(turned.astype(f32), axis=0, keepdims=True)
        down = dot_nn(act, weight[i % 2, 1])
        back = dot_nn(turned, weight[i % 2, 0])
        if i == 0:
            total[rows, :] = middle_ref[rows, :] + down_bias + down
            slope[rows, :] = back
            sums[0:1, :] += jnp.sum(cot.astype(f32), axis=0, keepdims=True)
        else:
            total[rows, :] += down
            slope[rows, :] += back
        return 0

    def grad_rows(m, b, _):
        lanes = rows_of(b)
        left, right = (hidden_slope, normed) if m == 0 else (active, cotangent_ref)
        grads[m, lanes, :] = dot_tn(left[:, lanes], right[...])
        return 0

    for i in range(4):
        bias_rows = 5 + 2 * (order[i] % 2)
        lanes = slice((order[i] // 2) * HALF, (order[i] // 2 + 1) * HALF)
        bias = jnp.concatenate(
            [vector_ref[bias_rows : bias_rows + 1, lanes], vector_ref[bias_rows + 1 : bias_rows + 2, lanes]],
            axis=1,
        )
        load(i).wait()
        if i < 3:
            load(i + 1).start()
        lax.fori_loop(0, 2, functools.partial(dense_block, i, bias), 0)
        if i >= 1:
            sum_event(i - 1)
        if i >= 2:
            line_event(i - 2)
        if i >= 3:
            hop_event(i - 3, 2)
        lax.fori_loop(2, 4, functools.partial(dense_block, i, bias), 0)
        for m in range(2):
            lax.fori_loop(0, GROUP // block, functools.partial(grad_rows, m), 0)
        twin_event(i)
        if i >= 1:
            second_event(i - 1)
        if i >= 2:
            hop_event(i - 2, 1)
        if i >= 3:
            hop_event(i - 3, 3)

    def finish(b, _):
        rows = rows_of(b)
        unit, reciprocal = unit_of(middle_ref[rows, :])
        raw = slope[rows, :]
        sums[1:2, :] += jnp.sum(raw * unit, axis=0, keepdims=True)
        sums[2:3, :] += jnp.sum(raw, axis=0, keepdims=True)
        moved = cotangent_ref[rows, :].astype(f32) + norm_slope(raw, unit, reciprocal, gain)
        slope[rows, :] = moved
        low = moved.astype(bf16)
        active[rows, :] = low
        hidden_slope[rows, :] = dot_nt(low, output_ref[...]).astype(bf16)
        result_out[rows, :] = total[rows, :].astype(bf16)
        return 0

    lax.fori_loop(0, 2, finish, 0)
    sum_event(3)
    line_event(2)
    hop_event(1, 2)
    lax.fori_loop(2, 4, finish, 0)
    outs = [
        pltpu.make_async_copy(slope, slope_out, out_sem.at[0]),
        pltpu.make_async_copy(hidden_slope, blended_slope_out, out_sem.at[1]),
        pltpu.make_async_copy(grads.at[0], output_grad_out, out_sem.at[2]),
    ]
    outs[0].start()
    outs[1].start()

    def project_grad(b, _):
        lanes = rows_of(b)
        grads[0, lanes, :] = dot_tn(blended_ref[:, lanes], active[...])
        return 0

    lax.fori_loop(0, D // block, project_grad, 0)
    outs[2].start()
    sums_out[...] = sums[...]
    second_event(3)
    hop_event(2, 1)
    hop_event(1, 3)
    line_event(3)
    hop_event(2, 2)
    hop_event(3, 1)
    hop_event(3, 2)
    for copy in outs:
        copy.wait()
    for i in range(4):
        k = order[i]
        for m in range(2):
            if i >= 2:
                twin_copy(i, m).wait_send()
            first_copy(k, m).wait_send()
            second_copy(k, m).wait_send()
            if k > 0:

                @pl.when(z < k)
                def _():
                    line_copy(k, m, True).wait_send()

            if k < 3:

                @pl.when(z > k)
                def _():
                    line_copy(k, m, False).wait_send()


def dense_call(middle, cotangent, blended, output_full, vectors, full):
    tokens = middle.shape[0]
    any_spec = pl.BlockSpec(memory_space=pl.ANY)
    vmem = pl.BlockSpec(memory_space=pltpu.VMEM)
    shape = jax.ShapeDtypeStruct
    dma = pltpu.SemaphoreType.DMA
    piece = (CHUNK, HALF)
    return pl.pallas_call(
        dense_kernel,
        out_shape=(
            shape((tokens, D), bf16), shape((tokens, D), f32), shape((tokens, D), bf16),
            shape((D, D), f32), shape((8, D), f32), shape(piece, f32), shape(piece, f32),
        ),
        in_specs=[vmem] * 5 + [any_spec],
        out_specs=[vmem, any_spec, any_spec, any_spec, vmem, vmem, vmem],
        scratch_shapes=[
            pltpu.VMEM((tokens, D), bf16), pltpu.VMEM((tokens, D), f32), pltpu.VMEM((tokens, D), f32),
            pltpu.VMEM((tokens, GROUP), bf16), pltpu.VMEM((tokens, GROUP), bf16),
            pltpu.VMEM((2, 2, GROUP, D), bf16), pltpu.VMEM((2, GROUP, D), f32),
            pltpu.VMEM((2, 2, GROUP, HALF), bf16), pltpu.VMEM((4, 2, GROUP, HALF), bf16),
            pltpu.VMEM((4, 2, 2, 2) + piece, bf16),
            pltpu.VMEM((4, 2) + piece, bf16), pltpu.VMEM((4, 2) + piece, bf16),
            pltpu.VMEM((4,) + piece, bf16), pltpu.VMEM((4,) + piece, bf16),
            pltpu.VMEM((2, 4, 2) + piece, bf16), pltpu.VMEM((8, D), f32),
            dma((2,)), dma((4, 2)), dma((4, 2)), dma((4,)), dma((4,)), dma((4,)), dma((4,)),
            dma((4,)), dma((4,)), dma((4,)), dma((4,)), dma((4, 2)), dma((4, 2)), dma((2, 4, 2)),
            dma((3,)),
        ],
        compiler_params=pltpu.CompilerParams(
            collective_id=1, has_side_effects=True, vmem_limit_bytes=60 << 20
        ),
    )(middle, cotangent, blended, output_full, vectors, full)


class Reduce:
    def __init__(self, part, refs):
        self.part = part
        (
            self.first_y, self.first_x, self.second_x, self.second_y, self.line_in,
            self.first_sent, self.first_recv, self.second_sent, self.second_recv,
            self.line_sent, self.line_recv,
        ) = refs
        core, x, y, z = place()
        self.x, self.y, self.z = x, y, z
        self.near_x, self.near_y = seat(core, 1 - x, y, z), seat(core, x, 1 - y, z)
        self.above, self.below = seat(core, x, y, z + 1), seat(core, x, y, z - 1)

    @staticmethod
    def scratch(piece):
        dma = pltpu.SemaphoreType.DMA
        return [
            pltpu.VMEM((4, 2) + piece, bf16), pltpu.VMEM((4, 2) + piece, bf16),
            pltpu.VMEM((4,) + piece, bf16), pltpu.VMEM((4,) + piece, bf16),
            pltpu.VMEM((2, 4, 2) + piece, bf16),
            dma((4, 2)), dma((4, 2)), dma((4, 2)), dma((4, 2)), dma((2, 4, 2)), dma((2, 4, 2)),
        ]

    def first_copy(self, k, m):
        sems = self.first_sent.at[k, m], self.first_recv.at[k, m]
        if m == 0:
            return remote(self.part.at[k, 0, 1 - self.y], self.first_y.at[k], *sems, self.near_y)
        return remote(self.part.at[k, 1, :, 1 - self.x], self.first_x.at[k], *sems, self.near_x)

    def second_copy(self, k, m):
        x, y = self.x, self.y
        sems = self.second_sent.at[k, m], self.second_recv.at[k, m]
        if m == 0:
            return remote(self.part.at[k, 0, y, 1 - x], self.second_x.at[k], *sems, self.near_x)
        return remote(self.part.at[k, 1, 1 - y, x], self.second_y.at[k], *sems, self.near_y)

    def line_copy(self, k, m, down):
        return remote(
            self.part.at[k, m, self.y, self.x], self.line_in.at[down, k, m],
            self.line_sent.at[down, k, m], self.line_recv.at[down, k, m],
            self.below if down else self.above,
        )

    def add_in(self, k, m, y_of, x_of, got):
        old = self.part[k, m, y_of, x_of].astype(f32)
        self.part[k, m, y_of, x_of] = (old + got.astype(f32)).astype(bf16)

    def first(self, k):
        for m in range(2):
            self.first_copy(k, m).start()

    def second(self, k):
        x, y = self.x, self.y
        self.first_copy(k, 0).wait_recv()
        self.add_in(k, 0, y, 1 - x, self.first_y[k, 1 - x])
        self.second_copy(k, 0).start()
        self.first_copy(k, 1).wait_recv()
        self.add_in(k, 1, 1 - y, x, self.first_x[k, 1 - y])
        self.second_copy(k, 1).start()
        self.add_in(k, 0, y, x, self.first_y[k, x])
        self.add_in(k, 1, y, x, self.first_x[k, y])

    def line(self, k):
        for m, got in enumerate((self.second_x, self.second_y)):
            self.second_copy(k, m).wait_recv()
            self.add_in(k, m, self.y, self.x, got[k])
        self.hop(k, 0)

    def hop(self, k, hop):
        x, y, z = self.x, self.y, self.z
        for down, length, seat_z in ((0, k, hop), (1, 3 - k, 3 - hop)):
            if hop < length:

                @pl.when(z == seat_z)
                def _():
                    for m in range(2):
                        if hop > 0:
                            self.line_copy(k, m, down).wait_recv()
                            self.add_in(k, m, y, x, self.line_in[down, k, m])
                        self.line_copy(k, m, down).start()

        if hop == max(k, 3 - k):

            @pl.when(z == k)
            def _():
                for m in range(2):
                    for down, length in ((0, k), (1, 3 - k)):
                        if length > 0:
                            self.line_copy(k, m, down).wait_recv()
                            self.add_in(k, m, y, x, self.line_in[down, k, m])

    def settle(self, k):
        for m in range(2):
            self.first_copy(k, m).wait_send()
            self.second_copy(k, m).wait_send()
            if k > 0:

                @pl.when(self.z < k)
                def _():
                    self.line_copy(k, m, 0).wait_send()

            if k < 3:

                @pl.when(self.z > k)
                def _():
                    self.line_copy(k, m, 1).wait_send()


class Gather:
    def __init__(self, whole, refs):
        self.whole = whole
        self.recv, self.sent_x, self.sent_y, self.sent_z = refs
        core, x, y, z = place()
        self.x, self.y, self.z = x, y, z
        self.near_x, self.near_y = seat(core, 1 - x, y, z), seat(core, x, 1 - y, z)
        self.above, self.below = seat(core, x, y, z + 1), seat(core, x, y, z - 1)

    @staticmethod
    def scratch(piece):
        dma = pltpu.SemaphoreType.DMA
        return [
            pltpu.VMEM((4, 2, 2, 2) + piece, bf16),
            dma((4, 2, 2, 2)), dma((4, 2, 2)), dma((4, 2, 2)), dma((2, 4, 2)),
        ]

    def send(self, k, m, y_of, x_of, sem, device):
        src = self.whole.at[k, m, y_of, x_of]
        return remote(src, src, sem, self.recv.at[k, m, y_of, x_of], device)

    def to_x(self, k, m, y_of):
        return self.send(k, m, y_of, self.x, self.sent_x.at[k, m, y_of], self.near_x)

    def to_y(self, k, m, x_of):
        return self.send(k, m, self.y, x_of, self.sent_y.at[k, m, x_of], self.near_y)

    def along(self, k, m, down):
        device = self.below if down else self.above
        return self.send(k, m, self.y, self.x, self.sent_z.at[down, k, m], device)

    def arrived(self, k, m, y_of, x_of):
        self.send(k, m, y_of, x_of, self.sent_x.at[k, m, 0], self.near_x).wait_recv()

    def line(self, k, part):
        x, y, z = self.x, self.y, self.z

        @pl.when(z == k)
        def _():
            for m in range(2):
                self.whole[k, m, y, x] = part[k, m, y, x]
                if k < 3:
                    self.along(k, m, 0).start()
                if k > 0:
                    self.along(k, m, 1).start()

        @pl.when(z != k)
        def _():
            for m in range(2):
                self.arrived(k, m, y, x)
                if k < 2:

                    @pl.when(jnp.logical_and(z > k, z < 3))
                    def _():
                        self.along(k, m, 0).start()

                if k > 1:

                    @pl.when(jnp.logical_and(z < k, z > 0))
                    def _():
                        self.along(k, m, 1).start()

        self.to_x(k, 0, y).start()
        self.to_y(k, 1, x).start()
        self.to_x(k, 1, y).start()
        self.to_y(k, 0, x).start()

    def cross(self, k):
        x, y = self.x, self.y
        self.arrived(k, 0, y, 1 - x)
        self.to_y(k, 0, 1 - x).start()
        self.arrived(k, 1, 1 - y, x)
        self.to_x(k, 1, 1 - y).start()

    def rest(self, k):
        x, y, z = self.x, self.y, self.z
        self.arrived(k, 1, y, 1 - x)
        self.arrived(k, 0, 1 - y, x)
        for m in range(2):
            self.arrived(k, m, 1 - y, 1 - x)
            self.to_x(k, m, y).wait_send()
            self.to_y(k, m, x).wait_send()
            if k < 3:

                @pl.when(jnp.logical_and(z >= k, z < 3))
                def _():
                    self.along(k, m, 0).wait_send()

            if k > 0:

                @pl.when(jnp.logical_and(z <= k, z > 0))
                def _():
                    self.along(k, m, 1).wait_send()

        self.to_y(k, 0, 1 - x).wait_send()
        self.to_x(k, 1, 1 - y).wait_send()


BLOCKS = (
    ((0, 0), (0, 1), (0, 2), (1, 0), (1, 1), (1, 2), (1, 3)),
    ((0, 0), (0, 1), (0, 2), (0, 3), (1, 1), (1, 2), (1, 3)),
)
TRIPLE = HEADS // 4
MIX_PIECE = (TRIPLE, 7, 16, 128)
WEIGHT_PIECE = (48, HALF)


def backward_kernel(
    raised_ref, docs_ref, values_ref, blended_ref, share_ref, slope_ref, output_grad_ref, normed_ref,
    value_ref, x_ref, middle_slope_ref, sums_ref, vector_ref,
    inputs_out, mixing_out, weights_out, sums_out, *scratch,
):
    scratch = list(scratch)

    def take(n):
        got = scratch[:n]
        del scratch[:n]
        return got

    mask, raised, chance, scaled, scaled_t, value_t, value_slope, grads = take(8)
    half, mix_from, weights_to, weights_from, weights_part, small, small_in = take(7)
    raised_sem, mix_sent, mix_recv, weights_sent, weights_recv, small_sent, small_recv = take(7)
    mix_reduce_refs = take(11)
    weights_reduce_refs = take(11)
    mix_whole, *mix_gather_refs = take(5)
    weights_whole, *weights_gather_refs = take(5)

    core, x, y, z = place()
    mine, other = halves(core)
    twin = seat(1 - core, x, y, z)
    tokens = x_ref.shape[0]
    rows_count = tokens // SEQ
    block = 256
    order = (0, 3, 1, 2)
    mix_part = half.at[core]
    mix = Reduce(mix_part, mix_reduce_refs)
    weights = Reduce(weights_part, weights_reduce_refs)
    mix_all = Gather(mix_whole, mix_gather_refs)
    weights_all = Gather(weights_whole, weights_gather_refs)

    def load(h, buffer):
        return pltpu.make_async_copy(raised_ref.at[h], raised.at[buffer], raised_sem.at[buffer])

    load(order[0] * TRIPLE, 0).start()
    pairs = (seat(core, x, y, z + 1 - 2 * lax.rem(z, 2)), seat(core, x, y, lax.rem(z + 2, 4)))
    rounds = (twin, seat(core, 1 - x, y, z), seat(core, x, 1 - y, z)) + pairs
    greet(core, x, y, z, (pairs[1],))
    fill_mask(docs_ref, mask, rows_count)

    def scale_pair(p, _):
        lanes = pl.ds(pl.multiple_of(p * 128, 128), 128)
        for r in range(rows_count):
            rows = pl.ds(r * SEQ, SEQ)
            low = (slope_ref[rows, lanes].astype(f32) * share_ref[rows, lanes]).astype(bf16)
            scaled[rows, lanes] = low
            scaled_t[lanes, rows] = low.T
        return 0

    lax.fori_loop(0, HEADS // 2, scale_pair, 0)

    def head(k, first, last, n, _):
        hh = n
        h = k * TRIPLE + n
        buffer = lax.rem(first + n, 2)
        load(h, buffer).wait()

        if last is None:

            @pl.when(n < TRIPLE - 1)
            def _():
                load(h + 1, 1 - buffer).start()

        else:
            load(jnp.where(n < TRIPLE - 1, h + 1, last), 1 - buffer).start()

        lanes = pl.ds(pl.multiple_of(lax.div(h, 2) * 128, 128), 128)
        side = lax.rem(h, 2)
        lane = lane_ids(SEQ)
        inside = lax.div(lane, HEAD) == side
        spot = lane - HEAD * (1 - side)
        lefts, rights = [], []
        for r in range(rows_count):
            rows = pl.ds(r * SEQ, SEQ)
            low = scaled[rows, lanes]
            wide = low.astype(f32)
            delta = jnp.sum(
                jnp.where(inside, wide * blended_ref[rows, lanes].astype(f32), 0.0),
                axis=-1, keepdims=True,
            )
            coarse = delta.astype(bf16).astype(f32)
            fine = delta - coarse
            extra = jnp.where(spot == 0, -coarse, jnp.where(spot == 1, -fine, 0.0))
            lefts.append(jnp.where(inside, wide, extra).astype(bf16))
            pair = values_ref[rows, lanes]
            rights.append(jnp.where(inside, pair.astype(f32), 1.0).astype(bf16))
        for i in range(0, SEQ, block):
            total = None
            for r in range(rows_count):
                part = raised[buffer, i : i + block] * mask[r, i : i + block]
                chance[r, i : i + block] = part
                term = part.astype(f32) * dot_nt(lefts[r][i : i + block], rights[r])
                total = term if total is None else total + term
            total = total.astype(bf16)
            for p, (row, column) in enumerate(BLOCKS[i // block]):
                for q in range(8):
                    start = row * 128 + q * 16
                    half[i // block, k, q % 2, q // 4, (q // 2) % 2, hh, p] = total[
                        start : start + 16, column * 128 : column * 128 + 128
                    ]
        for r in range(rows_count):
            rows = pl.ds(pl.multiple_of(h * HEAD, HEAD), HEAD)
            value_t[rows, r * SEQ : (r + 1) * SEQ] = dot_nn(
                scaled_t[rows, r * SEQ : (r + 1) * SEQ], chance[r]
            ).astype(bf16)
        return 0

    def mix_twin(k):
        return remote(half.at[1 - core, k], mix_from.at[k], mix_sent.at[k], mix_recv.at[k], twin)

    def mix_sum(k):
        mix_twin(k).wait_recv()
        for m in range(2):
            for y_of in range(2):
                for x_of in range(2):
                    mix.add_in(k, m, y_of, x_of, mix_from[k, m, y_of, x_of])
        mix.first(k)

    for i in range(4):
        k = order[i]
        last = order[i + 1] * TRIPLE if i < 3 else None
        lax.fori_loop(0, TRIPLE, functools.partial(head, k, TRIPLE * i, last), 0)
        mix_twin(k).start()
        if i >= 1:
            mix_sum(order[i - 1])
        if i >= 2:
            (mix.second, mix.line)[i - 2](order[0])

    def turn(p, _):
        lanes = pl.ds(pl.multiple_of(p * 128, 128), 128)
        value_slope[:, lanes] = value_t[lanes, :].T
        return 0

    lax.fori_loop(0, D // 128, turn, 0)
    mix_sum(order[3])

    def rows_of(b):
        return pl.ds(pl.multiple_of(b * block, block), block)

    def value_rows(b, _):
        lanes = rows_of(b)
        grads[lanes, :] = dot_tn(normed_ref[:, lanes], value_slope[...])
        return 0

    lax.fori_loop(0, D // block, value_rows, 0)
    other_rows = pl.ds(pl.multiple_of((1 - core) * HALF, HALF), HALF)
    my_rows = pl.ds(pl.multiple_of(core * HALF, HALF), HALF)
    weights_to[0] = grads[:, other].astype(bf16)
    for side in range(2):
        weights_to[1, side * HALF : (side + 1) * HALF] = output_grad_ref[
            other_rows, side * HALF : (side + 1) * HALF
        ].astype(bf16)
    weights_twin = remote(weights_to, weights_from, weights_sent, weights_recv, twin)
    weights_twin.start()
    small[0] = jnp.zeros_like(small[0])
    small[0, 0:8] = sums_ref[...]
    gain = vector_ref[0:1, :]

    def finish(b, _):
        rows = rows_of(b)
        back = dot_nt(value_slope[rows, :], value_ref[...])
        unit, reciprocal = unit_of(x_ref[rows, :].astype(f32))
        small[0, 7:8, :] += jnp.sum(back * unit, axis=0, keepdims=True)
        small[0, 8:9, :] += jnp.sum(back, axis=0, keepdims=True)
        moved = middle_slope_ref[rows, :] + norm_slope(back, unit, reciprocal, gain)
        inputs_out[rows, :] = moved.astype(bf16)
        return 0

    def small_copy(n):
        return remote(small.at[n], small_in.at[n], small_sent.at[n], small_recv.at[n], rounds[n])

    def small_sum(n):
        small_copy(n).wait_recv()
        small[n + 1] = small[n] + small_in[n]
        if n + 1 < len(rounds):
            small_copy(n + 1).start()

    mix.second(order[1])
    lax.fori_loop(0, 2, finish, 0)
    mix.hop(order[0], 1)
    lax.fori_loop(2, 4, finish, 0)
    small_copy(0).start()
    weights_twin.wait_recv()
    share_rows = D // 4
    for k in range(4):
        rows = slice(k * share_rows, (k + 1) * share_rows)
        own = pl.ds(pl.multiple_of(core * HALF + (k % 2) * share_rows, 64), share_rows)
        side = slice((k // 2) * HALF, (k // 2 + 1) * HALF)
        shape = (2, 2) + WEIGHT_PIECE
        first = grads[rows, mine] + weights_from[0, rows].astype(f32)
        weights_part[k, 0] = first.astype(bf16).reshape(shape)
        second = output_grad_ref[own, side] + weights_from[1, rows].astype(f32)
        weights_part[k, 1] = second.astype(bf16).reshape(shape)
        weights.first(k)
    mix.line(order[1])
    small_sum(0)
    mix.hop(order[0], 2)
    mix.second(order[2])
    mix.hop(order[1], 1)
    small_sum(1)
    mix.line(order[2])
    mix.hop(order[0], 3)
    mix_all.line(order[0], mix_part)
    small_sum(2)
    mix.hop(order[1], 2)
    mix.second(order[3])
    mix.hop(order[2], 1)
    small_sum(3)
    mix.line(order[3])
    mix.hop(order[1], 3)
    mix_all.line(order[1], mix_part)
    small_sum(4)
    mix.hop(order[2], 2)
    mix_all.line(order[2], mix_part)
    mix_all.cross(order[0])
    mix.hop(order[3], 1)
    for k in range(4):
        weights.second(k)
    mix.hop(order[3], 2)
    mix_all.line(order[3], mix_part)
    mix_all.cross(order[1])
    for k in range(4):
        weights.line(k)
    mix_all.cross(order[2])
    for k in range(4):
        weights.hop(k, 1)
    mix_all.cross(order[3])
    for k in range(4):
        weights.hop(k, 2)

    def mixing_copy(k):
        return pltpu.make_async_copy(mix_whole.at[k], mixing_out.at[k], raised_sem.at[2 + k])

    mix_all.rest(order[0])
    mixing_copy(order[0]).start()
    for k in range(4):
        weights.hop(k, 3)
        weights_all.line(k, weights_part)
    mix_all.rest(order[1])
    mixing_copy(order[1]).start()
    for k in range(4):
        weights_all.cross(k)
    for k in order[2:]:
        mix_all.rest(k)
        mixing_copy(k).start()
    for k in range(4):
        weights_all.rest(k)
    weights_out[...] = weights_whole[...]
    for n, row in enumerate((0, 1, 2, 7, 8)):
        sums_out[n : n + 1, :] = small[5, row : row + 1, mine]
    for n in range(4):
        line = pl.ds(3 + 2 * core + n // 2, 1)
        sums_out[5 + n : 6 + n, :] = small[5, line, (n % 2) * HALF : (n % 2 + 1) * HALF]
    sums_out[9:16, :] = jnp.zeros((7, HALF), f32)
    for n in range(5):
        small_copy(n).wait_send()
    weights_twin.wait_send()
    for k in range(4):
        mix_twin(k).wait_send()
        mix.settle(k)
        weights.settle(k)
        mixing_copy(k).wait()


def backward_call(
    raised, documents, values, blended, share, slope, output_grad, normed, value_full, x,
    middle_slope, sums, vectors,
):
    tokens = x.shape[0]
    rows = tokens // SEQ
    any_spec = pl.BlockSpec(memory_space=pl.ANY)
    vmem = pl.BlockSpec(memory_space=pltpu.VMEM)
    shape = jax.ShapeDtypeStruct
    dma = pltpu.SemaphoreType.DMA
    return pl.pallas_call(
        backward_kernel,
        out_shape=(
            shape((tokens, D), bf16), shape((4, 2, 2, 2) + MIX_PIECE, bf16),
            shape((4, 2, 2, 2) + WEIGHT_PIECE, bf16), shape((16, HALF), f32),
        ),
        in_specs=[any_spec] + [vmem] * 12,
        out_specs=[vmem, any_spec, vmem, vmem],
        scratch_shapes=[
            pltpu.VMEM((rows, SEQ, SEQ), bf16), pltpu.VMEM((2, SEQ, SEQ), bf16),
            pltpu.VMEM((rows, SEQ, SEQ), bf16), pltpu.VMEM((tokens, D), bf16),
            pltpu.VMEM((D, tokens), bf16), pltpu.VMEM((D, tokens), bf16),
            pltpu.VMEM((tokens, D), bf16), pltpu.VMEM((D, D), f32),
            pltpu.VMEM((2, 4, 2, 2, 2) + MIX_PIECE, bf16), pltpu.VMEM((4, 2, 2, 2) + MIX_PIECE, bf16),
            pltpu.VMEM((2, D, HALF), bf16), pltpu.VMEM((2, D, HALF), bf16),
            pltpu.VMEM((4, 2, 2, 2) + WEIGHT_PIECE, bf16),
            pltpu.VMEM((6, 16, D), f32), pltpu.VMEM((5, 16, D), f32),
            dma((6,)), dma((4,)), dma((4,)), dma, dma, dma((5,)), dma((5,)),
            *Reduce.scratch(MIX_PIECE), *Reduce.scratch(WEIGHT_PIECE),
            *Gather.scratch(MIX_PIECE), *Gather.scratch(WEIGHT_PIECE),
        ],
        compiler_params=pltpu.CompilerParams(
            collective_id=2, has_side_effects=True, vmem_limit_bytes=62 << 20
        ),
    )(
        raised, documents, values, blended, share, slope, output_grad, normed, value_full, x,
        middle_slope, sums, vectors,
    )


def local(
    inputs, documents, mixing, value_weight, output_weight, mixer_gain, mixer_shift, dense_gain,
    dense_shift, hidden_weight, hidden_bias, down_weight, down_bias, cotangent,
):
    row_count = inputs.shape[0]
    tokens = row_count * SEQ
    shard = jnp.stack([hidden_weight.T, down_weight])
    small = jnp.stack([mixer_gain, mixer_shift, dense_gain, dense_shift, down_bias])
    vectors = jnp.concatenate(
        [small, hidden_bias.reshape(4, HALF), jnp.zeros((7, HALF), bf16)]
    ).astype(f32)
    (
        full, raised, value_full, output_full, vector_full, normed_low, values, blended, share, middle,
    ) = forward_call(
        inputs.reshape(tokens, D), documents, mixing, value_weight, output_weight, shard, vectors
    )
    (
        result, middle_slope, blended_slope, output_grad, sums_two, hidden_share, down_share,
    ) = dense_call(middle, cotangent.reshape(tokens, D), blended, output_full, vector_full, full)
    hidden_share = hidden_share.T
    inputs_slope, mixing_packed, weights_packed, sums = backward_call(
        raised, documents, values, blended, share, blended_slope, output_grad, normed_low,
        value_full, inputs.reshape(tokens, D), middle_slope, sums_two, vector_full,
    )
    blocks = mixing_packed.transpose(0, 4, 5, 2, 3, 1, 6, 7).reshape(HEADS, 7, 128, 128)
    blocks = blocks.astype(f32)
    nothing = jnp.zeros((HEADS, 128, 128), f32)

    def lay(half):
        found = {spot: blocks[:, n] for n, spot in enumerate(BLOCKS[half])}
        rows = [
            jnp.concatenate([found.get((row, column), nothing) for column in range(4)], axis=2)
            for row in range(2)
        ]
        return jnp.concatenate(rows, axis=1)

    mixing_grad = jnp.where(lax.axis_index("narrow") == 0, lay(0), lay(1))
    value_grad = weights_packed[:, 0].reshape(D, HALF).astype(f32)
    output_grad = weights_packed[:, 1].reshape(2, HALF, HALF).swapaxes(0, 1).reshape(HALF, D)
    shape = inputs.shape
    return (
        result.reshape(shape), inputs_slope.reshape(shape), mixing_grad, value_grad,
        output_grad.astype(f32), sums[3], sums[4], sums[1], sums[2], hidden_share,
        sums[5:9].reshape(4 * HALF), down_share, sums[0],
    )


def normalize(matrix, norm_gain, norm_shift):
    average = jnp.mean(matrix, axis=-1, keepdims=True)
    center = matrix - average
    reciprocal = lax.rsqrt(jnp.mean(center * center, axis=-1, keepdims=True) + epsilon)
    unit_rows = center * reciprocal
    return (unit_rows * norm_gain + norm_shift, unit_rows, reciprocal)


def plain_norm_back(slope_rows, unit_rows, reciprocal, norm_gain):
    tilted = slope_rows * norm_gain
    centered_slope = tilted - jnp.mean(tilted, axis=-1, keepdims=True)
    centered_slope = centered_slope - unit_rows * jnp.mean(
        tilted * unit_rows, axis=-1, keepdims=True
    )
    return (
        centered_slope * reciprocal,
        jnp.sum(slope_rows * unit_rows, axis=0),
        jnp.sum(slope_rows, axis=0),
    )


def plain_contract(left_side, right_side):
    return lax.dot_general(
        left_side, right_side, (((0,), (0,)), ((), ())), preferred_element_type=jnp.float32
    )


def times_transpose(left_side, right_side):
    return lax.dot_general(
        left_side, right_side, (((1,), (1,)), ((), ())), preferred_element_type=jnp.float32
    )


def row_chances(mixing_full, row_docs):
    same_doc = row_docs[:, None] == row_docs[None, :]
    scores = jnp.where(same_doc[None, :, :], mixing_full.astype(jnp.float32), -1e30)
    row_top = jnp.max(scores, axis=-1, keepdims=True)
    raised = jnp.exp(scores - row_top)
    return raised / jnp.sum(raised, axis=-1, keepdims=True)


def plain(
    inputs,
    documents,
    mixing,
    value_weight,
    output_weight,
    mixer_gain,
    mixer_shift,
    dense_gain,
    dense_shift,
    hidden_weight,
    hidden_bias,
    down_weight,
    down_bias,
    cotangent,
):
    gathered = (
        lax.all_gather(mixing, "narrow", axis=1, tiled=True),
        lax.all_gather(value_weight, "narrow", axis=1, tiled=True),
        lax.all_gather(output_weight, "narrow", axis=0, tiled=True),
        lax.all_gather(mixer_gain, "narrow", axis=0, tiled=True),
        lax.all_gather(mixer_shift, "narrow", axis=0, tiled=True),
        lax.all_gather(dense_gain, "narrow", axis=0, tiled=True),
        lax.all_gather(dense_shift, "narrow", axis=0, tiled=True),
        lax.all_gather(hidden_bias, "narrow", axis=0, tiled=True),
        lax.all_gather(down_bias, "narrow", axis=0, tiled=True),
    )
    mixing_full, value_full, output_full = (gathered[0], gathered[1], gathered[2])
    gain_first = gathered[3].astype(jnp.float32)
    shift_first = gathered[4].astype(jnp.float32)
    gain_second = gathered[5].astype(jnp.float32)
    shift_second = gathered[6].astype(jnp.float32)
    bias_hidden = gathered[7].astype(jnp.float32)
    bias_down = gathered[8].astype(jnp.float32)
    halfway = (
        lax.all_gather(hidden_weight, "narrow", axis=0, tiled=True),
        lax.all_gather(down_weight, "narrow", axis=1, tiled=True),
    )
    hidden_full, down_full = (
        lax.all_gather(halfway[0], "wide", axis=1, tiled=True),
        lax.all_gather(halfway[1], "wide", axis=0, tiled=True),
    )
    row_count = inputs.shape[0]
    stream = inputs.reshape(row_count * SEQ, D).astype(jnp.float32)
    normed, unit_first, recip_first = normalize(stream, gain_first, shift_first)
    normed_low = normed.astype(jnp.bfloat16)
    values = jnp.dot(normed_low, value_full, preferred_element_type=jnp.float32).astype(
        jnp.bfloat16
    )
    value_rows = values.reshape(row_count, SEQ, D)

    def mix_one(bundle):
        row_values, row_docs = bundle
        chances_low = row_chances(mixing_full, row_docs).astype(jnp.bfloat16)
        per_head = row_values.reshape(SEQ, HEADS, HEAD)
        blended_row = jnp.einsum(
            "hij,jhd->ihd", chances_low, per_head, preferred_element_type=jnp.float32
        )
        return blended_row.reshape(SEQ, D).astype(jnp.bfloat16)

    blended = lax.map(mix_one, (value_rows, documents)).reshape(row_count * SEQ, D)
    middle = stream + jnp.dot(blended, output_full, preferred_element_type=jnp.float32)
    normed_two, unit_second, recip_second = normalize(middle, gain_second, shift_second)
    normed_two_low = normed_two.astype(jnp.bfloat16)
    hidden = jnp.dot(normed_two_low, hidden_full, preferred_element_type=jnp.float32) + bias_hidden
    activated, gelu_pull = jax.vjp(jax.nn.gelu, hidden)
    active = activated.astype(jnp.bfloat16)
    result = middle + jnp.dot(active, down_full, preferred_element_type=jnp.float32) + bias_down
    slope_low = cotangent.reshape(row_count * SEQ, D)
    slope_wide = slope_low.astype(jnp.float32)
    down_bias_sum = jnp.sum(slope_wide, axis=0)
    down_grad = plain_contract(active, slope_low)
    active_slope = times_transpose(slope_low, down_full)
    hidden_slope_wide = gelu_pull(active_slope)[0]
    hidden_slope = hidden_slope_wide.astype(jnp.bfloat16)
    hidden_bias_sum = jnp.sum(hidden_slope.astype(jnp.float32), axis=0)
    hidden_grad = plain_contract(normed_two_low, hidden_slope)
    normed_two_slope = times_transpose(hidden_slope, hidden_full)
    back_second, gain_second_sum, shift_second_sum = plain_norm_back(
        normed_two_slope, unit_second, recip_second, gain_second
    )
    middle_slope = slope_wide + back_second
    attended_slope = middle_slope.astype(jnp.bfloat16)
    output_grad = plain_contract(blended, attended_slope)
    blended_slope = times_transpose(attended_slope, output_full).astype(jnp.bfloat16)

    def mix_back(running, bundle):
        row_values, row_docs, row_slope = bundle
        chances = row_chances(mixing_full, row_docs)
        per_head = row_values.reshape(SEQ, HEADS, HEAD)
        head_slope = row_slope.reshape(SEQ, HEADS, HEAD)
        chance_slope = jnp.einsum(
            "ihd,jhd->hij", head_slope, per_head, preferred_element_type=jnp.float32
        )
        score_slope = chances * (
            chance_slope - jnp.sum(chances * chance_slope, axis=-1, keepdims=True)
        )
        value_part = jnp.einsum(
            "hij,ihd->jhd",
            chances.astype(jnp.bfloat16),
            head_slope,
            preferred_element_type=jnp.float32,
        )
        return (running + score_slope, value_part.reshape(SEQ, D).astype(jnp.bfloat16))

    mixing_start = jnp.zeros((HEADS, SEQ, SEQ), jnp.float32)
    mixing_grad, value_slopes = lax.scan(
        mix_back, mixing_start, (value_rows, documents, blended_slope.reshape(row_count, SEQ, D))
    )
    value_slope = value_slopes.reshape(row_count * SEQ, D)
    value_grad = plain_contract(normed_low, value_slope)
    normed_slope = times_transpose(value_slope, value_full)
    back_first, gain_first_sum, shift_first_sum = plain_norm_back(
        normed_slope, unit_first, recip_first, gain_first
    )
    inputs_slope = (middle_slope + back_first).astype(jnp.bfloat16)
    sums_half = (
        lax.psum_scatter(
            hidden_grad.astype(jnp.bfloat16), "wide", scatter_dimension=1, tiled=True
        ).astype(jnp.float32),
        lax.psum_scatter(
            down_grad.astype(jnp.bfloat16), "wide", scatter_dimension=0, tiled=True
        ).astype(jnp.float32),
    )
    hidden_share, down_share = (
        lax.psum_scatter(
            sums_half[0].astype(jnp.bfloat16), "narrow", scatter_dimension=0, tiled=True
        ).astype(jnp.float32),
        lax.psum_scatter(
            sums_half[1].astype(jnp.bfloat16), "narrow", scatter_dimension=1, tiled=True
        ).astype(jnp.float32),
    )
    shares = (
        lax.psum_scatter(
            mixing_grad.astype(jnp.bfloat16), "narrow", scatter_dimension=1, tiled=True
        ).astype(jnp.float32),
        lax.psum_scatter(
            value_grad.astype(jnp.bfloat16), "narrow", scatter_dimension=1, tiled=True
        ).astype(jnp.float32),
        lax.psum_scatter(
            output_grad.astype(jnp.bfloat16), "narrow", scatter_dimension=0, tiled=True
        ).astype(jnp.float32),
        lax.psum_scatter(
            gain_first_sum.astype(jnp.bfloat16), "narrow", scatter_dimension=0, tiled=True
        ).astype(jnp.float32),
        lax.psum_scatter(
            shift_first_sum.astype(jnp.bfloat16), "narrow", scatter_dimension=0, tiled=True
        ).astype(jnp.float32),
        lax.psum_scatter(
            gain_second_sum.astype(jnp.bfloat16), "narrow", scatter_dimension=0, tiled=True
        ).astype(jnp.float32),
        lax.psum_scatter(
            shift_second_sum.astype(jnp.bfloat16), "narrow", scatter_dimension=0, tiled=True
        ).astype(jnp.float32),
        lax.psum_scatter(
            hidden_bias_sum.astype(jnp.bfloat16), "narrow", scatter_dimension=0, tiled=True
        ).astype(jnp.float32),
        lax.psum_scatter(
            down_bias_sum.astype(jnp.bfloat16), "narrow", scatter_dimension=0, tiled=True
        ).astype(jnp.float32),
    )
    totals = (
        lax.psum(shares[0].astype(jnp.bfloat16), "wide").astype(jnp.float32),
        lax.psum(shares[1].astype(jnp.bfloat16), "wide").astype(jnp.float32),
        lax.psum(shares[2].astype(jnp.bfloat16), "wide").astype(jnp.float32),
        lax.psum(shares[3].astype(jnp.bfloat16), "wide").astype(jnp.float32),
        lax.psum(shares[4].astype(jnp.bfloat16), "wide").astype(jnp.float32),
        lax.psum(shares[5].astype(jnp.bfloat16), "wide").astype(jnp.float32),
        lax.psum(shares[6].astype(jnp.bfloat16), "wide").astype(jnp.float32),
        lax.psum(shares[7].astype(jnp.bfloat16), "wide").astype(jnp.float32),
        lax.psum(shares[8].astype(jnp.bfloat16), "wide").astype(jnp.float32),
    )
    return (
        result.reshape(row_count, SEQ, D).astype(jnp.bfloat16),
        inputs_slope.reshape(row_count, SEQ, D),
        totals[0],
        totals[1],
        totals[2],
        totals[3],
        totals[4],
        totals[5],
        totals[6],
        hidden_share,
        totals[7],
        down_share,
        totals[8],
    )


def solution(mesh):
    inner = local if dict(mesh.shape) == {"narrow": 2, "wide": 16} else plain
    return jax.shard_map(
        inner,
        mesh=mesh,
        in_specs=(
            P(("narrow", "wide"), None, None),
            P(("narrow", "wide"), None),
            P(None, "narrow", None),
            P(None, "narrow"),
            P("narrow", None),
            P("narrow"),
            P("narrow"),
            P("narrow"),
            P("narrow"),
            P("narrow", "wide"),
            P("narrow"),
            P("wide", "narrow"),
            P("narrow"),
            P(("narrow", "wide"), None, None),
        ),
        out_specs=(
            P(("narrow", "wide"), None, None),
            P(("narrow", "wide"), None, None),
            P(None, "narrow", None),
            P(None, "narrow"),
            P("narrow", None),
            P("narrow"),
            P("narrow"),
            P("narrow"),
            P("narrow"),
            P("narrow", "wide"),
            P("narrow"),
            P("wide", "narrow"),
            P("narrow"),
        ),
        check_vma=False,
    )
```

```python
import functools

import jax
import jax.numpy as jnp
from jax import lax
from jax.experimental import pallas as pl
from jax.experimental.pallas import tpu as pltpu
from jax.sharding import PartitionSpec as P

D = 768
HEADS = 12
HEAD = 64
SEQ = 512
FF = 3072
HALF = D // 2
CHUNK = 192
GROUP = 4 * CHUNK
epsilon = 1e-05

MESH = pl.DeviceIdType.MESH
f32 = jnp.float32
bf16 = jnp.bfloat16


def place():
    core = lax.axis_index("narrow")
    wide = lax.axis_index("wide")
    return core, lax.rem(wide, 2), lax.rem(lax.div(wide, 2), 2), lax.div(wide, 4)


def seat(core, x, y, z):
    return (core, z * 4 + y * 2 + x)


def remote(src, dst, send_sem, recv_sem, device):
    return pltpu.make_async_remote_copy(
        src_ref=src,
        dst_ref=dst,
        send_sem=send_sem,
        recv_sem=recv_sem,
        device_id=device,
        device_id_type=MESH,
    )


def greet(core, x, y, z, more=()):
    barrier = pltpu.get_barrier_semaphore()
    near = (seat(1 - core, x, y, z), seat(core, 1 - x, y, z), seat(core, x, 1 - y, z)) + more
    for device in near:
        pl.semaphore_signal(barrier, inc=1, device_id=device, device_id_type=MESH)

    @pl.when(z < 3)
    def _():
        pl.semaphore_signal(
            barrier, inc=1, device_id=seat(core, x, y, z + 1), device_id_type=MESH
        )

    @pl.when(z > 0)
    def _():
        pl.semaphore_signal(
            barrier, inc=1, device_id=seat(core, x, y, z - 1), device_id_type=MESH
        )

    above, below = jnp.where(z < 3, 1, 0), jnp.where(z > 0, 1, 0)
    pl.semaphore_wait(barrier, len(near) + above + below)


def halves(core):
    mine = pl.ds(pl.multiple_of(core * HALF, 128), HALF)
    other = pl.ds(pl.multiple_of((1 - core) * HALF, 128), HALF)
    return mine, other


def line_order(z, step):
    table = ((0, 1, 2, 3), (1, 0, 2, 3), (2, 1, 3, 0), (3, 2, 1, 0))
    return jnp.where(
        z == 0,
        table[0][step],
        jnp.where(z == 1, table[1][step], jnp.where(z == 2, table[2][step], table[3][step])),
    )


def unit_of(rows):
    center = rows - jnp.mean(rows, axis=-1, keepdims=True)
    reciprocal = lax.rsqrt(jnp.mean(center * center, axis=-1, keepdims=True) + epsilon)
    return center * reciprocal, reciprocal


def dot_nn(left, right):
    return lax.dot_general(left, right, (((1,), (0,)), ((), ())), preferred_element_type=f32)


def dot_nt(left, right):
    return lax.dot_general(left, right, (((1,), (1,)), ((), ())), preferred_element_type=f32)


def dot_tn(left, right):
    return lax.dot_general(left, right, (((0,), (0,)), ((), ())), preferred_element_type=f32)


def lane_ids(rows):
    return lax.broadcasted_iota(jnp.int32, (rows, 128), 1)


def fill_mask(docs_ref, mask, rows):
    for r in range(rows):
        flat = docs_ref[r : r + 1, :].astype(f32)
        for i in range(0, SEQ, 128):
            tall = jnp.broadcast_to(flat[:, i : i + 128], (128, 128)).T
            for j in range(0, SEQ, 128):
                wide = jnp.broadcast_to(flat[:, j : j + 128], (128, 128))
                mask[r, i : i + 128, j : j + 128] = jnp.where(tall == wide, 1.0, 0.0).astype(bf16)


def gelu_and_slope(v):
    scale = 0.7978845608028654
    square = v * v
    t = jnp.tanh(scale * v * (1.0 + 0.044715 * square))
    rise = 0.5 * (1.0 + t)
    slope = rise + 0.5 * scale * v * (1.0 - t * t) * (1.0 + 3.0 * 0.044715 * square)
    return v * rise, slope


def norm_slope(slope, unit, reciprocal, gain):
    tilted = slope * gain
    centered = tilted - jnp.mean(tilted, axis=-1, keepdims=True)
    centered = centered - unit * jnp.mean(tilted * unit, axis=-1, keepdims=True)
    return centered * reciprocal


class Reduce:
    def __init__(self, part, refs):
        self.part = part
        (
            self.first_y, self.first_x, self.second_x, self.second_y, self.line_in,
            self.first_sent, self.first_recv, self.second_sent, self.second_recv,
            self.line_sent, self.line_recv,
        ) = refs
        core, x, y, z = place()
        self.x, self.y, self.z = x, y, z
        self.near_x, self.near_y = seat(core, 1 - x, y, z), seat(core, x, 1 - y, z)
        self.above, self.below = seat(core, x, y, z + 1), seat(core, x, y, z - 1)

    @staticmethod
    def scratch(piece):
        dma = pltpu.SemaphoreType.DMA
        return [
            pltpu.VMEM((4, 2) + piece, bf16), pltpu.VMEM((4, 2) + piece, bf16),
            pltpu.VMEM((4,) + piece, bf16), pltpu.VMEM((4,) + piece, bf16),
            pltpu.VMEM((2, 4, 2) + piece, bf16),
            dma((4, 2)), dma((4, 2)), dma((4, 2)), dma((4, 2)), dma((2, 4, 2)), dma((2, 4, 2)),
        ]

    def first_copy(self, k, m):
        sems = self.first_sent.at[k, m], self.first_recv.at[k, m]
        if m == 0:
            return remote(self.part.at[k, 0, 1 - self.y], self.first_y.at[k], *sems, self.near_y)
        return remote(self.part.at[k, 1, :, 1 - self.x], self.first_x.at[k], *sems, self.near_x)

    def second_copy(self, k, m):
        x, y = self.x, self.y
        sems = self.second_sent.at[k, m], self.second_recv.at[k, m]
        if m == 0:
            return remote(self.part.at[k, 0, y, 1 - x], self.second_x.at[k], *sems, self.near_x)
        return remote(self.part.at[k, 1, 1 - y, x], self.second_y.at[k], *sems, self.near_y)

    def line_copy(self, k, m, down):
        return remote(
            self.part.at[k, m, self.y, self.x], self.line_in.at[down, k, m],
            self.line_sent.at[down, k, m], self.line_recv.at[down, k, m],
            self.below if down else self.above,
        )

    def add_in(self, k, m, y_of, x_of, got):
        old = self.part[k, m, y_of, x_of].astype(f32)
        self.part[k, m, y_of, x_of] = (old + got.astype(f32)).astype(bf16)

    def first(self, k, m):
        self.first_copy(k, m).start()

    def second(self, k, m):
        x, y = self.x, self.y
        self.first_copy(k, m).wait_recv()
        if m == 0:
            self.add_in(k, 0, y, 1 - x, self.first_y[k, 1 - x])
            self.second_copy(k, 0).start()
            self.add_in(k, 0, y, x, self.first_y[k, x])
        else:
            self.add_in(k, 1, 1 - y, x, self.first_x[k, 1 - y])
            self.second_copy(k, 1).start()
            self.add_in(k, 1, y, x, self.first_x[k, y])

    def line(self, k, m):
        self.second_copy(k, m).wait_recv()
        self.add_in(k, m, self.y, self.x, (self.second_x, self.second_y)[m][k])

    def hop(self, k, m, hop):
        x, y, z = self.x, self.y, self.z
        for down, length, seat_z in ((0, k, hop), (1, 3 - k, 3 - hop)):
            if hop < length:

                @pl.when(z == seat_z)
                def _():
                    if hop > 0:
                        self.line_copy(k, m, down).wait_recv()
                        self.add_in(k, m, y, x, self.line_in[down, k, m])
                    self.line_copy(k, m, down).start()

        if hop == max(k, 3 - k):

            @pl.when(z == k)
            def _():
                for down, length in ((0, k), (1, 3 - k)):
                    if length > 0:
                        self.line_copy(k, m, down).wait_recv()
                        self.add_in(k, m, y, x, self.line_in[down, k, m])

    def settle(self, k):
        for m in range(2):
            self.first_copy(k, m).wait_send()
            self.second_copy(k, m).wait_send()
            if k > 0:

                @pl.when(self.z < k)
                def _():
                    self.line_copy(k, m, 0).wait_send()

            if k < 3:

                @pl.when(self.z > k)
                def _():
                    self.line_copy(k, m, 1).wait_send()


class Gather:
    def __init__(self, whole, refs):
        self.whole = whole
        self.recv, self.sent_x, self.sent_y, self.sent_z = refs
        core, x, y, z = place()
        self.x, self.y, self.z = x, y, z
        self.near_x, self.near_y = seat(core, 1 - x, y, z), seat(core, x, 1 - y, z)
        self.above, self.below = seat(core, x, y, z + 1), seat(core, x, y, z - 1)

    @staticmethod
    def scratch(piece):
        dma = pltpu.SemaphoreType.DMA
        return [
            pltpu.VMEM((4, 2, 2, 2) + piece, bf16),
            dma((4, 2, 2, 2)), dma((4, 2, 2)), dma((4, 2, 2)), dma((2, 4, 2)),
        ]

    def send(self, k, m, y_of, x_of, sem, device):
        src = self.whole.at[k, m, y_of, x_of]
        return remote(src, src, sem, self.recv.at[k, m, y_of, x_of], device)

    def to_x(self, k, m, y_of):
        return self.send(k, m, y_of, self.x, self.sent_x.at[k, m, y_of], self.near_x)

    def to_y(self, k, m, x_of):
        return self.send(k, m, self.y, x_of, self.sent_y.at[k, m, x_of], self.near_y)

    def along(self, k, m, down):
        device = self.below if down else self.above
        return self.send(k, m, self.y, self.x, self.sent_z.at[down, k, m], device)

    def arrived(self, k, m, y_of, x_of):
        self.send(k, m, y_of, x_of, self.sent_x.at[k, m, 0], self.near_x).wait_recv()

    def at(self, k, m, distance, part=None):
        x, y, z = self.x, self.y, self.z
        up, down = k + distance, k - distance
        for seat_z in sorted({up, down}):
            if 0 <= seat_z < 4:

                @pl.when(z == seat_z)
                def _():
                    if distance:
                        self.arrived(k, m, y, x)
                    elif part is not None:
                        self.whole[k, m, y, x] = part[k, m, y, x]
                    if k <= seat_z < 3:
                        self.along(k, m, 0).start()
                    if k >= seat_z > 0:
                        self.along(k, m, 1).start()
                    if m == 0:
                        self.to_x(k, 0, y).start()
                        self.to_y(k, 0, x).start()
                    else:
                        self.to_y(k, 1, x).start()
                        self.to_x(k, 1, y).start()

    def cross(self, k, m, distance):
        x, y, z = self.x, self.y, self.z
        up, down = k + distance, k - distance
        for seat_z in sorted({up, down}):
            if 0 <= seat_z < 4:

                @pl.when(z == seat_z)
                def _():
                    if m == 0:
                        self.arrived(k, 0, y, 1 - x)
                        self.to_y(k, 0, 1 - x).start()
                    else:
                        self.arrived(k, 1, 1 - y, x)
                        self.to_x(k, 1, 1 - y).start()

    def rest(self, k, m):
        x, y = self.x, self.y
        if m == 0:
            self.arrived(k, 0, 1 - y, x)
        else:
            self.arrived(k, 1, y, 1 - x)
        self.arrived(k, m, 1 - y, 1 - x)

    def settle(self, k):
        x, y, z = self.x, self.y, self.z
        for m in range(2):
            self.to_x(k, m, y).wait_send()
            self.to_y(k, m, x).wait_send()
            if k < 3:

                @pl.when(jnp.logical_and(z >= k, z < 3))
                def _():
                    self.along(k, m, 0).wait_send()

            if k > 0:

                @pl.when(jnp.logical_and(z <= k, z > 0))
                def _():
                    self.along(k, m, 1).wait_send()

        self.to_y(k, 0, 1 - x).wait_send()
        self.to_x(k, 1, 1 - y).wait_send()


BLOCKS = ((0, 0), (0, 1), (0, 2), (1, 0), (1, 1), (1, 2), (1, 3))
TRIPLE = HEADS // 4
MIX_PIECE = (TRIPLE, 7, 16, 128)
WEIGHT_PIECE = (48, HALF)
DENSE_PIECE = (CHUNK, HALF)
ORDER = (0, 3, 1, 2)


def layer_kernel(
    x_hbm, docs_ref, mixing_ref, value_ref, output_ref, hidden_ref, down_ref, vector_ref, cotangent_hbm,
    result_out, inputs_out, mixing_out, weights_out, hidden_out, down_out, sums_out,
    full_ref, mixing_full, normed_hbm, share_hbm, middle_hbm,
    *scratch,
):
    scratch = list(scratch)

    def take(n):
        got = scratch[:n]
        del scratch[:n]
        return got

    b0, b1, b2, b3, b4, b5 = take(6)
    value_full, output_full, vector_full, shard, mask, raised = take(6)
    total, slope, weight, grads, to_twin, from_twin, dense_part = take(7)
    chance, block_t, mix_part, mix_to, mix_from, weights_from, weights_part = take(7)
    small, small_in, sums = take(3)
    dense_refs = take(11)
    mix_reduce_refs = take(11)
    weights_reduce_refs = take(11)
    mix_whole, *mix_gather_refs = take(5)
    weights_whole, *weights_gather_refs = take(5)
    early_send, early_recv, early_local, shard_sem = take(4)
    full_recv, full_core_recv, full_x, full_y, full_up, full_down, full_core = take(7)
    pair_sem, back_sem, head_sem, weight_sem, move_sem, out_sem = take(6)
    twin_sent, twin_recv, twin_credit, mix_sent, mix_recv, mix_credit = take(6)
    weights_sent, weights_recv, small_sent, small_recv = take(4)

    core, x, y, z = place()
    mine, other = halves(core)
    near_x, near_y = seat(core, 1 - x, y, z), seat(core, x, 1 - y, z)
    above, below = seat(core, x, y, z + 1), seat(core, x, y, z - 1)
    twin = seat(1 - core, x, y, z)
    tokens = b0.shape[0]
    rows_count = tokens // SEQ
    block = 256
    dense = Reduce(dense_part, dense_refs)
    families = {
        "m": (Reduce(mix_part, mix_reduce_refs), Gather(mix_whole, mix_gather_refs), mix_part),
        "w": (Reduce(weights_part, weights_reduce_refs), Gather(weights_whole, weights_gather_refs), weights_part),
    }
    pairs = (seat(core, x, y, z + 1 - 2 * lax.rem(z, 2)), seat(core, x, y, lax.rem(z + 2, 4)))
    rounds = (twin, near_x, near_y) + pairs
    ks = [line_order(z, i) for i in range(4)]

    def rows_of(b):
        return pl.ds(pl.multiple_of(b * block, block), block)

    def move(n, src, dst):
        return pltpu.make_async_copy(src, dst, move_sem.at[n])

    load_x = move(0, x_hbm, b0)
    keep_normed = move(1, b1, normed_hbm)
    load_cotangent = move(2, cotangent_hbm, b1)
    keep_share = move(3, slope, share_hbm)
    keep_middle = move(4, total, middle_hbm)
    load_share = move(5, share_hbm, total)
    load_normed = move(6, normed_hbm, b0)
    keep_result = move(7, b1, result_out)
    load_x_again = move(8, x_hbm, b1)
    keep_inputs = move(9, b0, inputs_out)

    def load_middle(b):
        return move(10 + b, middle_hbm.at[rows_of(b)], grads.at[pl.ds((b % 3) * block, block)])

    my_rows = pl.ds(pl.multiple_of(core * (SEQ // 2), SEQ // 2), SEQ // 2)
    early = {"vec": (vector_ref, vector_full.at[:, mine]), "vw": (value_ref, value_full.at[:, mine])}
    for p in range(HEADS // 2):
        heads_of = pl.ds(2 * p, 2)
        early["mx%d" % p] = (mixing_ref.at[heads_of], mixing_full.at[heads_of, my_rows])
    early["ow"] = (output_ref, output_full.at[mine, :])
    names = list(early)

    def early_copy(name):
        n = names.index(name)
        return remote(*early[name], early_send.at[n], early_recv.at[n], twin)

    def early_own(name):
        src, dst = early[name]
        if name.startswith("mx"):
            dst = raised.at[int(name[2:]) % 2, :, my_rows]
        return pltpu.make_async_copy(src, dst, early_local.at[names.index(name)])

    def chunk_of(k, y_of, x_of):
        return k * 4 + y_of * 2 + x_of

    own = chunk_of(z, y, x)

    def slot(m, chunk):
        return full_ref.at[m, pl.ds(pl.multiple_of(chunk * CHUNK, CHUNK), CHUNK), mine]

    def full_copy(m, chunk, sems, device, src=None):
        dst = slot(m, chunk)
        return remote(dst if src is None else src, dst, sems.at[m, chunk], full_recv.at[m, chunk], device)

    def full_arrived(m, chunk):
        full_copy(m, chunk, full_x, near_x).wait_recv()

    def own_copy(m):
        return pltpu.make_async_copy(shard.at[m], slot(m, own), shard_sem.at[m])

    def gather(step, i, m):
        k = ks[i]
        if step == "at":
            chunk = chunk_of(k, y, x)
            src = shard.at[m] if i == 0 else None
            if i > 0:
                full_arrived(m, chunk)

            @pl.when(jnp.logical_and(k <= z, z < 3))
            def _():
                full_copy(m, chunk, full_up, above, src).start()

            @pl.when(jnp.logical_and(k >= z, z > 0))
            def _():
                full_copy(m, chunk, full_down, below, src).start()

            to_x = full_copy(m, chunk, full_x, near_x, src)
            to_y = full_copy(m, chunk, full_y, near_y, src)
            for copy in (to_x, to_y) if m == 0 else (to_y, to_x):
                copy.start()
        elif step == "cross":
            if m == 0:
                full_arrived(0, chunk_of(k, y, 1 - x))
                full_copy(0, chunk_of(k, y, 1 - x), full_y, near_y).start()
            else:
                full_arrived(1, chunk_of(k, 1 - y, x))
                full_copy(1, chunk_of(k, 1 - y, x), full_x, near_x).start()
        else:
            full_arrived(m, chunk_of(k, 1 - y, x) if m == 0 else chunk_of(k, y, 1 - x))
            full_arrived(m, chunk_of(k, 1 - y, 1 - x))

    def full_twin(i, m):
        src = full_ref.at[m, pl.ds(pl.multiple_of(ks[i] * GROUP, GROUP), GROUP), mine]
        return remote(src, src, full_core.at[m, i], full_core_recv.at[m, i], twin)

    def pass_full(i, m):
        if i == 0:
            own_copy(m).wait()
        full_twin(i, m).start()

    def load_weight(i):
        rows = pl.ds(pl.multiple_of(ks[i] * GROUP, GROUP), GROUP)
        return pltpu.make_async_copy(full_ref.at[:, rows], weight.at[i % 2], weight_sem.at[i % 2])

    def fetch(i):
        for m in range(2):
            full_twin(i, m).wait_recv()
        load_weight(i).start()

    def first_norm(b):
        if b == 0:
            load_x.wait()
        rows = rows_of(b)
        unit, _ = unit_of(b0[rows, :].astype(f32))
        low = (unit * vector_full[0:1, :] + vector_full[1:2, :]).astype(bf16)
        b1[rows, :] = low
        b2[rows, :] = dot_nn(low, value_full[...]).astype(bf16)
        if b == tokens // block - 1:
            keep_normed.start()

    twin_rows = pl.ds(pl.multiple_of((1 - core) * (SEQ // 2), SEQ // 2), SEQ // 2)

    def load_pair(p):
        return pltpu.make_async_copy(
            mixing_full.at[pl.ds(2 * p, 2), twin_rows], raised.at[p % 2, :, twin_rows], pair_sem.at[p % 2]
        )

    def keep_pair(p):
        return pltpu.make_async_copy(raised.at[p % 2], mixing_full.at[pl.ds(2 * p, 2)], back_sem.at[p % 2])

    def mix(p):
        if p == 0:
            early_own("mx0").start()
            load_pair(0).start()
        early_own("mx%d" % p).wait()
        load_pair(p).wait()
        if p + 1 < HEADS // 2:
            early_copy("mx%d" % (p + 1)).wait_recv()
            if p >= 1:
                keep_pair(p - 1).wait()
            early_own("mx%d" % (p + 1)).start()
            load_pair(p + 1).start()
        lanes = slice(p * 128, (p + 1) * 128)
        low_lanes = lane_ids(block) < HEAD
        pair_raised = raised.at[p % 2]
        for half in range(2):
            for i in range(0, SEQ, block):
                part = pair_raised[half, i : i + block].astype(f32)
                pair_raised[half, i : i + block] = jnp.exp(part).astype(bf16)
        keep_pair(p).start()

        def mix_row(r, _):
            pair = b2[pl.ds(pl.multiple_of(r * SEQ, SEQ), SEQ), lanes]
            left_half = lane_ids(SEQ) < HEAD
            ones = jnp.ones_like(pair)
            first = jnp.where(left_half, pair, ones)
            second = jnp.where(left_half, ones, pair)
            for i in range(0, SEQ, block):
                keep = mask[r, i : i + block]
                one = dot_nn(pair_raised[0, i : i + block] * keep, first)
                two = dot_nn(pair_raised[1, i : i + block] * keep, second)
                part = 1.0 / pltpu.roll(jnp.where(low_lanes, two, one), HEAD, 1)
                done = pl.ds(pl.multiple_of(r * SEQ + i, block), block)
                slope[done, lanes] = part
                b3[done, lanes] = (jnp.where(low_lanes, one, two) * part).astype(bf16)
            return 0

        lax.fori_loop(0, rows_count, mix_row, 0)
        if p == HEADS // 2 - 1:
            keep_share.start()
            keep_normed.wait()
            load_cotangent.start()

    def early_ready(name):
        if not name.startswith("mx"):
            early_own(name).wait()
        early_copy(name).wait_recv()

    def project(b):
        rows = rows_of(b)
        middle = b0[rows, :].astype(f32) + dot_nn(b3[rows, :], output_full[...])
        total[rows, :] = middle
        unit, _ = unit_of(middle)
        b0[rows, :] = (unit * vector_full[2:3, :] + vector_full[3:4, :]).astype(bf16)
        if b == tokens // block - 1:
            keep_middle.start()
            keep_share.wait()
            sums[...] = jnp.zeros_like(sums)

    def dense_units(i, u):
        k = ks[i]
        if u == 0:
            load_weight(i).wait()
        if i == 0 and u == 0:
            load_cotangent.wait()
        units = slice(u * 256, (u + 1) * 256)
        lanes = pl.ds(pl.multiple_of(lax.div(k, 2) * HALF, 128), HALF)
        row = 5 + 2 * lax.rem(k, 2)
        bias = jnp.concatenate(
            [vector_full[pl.ds(row, 1), lanes], vector_full[pl.ds(row + 1, 1), lanes]], axis=1
        )[:, units]
        hidden = dot_nt(b0[...], weight[i % 2, 0, units, :]) + bias
        pulled = dot_nt(b1[...], weight[i % 2, 1, units, :])
        act, pull = gelu_and_slope(hidden)
        turned = (pulled * pull).astype(bf16)
        b4[:, units] = act.astype(bf16)
        b5[:, units] = turned
        sums[pl.ds(3 + k, 1), units] = jnp.sum(turned.astype(f32), axis=0, keepdims=True)

    def dense_grad(i, m):
        left, right = ((b5, b0), (b4, b1))[m]
        grads[...] = dot_tn(left[...], right[...])

    def dense_back(i, m):
        if m == 1:
            if i == 0:
                keep_middle.wait()
            total[...] += dot_nn(b4[...], weight[i % 2, 1])
        elif i == 0:
            slope[...] = dot_nn(b5[...], weight[i % 2, 0])
        else:
            slope[...] += dot_nn(b5[...], weight[i % 2, 0])
        if i == 3 and m == 1:
            for b in range(3):
                load_middle(b).start()

    def dense_twin(i, m):
        return remote(
            to_twin.at[m], from_twin.at[i % 2, m], twin_sent.at[i, m], twin_recv.at[i, m], twin
        )

    def swap_dense(i, m):
        if i >= 1:
            dense_twin(i - 1, m).wait_send()
        to_twin[m] = grads[:, other].astype(bf16)
        dense_part[ks[i], m] = grads[:, mine].astype(bf16).reshape((2, 2) + DENSE_PIECE)
        if i >= 2:
            pl.semaphore_wait(twin_credit.at[i % 2, m], 1)
        dense_twin(i, m).start()

    def swapped_dense(i, m):
        dense_twin(i, m).wait_recv()
        k = ks[i]
        both = dense_part[k, m].astype(f32) + from_twin[i % 2, m].reshape((2, 2) + DENSE_PIECE).astype(f32)
        dense_part[k, m] = both.astype(bf16)
        if i < 2:
            pl.semaphore_signal(twin_credit.at[i % 2, m], inc=1, device_id=twin, device_id_type=MESH)

    def second_finish(b):
        load_middle(b).wait()
        rows = rows_of(b)
        unit, reciprocal = unit_of(grads[pl.ds((b % 3) * block, block), :])
        if b == 0:
            load_middle(3).start()
        raw = slope[rows, :]
        cot = b1[rows, :].astype(f32)
        sums[0:1, :] += jnp.sum(cot, axis=0, keepdims=True)
        sums[1:2, :] += jnp.sum(raw * unit, axis=0, keepdims=True)
        sums[2:3, :] += jnp.sum(raw, axis=0, keepdims=True)
        moved = cot + norm_slope(raw, unit, reciprocal, vector_full[2:3, :])
        slope[rows, :] = moved
        low = moved.astype(bf16)
        b4[rows, :] = low
        b5[rows, :] = dot_nt(low, output_full[...]).astype(bf16)
        b1[rows, :] = (total[rows, :] + vector_full[4:5, :]).astype(bf16)
        if b == tokens // block - 1:
            keep_result.start()
            load_share.start()
            load_normed.start()

    def output_grad():
        grads[...] = dot_tn(b3[...], b4[...])
        keep_result.wait()
        load_x_again.start()

    def scale_pair(p, _):
        lanes = pl.ds(pl.multiple_of(p * 128, 128), 128)
        for r in range(rows_count):
            rows = pl.ds(r * SEQ, SEQ)
            low = (b5[rows, lanes].astype(f32) * total[rows, lanes]).astype(bf16)
            b5[rows, lanes] = low
            weight[r, 0, lanes, 0:SEQ] = low.T
        return 0

    def load_head(n):
        h = ORDER[n // TRIPLE] * TRIPLE + n % TRIPLE
        return pltpu.make_async_copy(mixing_full.at[h], raised.at[n // 2 % 2, n % 2], head_sem.at[n % 4])

    def prepare():
        load_share.wait()
        for p in range(HEADS // 2 - 2, HEADS // 2):
            keep_pair(p).wait()
        for n in range(3):
            load_head(n).start()
        lax.fori_loop(0, HEADS // 2, scale_pair, 0)

    def head(i, n):
        k, step = ORDER[i], i * TRIPLE + n
        load_head(step).wait()
        if step + 3 < HEADS:
            load_head(step + 3).start()
        if n == 0 and i >= 2:
            mix_twin(i - 2).wait_send()
        h = k * TRIPLE + n
        lanes = slice((h // 2) * 128, (h // 2 + 1) * 128)
        side = h % 2
        lane = lane_ids(block)
        inside = lane < HEAD if side == 0 else lane >= HEAD
        inside_all = lane_ids(SEQ) < HEAD if side == 0 else lane_ids(SEQ) >= HEAD
        spot = lane - HEAD * (1 - side)
        for where in range(2):
            half = core if where == 0 else 1 - core
            start = pl.multiple_of(half * block, block)
            here = pl.ds(start, block)
            sum_rows = None
            for r in range(rows_count):
                rows = pl.ds(pl.multiple_of(r * SEQ + start, block), block)
                low = b5[rows, lanes].astype(f32)
                delta = jnp.sum(
                    jnp.where(inside, low * b3[rows, lanes].astype(f32), 0.0), axis=-1, keepdims=True
                )
                coarse = delta.astype(bf16).astype(f32)
                extra = jnp.where(spot == 0, -coarse, jnp.where(spot == 1, coarse - delta, 0.0))
                left = jnp.where(inside, low, extra).astype(bf16)
                pair = b2[r * SEQ : (r + 1) * SEQ, lanes].astype(f32)
                right = jnp.where(inside_all, pair, 1.0).astype(bf16)
                part = raised[step // 2 % 2, step % 2, here] * mask[r, here]
                chance[r, here] = part
                term = part.astype(f32) * dot_nt(left, right)
                sum_rows = term if sum_rows is None else sum_rows + term
            block_t[...] = sum_rows.astype(bf16)
            for p, (row, column) in enumerate(BLOCKS):
                top = pl.multiple_of((row + half * (1 - 2 * row)) * 128, 128)
                side_lanes = pl.ds(pl.multiple_of((column + half * (3 - 2 * column)) * 128, 128), 128)
                for q in range(8):
                    strip = block_t[pl.ds(pl.multiple_of(top + q * 16, 16), 16), side_lanes]
                    spot_of = (q % 2, q // 4, (q // 2) % 2, n, p)
                    if where == 0:
                        mix_part[(k,) + spot_of] = strip
                    else:
                        mix_to[(i % 2,) + spot_of] = strip
        heads_rows = slice(h * HEAD, (h + 1) * HEAD)
        for r in range(rows_count):
            weight[r, 1, heads_rows, 0:SEQ] = dot_nn(
                weight[r, 0, heads_rows, 0:SEQ], chance[r]
            ).astype(bf16)

    def turn():
        def turn_pair(p, _):
            lanes = pl.ds(pl.multiple_of(p * 128, 128), 128)
            for r in range(rows_count):
                b4[r * SEQ : (r + 1) * SEQ, lanes] = weight[r, 1, lanes, 0:SEQ].T
            return 0

        lax.fori_loop(0, D // 128, turn_pair, 0)

    def value_grad():
        load_normed.wait()
        grads[...] = dot_tn(b0[...], b4[...])

    def first_finish(b):
        if b == 0:
            load_x_again.wait()
            small[0] = jnp.zeros_like(small[0])
            small[0, 0:8] = sums[...]
        rows = rows_of(b)
        back = dot_nt(b4[rows, :], value_full[...])
        unit, reciprocal = unit_of(b1[rows, :].astype(f32))
        small[0, 7:8, :] += jnp.sum(back * unit, axis=0, keepdims=True)
        small[0, 8:9, :] += jnp.sum(back, axis=0, keepdims=True)
        moved = slope[rows, :] + norm_slope(back, unit, reciprocal, vector_full[0:1, :])
        b0[rows, :] = moved.astype(bf16)
        if b == tokens // block - 1:
            keep_inputs.start()

    other_rows = pl.ds(pl.multiple_of((1 - core) * HALF, HALF), HALF)
    share_rows = D // 4

    def weights_twin(m):
        return remote(to_twin.at[m], weights_from.at[m], weights_sent.at[m], weights_recv.at[m], twin)

    def mix_twin(i):
        return remote(mix_to.at[i % 2], mix_from.at[i % 2], mix_sent.at[i], mix_recv.at[i], twin)

    def swap(what):
        if what == "vg" or what == "og":
            m = 0 if what == "vg" else 1
            dense_twin(3, m).wait_send()
            if m == 0:
                to_twin[0] = grads[:, other].astype(bf16)
            else:
                for side in range(2):
                    to_twin[1, side * HALF : (side + 1) * HALF] = grads[
                        other_rows, side * HALF : (side + 1) * HALF
                    ].astype(bf16)
            for k in range(4):
                rows = slice(k * share_rows, (k + 1) * share_rows)
                own_rows = pl.ds(pl.multiple_of(core * HALF + (k % 2) * share_rows, 64), share_rows)
                side = slice((k // 2) * HALF, (k // 2 + 1) * HALF)
                part = grads[rows, mine] if m == 0 else grads[own_rows, side]
                weights_part[k, m] = part.astype(bf16).reshape((2, 2) + WEIGHT_PIECE)
            weights_twin(m).start()
        else:
            if what >= 2:
                pl.semaphore_wait(mix_credit.at[what % 2], 1)
            mix_twin(what).start()

    def swapped(what):
        if what == "vg" or what == "og":
            m = 0 if what == "vg" else 1
            weights_twin(m).wait_recv()
            for k in range(4):
                got = weights_from[m, k * share_rows : (k + 1) * share_rows].astype(f32)
                both = weights_part[k, m].astype(f32) + got.reshape((2, 2) + WEIGHT_PIECE)
                weights_part[k, m] = both.astype(bf16)
        else:
            mix_twin(what).wait_recv()
            k = ORDER[what]
            for m in range(2):
                for y_of in range(2):
                    for x_of in range(2):
                        families["m"][0].add_in(k, m, y_of, x_of, mix_from[what % 2, m, y_of, x_of])
            if what < 2:
                pl.semaphore_signal(mix_credit.at[what % 2], inc=1, device_id=twin, device_id_type=MESH)

    def small_copy(n):
        return remote(small.at[n], small_in.at[n], small_sent.at[n], small_recv.at[n], rounds[n])

    def small_round(n):
        if n > 0:
            small_copy(n - 1).wait_recv()
            small[n] = small[n - 1] + small_in[n - 1]
        if n < len(rounds):
            small_copy(n).start()

    def dense_reduce(step, *rest):
        if step == "hop":
            dense.hop(*rest)
        else:
            i, m = rest
            getattr(dense, step)(ks[i], m)

    load_x.start()
    shard[0] = hidden_ref[...].T
    shard[1] = down_ref[...]
    greet(core, x, y, z, (pairs[1],))
    for m in range(2):
        own_copy(m).start()
    for name in ("vec", "vw", "ow"):
        early_own(name).start()

    local_steps = {
        "early": lambda name: early_copy(name).start(), "ready": early_ready, "gs": gather,
        "pass": pass_full, "fetch": fetch, "norm": first_norm,
        "mask": lambda: fill_mask(docs_ref, mask, rows_count), "mix": mix, "proj": project,
        "dense": dense_units, "grad": dense_grad, "acc": dense_back, "swapF": swap_dense,
        "swappedF": swapped_dense, "Fs": dense_reduce, "fin2": second_finish, "og": output_grad,
        "scale": prepare, "head": head, "turn": turn, "vg": value_grad, "fin1": first_finish,
        "swap": swap, "swapped": swapped, "small": small_round,
    }
    for name, *rest in SCHEDULE:
        if name in local_steps:
            local_steps[name](*rest)
            continue
        reduce, spread, part = families[name]
        step, *rest = rest
        if step == "at":
            spread.at(*rest, part)
        elif step in ("cross", "rest"):
            getattr(spread, step)(*rest)
        else:
            getattr(reduce, step)(*rest)
            if step == "line":
                reduce.hop(*rest, 0)

    def out_copy(n, src, dst):
        return pltpu.make_async_copy(src, dst, out_sem.at[n])

    outs = [out_copy(0, mix_whole, mixing_out), out_copy(1, weights_whole, weights_out)]
    for copy in outs:
        copy.start()
    for k in range(4):

        @pl.when(z == k)
        def _():
            for m, out in enumerate((hidden_out, down_out)):
                out[...] = dense_part[k, m, y, x].astype(f32)

    for n, row in enumerate((0, 1, 2, 7, 8)):
        sums_out[n : n + 1, :] = small[5, row : row + 1, mine]
    for n in range(4):
        line = pl.ds(3 + 2 * core + n // 2, 1)
        sums_out[5 + n : 6 + n, :] = small[5, line, (n % 2) * HALF : (n % 2 + 1) * HALF]
    sums_out[9:16, :] = jnp.zeros((7, HALF), f32)
    for name in names:
        early_copy(name).wait_send()
    for n in range(5):
        small_copy(n).wait_send()
    for m in range(2):
        weights_twin(m).wait_send()
        for i in range(4):
            full_twin(i, m).wait_send()
    for i in (2, 3):
        mix_twin(i).wait_send()

    def settle_line(k, _):
        line = chunk_of(k, y, x)
        for m in range(2):
            full_copy(m, line, full_x, near_x).wait_send()
            full_copy(m, line, full_y, near_y).wait_send()

            @pl.when(jnp.logical_and(k <= z, z < 3))
            def _():
                full_copy(m, line, full_up, above).wait_send()

            @pl.when(jnp.logical_and(k >= z, z > 0))
            def _():
                full_copy(m, line, full_down, below).wait_send()

        full_copy(0, chunk_of(k, y, 1 - x), full_y, near_y).wait_send()
        full_copy(1, chunk_of(k, 1 - y, x), full_x, near_x).wait_send()
        return 0

    lax.fori_loop(0, 4, settle_line, 0)
    for k in range(4):
        dense.settle(k)
        for reduce, spread, _ in families.values():
            reduce.settle(k)
            spread.settle(k)
    keep_inputs.wait()
    for copy in outs:
        copy.wait()


def layer_call(x, documents, mixing, value_weight, output_weight, hidden_weight, down_weight, vectors, cotangent):
    tokens = x.shape[0]
    rows = tokens // SEQ
    any_spec = pl.BlockSpec(memory_space=pl.ANY)
    vmem = pl.BlockSpec(memory_space=pltpu.VMEM)
    shape = jax.ShapeDtypeStruct
    dma = pltpu.SemaphoreType.DMA
    credit = pltpu.SemaphoreType.REGULAR
    token_rows = pltpu.VMEM((tokens, D), bf16)
    half_grads = (2, D, HALF)
    quads = (2, 2, 2)
    return pl.pallas_call(
        layer_kernel,
        out_shape=(
            shape((tokens, D), bf16), shape((tokens, D), bf16), shape((4,) + quads + MIX_PIECE, bf16),
            shape((4,) + quads + WEIGHT_PIECE, bf16), shape(DENSE_PIECE, f32), shape(DENSE_PIECE, f32),
            shape((16, HALF), f32),
            shape((2, FF, D), bf16), shape((HEADS, SEQ, SEQ), bf16), shape((tokens, D), bf16),
            shape((tokens, D), f32), shape((tokens, D), f32),
        ),
        in_specs=[any_spec, vmem, any_spec, any_spec, any_spec, vmem, vmem, any_spec, any_spec],
        out_specs=[any_spec] * 4 + [vmem] * 3 + [any_spec] * 5,
        scratch_shapes=[
            *[token_rows] * 6,
            pltpu.VMEM((D, D), bf16), pltpu.VMEM((D, D), bf16), pltpu.VMEM((16, D), f32),
            pltpu.VMEM((2,) + DENSE_PIECE, bf16), pltpu.VMEM((rows, SEQ, SEQ), bf16),
            pltpu.VMEM((2, 2, SEQ, SEQ), bf16),
            pltpu.VMEM((tokens, D), f32), pltpu.VMEM((tokens, D), f32),
            pltpu.VMEM((2, 2, GROUP, D), bf16), pltpu.VMEM((D, D), f32), pltpu.VMEM(half_grads, bf16),
            pltpu.VMEM((2,) + half_grads, bf16), pltpu.VMEM((4,) + quads + DENSE_PIECE, bf16),
            pltpu.VMEM((rows, SEQ, SEQ), bf16), pltpu.VMEM((SEQ // 2, SEQ), bf16),
            pltpu.VMEM((4,) + quads + MIX_PIECE, bf16), pltpu.VMEM((2,) + quads + MIX_PIECE, bf16),
            pltpu.VMEM((2,) + quads + MIX_PIECE, bf16), pltpu.VMEM(half_grads, bf16),
            pltpu.VMEM((4,) + quads + WEIGHT_PIECE, bf16),
            pltpu.VMEM((6, 16, D), f32), pltpu.VMEM((5, 16, D), f32), pltpu.VMEM((8, D), f32),
            *Reduce.scratch(DENSE_PIECE), *Reduce.scratch(MIX_PIECE), *Reduce.scratch(WEIGHT_PIECE),
            *Gather.scratch(MIX_PIECE), *Gather.scratch(WEIGHT_PIECE),
            dma((9,)), dma((9,)), dma((9,)), dma((2,)),
            dma((2, 16)), dma((2, 4)), dma((2, 16)), dma((2, 16)), dma((2, 16)), dma((2, 16)), dma((2, 4)),
            dma((2,)), dma((2,)), dma((4,)), dma((2,)), dma((14,)), dma((2,)),
            dma((4, 2)), dma((4, 2)), credit((2, 2)), dma((4,)), dma((4,)), credit((2,)),
            dma((2,)), dma((2,)), dma((5,)), dma((5,)),
        ],
        compiler_params=pltpu.CompilerParams(
            collective_id=0, has_side_effects=True, vmem_limit_bytes=64 << 20
        ),
    )(x, documents, mixing, value_weight, output_weight, hidden_weight, down_weight, vectors, cotangent)


def local(
    inputs, documents, mixing, value_weight, output_weight, mixer_gain, mixer_shift, dense_gain,
    dense_shift, hidden_weight, hidden_bias, down_weight, down_bias, cotangent,
):
    tokens = inputs.shape[0] * SEQ
    flat = jnp.concatenate(
        [mixer_gain, mixer_shift, dense_gain, dense_shift, down_bias, hidden_bias, jnp.zeros((7 * HALF,), bf16)]
    )
    vectors = flat.astype(f32).reshape(16, HALF)
    result, inputs_slope, mixing_packed, weights_packed, hidden_share, down_share, sums, *_ = layer_call(
        inputs.reshape(tokens, D), documents, mixing, value_weight, output_weight, hidden_weight,
        down_weight, vectors, cotangent.reshape(tokens, D),
    )
    blocks = mixing_packed.transpose(0, 4, 5, 2, 3, 1, 6, 7).reshape(HEADS, 7, 128, 128)
    blocks = blocks.astype(f32)
    nothing = jnp.zeros((HEADS, 128, 128), f32)

    def lay(half):
        found = {}
        for n, (row, column) in enumerate(BLOCKS):
            found[(1 - row, 3 - column) if half else (row, column)] = blocks[:, n]
        rows = [
            jnp.concatenate([found.get((row, column), nothing) for column in range(4)], axis=2)
            for row in range(2)
        ]
        return jnp.concatenate(rows, axis=1)

    mixing_grad = jnp.where(lax.axis_index("narrow") == 0, lay(0), lay(1))
    value_grad = weights_packed[:, 0].reshape(D, HALF).astype(f32)
    output_grad = weights_packed[:, 1].reshape(2, HALF, HALF).swapaxes(0, 1).reshape(HALF, D)
    shape = inputs.shape
    return (
        result.reshape(shape), inputs_slope.reshape(shape), mixing_grad, value_grad,
        output_grad.astype(f32), sums[3], sums[4], sums[1], sums[2], hidden_share.T,
        sums[5:9].reshape(4 * HALF), down_share, sums[0],
    )


SCHEDULE = (
    ("early", "vec"), ("early", "vw"), ("early", "mx0"), ("early", "mx1"), ("early", "mx2"), ("early", "mx3"),
    ("early", "mx4"), ("early", "mx5"), ("early", "ow"), ("gs", "at", 0, 0), ("gs", "at", 0, 1),
    ("ready", "vec"), ("ready", "vw"), ("norm", 0), ("ready", "mx0"), ("norm", 1), ("norm", 2),
    ("gs", "at", 1, 0), ("gs", "cross", 0, 0), ("norm", 3), ("mask",), ("gs", "at", 1, 1),
    ("gs", "cross", 0, 1), ("mix", 0), ("gs", "at", 2, 0), ("mix", 1), ("gs", "at", 2, 1), ("ready", "ow"),
    ("gs", "cross", 1, 0), ("mix", 2), ("mix", 3), ("gs", "at", 3, 0), ("mix", 4), ("gs", "rest", 0, 0),
    ("pass", 0, 0), ("gs", "at", 3, 1), ("gs", "cross", 2, 0), ("mix", 5), ("gs", "cross", 1, 1), ("proj", 0),
    ("gs", "rest", 0, 1), ("pass", 0, 1), ("proj", 1), ("proj", 2), ("proj", 3), ("fetch", 0),
    ("dense", 0, 0), ("gs", "cross", 2, 1), ("dense", 0, 1), ("dense", 0, 2), ("gs", "rest", 1, 0),
    ("gs", "cross", 3, 0), ("pass", 1, 0), ("grad", 0, 0), ("swapF", 0, 0), ("grad", 0, 1), ("swapF", 0, 1),
    ("acc", 0, 0), ("swappedF", 0, 0), ("Fs", "first", 0, 0), ("gs", "rest", 1, 1), ("pass", 1, 1),
    ("acc", 0, 1), ("gs", "cross", 3, 1), ("swappedF", 0, 1), ("Fs", "first", 0, 1), ("fetch", 1),
    ("dense", 1, 0), ("gs", "rest", 2, 0), ("dense", 1, 1), ("pass", 2, 0), ("gs", "rest", 2, 1),
    ("pass", 2, 1), ("dense", 1, 2), ("grad", 1, 0), ("gs", "rest", 3, 0), ("pass", 3, 0), ("swapF", 1, 0),
    ("grad", 1, 1), ("fetch", 2), ("swapF", 1, 1), ("acc", 1, 0), ("gs", "rest", 3, 1), ("pass", 3, 1),
    ("acc", 1, 1), ("swappedF", 1, 0), ("swappedF", 1, 1), ("Fs", "first", 1, 0), ("Fs", "first", 1, 1),
    ("Fs", "second", 0, 1), ("dense", 2, 0), ("Fs", "second", 0, 0), ("dense", 2, 1), ("fetch", 3),
    ("dense", 2, 2), ("grad", 2, 0), ("swapF", 2, 0), ("grad", 2, 1), ("swapF", 2, 1), ("acc", 2, 0),
    ("swappedF", 2, 0), ("Fs", "first", 2, 0), ("Fs", "second", 1, 0), ("Fs", "second", 1, 1),
    ("swappedF", 2, 1), ("Fs", "first", 2, 1), ("acc", 2, 1), ("Fs", "line", 0, 0), ("Fs", "line", 0, 1),
    ("dense", 3, 0), ("dense", 3, 1), ("dense", 3, 2), ("Fs", "line", 1, 0), ("grad", 3, 0), ("swapF", 3, 0),
    ("grad", 3, 1), ("swapF", 3, 1), ("Fs", "second", 2, 0), ("acc", 3, 0), ("swappedF", 3, 0),
    ("Fs", "first", 3, 0), ("acc", 3, 1), ("swappedF", 3, 1), ("Fs", "first", 3, 1), ("Fs", "second", 2, 1),
    ("Fs", "line", 1, 1), ("fin2", 0), ("Fs", "line", 2, 0), ("Fs", "hop", 1, 0, 0), ("Fs", "hop", 2, 0, 0),
    ("fin2", 1), ("fin2", 2), ("fin2", 3), ("Fs", "hop", 1, 0, 1), ("Fs", "second", 3, 0), ("og",),
    ("swap", "og"), ("Fs", "second", 3, 1), ("scale",), ("Fs", "line", 2, 1), ("Fs", "hop", 1, 1, 0),
    ("Fs", "hop", 2, 1, 0), ("Fs", "hop", 2, 0, 1), ("head", 0, 0), ("swapped", "og"), ("w", "first", 0, 1),
    ("Fs", "hop", 1, 0, 2), ("w", "first", 1, 1), ("w", "first", 2, 1), ("w", "first", 3, 1),
    ("Fs", "line", 3, 0), ("Fs", "hop", 0, 0, 0), ("Fs", "hop", 3, 0, 0), ("head", 0, 1),
    ("Fs", "hop", 1, 1, 1), ("head", 0, 2), ("Fs", "line", 3, 1), ("Fs", "hop", 0, 1, 0),
    ("Fs", "hop", 3, 1, 0), ("swap", 0), ("w", "second", 0, 1), ("head", 1, 0), ("Fs", "hop", 2, 0, 2),
    ("Fs", "hop", 2, 1, 1), ("head", 1, 1), ("w", "second", 1, 1), ("swapped", 0), ("w", "second", 2, 1),
    ("Fs", "hop", 1, 1, 2), ("w", "line", 0, 1), ("m", "first", 0, 0), ("m", "first", 0, 1), ("head", 1, 2),
    ("w", "second", 3, 1), ("Fs", "hop", 0, 0, 1), ("swap", 1), ("head", 2, 0), ("Fs", "hop", 3, 0, 1),
    ("head", 2, 1), ("Fs", "hop", 2, 1, 2), ("w", "line", 1, 1), ("swapped", 1), ("m", "first", 3, 0),
    ("m", "first", 3, 1), ("Fs", "hop", 0, 1, 1), ("Fs", "hop", 3, 1, 1), ("w", "line", 2, 1),
    ("w", "hop", 0, 1, 1), ("head", 2, 2), ("m", "second", 0, 0), ("m", "second", 0, 1), ("swap", 2),
    ("w", "line", 3, 1), ("head", 3, 0), ("Fs", "hop", 0, 0, 2), ("Fs", "hop", 3, 0, 2),
    ("w", "hop", 2, 1, 1), ("w", "hop", 1, 1, 1), ("head", 3, 1), ("w", "hop", 3, 1, 1), ("swapped", 2),
    ("m", "first", 1, 0), ("m", "first", 1, 1), ("m", "second", 3, 1), ("Fs", "hop", 0, 1, 2),
    ("Fs", "hop", 3, 1, 2), ("w", "hop", 0, 1, 2), ("w", "hop", 2, 1, 2), ("w", "at", 2, 1, 0),
    ("m", "second", 3, 0), ("head", 3, 2), ("m", "line", 0, 0), ("swap", 3), ("Fs", "hop", 0, 0, 3),
    ("Fs", "hop", 3, 0, 3), ("turn",), ("vg",), ("m", "line", 0, 1), ("w", "hop", 1, 1, 2),
    ("w", "at", 1, 1, 0), ("w", "hop", 3, 1, 2), ("m", "hop", 0, 0, 1), ("swap", "vg"), ("swapped", 3),
    ("Fs", "hop", 0, 1, 3), ("Fs", "hop", 3, 1, 3), ("w", "cross", 2, 1, 0), ("w", "at", 2, 1, 1),
    ("m", "first", 2, 0), ("m", "first", 2, 1), ("fin1", 0), ("m", "hop", 0, 1, 1), ("m", "second", 1, 0),
    ("w", "at", 1, 1, 1), ("m", "second", 1, 1), ("w", "hop", 0, 1, 3), ("w", "at", 0, 1, 0),
    ("w", "hop", 3, 1, 3), ("w", "at", 3, 1, 0), ("swapped", "vg"), ("w", "first", 0, 0),
    ("m", "hop", 0, 0, 2), ("w", "first", 1, 0), ("w", "first", 2, 0), ("w", "first", 3, 0),
    ("m", "line", 3, 0), ("fin1", 1), ("w", "at", 1, 1, 2), ("w", "at", 2, 1, 2), ("m", "line", 3, 1),
    ("fin1", 2), ("m", "hop", 0, 1, 2), ("m", "hop", 0, 0, 3), ("m", "hop", 3, 0, 1), ("w", "at", 3, 1, 1),
    ("m", "at", 0, 0, 0), ("m", "hop", 3, 1, 1), ("w", "at", 0, 1, 1), ("fin1", 3), ("w", "cross", 1, 1, 0),
    ("m", "second", 2, 1), ("m", "line", 1, 0), ("m", "second", 2, 0), ("small", 0), ("m", "hop", 0, 1, 3),
    ("small", 1), ("w", "at", 3, 1, 2), ("w", "second", 0, 0), ("m", "at", 0, 1, 0), ("w", "cross", 2, 1, 1),
    ("w", "cross", 1, 1, 1), ("m", "hop", 3, 0, 2), ("w", "second", 1, 0), ("m", "at", 0, 0, 1),
    ("m", "hop", 3, 1, 2), ("w", "at", 3, 1, 3), ("m", "line", 1, 1), ("m", "cross", 0, 0, 0),
    ("m", "hop", 1, 0, 1), ("w", "at", 0, 1, 2), ("w", "second", 2, 0), ("m", "line", 2, 0),
    ("w", "cross", 0, 1, 0), ("w", "cross", 3, 1, 0), ("w", "second", 3, 0), ("m", "hop", 3, 0, 3),
    ("m", "at", 3, 0, 0), ("m", "at", 0, 0, 2), ("w", "line", 0, 0), ("m", "at", 0, 1, 1), ("small", 2),
    ("m", "hop", 1, 0, 2), ("m", "at", 1, 0, 0), ("m", "hop", 3, 1, 3), ("m", "at", 3, 1, 0),
    ("m", "hop", 1, 1, 1), ("w", "line", 1, 0), ("m", "hop", 2, 0, 1), ("w", "cross", 1, 1, 2),
    ("w", "cross", 2, 1, 2), ("w", "rest", 2, 1), ("w", "rest", 1, 1), ("w", "at", 0, 1, 3),
    ("w", "hop", 0, 0, 1), ("m", "cross", 3, 0, 0), ("m", "at", 0, 1, 2), ("m", "cross", 0, 0, 1),
    ("w", "cross", 3, 1, 1), ("w", "cross", 0, 1, 1), ("w", "line", 2, 0), ("m", "at", 0, 0, 3),
    ("m", "line", 2, 1), ("w", "hop", 1, 0, 1), ("m", "at", 3, 0, 1), ("w", "cross", 3, 1, 2),
    ("m", "at", 1, 0, 1), ("m", "hop", 1, 1, 2), ("w", "line", 3, 0), ("m", "at", 1, 1, 0),
    ("m", "cross", 0, 1, 0), ("w", "hop", 0, 0, 2), ("m", "cross", 0, 0, 2), ("w", "cross", 0, 1, 2),
    ("w", "cross", 3, 1, 3), ("w", "hop", 1, 0, 2), ("m", "cross", 3, 1, 0), ("w", "at", 1, 0, 0),
    ("m", "at", 0, 1, 3), ("m", "hop", 2, 0, 2), ("m", "at", 2, 0, 0), ("w", "cross", 0, 1, 3),
    ("m", "at", 3, 1, 1), ("m", "hop", 2, 1, 1), ("m", "at", 3, 0, 2), ("m", "at", 1, 0, 2),
    ("m", "cross", 0, 0, 3), ("m", "at", 1, 1, 1), ("w", "rest", 3, 1), ("small", 3), ("w", "hop", 0, 0, 3),
    ("w", "at", 0, 0, 0), ("m", "cross", 1, 0, 0), ("w", "at", 1, 0, 1), ("m", "cross", 0, 1, 1),
    ("w", "hop", 2, 0, 1), ("m", "cross", 0, 1, 2), ("m", "at", 2, 0, 1), ("m", "cross", 1, 0, 1),
    ("w", "rest", 0, 1), ("w", "hop", 3, 0, 1), ("m", "hop", 2, 1, 2), ("w", "at", 0, 0, 1),
    ("m", "at", 2, 1, 0), ("m", "at", 3, 0, 3), ("m", "cross", 3, 0, 1), ("m", "at", 1, 1, 2),
    ("m", "at", 3, 1, 2), ("m", "cross", 0, 1, 3), ("w", "hop", 2, 0, 2), ("w", "cross", 0, 0, 0),
    ("w", "at", 2, 0, 0), ("small", 4), ("w", "at", 1, 0, 2), ("m", "rest", 0, 0), ("w", "hop", 3, 0, 2),
    ("m", "at", 2, 0, 2), ("w", "at", 0, 0, 2), ("m", "cross", 1, 0, 2), ("w", "cross", 1, 0, 0),
    ("m", "at", 2, 1, 1), ("m", "at", 3, 1, 3), ("m", "cross", 2, 0, 0), ("w", "at", 2, 0, 1),
    ("m", "cross", 1, 1, 0), ("w", "hop", 3, 0, 3), ("w", "at", 3, 0, 0), ("w", "cross", 1, 0, 1),
    ("m", "cross", 3, 0, 2), ("m", "cross", 3, 0, 3), ("small", 5), ("w", "at", 0, 0, 3), ("m", "rest", 0, 1),
    ("m", "cross", 1, 1, 1), ("m", "cross", 2, 0, 1), ("m", "cross", 2, 0, 2), ("m", "at", 2, 1, 2),
    ("w", "at", 2, 0, 2), ("w", "at", 3, 0, 1), ("m", "cross", 3, 1, 1), ("m", "cross", 1, 1, 2),
    ("w", "cross", 1, 0, 2), ("m", "rest", 1, 0), ("w", "cross", 0, 0, 1), ("w", "at", 3, 0, 2),
    ("m", "rest", 3, 0), ("m", "cross", 2, 1, 0), ("w", "at", 3, 0, 3), ("w", "cross", 3, 0, 0),
    ("w", "cross", 2, 0, 0), ("w", "cross", 2, 0, 1), ("w", "cross", 2, 0, 2), ("m", "cross", 3, 1, 2),
    ("m", "cross", 3, 1, 3), ("m", "rest", 3, 1), ("w", "cross", 0, 0, 2), ("w", "cross", 0, 0, 3),
    ("m", "rest", 1, 1), ("m", "cross", 2, 1, 1), ("w", "cross", 3, 0, 1), ("w", "rest", 1, 0),
    ("m", "cross", 2, 1, 2), ("w", "cross", 3, 0, 2), ("w", "cross", 3, 0, 3), ("m", "rest", 2, 0),
    ("w", "rest", 0, 0), ("m", "rest", 2, 1), ("w", "rest", 2, 0), ("w", "rest", 3, 0),
)


def normalize(matrix, norm_gain, norm_shift):
    average = jnp.mean(matrix, axis=-1, keepdims=True)
    center = matrix - average
    reciprocal = lax.rsqrt(jnp.mean(center * center, axis=-1, keepdims=True) + epsilon)
    unit_rows = center * reciprocal
    return (unit_rows * norm_gain + norm_shift, unit_rows, reciprocal)


def plain_norm_back(slope_rows, unit_rows, reciprocal, norm_gain):
    tilted = slope_rows * norm_gain
    centered_slope = tilted - jnp.mean(tilted, axis=-1, keepdims=True)
    centered_slope = centered_slope - unit_rows * jnp.mean(
        tilted * unit_rows, axis=-1, keepdims=True
    )
    return (
        centered_slope * reciprocal,
        jnp.sum(slope_rows * unit_rows, axis=0),
        jnp.sum(slope_rows, axis=0),
    )


def plain_contract(left_side, right_side):
    return lax.dot_general(
        left_side, right_side, (((0,), (0,)), ((), ())), preferred_element_type=jnp.float32
    )


def times_transpose(left_side, right_side):
    return lax.dot_general(
        left_side, right_side, (((1,), (1,)), ((), ())), preferred_element_type=jnp.float32
    )


def row_chances(mixing_full, row_docs):
    same_doc = row_docs[:, None] == row_docs[None, :]
    scores = jnp.where(same_doc[None, :, :], mixing_full.astype(jnp.float32), -1e30)
    row_top = jnp.max(scores, axis=-1, keepdims=True)
    raised = jnp.exp(scores - row_top)
    return raised / jnp.sum(raised, axis=-1, keepdims=True)


def plain(
    inputs,
    documents,
    mixing,
    value_weight,
    output_weight,
    mixer_gain,
    mixer_shift,
    dense_gain,
    dense_shift,
    hidden_weight,
    hidden_bias,
    down_weight,
    down_bias,
    cotangent,
):
    gathered = (
        lax.all_gather(mixing, "narrow", axis=1, tiled=True),
        lax.all_gather(value_weight, "narrow", axis=1, tiled=True),
        lax.all_gather(output_weight, "narrow", axis=0, tiled=True),
        lax.all_gather(mixer_gain, "narrow", axis=0, tiled=True),
        lax.all_gather(mixer_shift, "narrow", axis=0, tiled=True),
        lax.all_gather(dense_gain, "narrow", axis=0, tiled=True),
        lax.all_gather(dense_shift, "narrow", axis=0, tiled=True),
        lax.all_gather(hidden_bias, "narrow", axis=0, tiled=True),
        lax.all_gather(down_bias, "narrow", axis=0, tiled=True),
    )
    mixing_full, value_full, output_full = (gathered[0], gathered[1], gathered[2])
    gain_first = gathered[3].astype(jnp.float32)
    shift_first = gathered[4].astype(jnp.float32)
    gain_second = gathered[5].astype(jnp.float32)
    shift_second = gathered[6].astype(jnp.float32)
    bias_hidden = gathered[7].astype(jnp.float32)
    bias_down = gathered[8].astype(jnp.float32)
    halfway = (
        lax.all_gather(hidden_weight, "narrow", axis=0, tiled=True),
        lax.all_gather(down_weight, "narrow", axis=1, tiled=True),
    )
    hidden_full, down_full = (
        lax.all_gather(halfway[0], "wide", axis=1, tiled=True),
        lax.all_gather(halfway[1], "wide", axis=0, tiled=True),
    )
    row_count = inputs.shape[0]
    stream = inputs.reshape(row_count * SEQ, D).astype(jnp.float32)
    normed, unit_first, recip_first = normalize(stream, gain_first, shift_first)
    normed_low = normed.astype(jnp.bfloat16)
    values = jnp.dot(normed_low, value_full, preferred_element_type=jnp.float32).astype(
        jnp.bfloat16
    )
    value_rows = values.reshape(row_count, SEQ, D)

    def mix_one(bundle):
        row_values, row_docs = bundle
        chances_low = row_chances(mixing_full, row_docs).astype(jnp.bfloat16)
        per_head = row_values.reshape(SEQ, HEADS, HEAD)
        blended_row = jnp.einsum(
            "hij,jhd->ihd", chances_low, per_head, preferred_element_type=jnp.float32
        )
        return blended_row.reshape(SEQ, D).astype(jnp.bfloat16)

    blended = lax.map(mix_one, (value_rows, documents)).reshape(row_count * SEQ, D)
    middle = stream + jnp.dot(blended, output_full, preferred_element_type=jnp.float32)
    normed_two, unit_second, recip_second = normalize(middle, gain_second, shift_second)
    normed_two_low = normed_two.astype(jnp.bfloat16)
    hidden = jnp.dot(normed_two_low, hidden_full, preferred_element_type=jnp.float32) + bias_hidden
    activated, gelu_pull = jax.vjp(jax.nn.gelu, hidden)
    active = activated.astype(jnp.bfloat16)
    result = middle + jnp.dot(active, down_full, preferred_element_type=jnp.float32) + bias_down
    slope_low = cotangent.reshape(row_count * SEQ, D)
    slope_wide = slope_low.astype(jnp.float32)
    down_bias_sum = jnp.sum(slope_wide, axis=0)
    down_grad = plain_contract(active, slope_low)
    active_slope = times_transpose(slope_low, down_full)
    hidden_slope_wide = gelu_pull(active_slope)[0]
    hidden_slope = hidden_slope_wide.astype(jnp.bfloat16)
    hidden_bias_sum = jnp.sum(hidden_slope.astype(jnp.float32), axis=0)
    hidden_grad = plain_contract(normed_two_low, hidden_slope)
    normed_two_slope = times_transpose(hidden_slope, hidden_full)
    back_second, gain_second_sum, shift_second_sum = plain_norm_back(
        normed_two_slope, unit_second, recip_second, gain_second
    )
    middle_slope = slope_wide + back_second
    attended_slope = middle_slope.astype(jnp.bfloat16)
    output_grad = plain_contract(blended, attended_slope)
    blended_slope = times_transpose(attended_slope, output_full).astype(jnp.bfloat16)

    def mix_back(running, bundle):
        row_values, row_docs, row_slope = bundle
        chances = row_chances(mixing_full, row_docs)
        per_head = row_values.reshape(SEQ, HEADS, HEAD)
        head_slope = row_slope.reshape(SEQ, HEADS, HEAD)
        chance_slope = jnp.einsum(
            "ihd,jhd->hij", head_slope, per_head, preferred_element_type=jnp.float32
        )
        score_slope = chances * (
            chance_slope - jnp.sum(chances * chance_slope, axis=-1, keepdims=True)
        )
        value_part = jnp.einsum(
            "hij,ihd->jhd",
            chances.astype(jnp.bfloat16),
            head_slope,
            preferred_element_type=jnp.float32,
        )
        return (running + score_slope, value_part.reshape(SEQ, D).astype(jnp.bfloat16))

    mixing_start = jnp.zeros((HEADS, SEQ, SEQ), jnp.float32)
    mixing_grad, value_slopes = lax.scan(
        mix_back, mixing_start, (value_rows, documents, blended_slope.reshape(row_count, SEQ, D))
    )
    value_slope = value_slopes.reshape(row_count * SEQ, D)
    value_grad = plain_contract(normed_low, value_slope)
    normed_slope = times_transpose(value_slope, value_full)
    back_first, gain_first_sum, shift_first_sum = plain_norm_back(
        normed_slope, unit_first, recip_first, gain_first
    )
    inputs_slope = (middle_slope + back_first).astype(jnp.bfloat16)
    sums_half = (
        lax.psum_scatter(
            hidden_grad.astype(jnp.bfloat16), "wide", scatter_dimension=1, tiled=True
        ).astype(jnp.float32),
        lax.psum_scatter(
            down_grad.astype(jnp.bfloat16), "wide", scatter_dimension=0, tiled=True
        ).astype(jnp.float32),
    )
    hidden_share, down_share = (
        lax.psum_scatter(
            sums_half[0].astype(jnp.bfloat16), "narrow", scatter_dimension=0, tiled=True
        ).astype(jnp.float32),
        lax.psum_scatter(
            sums_half[1].astype(jnp.bfloat16), "narrow", scatter_dimension=1, tiled=True
        ).astype(jnp.float32),
    )
    shares = (
        lax.psum_scatter(
            mixing_grad.astype(jnp.bfloat16), "narrow", scatter_dimension=1, tiled=True
        ).astype(jnp.float32),
        lax.psum_scatter(
            value_grad.astype(jnp.bfloat16), "narrow", scatter_dimension=1, tiled=True
        ).astype(jnp.float32),
        lax.psum_scatter(
            output_grad.astype(jnp.bfloat16), "narrow", scatter_dimension=0, tiled=True
        ).astype(jnp.float32),
        lax.psum_scatter(
            gain_first_sum.astype(jnp.bfloat16), "narrow", scatter_dimension=0, tiled=True
        ).astype(jnp.float32),
        lax.psum_scatter(
            shift_first_sum.astype(jnp.bfloat16), "narrow", scatter_dimension=0, tiled=True
        ).astype(jnp.float32),
        lax.psum_scatter(
            gain_second_sum.astype(jnp.bfloat16), "narrow", scatter_dimension=0, tiled=True
        ).astype(jnp.float32),
        lax.psum_scatter(
            shift_second_sum.astype(jnp.bfloat16), "narrow", scatter_dimension=0, tiled=True
        ).astype(jnp.float32),
        lax.psum_scatter(
            hidden_bias_sum.astype(jnp.bfloat16), "narrow", scatter_dimension=0, tiled=True
        ).astype(jnp.float32),
        lax.psum_scatter(
            down_bias_sum.astype(jnp.bfloat16), "narrow", scatter_dimension=0, tiled=True
        ).astype(jnp.float32),
    )
    totals = (
        lax.psum(shares[0].astype(jnp.bfloat16), "wide").astype(jnp.float32),
        lax.psum(shares[1].astype(jnp.bfloat16), "wide").astype(jnp.float32),
        lax.psum(shares[2].astype(jnp.bfloat16), "wide").astype(jnp.float32),
        lax.psum(shares[3].astype(jnp.bfloat16), "wide").astype(jnp.float32),
        lax.psum(shares[4].astype(jnp.bfloat16), "wide").astype(jnp.float32),
        lax.psum(shares[5].astype(jnp.bfloat16), "wide").astype(jnp.float32),
        lax.psum(shares[6].astype(jnp.bfloat16), "wide").astype(jnp.float32),
        lax.psum(shares[7].astype(jnp.bfloat16), "wide").astype(jnp.float32),
        lax.psum(shares[8].astype(jnp.bfloat16), "wide").astype(jnp.float32),
    )
    return (
        result.reshape(row_count, SEQ, D).astype(jnp.bfloat16),
        inputs_slope.reshape(row_count, SEQ, D),
        totals[0],
        totals[1],
        totals[2],
        totals[3],
        totals[4],
        totals[5],
        totals[6],
        hidden_share,
        totals[7],
        down_share,
        totals[8],
    )


def solution(mesh):
    inner = local if dict(mesh.shape) == {"narrow": 2, "wide": 16} else plain
    return jax.shard_map(
        inner,
        mesh=mesh,
        in_specs=(
            P(("narrow", "wide"), None, None),
            P(("narrow", "wide"), None),
            P(None, "narrow", None),
            P(None, "narrow"),
            P("narrow", None),
            P("narrow"),
            P("narrow"),
            P("narrow"),
            P("narrow"),
            P("narrow", "wide"),
            P("narrow"),
            P("wide", "narrow"),
            P("narrow"),
            P(("narrow", "wide"), None, None),
        ),
        out_specs=(
            P(("narrow", "wide"), None, None),
            P(("narrow", "wide"), None, None),
            P(None, "narrow", None),
            P(None, "narrow"),
            P("narrow", None),
            P("narrow"),
            P("narrow"),
            P("narrow"),
            P("narrow"),
            P("narrow", "wide"),
            P("narrow"),
            P("wide", "narrow"),
            P("narrow"),
        ),
        check_vma=False,
    )
```

```python
import functools

import jax
import jax.numpy as jnp
from jax import lax
from jax.experimental import pallas as pl
from jax.experimental.pallas import tpu as pltpu
from jax.sharding import PartitionSpec as P

D = 768
HEADS = 12
HEAD = 64
SEQ = 512
FF = 3072
HALF = D // 2
CHUNK = 192
GROUP = 4 * CHUNK
epsilon = 1e-05

MESH = pl.DeviceIdType.MESH
f32 = jnp.float32
bf16 = jnp.bfloat16


def place():
    core = lax.axis_index("narrow")
    wide = lax.axis_index("wide")
    return core, lax.rem(wide, 2), lax.rem(lax.div(wide, 2), 2), lax.div(wide, 4)


def seat(core, x, y, z):
    return (core, z * 4 + y * 2 + x)


def remote(src, dst, send_sem, recv_sem, device):
    return pltpu.make_async_remote_copy(
        src_ref=src,
        dst_ref=dst,
        send_sem=send_sem,
        recv_sem=recv_sem,
        device_id=device,
        device_id_type=MESH,
    )


def greet(core, x, y, z, more=()):
    barrier = pltpu.get_barrier_semaphore()
    near = (seat(1 - core, x, y, z), seat(core, 1 - x, y, z), seat(core, x, 1 - y, z)) + more
    for device in near:
        pl.semaphore_signal(barrier, inc=1, device_id=device, device_id_type=MESH)

    @pl.when(z < 3)
    def _():
        pl.semaphore_signal(
            barrier, inc=1, device_id=seat(core, x, y, z + 1), device_id_type=MESH
        )

    @pl.when(z > 0)
    def _():
        pl.semaphore_signal(
            barrier, inc=1, device_id=seat(core, x, y, z - 1), device_id_type=MESH
        )

    above, below = jnp.where(z < 3, 1, 0), jnp.where(z > 0, 1, 0)
    pl.semaphore_wait(barrier, len(near) + above + below)


def halves(core):
    mine = pl.ds(pl.multiple_of(core * HALF, 128), HALF)
    other = pl.ds(pl.multiple_of((1 - core) * HALF, 128), HALF)
    return mine, other


def line_order(z, step):
    table = ((0, 1, 2, 3), (1, 0, 2, 3), (2, 1, 3, 0), (3, 2, 1, 0))
    return jnp.where(
        z == 0,
        table[0][step],
        jnp.where(z == 1, table[1][step], jnp.where(z == 2, table[2][step], table[3][step])),
    )


def unit_of(rows):
    center = rows - jnp.mean(rows, axis=-1, keepdims=True)
    reciprocal = lax.rsqrt(jnp.mean(center * center, axis=-1, keepdims=True) + epsilon)
    return center * reciprocal, reciprocal


def dot_nn(left, right):
    return lax.dot_general(left, right, (((1,), (0,)), ((), ())), preferred_element_type=f32)


def dot_nt(left, right):
    return lax.dot_general(left, right, (((1,), (1,)), ((), ())), preferred_element_type=f32)


def dot_tn(left, right):
    return lax.dot_general(left, right, (((0,), (0,)), ((), ())), preferred_element_type=f32)


def lane_ids(rows):
    return lax.broadcasted_iota(jnp.int32, (rows, 128), 1)


def fill_mask(docs_ref, mask, rows):
    for r in range(rows):
        flat = docs_ref[r : r + 1, :].astype(f32)
        for i in range(0, SEQ, 128):
            tall = jnp.broadcast_to(flat[:, i : i + 128], (128, 128)).T
            for j in range(0, SEQ, 128):
                wide = jnp.broadcast_to(flat[:, j : j + 128], (128, 128))
                mask[r, i : i + 128, j : j + 128] = jnp.where(tall == wide, 1.0, 0.0).astype(bf16)


def gelu_and_slope(v):
    scale = 0.7978845608028654
    square = v * v
    t = jnp.tanh(scale * v * (1.0 + 0.044715 * square))
    rise = 0.5 * (1.0 + t)
    slope = rise + 0.5 * scale * v * (1.0 - t * t) * (1.0 + 3.0 * 0.044715 * square)
    return v * rise, slope


def norm_slope(slope, unit, reciprocal, gain):
    tilted = slope * gain
    centered = tilted - jnp.mean(tilted, axis=-1, keepdims=True)
    centered = centered - unit * jnp.mean(tilted * unit, axis=-1, keepdims=True)
    return centered * reciprocal


class Reduce:
    def __init__(self, part, refs):
        self.part = part
        (
            self.first_y, self.first_x, self.second_x, self.second_y, self.line_in,
            self.first_sent, self.first_recv, self.second_sent, self.second_recv,
            self.line_sent, self.line_recv,
        ) = refs
        core, x, y, z = place()
        self.x, self.y, self.z = x, y, z
        self.near_x, self.near_y = seat(core, 1 - x, y, z), seat(core, x, 1 - y, z)
        self.above, self.below = seat(core, x, y, z + 1), seat(core, x, y, z - 1)

    @staticmethod
    def scratch(piece):
        dma = pltpu.SemaphoreType.DMA
        return [
            pltpu.VMEM((4, 2) + piece, bf16), pltpu.VMEM((4, 2) + piece, bf16),
            pltpu.VMEM((4,) + piece, bf16), pltpu.VMEM((4,) + piece, bf16),
            pltpu.VMEM((2, 4, 2) + piece, bf16),
            dma((4, 2)), dma((4, 2)), dma((4, 2)), dma((4, 2)), dma((2, 4, 2)), dma((2, 4, 2)),
        ]

    def first_copy(self, k, m):
        sems = self.first_sent.at[k, m], self.first_recv.at[k, m]
        if m == 0:
            return remote(self.part.at[k, 0, 1 - self.y], self.first_y.at[k], *sems, self.near_y)
        return remote(self.part.at[k, 1, :, 1 - self.x], self.first_x.at[k], *sems, self.near_x)

    def second_copy(self, k, m):
        x, y = self.x, self.y
        sems = self.second_sent.at[k, m], self.second_recv.at[k, m]
        if m == 0:
            return remote(self.part.at[k, 0, y, 1 - x], self.second_x.at[k], *sems, self.near_x)
        return remote(self.part.at[k, 1, 1 - y, x], self.second_y.at[k], *sems, self.near_y)

    def line_copy(self, k, m, down):
        return remote(
            self.part.at[k, m, self.y, self.x], self.line_in.at[down, k, m],
            self.line_sent.at[down, k, m], self.line_recv.at[down, k, m],
            self.below if down else self.above,
        )

    def add_in(self, k, m, y_of, x_of, got):
        old = self.part[k, m, y_of, x_of].astype(f32)
        self.part[k, m, y_of, x_of] = (old + got.astype(f32)).astype(bf16)

    def first(self, k, m):
        self.first_copy(k, m).start()

    def second(self, k, m):
        x, y = self.x, self.y
        self.first_copy(k, m).wait_recv()
        if m == 0:
            self.add_in(k, 0, y, 1 - x, self.first_y[k, 1 - x])
            self.second_copy(k, 0).start()
            self.add_in(k, 0, y, x, self.first_y[k, x])
        else:
            self.add_in(k, 1, 1 - y, x, self.first_x[k, 1 - y])
            self.second_copy(k, 1).start()
            self.add_in(k, 1, y, x, self.first_x[k, y])

    def line(self, k, m):
        self.second_copy(k, m).wait_recv()
        self.add_in(k, m, self.y, self.x, (self.second_x, self.second_y)[m][k])

    def hop(self, k, m, hop):
        x, y, z = self.x, self.y, self.z
        for down, length, seat_z in ((0, k, hop), (1, 3 - k, 3 - hop)):
            if hop < length:

                @pl.when(z == seat_z)
                def _():
                    if hop > 0:
                        self.line_copy(k, m, down).wait_recv()
                        self.add_in(k, m, y, x, self.line_in[down, k, m])
                    self.line_copy(k, m, down).start()

        if hop == max(k, 3 - k):

            @pl.when(z == k)
            def _():
                for down, length in ((0, k), (1, 3 - k)):
                    if length > 0:
                        self.line_copy(k, m, down).wait_recv()
                        self.add_in(k, m, y, x, self.line_in[down, k, m])

    def settle(self, k):
        for m in range(2):
            self.first_copy(k, m).wait_send()
            self.second_copy(k, m).wait_send()
            if k > 0:

                @pl.when(self.z < k)
                def _():
                    self.line_copy(k, m, 0).wait_send()

            if k < 3:

                @pl.when(self.z > k)
                def _():
                    self.line_copy(k, m, 1).wait_send()


class Gather:
    def __init__(self, whole, refs):
        self.whole = whole
        self.recv, self.sent_x, self.sent_y, self.sent_z = refs
        core, x, y, z = place()
        self.x, self.y, self.z = x, y, z
        self.near_x, self.near_y = seat(core, 1 - x, y, z), seat(core, x, 1 - y, z)
        self.above, self.below = seat(core, x, y, z + 1), seat(core, x, y, z - 1)

    @staticmethod
    def scratch(piece):
        dma = pltpu.SemaphoreType.DMA
        return [
            pltpu.VMEM((4, 2, 2, 2) + piece, bf16),
            dma((4, 2, 2, 2)), dma((4, 2, 2)), dma((4, 2, 2)), dma((2, 4, 2)),
        ]

    def send(self, k, m, y_of, x_of, sem, device):
        src = self.whole.at[k, m, y_of, x_of]
        return remote(src, src, sem, self.recv.at[k, m, y_of, x_of], device)

    def to_x(self, k, m, y_of):
        return self.send(k, m, y_of, self.x, self.sent_x.at[k, m, y_of], self.near_x)

    def to_y(self, k, m, x_of):
        return self.send(k, m, self.y, x_of, self.sent_y.at[k, m, x_of], self.near_y)

    def along(self, k, m, down):
        device = self.below if down else self.above
        return self.send(k, m, self.y, self.x, self.sent_z.at[down, k, m], device)

    def arrived(self, k, m, y_of, x_of):
        self.send(k, m, y_of, x_of, self.sent_x.at[k, m, 0], self.near_x).wait_recv()

    def at(self, k, m, distance, part=None):
        x, y, z = self.x, self.y, self.z
        up, down = k + distance, k - distance
        for seat_z in sorted({up, down}):
            if 0 <= seat_z < 4:

                @pl.when(z == seat_z)
                def _():
                    if distance:
                        self.arrived(k, m, y, x)
                    elif part is not None:
                        self.whole[k, m, y, x] = part[k, m, y, x]
                    if k <= seat_z < 3:
                        self.along(k, m, 0).start()
                    if k >= seat_z > 0:
                        self.along(k, m, 1).start()
                    if m == 0:
                        self.to_x(k, 0, y).start()
                    else:
                        self.to_y(k, 1, x).start()

    def two(self, k, m, distance):
        x, y, z = self.x, self.y, self.z
        for seat_z in sorted({k + distance, k - distance}):
            if 0 <= seat_z < 4:

                @pl.when(z == seat_z)
                def _():
                    if m == 0:
                        self.to_y(k, 0, x).start()
                    else:
                        self.to_x(k, 1, y).start()

    def cross(self, k, m, distance):
        x, y, z = self.x, self.y, self.z
        up, down = k + distance, k - distance
        for seat_z in sorted({up, down}):
            if 0 <= seat_z < 4:

                @pl.when(z == seat_z)
                def _():
                    if m == 0:
                        self.arrived(k, 0, y, 1 - x)
                        self.to_y(k, 0, 1 - x).start()
                    else:
                        self.arrived(k, 1, 1 - y, x)
                        self.to_x(k, 1, 1 - y).start()

    def rest(self, k, m):
        x, y = self.x, self.y
        if m == 0:
            self.arrived(k, 0, 1 - y, x)
        else:
            self.arrived(k, 1, y, 1 - x)
        self.arrived(k, m, 1 - y, 1 - x)

    def settle(self, k):
        x, y, z = self.x, self.y, self.z
        for m in range(2):
            self.to_x(k, m, y).wait_send()
            self.to_y(k, m, x).wait_send()
            if k < 3:

                @pl.when(jnp.logical_and(z >= k, z < 3))
                def _():
                    self.along(k, m, 0).wait_send()

            if k > 0:

                @pl.when(jnp.logical_and(z <= k, z > 0))
                def _():
                    self.along(k, m, 1).wait_send()

        self.to_y(k, 0, 1 - x).wait_send()
        self.to_x(k, 1, 1 - y).wait_send()


BLOCKS = ((0, 0), (0, 1), (0, 2), (1, 0), (1, 1), (1, 2), (1, 3))
TRIPLE = HEADS // 4
MIX_PIECE = (TRIPLE, 7, 16, 128)
WEIGHT_PIECE = (48, HALF)
DENSE_PIECE = (CHUNK, HALF)
ORDER = (0, 3, 1, 2)


def layer_kernel(
    x_hbm, docs_ref, mixing_ref, value_ref, output_ref, hidden_ref, down_ref, cotangent_hbm,
    first_gain_ref, first_shift_ref, second_gain_ref, second_shift_ref, down_bias_ref, hidden_bias_ref,
    result_out, inputs_out, mixing_out, weights_out, hidden_out, down_out, sums_out,
    full_ref, mixing_full, normed_hbm, share_hbm, middle_hbm,
    *scratch,
):
    scratch = list(scratch)

    def take(n):
        got = scratch[:n]
        del scratch[:n]
        return got

    b0, b1, b2, b3, b4, b5 = take(6)
    value_full, output_full, vector_full, vector_own, shard, mask, raised = take(7)
    total, slope, weight, grads, to_twin, from_twin, dense_part = take(7)
    chance, block_t, mix_part, mix_to, mix_from, weights_from, weights_part = take(7)
    small, small_in, sums = take(3)
    dense_refs = take(11)
    mix_reduce_refs = take(11)
    weights_reduce_refs = take(11)
    mix_whole, *mix_gather_refs = take(5)
    weights_whole, *weights_gather_refs = take(5)
    early_send, early_recv, early_local, shard_sem = take(4)
    full_recv, full_core_recv, full_x, full_y, full_up, full_down, full_core = take(7)
    pair_sem, back_sem, head_sem, weight_sem, move_sem, out_sem = take(6)
    twin_sent, twin_recv, twin_credit, mix_sent, mix_recv, mix_credit = take(6)
    weights_sent, weights_recv, small_sent, small_recv = take(4)

    core, x, y, z = place()
    mine, other = halves(core)
    near_x, near_y = seat(core, 1 - x, y, z), seat(core, x, 1 - y, z)
    above, below = seat(core, x, y, z + 1), seat(core, x, y, z - 1)
    twin = seat(1 - core, x, y, z)
    tokens = b0.shape[0]
    rows_count = tokens // SEQ
    block = 256
    dense = Reduce(dense_part, dense_refs)
    families = {
        "m": (Reduce(mix_part, mix_reduce_refs), Gather(mix_whole, mix_gather_refs), mix_part),
        "w": (Reduce(weights_part, weights_reduce_refs), Gather(weights_whole, weights_gather_refs), weights_part),
    }
    pairs = (seat(core, x, y, z + 1 - 2 * lax.rem(z, 2)), seat(core, x, y, lax.rem(z + 2, 4)))
    rounds = (twin, near_x, near_y) + pairs
    ks = [line_order(z, i) for i in range(4)]

    def rows_of(b):
        return pl.ds(pl.multiple_of(b * block, block), block)

    def move(n, src, dst):
        return pltpu.make_async_copy(src, dst, move_sem.at[n])

    load_x = move(0, x_hbm, b0)
    keep_normed = move(1, b1, normed_hbm)
    load_cotangent = move(2, cotangent_hbm, b1)
    keep_share = move(3, slope, share_hbm)
    keep_middle = move(4, total, middle_hbm)
    load_share = move(5, share_hbm, total)
    load_normed = move(6, normed_hbm, b0)
    keep_result = move(7, b1, result_out)
    load_x_again = move(8, x_hbm, b1)
    keep_inputs = move(9, b0, inputs_out)

    def load_middle(b):
        return move(10 + b, middle_hbm.at[rows_of(b)], grads.at[pl.ds((b % 3) * block, block)])

    my_rows = pl.ds(pl.multiple_of(core * (SEQ // 2), SEQ // 2), SEQ // 2)
    early = {"vec": (vector_own, vector_full.at[:, mine]), "vw": (value_ref, value_full.at[:, mine])}
    for p in range(HEADS // 2):
        heads_of = pl.ds(2 * p, 2)
        early["mx%d" % p] = (mixing_ref.at[heads_of], mixing_full.at[heads_of, my_rows])
    early["ow"] = (output_ref, output_full.at[mine, :])
    names = list(early)

    def early_copy(name):
        n = names.index(name)
        return remote(*early[name], early_send.at[n], early_recv.at[n], twin)

    def early_own(name):
        src, dst = early[name]
        if name.startswith("mx"):
            dst = raised.at[int(name[2:]) % 2, :, my_rows]
        return pltpu.make_async_copy(src, dst, early_local.at[names.index(name)])

    def chunk_of(k, y_of, x_of):
        return k * 4 + y_of * 2 + x_of

    own = chunk_of(z, y, x)

    def slot(m, chunk):
        return full_ref.at[m, pl.ds(pl.multiple_of(chunk * CHUNK, CHUNK), CHUNK), mine]

    def full_copy(m, chunk, sems, device, src=None):
        dst = slot(m, chunk)
        return remote(dst if src is None else src, dst, sems.at[m, chunk], full_recv.at[m, chunk], device)

    def full_arrived(m, chunk):
        full_copy(m, chunk, full_x, near_x).wait_recv()

    def own_copy(m):
        return pltpu.make_async_copy(shard.at[m], slot(m, own), shard_sem.at[m])

    def gather(step, i, m):
        k = ks[i]
        if step == "at":
            chunk = chunk_of(k, y, x)
            src = shard.at[m] if i == 0 else None
            if i > 0:
                full_arrived(m, chunk)

            @pl.when(jnp.logical_and(k <= z, z < 3))
            def _():
                full_copy(m, chunk, full_up, above, src).start()

            @pl.when(jnp.logical_and(k >= z, z > 0))
            def _():
                full_copy(m, chunk, full_down, below, src).start()

            sems, device = ((full_x, near_x), (full_y, near_y))[m]
            full_copy(m, chunk, sems, device, src).start()
        elif step == "two":
            sems, device = ((full_y, near_y), (full_x, near_x))[m]
            full_copy(m, chunk_of(k, y, x), sems, device, shard.at[m] if i == 0 else None).start()
        elif step == "cross":
            if m == 0:
                full_arrived(0, chunk_of(k, y, 1 - x))
                full_copy(0, chunk_of(k, y, 1 - x), full_y, near_y).start()
            else:
                full_arrived(1, chunk_of(k, 1 - y, x))
                full_copy(1, chunk_of(k, 1 - y, x), full_x, near_x).start()
        else:
            full_arrived(m, chunk_of(k, 1 - y, x) if m == 0 else chunk_of(k, y, 1 - x))
            full_arrived(m, chunk_of(k, 1 - y, 1 - x))

    def full_twin(i, m):
        src = full_ref.at[m, pl.ds(pl.multiple_of(ks[i] * GROUP, GROUP), GROUP), mine]
        return remote(src, src, full_core.at[m, i], full_core_recv.at[m, i], twin)

    def pass_full(i, m):
        if i == 0:
            own_copy(m).wait()
        full_twin(i, m).start()

    def load_weight(i):
        rows = pl.ds(pl.multiple_of(ks[i] * GROUP, GROUP), GROUP)
        return pltpu.make_async_copy(full_ref.at[:, rows], weight.at[i % 2], weight_sem.at[i % 2])

    def fetch(i):
        for m in range(2):
            full_twin(i, m).wait_recv()
        load_weight(i).start()

    def first_norm(b):
        if b == 0:
            load_x.wait()
        rows = rows_of(b)
        unit, _ = unit_of(b0[rows, :].astype(f32))
        low = (unit * vector_full[0:1, :] + vector_full[1:2, :]).astype(bf16)
        b1[rows, :] = low
        b2[rows, :] = dot_nn(low, value_full[...]).astype(bf16)
        if b == tokens // block - 1:
            keep_normed.start()

    twin_rows = pl.ds(pl.multiple_of((1 - core) * (SEQ // 2), SEQ // 2), SEQ // 2)

    def load_pair(p):
        return pltpu.make_async_copy(
            mixing_full.at[pl.ds(2 * p, 2), twin_rows], raised.at[p % 2, :, twin_rows], pair_sem.at[p % 2]
        )

    def keep_pair(p):
        return pltpu.make_async_copy(raised.at[p % 2], mixing_full.at[pl.ds(2 * p, 2)], back_sem.at[p % 2])

    def mix(p):
        early_own("mx%d" % p).wait()
        load_pair(p).wait()
        if p + 1 < HEADS // 2:
            early_copy("mx%d" % (p + 1)).wait_recv()
            if p >= 1:
                keep_pair(p - 1).wait()
            early_own("mx%d" % (p + 1)).start()
            load_pair(p + 1).start()
        lanes = slice(p * 128, (p + 1) * 128)
        low_lanes = lane_ids(block) < HEAD
        pair_raised = raised.at[p % 2]
        for half in range(2):
            for i in range(0, SEQ, block):
                part = pair_raised[half, i : i + block].astype(f32)
                pair_raised[half, i : i + block] = jnp.exp(part).astype(bf16)
        keep_pair(p).start()

        def mix_row(r, _):
            pair = b2[pl.ds(pl.multiple_of(r * SEQ, SEQ), SEQ), lanes]
            left_half = lane_ids(SEQ) < HEAD
            ones = jnp.ones_like(pair)
            first = jnp.where(left_half, pair, ones)
            second = jnp.where(left_half, ones, pair)
            for i in range(0, SEQ, block):
                keep = mask[r, i : i + block]
                one = dot_nn(pair_raised[0, i : i + block] * keep, first)
                two = dot_nn(pair_raised[1, i : i + block] * keep, second)
                part = 1.0 / pltpu.roll(jnp.where(low_lanes, two, one), HEAD, 1)
                done = pl.ds(pl.multiple_of(r * SEQ + i, block), block)
                slope[done, lanes] = part
                b3[done, lanes] = (jnp.where(low_lanes, one, two) * part).astype(bf16)
            return 0

        lax.fori_loop(0, rows_count, mix_row, 0)
        if p == HEADS // 2 - 1:
            keep_share.start()
            keep_normed.wait()
            load_cotangent.start()

    def early_ready(name):
        if name in ("vw", "ow"):
            early_own(name).wait()
        early_copy(name).wait_recv()
        if name == "mx0":
            early_own("mx0").start()
            load_pair(0).start()

    def project(b):
        rows = rows_of(b)
        middle = b0[rows, :].astype(f32) + dot_nn(b3[rows, :], output_full[...])
        total[rows, :] = middle
        unit, _ = unit_of(middle)
        b0[rows, :] = (unit * vector_full[2:3, :] + vector_full[3:4, :]).astype(bf16)
        if b == tokens // block - 1:
            keep_middle.start()
            keep_share.wait()
            sums[...] = jnp.zeros_like(sums)

    def dense_units(i, u):
        k = ks[i]
        if u == 0:
            load_weight(i).wait()
        if i == 0 and u == 0:
            load_cotangent.wait()
        units = slice(u * 256, (u + 1) * 256)
        lanes = pl.ds(pl.multiple_of(lax.div(k, 2) * HALF, 128), HALF)
        row = 5 + 2 * lax.rem(k, 2)
        bias = jnp.concatenate(
            [vector_full[pl.ds(row, 1), lanes], vector_full[pl.ds(row + 1, 1), lanes]], axis=1
        )[:, units]
        hidden = dot_nt(b0[...], weight[i % 2, 0, units, :]) + bias
        pulled = dot_nt(b1[...], weight[i % 2, 1, units, :])
        act, pull = gelu_and_slope(hidden)
        turned = (pulled * pull).astype(bf16)
        b4[:, units] = act.astype(bf16)
        b5[:, units] = turned
        sums[pl.ds(3 + k, 1), units] = jnp.sum(turned.astype(f32), axis=0, keepdims=True)

    def dense_grad(i, m):
        left, right = ((b5, b0), (b4, b1))[m]
        grads[...] = dot_tn(left[...], right[...])

    def dense_back(i, m):
        if m == 1:
            if i == 0:
                keep_middle.wait()
            total[...] += dot_nn(b4[...], weight[i % 2, 1])
        elif i == 0:
            slope[...] = dot_nn(b5[...], weight[i % 2, 0])
        else:
            slope[...] += dot_nn(b5[...], weight[i % 2, 0])
        if i == 3 and m == 0:
            for b in range(3):
                load_middle(b).start()

    def dense_twin(i, m):
        return remote(
            to_twin.at[m], from_twin.at[i % 2, m], twin_sent.at[i, m], twin_recv.at[i, m], twin
        )

    def swap_dense(i, m):
        if i >= 1:
            dense_twin(i - 1, m).wait_send()
        to_twin[m] = grads[:, other].astype(bf16)
        dense_part[ks[i], m] = grads[:, mine].astype(bf16).reshape((2, 2) + DENSE_PIECE)
        if i >= 2:
            pl.semaphore_wait(twin_credit.at[i % 2, m], 1)
        dense_twin(i, m).start()

    def swapped_dense(i, m):
        dense_twin(i, m).wait_recv()
        k = ks[i]
        both = dense_part[k, m].astype(f32) + from_twin[i % 2, m].reshape((2, 2) + DENSE_PIECE).astype(f32)
        dense_part[k, m] = both.astype(bf16)
        if i < 2:
            pl.semaphore_signal(twin_credit.at[i % 2, m], inc=1, device_id=twin, device_id_type=MESH)

    def second_finish(b):
        load_middle(b).wait()
        rows = rows_of(b)
        unit, reciprocal = unit_of(grads[pl.ds((b % 3) * block, block), :])
        if b == 0:
            load_middle(3).start()
        raw = slope[rows, :]
        cot = b1[rows, :].astype(f32)
        sums[0:1, :] += jnp.sum(cot, axis=0, keepdims=True)
        sums[1:2, :] += jnp.sum(raw * unit, axis=0, keepdims=True)
        sums[2:3, :] += jnp.sum(raw, axis=0, keepdims=True)
        moved = cot + norm_slope(raw, unit, reciprocal, vector_full[2:3, :])
        slope[rows, :] = moved
        low = moved.astype(bf16)
        b4[rows, :] = low
        b5[rows, :] = dot_nt(low, output_full[...]).astype(bf16)
        b1[rows, :] = (total[rows, :] + vector_full[4:5, :]).astype(bf16)
        if b == tokens // block - 1:
            keep_result.start()
            load_share.start()
            load_normed.start()

    def output_grad():
        grads[...] = dot_tn(b3[...], b4[...])
        keep_result.wait()
        load_x_again.start()

    def scale_pair(p, _):
        lanes = pl.ds(pl.multiple_of(p * 128, 128), 128)
        for r in range(rows_count):
            rows = pl.ds(r * SEQ, SEQ)
            low = (b5[rows, lanes].astype(f32) * total[rows, lanes]).astype(bf16)
            b5[rows, lanes] = low
            weight[r, 0, lanes, 0:SEQ] = low.T
        return 0

    def load_head(n):
        h = ORDER[n // TRIPLE] * TRIPLE + n % TRIPLE
        return pltpu.make_async_copy(mixing_full.at[h], raised.at[n // 2 % 2, n % 2], head_sem.at[n % 4])

    def prepare():
        load_share.wait()
        for p in range(HEADS // 2 - 2, HEADS // 2):
            keep_pair(p).wait()
        for n in range(3):
            load_head(n).start()
        lax.fori_loop(0, HEADS // 2, scale_pair, 0)

    def head(i, n):
        k, step = ORDER[i], i * TRIPLE + n
        load_head(step).wait()
        if step + 3 < HEADS:
            load_head(step + 3).start()
        if n == 0 and i >= 2:
            mix_twin(i - 2).wait_send()
        h = k * TRIPLE + n
        lanes = slice((h // 2) * 128, (h // 2 + 1) * 128)
        side = h % 2
        lane = lane_ids(block)
        inside = lane < HEAD if side == 0 else lane >= HEAD
        inside_all = lane_ids(SEQ) < HEAD if side == 0 else lane_ids(SEQ) >= HEAD
        spot = lane - HEAD * (1 - side)
        for where in range(2):
            half = core if where == 0 else 1 - core
            start = pl.multiple_of(half * block, block)
            here = pl.ds(start, block)
            sum_rows = None
            for r in range(rows_count):
                rows = pl.ds(pl.multiple_of(r * SEQ + start, block), block)
                low = b5[rows, lanes].astype(f32)
                delta = jnp.sum(
                    jnp.where(inside, low * b3[rows, lanes].astype(f32), 0.0), axis=-1, keepdims=True
                )
                coarse = delta.astype(bf16).astype(f32)
                extra = jnp.where(spot == 0, -coarse, jnp.where(spot == 1, coarse - delta, 0.0))
                left = jnp.where(inside, low, extra).astype(bf16)
                pair = b2[r * SEQ : (r + 1) * SEQ, lanes].astype(f32)
                right = jnp.where(inside_all, pair, 1.0).astype(bf16)
                part = raised[step // 2 % 2, step % 2, here] * mask[r, here]
                chance[r, here] = part
                term = part.astype(f32) * dot_nt(left, right)
                sum_rows = term if sum_rows is None else sum_rows + term
            block_t[...] = sum_rows.astype(bf16)
            for p, (row, column) in enumerate(BLOCKS):
                top = pl.multiple_of((row + half * (1 - 2 * row)) * 128, 128)
                side_lanes = pl.ds(pl.multiple_of((column + half * (3 - 2 * column)) * 128, 128), 128)
                for q in range(8):
                    strip = block_t[pl.ds(pl.multiple_of(top + q * 16, 16), 16), side_lanes]
                    spot_of = (q % 2, q // 4, (q // 2) % 2, n, p)
                    if where == 0:
                        mix_part[(k,) + spot_of] = strip
                    else:
                        mix_to[(i % 2,) + spot_of] = strip
        heads_rows = slice(h * HEAD, (h + 1) * HEAD)
        for r in range(rows_count):
            weight[r, 1, heads_rows, 0:SEQ] = dot_nn(
                weight[r, 0, heads_rows, 0:SEQ], chance[r]
            ).astype(bf16)

    def turn():
        def turn_pair(p, _):
            lanes = pl.ds(pl.multiple_of(p * 128, 128), 128)
            for r in range(rows_count):
                b4[r * SEQ : (r + 1) * SEQ, lanes] = weight[r, 1, lanes, 0:SEQ].T
            return 0

        lax.fori_loop(0, D // 128, turn_pair, 0)

    def value_grad():
        load_normed.wait()
        grads[...] = dot_tn(b0[...], b4[...])

    def first_finish(b):
        if b == 0:
            load_x_again.wait()
            small[0] = jnp.zeros_like(small[0])
            small[0, 0:8] = sums[...]
        rows = rows_of(b)
        back = dot_nt(b4[rows, :], value_full[...])
        unit, reciprocal = unit_of(b1[rows, :].astype(f32))
        small[0, 7:8, :] += jnp.sum(back * unit, axis=0, keepdims=True)
        small[0, 8:9, :] += jnp.sum(back, axis=0, keepdims=True)
        moved = slope[rows, :] + norm_slope(back, unit, reciprocal, vector_full[0:1, :])
        b0[rows, :] = moved.astype(bf16)
        if b == tokens // block - 1:
            keep_inputs.start()

    other_rows = pl.ds(pl.multiple_of((1 - core) * HALF, HALF), HALF)
    share_rows = D // 4

    def weights_twin(m):
        return remote(to_twin.at[m], weights_from.at[m], weights_sent.at[m], weights_recv.at[m], twin)

    def mix_twin(i):
        return remote(mix_to.at[i % 2], mix_from.at[i % 2], mix_sent.at[i], mix_recv.at[i], twin)

    def swap(what):
        if what == "vg" or what == "og":
            m = 0 if what == "vg" else 1
            dense_twin(3, m).wait_send()
            if m == 0:
                to_twin[0] = grads[:, other].astype(bf16)
            else:
                for side in range(2):
                    to_twin[1, side * HALF : (side + 1) * HALF] = grads[
                        other_rows, side * HALF : (side + 1) * HALF
                    ].astype(bf16)
            for k in range(4):
                rows = slice(k * share_rows, (k + 1) * share_rows)
                own_rows = pl.ds(pl.multiple_of(core * HALF + (k % 2) * share_rows, 64), share_rows)
                side = slice((k // 2) * HALF, (k // 2 + 1) * HALF)
                part = grads[rows, mine] if m == 0 else grads[own_rows, side]
                weights_part[k, m] = part.astype(bf16).reshape((2, 2) + WEIGHT_PIECE)
            weights_twin(m).start()
        else:
            if what >= 2:
                pl.semaphore_wait(mix_credit.at[what % 2], 1)
            mix_twin(what).start()

    def swapped(what):
        if what == "vg" or what == "og":
            m = 0 if what == "vg" else 1
            weights_twin(m).wait_recv()
            for k in range(4):
                got = weights_from[m, k * share_rows : (k + 1) * share_rows].astype(f32)
                both = weights_part[k, m].astype(f32) + got.reshape((2, 2) + WEIGHT_PIECE)
                weights_part[k, m] = both.astype(bf16)
        else:
            mix_twin(what).wait_recv()
            k = ORDER[what]
            for m in range(2):
                for y_of in range(2):
                    for x_of in range(2):
                        families["m"][0].add_in(k, m, y_of, x_of, mix_from[what % 2, m, y_of, x_of])
            if what < 2:
                pl.semaphore_signal(mix_credit.at[what % 2], inc=1, device_id=twin, device_id_type=MESH)

    def small_copy(n):
        return remote(small.at[n], small_in.at[n], small_sent.at[n], small_recv.at[n], rounds[n])

    def small_round(n):
        if n > 0:
            small_copy(n - 1).wait_recv()
            small[n] = small[n - 1] + small_in[n - 1]
        if n < len(rounds):
            small_copy(n).start()

    def dense_reduce(step, *rest):
        if step == "hop":
            dense.hop(*rest)
        else:
            i, m = rest
            getattr(dense, step)(ks[i], m)

    load_x.start()
    shard[0] = hidden_ref[...]
    shard[1] = down_ref[...]
    vector_own[...] = jnp.zeros_like(vector_own)
    singles = (first_gain_ref, first_shift_ref, second_gain_ref, second_shift_ref, down_bias_ref)
    for n, ref in enumerate(singles):
        vector_own[n : n + 1, :] = ref[...].astype(f32).reshape(1, HALF)
    for n in range(4):
        piece = hidden_bias_ref[n * HALF : (n + 1) * HALF]
        vector_own[5 + n : 6 + n, :] = piece.astype(f32).reshape(1, HALF)
    vector_full[:, mine] = vector_own[...]
    greet(core, x, y, z, (pairs[1],))
    for m in range(2):
        own_copy(m).start()
    for name in ("vw", "ow"):
        early_own(name).start()

    local_steps = {
        "early": lambda name: early_copy(name).start(), "ready": early_ready, "gs": gather,
        "pass": pass_full, "fetch": fetch, "norm": first_norm,
        "mask": lambda: fill_mask(docs_ref, mask, rows_count), "mix": mix, "proj": project,
        "dense": dense_units, "grad": dense_grad, "acc": dense_back, "swapF": swap_dense,
        "swappedF": swapped_dense, "Fs": dense_reduce, "fin2": second_finish, "og": output_grad,
        "scale": prepare, "head": head, "turn": turn, "vg": value_grad, "fin1": first_finish,
        "swap": swap, "swapped": swapped, "small": small_round,
    }
    for name, *rest in SCHEDULE:
        if name in local_steps:
            local_steps[name](*rest)
            continue
        reduce, spread, part = families[name]
        step, *rest = rest
        if step == "at":
            spread.at(*rest, part)
        elif step in ("two", "cross", "rest"):
            getattr(spread, step)(*rest)
        else:
            getattr(reduce, step)(*rest)
            if step == "line":
                reduce.hop(*rest, 0)

    def out_copy(n, src, dst):
        return pltpu.make_async_copy(src, dst, out_sem.at[n])

    outs = [out_copy(0, mix_whole, mixing_out), out_copy(1, weights_whole, weights_out)]
    for copy in outs:
        copy.start()
    for k in range(4):

        @pl.when(z == k)
        def _():
            for m, out in enumerate((hidden_out, down_out)):
                out[...] = dense_part[k, m, y, x].astype(f32)

    for n, row in enumerate((0, 1, 2, 7, 8)):
        sums_out[n : n + 1, :] = small[5, row : row + 1, mine]
    for n in range(4):
        line = pl.ds(3 + 2 * core + n // 2, 1)
        sums_out[5 + n : 6 + n, :] = small[5, line, (n % 2) * HALF : (n % 2 + 1) * HALF]
    sums_out[9:16, :] = jnp.zeros((7, HALF), f32)
    for name in names:
        early_copy(name).wait_send()
    for n in range(5):
        small_copy(n).wait_send()
    for m in range(2):
        weights_twin(m).wait_send()
        for i in range(4):
            full_twin(i, m).wait_send()
    for i in (2, 3):
        mix_twin(i).wait_send()

    def settle_line(k, _):
        line = chunk_of(k, y, x)
        for m in range(2):
            full_copy(m, line, full_x, near_x).wait_send()
            full_copy(m, line, full_y, near_y).wait_send()

            @pl.when(jnp.logical_and(k <= z, z < 3))
            def _():
                full_copy(m, line, full_up, above).wait_send()

            @pl.when(jnp.logical_and(k >= z, z > 0))
            def _():
                full_copy(m, line, full_down, below).wait_send()

        full_copy(0, chunk_of(k, y, 1 - x), full_y, near_y).wait_send()
        full_copy(1, chunk_of(k, 1 - y, x), full_x, near_x).wait_send()
        return 0

    lax.fori_loop(0, 4, settle_line, 0)
    for k in range(4):
        dense.settle(k)
        for reduce, spread, _ in families.values():
            reduce.settle(k)
            spread.settle(k)
    keep_inputs.wait()
    for copy in outs:
        copy.wait()


def layer_call(
    x, documents, mixing, value_weight, output_weight, hidden_weight, down_weight, cotangent, *vectors
):
    tokens = x.shape[0]
    rows = tokens // SEQ
    any_spec = pl.BlockSpec(memory_space=pl.ANY)
    vmem = pl.BlockSpec(memory_space=pltpu.VMEM)
    shape = jax.ShapeDtypeStruct
    dma = pltpu.SemaphoreType.DMA
    credit = pltpu.SemaphoreType.REGULAR
    token_rows = pltpu.VMEM((tokens, D), bf16)
    half_grads = (2, D, HALF)
    quads = (2, 2, 2)
    return pl.pallas_call(
        layer_kernel,
        out_shape=(
            shape((tokens, D), bf16), shape((tokens, D), bf16), shape((4,) + quads + MIX_PIECE, bf16),
            shape((4,) + quads + WEIGHT_PIECE, bf16), shape(DENSE_PIECE, f32), shape(DENSE_PIECE, f32),
            shape((16, HALF), f32),
            shape((2, FF, D), bf16), shape((HEADS, SEQ, SEQ), bf16), shape((tokens, D), bf16),
            shape((tokens, D), f32), shape((tokens, D), f32),
        ),
        in_specs=[any_spec, vmem, any_spec, any_spec, any_spec, vmem, vmem, any_spec] + [vmem] * 6,
        out_specs=[any_spec] * 4 + [vmem] * 3 + [any_spec] * 5,
        scratch_shapes=[
            *[token_rows] * 6,
            pltpu.VMEM((D, D), bf16), pltpu.VMEM((D, D), bf16), pltpu.VMEM((16, D), f32),
            pltpu.VMEM((16, HALF), f32), pltpu.VMEM((2,) + DENSE_PIECE, bf16), pltpu.VMEM((rows, SEQ, SEQ), bf16),
            pltpu.VMEM((2, 2, SEQ, SEQ), bf16),
            pltpu.VMEM((tokens, D), f32), pltpu.VMEM((tokens, D), f32),
            pltpu.VMEM((2, 2, GROUP, D), bf16), pltpu.VMEM((D, D), f32), pltpu.VMEM(half_grads, bf16),
            pltpu.VMEM((2,) + half_grads, bf16), pltpu.VMEM((4,) + quads + DENSE_PIECE, bf16),
            pltpu.VMEM((rows, SEQ, SEQ), bf16), pltpu.VMEM((SEQ // 2, SEQ), bf16),
            pltpu.VMEM((4,) + quads + MIX_PIECE, bf16), pltpu.VMEM((2,) + quads + MIX_PIECE, bf16),
            pltpu.VMEM((2,) + quads + MIX_PIECE, bf16), pltpu.VMEM(half_grads, bf16),
            pltpu.VMEM((4,) + quads + WEIGHT_PIECE, bf16),
            pltpu.VMEM((6, 16, D), f32), pltpu.VMEM((5, 16, D), f32), pltpu.VMEM((8, D), f32),
            *Reduce.scratch(DENSE_PIECE), *Reduce.scratch(MIX_PIECE), *Reduce.scratch(WEIGHT_PIECE),
            *Gather.scratch(MIX_PIECE), *Gather.scratch(WEIGHT_PIECE),
            dma((9,)), dma((9,)), dma((9,)), dma((2,)),
            dma((2, 16)), dma((2, 4)), dma((2, 16)), dma((2, 16)), dma((2, 16)), dma((2, 16)), dma((2, 4)),
            dma((2,)), dma((2,)), dma((4,)), dma((2,)), dma((14,)), dma((2,)),
            dma((4, 2)), dma((4, 2)), credit((2, 2)), dma((4,)), dma((4,)), credit((2,)),
            dma((2,)), dma((2,)), dma((5,)), dma((5,)),
        ],
        compiler_params=pltpu.CompilerParams(
            collective_id=0, has_side_effects=True, vmem_limit_bytes=64 << 20
        ),
    )(x, documents, mixing, value_weight, output_weight, hidden_weight, down_weight, cotangent, *vectors)


def unpack_kernel(
    mixing_ref, weights_ref, sums_ref, hidden_ref, down_ref, result_ref, inputs_ref,
    result_out, inputs_out, mixing_out, value_out, output_out, first_gain_out, first_shift_out,
    second_gain_out, second_shift_out, hidden_out, hidden_bias_out, down_out, down_bias_out,
):
    half = lax.axis_index("narrow")

    def corner(row, column):
        return (
            pl.multiple_of((row + half * (1 - 2 * row)) * 128, 128),
            pl.ds(pl.multiple_of((column + half * (3 - 2 * column)) * 128, 128), 128),
        )

    for h in range(TRIPLE):
        top, lanes = corner(0, 3)
        mixing_out[h, pl.ds(top, 128), lanes] = jnp.zeros((128, 128), f32)
        for p, (row, column) in enumerate(BLOCKS):
            top, lanes = corner(row, column)
            for q in range(8):
                strip = mixing_ref[0, q % 2, q // 4, (q // 2) % 2, h, p]
                mixing_out[h, pl.ds(pl.multiple_of(top + q * 16, 16), 16), lanes] = strip.astype(f32)
    value_out[...] = weights_ref[0, 0].astype(f32).reshape(D // 4, HALF)
    output_out[...] = weights_ref[0, 1].astype(f32).reshape(D // 4, HALF)
    result_out[...] = result_ref[...]
    inputs_out[...] = inputs_ref[...]

    @pl.when(pl.program_id(0) == 0)
    def _():
        hidden_out[...] = hidden_ref[...]
        down_out[...] = down_ref[...]
        singles = (down_bias_out, second_gain_out, second_shift_out, first_gain_out, first_shift_out)
        for n, out in enumerate(singles):
            out[...] = sums_ref[n]
        for n in range(4):
            hidden_bias_out[n * HALF : (n + 1) * HALF] = sums_ref[5 + n]


def unpack_call(mixing_packed, weights_packed, sums, hidden_share, down_share, result, inputs_slope):
    tokens = result.shape[0]
    shape = jax.ShapeDtypeStruct
    rows = pl.BlockSpec((tokens // 4, D), lambda k: (k, 0))
    piece = pl.BlockSpec(DENSE_PIECE, lambda k: (0, 0))
    single = pl.BlockSpec((HALF,), lambda k: (0,))
    quads = (1, 2, 2, 2)
    return pl.pallas_call(
        unpack_kernel,
        grid=(4,),
        out_shape=(
            shape((tokens, D), bf16), shape((tokens, D), bf16), shape((HEADS, SEQ // 2, SEQ), f32),
            shape((D, HALF), f32), shape((HALF, D), f32), *[shape((HALF,), f32)] * 4,
            shape(DENSE_PIECE, f32), shape((4 * HALF,), f32), shape(DENSE_PIECE, f32), shape((HALF,), f32),
        ),
        in_specs=[
            pl.BlockSpec(quads + MIX_PIECE, lambda k: (k,) + (0,) * 7),
            pl.BlockSpec(quads + WEIGHT_PIECE, lambda k: (k,) + (0,) * 5),
            pl.BlockSpec((16, HALF), lambda k: (0, 0)), piece, piece, rows, rows,
        ],
        out_specs=(
            rows, rows, pl.BlockSpec((TRIPLE, SEQ // 2, SEQ), lambda k: (k, 0, 0)),
            pl.BlockSpec((D // 4, HALF), lambda k: (k, 0)),
            pl.BlockSpec((D // 4, HALF), lambda k: (lax.rem(k, 2), lax.div(k, 2))),
            *[single] * 4, piece, pl.BlockSpec((4 * HALF,), lambda k: (0,)), piece, single,
        ),
        compiler_params=pltpu.CompilerParams(vmem_limit_bytes=62 << 20),
    )(mixing_packed, weights_packed, sums, hidden_share, down_share, result, inputs_slope)


def local(
    inputs, documents, mixing, value_weight, output_weight, mixer_gain, mixer_shift, dense_gain,
    dense_shift, hidden_weight, hidden_bias, down_weight, down_bias, cotangent,
):
    tokens = inputs.shape[0] * SEQ
    result, inputs_slope, mixing_packed, weights_packed, hidden_share, down_share, sums, *_ = layer_call(
        inputs.reshape(tokens, D), documents, mixing, value_weight, output_weight, hidden_weight.T,
        down_weight, cotangent.reshape(tokens, D), mixer_gain, mixer_shift, dense_gain, dense_shift,
        down_bias, hidden_bias,
    )
    outs = list(unpack_call(
        mixing_packed, weights_packed, sums, hidden_share, down_share, result, inputs_slope
    ))
    outs[0] = outs[0].reshape(inputs.shape)
    outs[1] = outs[1].reshape(inputs.shape)
    outs[9] = outs[9].T
    return tuple(outs)


SCHEDULE = (
    ("early", "vec"), ("early", "vw"), ("early", "mx0"), ("early", "mx1"), ("early", "mx2"), ("early", "mx3"),
    ("early", "mx4"), ("early", "mx5"), ("early", "ow"), ("gs", "at", 0, 0), ("gs", "at", 0, 1),
    ("gs", "two", 0, 0), ("gs", "two", 0, 1), ("ready", "vw"), ("ready", "vec"), ("norm", 0), ("norm", 1),
    ("norm", 2), ("ready", "mx0"), ("gs", "at", 1, 0), ("gs", "cross", 0, 1), ("gs", "cross", 0, 0),
    ("norm", 3), ("mask",), ("gs", "two", 1, 0), ("gs", "at", 2, 0), ("mix", 0), ("gs", "at", 1, 1),
    ("mix", 1), ("gs", "two", 1, 1), ("gs", "rest", 0, 0), ("pass", 0, 0), ("ready", "ow"),
    ("gs", "two", 2, 0), ("gs", "cross", 1, 0), ("gs", "at", 2, 1), ("gs", "two", 2, 1), ("mix", 2),
    ("mix", 3), ("mix", 4), ("mix", 5), ("gs", "rest", 0, 1), ("pass", 0, 1), ("gs", "at", 3, 0),
    ("gs", "two", 3, 0), ("proj", 0), ("proj", 1), ("proj", 2), ("fetch", 0), ("proj", 3), ("gs", "at", 3, 1),
    ("gs", "cross", 2, 0), ("gs", "cross", 1, 1), ("gs", "cross", 2, 1), ("gs", "two", 3, 1),
    ("gs", "cross", 3, 0), ("gs", "rest", 1, 0), ("dense", 0, 0), ("dense", 0, 1), ("dense", 0, 2),
    ("pass", 1, 0), ("grad", 0, 0), ("swapF", 0, 0), ("grad", 0, 1), ("swapF", 0, 1), ("acc", 0, 0),
    ("gs", "rest", 1, 1), ("pass", 1, 1), ("swappedF", 0, 0), ("Fs", "first", 0, 0), ("gs", "rest", 2, 0),
    ("gs", "rest", 2, 1), ("gs", "cross", 3, 1), ("acc", 0, 1), ("swappedF", 0, 1), ("pass", 2, 1),
    ("Fs", "first", 0, 1), ("pass", 2, 0), ("fetch", 1), ("dense", 1, 0), ("dense", 1, 1),
    ("gs", "rest", 3, 0), ("pass", 3, 0), ("gs", "rest", 3, 1), ("pass", 3, 1), ("dense", 1, 2), ("fetch", 2),
    ("grad", 1, 0), ("swapF", 1, 0), ("Fs", "second", 0, 0), ("grad", 1, 1), ("swapF", 1, 1), ("acc", 1, 0),
    ("swappedF", 1, 0), ("Fs", "second", 0, 1), ("acc", 1, 1), ("swappedF", 1, 1), ("Fs", "first", 1, 1),
    ("dense", 2, 0), ("Fs", "first", 1, 0), ("fetch", 3), ("dense", 2, 1), ("dense", 2, 2),
    ("Fs", "line", 0, 0), ("grad", 2, 0), ("Fs", "line", 0, 1), ("swapF", 2, 0), ("grad", 2, 1),
    ("swapF", 2, 1), ("acc", 2, 0), ("Fs", "second", 1, 1), ("acc", 2, 1), ("Fs", "second", 1, 0),
    ("swappedF", 2, 0), ("Fs", "first", 2, 0), ("swappedF", 2, 1), ("Fs", "first", 2, 1), ("dense", 3, 0),
    ("dense", 3, 1), ("dense", 3, 2), ("grad", 3, 0), ("swapF", 3, 0), ("Fs", "line", 1, 0), ("grad", 3, 1),
    ("swapF", 3, 1), ("acc", 3, 0), ("acc", 3, 1), ("swappedF", 3, 0), ("Fs", "second", 2, 0),
    ("swappedF", 3, 1), ("Fs", "second", 2, 1), ("Fs", "first", 3, 1), ("Fs", "first", 3, 0), ("fin2", 0),
    ("fin2", 1), ("Fs", "line", 1, 1), ("Fs", "line", 2, 0), ("Fs", "hop", 1, 0, 0), ("Fs", "hop", 2, 0, 0),
    ("fin2", 2), ("Fs", "line", 2, 1), ("Fs", "hop", 1, 1, 0), ("Fs", "hop", 2, 1, 0), ("fin2", 3), ("og",),
    ("Fs", "hop", 1, 0, 1), ("Fs", "second", 3, 0), ("Fs", "second", 3, 1), ("swap", "og"), ("scale",),
    ("head", 0, 0), ("Fs", "hop", 2, 0, 1), ("swapped", "og"), ("w", "first", 0, 1), ("w", "first", 1, 1),
    ("w", "first", 2, 1), ("head", 0, 1), ("head", 0, 2), ("Fs", "hop", 1, 1, 1), ("Fs", "line", 3, 0),
    ("Fs", "hop", 0, 0, 0), ("w", "first", 3, 1), ("Fs", "line", 3, 1), ("Fs", "hop", 3, 0, 0),
    ("Fs", "hop", 1, 0, 2), ("swap", 0), ("Fs", "hop", 3, 1, 0), ("head", 1, 0), ("head", 1, 1),
    ("w", "second", 0, 1), ("head", 1, 2), ("swap", 1), ("Fs", "hop", 2, 0, 2), ("swapped", 0),
    ("m", "first", 0, 1), ("Fs", "hop", 0, 1, 0), ("Fs", "hop", 2, 1, 1), ("m", "first", 0, 0),
    ("w", "line", 0, 1), ("w", "second", 1, 1), ("head", 2, 0), ("w", "second", 2, 1), ("swapped", 1),
    ("Fs", "hop", 1, 1, 2), ("Fs", "hop", 0, 0, 1), ("w", "second", 3, 1), ("Fs", "hop", 3, 0, 1),
    ("m", "first", 3, 1), ("head", 2, 1), ("head", 2, 2), ("swap", 2), ("m", "first", 3, 0), ("head", 3, 0),
    ("Fs", "hop", 3, 1, 1), ("Fs", "hop", 0, 1, 1), ("head", 3, 1), ("head", 3, 2), ("w", "hop", 0, 1, 1),
    ("w", "line", 1, 1), ("w", "line", 2, 1), ("Fs", "hop", 3, 0, 2), ("m", "second", 0, 0),
    ("Fs", "hop", 0, 0, 2), ("m", "second", 0, 1), ("swapped", 2), ("m", "first", 1, 0),
    ("w", "hop", 1, 1, 1), ("m", "first", 1, 1), ("swap", 3), ("w", "line", 3, 1), ("turn",),
    ("w", "hop", 2, 1, 1), ("Fs", "hop", 0, 1, 2), ("Fs", "hop", 2, 1, 2), ("vg",), ("swap", "vg"),
    ("Fs", "hop", 0, 0, 3), ("m", "second", 3, 1), ("swapped", 3), ("w", "hop", 3, 1, 1),
    ("Fs", "hop", 3, 0, 3), ("w", "hop", 1, 1, 2), ("w", "hop", 0, 1, 2), ("Fs", "hop", 3, 1, 2),
    ("m", "second", 3, 0), ("fin1", 0), ("m", "first", 2, 0), ("w", "at", 1, 1, 0), ("w", "hop", 2, 1, 2),
    ("m", "line", 0, 0), ("w", "hop", 3, 1, 2), ("w", "two", 1, 1, 0), ("m", "line", 0, 1), ("swapped", "vg"),
    ("m", "first", 2, 1), ("w", "at", 2, 1, 0), ("w", "first", 0, 0), ("fin1", 1), ("w", "first", 3, 0),
    ("m", "hop", 0, 0, 1), ("w", "first", 1, 0), ("w", "two", 2, 1, 0), ("w", "hop", 0, 1, 3),
    ("w", "at", 1, 1, 1), ("w", "at", 0, 1, 0), ("w", "hop", 3, 1, 3), ("w", "first", 2, 0),
    ("w", "at", 3, 1, 0), ("fin1", 2), ("Fs", "hop", 3, 1, 3), ("w", "at", 2, 1, 1), ("w", "two", 0, 1, 0),
    ("Fs", "hop", 0, 1, 3), ("m", "second", 1, 0), ("w", "two", 1, 1, 1), ("m", "line", 3, 1),
    ("m", "hop", 0, 1, 1), ("m", "line", 3, 0), ("w", "at", 1, 1, 2), ("m", "second", 1, 1),
    ("w", "two", 1, 1, 2), ("w", "two", 2, 1, 1), ("fin1", 3), ("m", "hop", 0, 0, 2), ("w", "at", 2, 1, 2),
    ("w", "cross", 1, 1, 0), ("w", "two", 2, 1, 2), ("w", "at", 0, 1, 1), ("w", "two", 0, 1, 1),
    ("m", "second", 2, 0), ("w", "at", 0, 1, 2), ("w", "two", 3, 1, 0), ("m", "hop", 0, 1, 2), ("small", 0),
    ("m", "hop", 3, 1, 1), ("w", "second", 0, 0), ("w", "at", 3, 1, 1), ("w", "two", 3, 1, 1),
    ("w", "two", 0, 1, 2), ("m", "line", 1, 0), ("m", "second", 2, 1), ("m", "hop", 1, 0, 1),
    ("m", "hop", 0, 0, 3), ("m", "at", 0, 0, 0), ("m", "hop", 3, 0, 1), ("w", "at", 0, 1, 3),
    ("m", "two", 0, 0, 0), ("small", 1), ("w", "second", 1, 0), ("w", "line", 0, 0), ("m", "hop", 0, 1, 3),
    ("m", "at", 0, 1, 0), ("w", "at", 3, 1, 2), ("m", "hop", 3, 1, 2), ("m", "line", 2, 0),
    ("m", "hop", 3, 0, 2), ("w", "second", 2, 0), ("w", "two", 3, 1, 2), ("m", "two", 0, 1, 0), ("small", 2),
    ("m", "at", 0, 0, 1), ("w", "at", 3, 1, 3), ("w", "cross", 0, 1, 0), ("w", "two", 3, 1, 3),
    ("m", "hop", 1, 0, 2), ("m", "at", 1, 0, 0), ("w", "two", 0, 1, 3), ("m", "cross", 0, 0, 0),
    ("w", "second", 3, 0), ("m", "at", 0, 1, 1), ("m", "two", 0, 1, 1), ("w", "cross", 2, 1, 0),
    ("m", "hop", 3, 1, 3), ("m", "at", 3, 1, 0), ("w", "cross", 0, 1, 1), ("m", "two", 3, 1, 0),
    ("m", "at", 0, 0, 2), ("m", "two", 0, 0, 1), ("m", "two", 0, 0, 2), ("w", "hop", 0, 0, 1),
    ("w", "cross", 2, 1, 1), ("w", "cross", 2, 1, 2), ("w", "line", 1, 0), ("m", "hop", 2, 0, 1),
    ("m", "line", 1, 1), ("w", "hop", 1, 0, 1), ("w", "line", 2, 0), ("w", "hop", 2, 0, 1),
    ("w", "cross", 1, 1, 1), ("m", "two", 1, 0, 0), ("m", "hop", 3, 0, 3), ("m", "at", 3, 0, 0),
    ("m", "at", 1, 0, 1), ("m", "two", 1, 0, 1), ("m", "two", 3, 0, 0), ("w", "hop", 0, 0, 2),
    ("m", "cross", 0, 0, 1), ("w", "cross", 1, 1, 2), ("m", "hop", 1, 1, 1), ("w", "hop", 1, 0, 2),
    ("w", "at", 1, 0, 0), ("m", "at", 3, 1, 1), ("m", "line", 2, 1), ("w", "cross", 0, 1, 2),
    ("w", "cross", 0, 1, 3), ("m", "at", 0, 0, 3), ("m", "two", 0, 0, 3), ("w", "cross", 3, 1, 0),
    ("w", "cross", 3, 1, 1), ("m", "cross", 0, 0, 2), ("m", "cross", 3, 1, 0), ("m", "at", 0, 1, 2),
    ("w", "cross", 3, 1, 2), ("w", "hop", 0, 0, 3), ("w", "at", 0, 0, 0), ("w", "rest", 1, 1),
    ("m", "cross", 3, 0, 0), ("m", "two", 0, 1, 2), ("m", "cross", 1, 0, 0), ("w", "two", 0, 0, 0),
    ("m", "hop", 2, 1, 1), ("m", "hop", 2, 0, 2), ("m", "at", 2, 0, 0), ("m", "at", 1, 0, 2),
    ("m", "two", 1, 0, 2), ("m", "hop", 1, 1, 2), ("w", "line", 3, 0), ("w", "at", 1, 0, 1),
    ("m", "two", 3, 1, 1), ("small", 3), ("w", "rest", 2, 1), ("m", "at", 1, 1, 0), ("m", "two", 1, 1, 0),
    ("m", "cross", 0, 1, 0), ("w", "two", 1, 0, 0), ("w", "two", 1, 0, 1), ("w", "hop", 3, 0, 1),
    ("m", "at", 0, 1, 3), ("m", "at", 3, 1, 2), ("m", "cross", 1, 0, 1), ("w", "hop", 2, 0, 2),
    ("w", "at", 2, 0, 0), ("w", "two", 2, 0, 0), ("w", "cross", 0, 0, 0), ("w", "at", 0, 0, 1),
    ("m", "at", 3, 0, 1), ("w", "cross", 3, 1, 3), ("m", "two", 3, 1, 2), ("m", "cross", 0, 0, 3),
    ("w", "cross", 1, 0, 0), ("w", "rest", 0, 1), ("m", "hop", 2, 1, 2), ("m", "at", 2, 1, 0),
    ("m", "two", 2, 1, 0), ("m", "at", 2, 0, 1), ("m", "two", 0, 1, 3), ("small", 4), ("w", "at", 2, 0, 1),
    ("m", "cross", 0, 1, 1), ("m", "at", 1, 1, 1), ("m", "two", 1, 1, 1), ("w", "at", 1, 0, 2),
    ("w", "two", 2, 0, 1), ("w", "two", 0, 0, 1), ("m", "cross", 1, 0, 2), ("m", "two", 2, 0, 0),
    ("m", "two", 3, 0, 1), ("m", "at", 3, 1, 3), ("m", "two", 3, 1, 3), ("m", "cross", 2, 0, 0),
    ("w", "cross", 0, 0, 1), ("small", 5), ("w", "hop", 3, 0, 2), ("m", "at", 3, 0, 2),
    ("w", "cross", 1, 0, 1), ("m", "two", 3, 0, 2), ("m", "two", 2, 0, 1), ("m", "cross", 1, 1, 0),
    ("m", "at", 2, 1, 1), ("m", "cross", 0, 1, 2), ("w", "rest", 3, 1), ("m", "at", 2, 0, 2),
    ("w", "at", 0, 0, 2), ("w", "two", 1, 0, 2), ("w", "at", 2, 0, 2), ("w", "two", 0, 0, 2),
    ("m", "two", 2, 0, 2), ("w", "two", 2, 0, 2), ("m", "rest", 0, 0), ("m", "cross", 0, 1, 3),
    ("m", "cross", 3, 1, 1), ("m", "at", 1, 1, 2), ("m", "cross", 2, 0, 1), ("m", "at", 3, 0, 3),
    ("m", "cross", 2, 0, 2), ("w", "cross", 2, 0, 0), ("w", "hop", 3, 0, 3), ("w", "at", 3, 0, 0),
    ("w", "at", 0, 0, 3), ("m", "two", 3, 0, 3), ("w", "two", 3, 0, 0), ("m", "two", 2, 1, 1),
    ("w", "two", 0, 0, 3), ("m", "two", 1, 1, 2), ("w", "at", 3, 0, 1), ("w", "cross", 1, 0, 2),
    ("w", "at", 3, 0, 2), ("w", "cross", 2, 0, 1), ("w", "cross", 2, 0, 2), ("m", "rest", 1, 0),
    ("m", "cross", 3, 1, 2), ("m", "at", 2, 1, 2), ("m", "cross", 3, 1, 3), ("m", "cross", 3, 0, 1),
    ("m", "rest", 0, 1), ("m", "cross", 3, 0, 2), ("m", "cross", 3, 0, 3), ("m", "cross", 2, 1, 0),
    ("w", "at", 3, 0, 3), ("m", "cross", 1, 1, 1), ("w", "two", 3, 0, 1), ("w", "two", 3, 0, 2),
    ("w", "two", 3, 0, 3), ("w", "cross", 0, 0, 2), ("m", "rest", 3, 1), ("w", "cross", 0, 0, 3),
    ("m", "cross", 2, 1, 1), ("m", "rest", 2, 0), ("m", "cross", 1, 1, 2), ("w", "cross", 3, 0, 0),
    ("w", "rest", 1, 0), ("m", "two", 2, 1, 2), ("m", "cross", 2, 1, 2), ("w", "cross", 3, 0, 1),
    ("w", "cross", 3, 0, 2), ("w", "cross", 3, 0, 3), ("m", "rest", 1, 1), ("m", "rest", 3, 0),
    ("w", "rest", 0, 0), ("w", "rest", 2, 0), ("w", "rest", 3, 0), ("m", "rest", 2, 1),
)


def normalize(matrix, norm_gain, norm_shift):
    average = jnp.mean(matrix, axis=-1, keepdims=True)
    center = matrix - average
    reciprocal = lax.rsqrt(jnp.mean(center * center, axis=-1, keepdims=True) + epsilon)
    unit_rows = center * reciprocal
    return (unit_rows * norm_gain + norm_shift, unit_rows, reciprocal)


def plain_norm_back(slope_rows, unit_rows, reciprocal, norm_gain):
    tilted = slope_rows * norm_gain
    centered_slope = tilted - jnp.mean(tilted, axis=-1, keepdims=True)
    centered_slope = centered_slope - unit_rows * jnp.mean(
        tilted * unit_rows, axis=-1, keepdims=True
    )
    return (
        centered_slope * reciprocal,
        jnp.sum(slope_rows * unit_rows, axis=0),
        jnp.sum(slope_rows, axis=0),
    )


def plain_contract(left_side, right_side):
    return lax.dot_general(
        left_side, right_side, (((0,), (0,)), ((), ())), preferred_element_type=jnp.float32
    )


def times_transpose(left_side, right_side):
    return lax.dot_general(
        left_side, right_side, (((1,), (1,)), ((), ())), preferred_element_type=jnp.float32
    )


def row_chances(mixing_full, row_docs):
    same_doc = row_docs[:, None] == row_docs[None, :]
    scores = jnp.where(same_doc[None, :, :], mixing_full.astype(jnp.float32), -1e30)
    row_top = jnp.max(scores, axis=-1, keepdims=True)
    raised = jnp.exp(scores - row_top)
    return raised / jnp.sum(raised, axis=-1, keepdims=True)


def plain(
    inputs,
    documents,
    mixing,
    value_weight,
    output_weight,
    mixer_gain,
    mixer_shift,
    dense_gain,
    dense_shift,
    hidden_weight,
    hidden_bias,
    down_weight,
    down_bias,
    cotangent,
):
    gathered = (
        lax.all_gather(mixing, "narrow", axis=1, tiled=True),
        lax.all_gather(value_weight, "narrow", axis=1, tiled=True),
        lax.all_gather(output_weight, "narrow", axis=0, tiled=True),
        lax.all_gather(mixer_gain, "narrow", axis=0, tiled=True),
        lax.all_gather(mixer_shift, "narrow", axis=0, tiled=True),
        lax.all_gather(dense_gain, "narrow", axis=0, tiled=True),
        lax.all_gather(dense_shift, "narrow", axis=0, tiled=True),
        lax.all_gather(hidden_bias, "narrow", axis=0, tiled=True),
        lax.all_gather(down_bias, "narrow", axis=0, tiled=True),
    )
    mixing_full, value_full, output_full = (gathered[0], gathered[1], gathered[2])
    gain_first = gathered[3].astype(jnp.float32)
    shift_first = gathered[4].astype(jnp.float32)
    gain_second = gathered[5].astype(jnp.float32)
    shift_second = gathered[6].astype(jnp.float32)
    bias_hidden = gathered[7].astype(jnp.float32)
    bias_down = gathered[8].astype(jnp.float32)
    halfway = (
        lax.all_gather(hidden_weight, "narrow", axis=0, tiled=True),
        lax.all_gather(down_weight, "narrow", axis=1, tiled=True),
    )
    hidden_full, down_full = (
        lax.all_gather(halfway[0], "wide", axis=1, tiled=True),
        lax.all_gather(halfway[1], "wide", axis=0, tiled=True),
    )
    row_count = inputs.shape[0]
    stream = inputs.reshape(row_count * SEQ, D).astype(jnp.float32)
    normed, unit_first, recip_first = normalize(stream, gain_first, shift_first)
    normed_low = normed.astype(jnp.bfloat16)
    values = jnp.dot(normed_low, value_full, preferred_element_type=jnp.float32).astype(
        jnp.bfloat16
    )
    value_rows = values.reshape(row_count, SEQ, D)

    def mix_one(bundle):
        row_values, row_docs = bundle
        chances_low = row_chances(mixing_full, row_docs).astype(jnp.bfloat16)
        per_head = row_values.reshape(SEQ, HEADS, HEAD)
        blended_row = jnp.einsum(
            "hij,jhd->ihd", chances_low, per_head, preferred_element_type=jnp.float32
        )
        return blended_row.reshape(SEQ, D).astype(jnp.bfloat16)

    blended = lax.map(mix_one, (value_rows, documents)).reshape(row_count * SEQ, D)
    middle = stream + jnp.dot(blended, output_full, preferred_element_type=jnp.float32)
    normed_two, unit_second, recip_second = normalize(middle, gain_second, shift_second)
    normed_two_low = normed_two.astype(jnp.bfloat16)
    hidden = jnp.dot(normed_two_low, hidden_full, preferred_element_type=jnp.float32) + bias_hidden
    activated, gelu_pull = jax.vjp(jax.nn.gelu, hidden)
    active = activated.astype(jnp.bfloat16)
    result = middle + jnp.dot(active, down_full, preferred_element_type=jnp.float32) + bias_down
    slope_low = cotangent.reshape(row_count * SEQ, D)
    slope_wide = slope_low.astype(jnp.float32)
    down_bias_sum = jnp.sum(slope_wide, axis=0)
    down_grad = plain_contract(active, slope_low)
    active_slope = times_transpose(slope_low, down_full)
    hidden_slope_wide = gelu_pull(active_slope)[0]
    hidden_slope = hidden_slope_wide.astype(jnp.bfloat16)
    hidden_bias_sum = jnp.sum(hidden_slope.astype(jnp.float32), axis=0)
    hidden_grad = plain_contract(normed_two_low, hidden_slope)
    normed_two_slope = times_transpose(hidden_slope, hidden_full)
    back_second, gain_second_sum, shift_second_sum = plain_norm_back(
        normed_two_slope, unit_second, recip_second, gain_second
    )
    middle_slope = slope_wide + back_second
    attended_slope = middle_slope.astype(jnp.bfloat16)
    output_grad = plain_contract(blended, attended_slope)
    blended_slope = times_transpose(attended_slope, output_full).astype(jnp.bfloat16)

    def mix_back(running, bundle):
        row_values, row_docs, row_slope = bundle
        chances = row_chances(mixing_full, row_docs)
        per_head = row_values.reshape(SEQ, HEADS, HEAD)
        head_slope = row_slope.reshape(SEQ, HEADS, HEAD)
        chance_slope = jnp.einsum(
            "ihd,jhd->hij", head_slope, per_head, preferred_element_type=jnp.float32
        )
        score_slope = chances * (
            chance_slope - jnp.sum(chances * chance_slope, axis=-1, keepdims=True)
        )
        value_part = jnp.einsum(
            "hij,ihd->jhd",
            chances.astype(jnp.bfloat16),
            head_slope,
            preferred_element_type=jnp.float32,
        )
        return (running + score_slope, value_part.reshape(SEQ, D).astype(jnp.bfloat16))

    mixing_start = jnp.zeros((HEADS, SEQ, SEQ), jnp.float32)
    mixing_grad, value_slopes = lax.scan(
        mix_back, mixing_start, (value_rows, documents, blended_slope.reshape(row_count, SEQ, D))
    )
    value_slope = value_slopes.reshape(row_count * SEQ, D)
    value_grad = plain_contract(normed_low, value_slope)
    normed_slope = times_transpose(value_slope, value_full)
    back_first, gain_first_sum, shift_first_sum = plain_norm_back(
        normed_slope, unit_first, recip_first, gain_first
    )
    inputs_slope = (middle_slope + back_first).astype(jnp.bfloat16)
    sums_half = (
        lax.psum_scatter(
            hidden_grad.astype(jnp.bfloat16), "wide", scatter_dimension=1, tiled=True
        ).astype(jnp.float32),
        lax.psum_scatter(
            down_grad.astype(jnp.bfloat16), "wide", scatter_dimension=0, tiled=True
        ).astype(jnp.float32),
    )
    hidden_share, down_share = (
        lax.psum_scatter(
            sums_half[0].astype(jnp.bfloat16), "narrow", scatter_dimension=0, tiled=True
        ).astype(jnp.float32),
        lax.psum_scatter(
            sums_half[1].astype(jnp.bfloat16), "narrow", scatter_dimension=1, tiled=True
        ).astype(jnp.float32),
    )
    shares = (
        lax.psum_scatter(
            mixing_grad.astype(jnp.bfloat16), "narrow", scatter_dimension=1, tiled=True
        ).astype(jnp.float32),
        lax.psum_scatter(
            value_grad.astype(jnp.bfloat16), "narrow", scatter_dimension=1, tiled=True
        ).astype(jnp.float32),
        lax.psum_scatter(
            output_grad.astype(jnp.bfloat16), "narrow", scatter_dimension=0, tiled=True
        ).astype(jnp.float32),
        lax.psum_scatter(
            gain_first_sum.astype(jnp.bfloat16), "narrow", scatter_dimension=0, tiled=True
        ).astype(jnp.float32),
        lax.psum_scatter(
            shift_first_sum.astype(jnp.bfloat16), "narrow", scatter_dimension=0, tiled=True
        ).astype(jnp.float32),
        lax.psum_scatter(
            gain_second_sum.astype(jnp.bfloat16), "narrow", scatter_dimension=0, tiled=True
        ).astype(jnp.float32),
        lax.psum_scatter(
            shift_second_sum.astype(jnp.bfloat16), "narrow", scatter_dimension=0, tiled=True
        ).astype(jnp.float32),
        lax.psum_scatter(
            hidden_bias_sum.astype(jnp.bfloat16), "narrow", scatter_dimension=0, tiled=True
        ).astype(jnp.float32),
        lax.psum_scatter(
            down_bias_sum.astype(jnp.bfloat16), "narrow", scatter_dimension=0, tiled=True
        ).astype(jnp.float32),
    )
    totals = (
        lax.psum(shares[0].astype(jnp.bfloat16), "wide").astype(jnp.float32),
        lax.psum(shares[1].astype(jnp.bfloat16), "wide").astype(jnp.float32),
        lax.psum(shares[2].astype(jnp.bfloat16), "wide").astype(jnp.float32),
        lax.psum(shares[3].astype(jnp.bfloat16), "wide").astype(jnp.float32),
        lax.psum(shares[4].astype(jnp.bfloat16), "wide").astype(jnp.float32),
        lax.psum(shares[5].astype(jnp.bfloat16), "wide").astype(jnp.float32),
        lax.psum(shares[6].astype(jnp.bfloat16), "wide").astype(jnp.float32),
        lax.psum(shares[7].astype(jnp.bfloat16), "wide").astype(jnp.float32),
        lax.psum(shares[8].astype(jnp.bfloat16), "wide").astype(jnp.float32),
    )
    return (
        result.reshape(row_count, SEQ, D).astype(jnp.bfloat16),
        inputs_slope.reshape(row_count, SEQ, D),
        totals[0],
        totals[1],
        totals[2],
        totals[3],
        totals[4],
        totals[5],
        totals[6],
        hidden_share,
        totals[7],
        down_share,
        totals[8],
    )


def solution(mesh):
    inner = local if dict(mesh.shape) == {"narrow": 2, "wide": 16} else plain
    return jax.shard_map(
        inner,
        mesh=mesh,
        in_specs=(
            P(("narrow", "wide"), None, None),
            P(("narrow", "wide"), None),
            P(None, "narrow", None),
            P(None, "narrow"),
            P("narrow", None),
            P("narrow"),
            P("narrow"),
            P("narrow"),
            P("narrow"),
            P("narrow", "wide"),
            P("narrow"),
            P("wide", "narrow"),
            P("narrow"),
            P(("narrow", "wide"), None, None),
        ),
        out_specs=(
            P(("narrow", "wide"), None, None),
            P(("narrow", "wide"), None, None),
            P(None, "narrow", None),
            P(None, "narrow"),
            P("narrow", None),
            P("narrow"),
            P("narrow"),
            P("narrow"),
            P("narrow"),
            P("narrow", "wide"),
            P("narrow"),
            P("wide", "narrow"),
            P("narrow"),
        ),
        check_vma=False,
    )
```

```python
import functools

import jax
import jax.numpy as jnp
from jax import lax
from jax.experimental import pallas as pl
from jax.experimental.pallas import tpu as pltpu
from jax.sharding import PartitionSpec as P

D = 768
HEADS = 12
HEAD = 64
SEQ = 512
FF = 3072
HALF = D // 2
CHUNK = 192
GROUP = 4 * CHUNK
epsilon = 1e-05

MESH = pl.DeviceIdType.MESH
f32 = jnp.float32
bf16 = jnp.bfloat16


def place():
    core = lax.axis_index("narrow")
    wide = lax.axis_index("wide")
    return core, lax.rem(wide, 2), lax.rem(lax.div(wide, 2), 2), lax.div(wide, 4)


def seat(core, x, y, z):
    return (core, z * 4 + y * 2 + x)


def remote(src, dst, send_sem, recv_sem, device):
    return pltpu.make_async_remote_copy(
        src_ref=src,
        dst_ref=dst,
        send_sem=send_sem,
        recv_sem=recv_sem,
        device_id=device,
        device_id_type=MESH,
    )


def greet(core, x, y, z, more=()):
    barrier = pltpu.get_barrier_semaphore()
    near = (seat(1 - core, x, y, z), seat(core, 1 - x, y, z), seat(core, x, 1 - y, z)) + more
    for device in near:
        pl.semaphore_signal(barrier, inc=1, device_id=device, device_id_type=MESH)

    @pl.when(z < 3)
    def _():
        pl.semaphore_signal(
            barrier, inc=1, device_id=seat(core, x, y, z + 1), device_id_type=MESH
        )

    @pl.when(z > 0)
    def _():
        pl.semaphore_signal(
            barrier, inc=1, device_id=seat(core, x, y, z - 1), device_id_type=MESH
        )

    above, below = jnp.where(z < 3, 1, 0), jnp.where(z > 0, 1, 0)
    pl.semaphore_wait(barrier, len(near) + above + below)


def halves(core):
    mine = pl.ds(pl.multiple_of(core * HALF, 128), HALF)
    other = pl.ds(pl.multiple_of((1 - core) * HALF, 128), HALF)
    return mine, other


def line_order(z, step):
    table = ((0, 1, 2, 3), (1, 0, 2, 3), (2, 1, 3, 0), (3, 2, 1, 0))
    return jnp.where(
        z == 0,
        table[0][step],
        jnp.where(z == 1, table[1][step], jnp.where(z == 2, table[2][step], table[3][step])),
    )


def unit_of(rows):
    center = rows - jnp.mean(rows, axis=-1, keepdims=True)
    reciprocal = lax.rsqrt(jnp.mean(center * center, axis=-1, keepdims=True) + epsilon)
    return center * reciprocal, reciprocal


def dot_nn(left, right):
    return lax.dot_general(left, right, (((1,), (0,)), ((), ())), preferred_element_type=f32)


def dot_nt(left, right):
    return lax.dot_general(left, right, (((1,), (1,)), ((), ())), preferred_element_type=f32)


def dot_tn(left, right):
    return lax.dot_general(left, right, (((0,), (0,)), ((), ())), preferred_element_type=f32)


def corner(half, row, column):
    return (
        pl.multiple_of((row + half * (1 - 2 * row)) * 128, 128),
        pl.ds(pl.multiple_of((column + half * (3 - 2 * column)) * 128, 128), 128),
    )


def lane_ids(rows):
    return lax.broadcasted_iota(jnp.int32, (rows, 128), 1)


def fill_mask(docs_ref, mask, rows):
    for r in range(rows):
        flat = docs_ref[r : r + 1, :].astype(f32)
        for i in range(0, SEQ, 128):
            tall = jnp.broadcast_to(flat[:, i : i + 128], (128, 128)).T
            for j in range(0, SEQ, 128):
                wide = jnp.broadcast_to(flat[:, j : j + 128], (128, 128))
                mask[r, i : i + 128, j : j + 128] = jnp.where(tall == wide, 1.0, 0.0).astype(bf16)


def gelu_and_slope(v):
    scale = 0.7978845608028654
    square = v * v
    t = jnp.tanh(scale * v * (1.0 + 0.044715 * square))
    rise = 0.5 * (1.0 + t)
    slope = rise + 0.5 * scale * v * (1.0 - t * t) * (1.0 + 3.0 * 0.044715 * square)
    return v * rise, slope


def norm_slope(slope, unit, reciprocal, gain):
    tilted = slope * gain
    centered = tilted - jnp.mean(tilted, axis=-1, keepdims=True)
    centered = centered - unit * jnp.mean(tilted * unit, axis=-1, keepdims=True)
    return centered * reciprocal


class Reduce:
    def __init__(self, part, refs):
        self.part = part
        (
            self.first_y, self.first_x, self.second_x, self.second_y, self.line_in,
            self.first_sent, self.first_recv, self.second_sent, self.second_recv,
            self.line_sent, self.line_recv,
        ) = refs
        core, x, y, z = place()
        self.x, self.y, self.z = x, y, z
        self.near_x, self.near_y = seat(core, 1 - x, y, z), seat(core, x, 1 - y, z)
        self.above, self.below = seat(core, x, y, z + 1), seat(core, x, y, z - 1)

    @staticmethod
    def scratch(piece):
        dma = pltpu.SemaphoreType.DMA
        return [
            pltpu.VMEM((4, 2) + piece, bf16), pltpu.VMEM((4, 2) + piece, bf16),
            pltpu.VMEM((4,) + piece, bf16), pltpu.VMEM((4,) + piece, bf16),
            pltpu.VMEM((2, 4, 2) + piece, bf16),
            dma((4, 2)), dma((4, 2)), dma((4, 2)), dma((4, 2)), dma((2, 4, 2)), dma((2, 4, 2)),
        ]

    def first_copy(self, k, m):
        sems = self.first_sent.at[k, m], self.first_recv.at[k, m]
        if m == 0:
            return remote(self.part.at[k, 0, 1 - self.y], self.first_y.at[k], *sems, self.near_y)
        return remote(self.part.at[k, 1, :, 1 - self.x], self.first_x.at[k], *sems, self.near_x)

    def second_copy(self, k, m):
        x, y = self.x, self.y
        sems = self.second_sent.at[k, m], self.second_recv.at[k, m]
        if m == 0:
            return remote(self.part.at[k, 0, y, 1 - x], self.second_x.at[k], *sems, self.near_x)
        return remote(self.part.at[k, 1, 1 - y, x], self.second_y.at[k], *sems, self.near_y)

    def line_copy(self, k, m, down):
        return remote(
            self.part.at[k, m, self.y, self.x], self.line_in.at[down, k, m],
            self.line_sent.at[down, k, m], self.line_recv.at[down, k, m],
            self.below if down else self.above,
        )

    def add_in(self, k, m, y_of, x_of, got):
        old = self.part[k, m, y_of, x_of].astype(f32)
        self.part[k, m, y_of, x_of] = (old + got.astype(f32)).astype(bf16)

    def first(self, k, m):
        self.first_copy(k, m).start()

    def second(self, k, m):
        x, y = self.x, self.y
        self.first_copy(k, m).wait_recv()
        if m == 0:
            self.add_in(k, 0, y, 1 - x, self.first_y[k, 1 - x])
            self.second_copy(k, 0).start()
            self.add_in(k, 0, y, x, self.first_y[k, x])
        else:
            self.add_in(k, 1, 1 - y, x, self.first_x[k, 1 - y])
            self.second_copy(k, 1).start()
            self.add_in(k, 1, y, x, self.first_x[k, y])

    def line(self, k, m):
        self.second_copy(k, m).wait_recv()
        self.add_in(k, m, self.y, self.x, (self.second_x, self.second_y)[m][k])

    def hop(self, k, m, hop):
        x, y, z = self.x, self.y, self.z
        for down, length, seat_z in ((0, k, hop), (1, 3 - k, 3 - hop)):
            if hop < length:

                @pl.when(z == seat_z)
                def _():
                    if hop > 0:
                        self.line_copy(k, m, down).wait_recv()
                        self.add_in(k, m, y, x, self.line_in[down, k, m])
                    self.line_copy(k, m, down).start()

        if hop == max(k, 3 - k):

            @pl.when(z == k)
            def _():
                for down, length in ((0, k), (1, 3 - k)):
                    if length > 0:
                        self.line_copy(k, m, down).wait_recv()
                        self.add_in(k, m, y, x, self.line_in[down, k, m])

    def settle(self, k):
        for m in range(2):
            self.first_copy(k, m).wait_send()
            self.second_copy(k, m).wait_send()
            if k > 0:

                @pl.when(self.z < k)
                def _():
                    self.line_copy(k, m, 0).wait_send()

            if k < 3:

                @pl.when(self.z > k)
                def _():
                    self.line_copy(k, m, 1).wait_send()


class Gather:
    def __init__(self, whole, refs):
        self.whole = whole
        self.recv, self.sent_x, self.sent_y, self.sent_z = refs
        core, x, y, z = place()
        self.x, self.y, self.z = x, y, z
        self.near_x, self.near_y = seat(core, 1 - x, y, z), seat(core, x, 1 - y, z)
        self.above, self.below = seat(core, x, y, z + 1), seat(core, x, y, z - 1)

    @staticmethod
    def scratch(piece):
        dma = pltpu.SemaphoreType.DMA
        return [
            pltpu.VMEM((4, 2, 2, 2) + piece, bf16),
            dma((4, 2, 2, 2)), dma((4, 2, 2)), dma((4, 2, 2)), dma((2, 4, 2)),
        ]

    def send(self, k, m, y_of, x_of, sem, device):
        src = self.whole.at[k, m, y_of, x_of]
        return remote(src, src, sem, self.recv.at[k, m, y_of, x_of], device)

    def to_x(self, k, m, y_of):
        return self.send(k, m, y_of, self.x, self.sent_x.at[k, m, y_of], self.near_x)

    def to_y(self, k, m, x_of):
        return self.send(k, m, self.y, x_of, self.sent_y.at[k, m, x_of], self.near_y)

    def along(self, k, m, down):
        device = self.below if down else self.above
        return self.send(k, m, self.y, self.x, self.sent_z.at[down, k, m], device)

    def arrived(self, k, m, y_of, x_of):
        self.send(k, m, y_of, x_of, self.sent_x.at[k, m, 0], self.near_x).wait_recv()

    def at(self, k, m, distance, part=None):
        x, y, z = self.x, self.y, self.z
        up, down = k + distance, k - distance
        for seat_z in sorted({up, down}):
            if 0 <= seat_z < 4:

                @pl.when(z == seat_z)
                def _():
                    if distance:
                        self.arrived(k, m, y, x)
                    elif part is not None:
                        self.whole[k, m, y, x] = part[k, m, y, x]
                    if k <= seat_z < 3:
                        self.along(k, m, 0).start()
                    if k >= seat_z > 0:
                        self.along(k, m, 1).start()
                    if m == 0:
                        self.to_x(k, 0, y).start()
                    else:
                        self.to_y(k, 1, x).start()

    def two(self, k, m, distance):
        x, y, z = self.x, self.y, self.z
        for seat_z in sorted({k + distance, k - distance}):
            if 0 <= seat_z < 4:

                @pl.when(z == seat_z)
                def _():
                    if m == 0:
                        self.to_y(k, 0, x).start()
                    else:
                        self.to_x(k, 1, y).start()

    def cross(self, k, m, distance):
        x, y, z = self.x, self.y, self.z
        up, down = k + distance, k - distance
        for seat_z in sorted({up, down}):
            if 0 <= seat_z < 4:

                @pl.when(z == seat_z)
                def _():
                    if m == 0:
                        self.arrived(k, 0, y, 1 - x)
                        self.to_y(k, 0, 1 - x).start()
                    else:
                        self.arrived(k, 1, 1 - y, x)
                        self.to_x(k, 1, 1 - y).start()

    def rest(self, k, m):
        x, y = self.x, self.y
        if m == 0:
            self.arrived(k, 0, 1 - y, x)
        else:
            self.arrived(k, 1, y, 1 - x)
        self.arrived(k, m, 1 - y, 1 - x)

    def settle(self, k):
        x, y, z = self.x, self.y, self.z
        for m in range(2):
            self.to_x(k, m, y).wait_send()
            self.to_y(k, m, x).wait_send()
            if k < 3:

                @pl.when(jnp.logical_and(z >= k, z < 3))
                def _():
                    self.along(k, m, 0).wait_send()

            if k > 0:

                @pl.when(jnp.logical_and(z <= k, z > 0))
                def _():
                    self.along(k, m, 1).wait_send()

        self.to_y(k, 0, 1 - x).wait_send()
        self.to_x(k, 1, 1 - y).wait_send()


BLOCKS = ((0, 0), (0, 1), (1, 0), (1, 1), (1, 2))
FOLDED = ((0, 2), (1, 3))
TRIPLE = HEADS // 4
MIX_PIECE = (TRIPLE, 6, 16, 128)
WEIGHT_PIECE = (48, HALF)
DENSE_PIECE = (CHUNK, HALF)
ORDER = (0, 3, 1, 2)


def layer_kernel(
    x_hbm, docs_ref, mixing_ref, value_ref, output_ref, hidden_ref, down_ref, cotangent_hbm,
    first_gain_ref, first_shift_ref, second_gain_ref, second_shift_ref, down_bias_ref, hidden_bias_ref,
    result_out, inputs_out, mixing_out, weights_out, hidden_out, down_out, sums_out,
    full_ref, mixing_full, normed_hbm, share_hbm, middle_hbm,
    *scratch,
):
    scratch = list(scratch)

    def take(n):
        got = scratch[:n]
        del scratch[:n]
        return got

    b0, b1, b2, b3, b4, b5 = take(6)
    value_full, output_full, vector_full, vector_own, shard, mask, raised = take(7)
    total, slope, weight, grads, to_twin, from_twin, dense_part = take(7)
    chance, block_t, mix_part, mix_to, mix_from, weights_from, weights_part = take(7)
    small, small_in, sums = take(3)
    dense_refs = take(11)
    mix_reduce_refs = take(11)
    weights_reduce_refs = take(11)
    mix_whole, *mix_gather_refs = take(5)
    weights_whole, *weights_gather_refs = take(5)
    early_send, early_recv, early_local, shard_sem = take(4)
    full_recv, full_core_recv, full_x, full_y, full_up, full_down, full_core = take(7)
    pair_sem, back_sem, head_sem, weight_sem, move_sem, out_sem = take(6)
    twin_sent, twin_recv, twin_credit, mix_sent, mix_recv, mix_credit = take(6)
    weights_sent, weights_recv, small_sent, small_recv = take(4)

    core, x, y, z = place()
    mine, other = halves(core)
    near_x, near_y = seat(core, 1 - x, y, z), seat(core, x, 1 - y, z)
    above, below = seat(core, x, y, z + 1), seat(core, x, y, z - 1)
    twin = seat(1 - core, x, y, z)
    tokens = b0.shape[0]
    rows_count = tokens // SEQ
    block = 256
    dense = Reduce(dense_part, dense_refs)
    families = {
        "m": (Reduce(mix_part, mix_reduce_refs), Gather(mix_whole, mix_gather_refs), mix_part),
        "w": (Reduce(weights_part, weights_reduce_refs), Gather(weights_whole, weights_gather_refs), weights_part),
    }
    pairs = (seat(core, x, y, z + 1 - 2 * lax.rem(z, 2)), seat(core, x, y, lax.rem(z + 2, 4)))
    rounds = (twin, near_x, near_y) + pairs
    ks = [line_order(z, i) for i in range(4)]

    def rows_of(b):
        return pl.ds(pl.multiple_of(b * block, block), block)

    def move(n, src, dst):
        return pltpu.make_async_copy(src, dst, move_sem.at[n])

    load_x = move(0, x_hbm, b0)
    keep_normed = move(1, b1, normed_hbm)
    load_cotangent = move(2, cotangent_hbm, b1)
    keep_share = move(3, slope, share_hbm)
    keep_middle = move(4, total, middle_hbm)
    load_share = move(5, share_hbm, total)
    load_normed = move(6, normed_hbm, b0)
    keep_result = move(7, b1, result_out)
    load_x_again = move(8, x_hbm, b1)
    keep_inputs = move(9, b0, inputs_out)

    def load_middle(b):
        return move(10 + b, middle_hbm.at[rows_of(b)], grads.at[pl.ds((b % 3) * block, block)])

    my_rows = pl.ds(pl.multiple_of(core * (SEQ // 2), SEQ // 2), SEQ // 2)
    early = {"vec": (vector_own, vector_full.at[:, mine]), "vw": (value_ref, value_full.at[:, mine])}
    for p in range(HEADS // 2):
        heads_of = pl.ds(2 * p, 2)
        early["mx%d" % p] = (mixing_ref.at[heads_of], mixing_full.at[heads_of, my_rows])
    early["ow"] = (output_ref, output_full.at[mine, :])
    names = list(early)

    def early_copy(name):
        n = names.index(name)
        return remote(*early[name], early_send.at[n], early_recv.at[n], twin)

    def early_own(name):
        src, dst = early[name]
        if name.startswith("mx"):
            dst = raised.at[int(name[2:]) % 2, :, my_rows]
        return pltpu.make_async_copy(src, dst, early_local.at[names.index(name)])

    def chunk_of(k, y_of, x_of):
        return k * 4 + y_of * 2 + x_of

    own = chunk_of(z, y, x)

    def slot(m, chunk):
        return full_ref.at[m, pl.ds(pl.multiple_of(chunk * CHUNK, CHUNK), CHUNK), mine]

    def full_copy(m, chunk, sems, device, src=None):
        dst = slot(m, chunk)
        return remote(dst if src is None else src, dst, sems.at[m, chunk], full_recv.at[m, chunk], device)

    def full_arrived(m, chunk):
        full_copy(m, chunk, full_x, near_x).wait_recv()

    def own_copy(m):
        return pltpu.make_async_copy(shard.at[m], slot(m, own), shard_sem.at[m])

    def gather(step, i, m):
        k = ks[i]
        if step == "at":
            chunk = chunk_of(k, y, x)
            src = shard.at[m] if i == 0 else None
            if i > 0:
                full_arrived(m, chunk)

            @pl.when(jnp.logical_and(k <= z, z < 3))
            def _():
                full_copy(m, chunk, full_up, above, src).start()

            @pl.when(jnp.logical_and(k >= z, z > 0))
            def _():
                full_copy(m, chunk, full_down, below, src).start()

            sems, device = ((full_x, near_x), (full_y, near_y))[m]
            full_copy(m, chunk, sems, device, src).start()
        elif step == "two":
            sems, device = ((full_y, near_y), (full_x, near_x))[m]
            full_copy(m, chunk_of(k, y, x), sems, device, shard.at[m] if i == 0 else None).start()
        elif step == "cross":
            if m == 0:
                full_arrived(0, chunk_of(k, y, 1 - x))
                full_copy(0, chunk_of(k, y, 1 - x), full_y, near_y).start()
            else:
                full_arrived(1, chunk_of(k, 1 - y, x))
                full_copy(1, chunk_of(k, 1 - y, x), full_x, near_x).start()
        else:
            full_arrived(m, chunk_of(k, 1 - y, x) if m == 0 else chunk_of(k, y, 1 - x))
            full_arrived(m, chunk_of(k, 1 - y, 1 - x))

    def full_twin(i, m):
        src = full_ref.at[m, pl.ds(pl.multiple_of(ks[i] * GROUP, GROUP), GROUP), mine]
        return remote(src, src, full_core.at[m, i], full_core_recv.at[m, i], twin)

    def pass_full(i, m):
        if i == 0:
            own_copy(m).wait()
        full_twin(i, m).start()

    def load_weight(i):
        rows = pl.ds(pl.multiple_of(ks[i] * GROUP, GROUP), GROUP)
        return pltpu.make_async_copy(full_ref.at[:, rows], weight.at[i % 2], weight_sem.at[i % 2])

    def fetch(i):
        for m in range(2):
            full_twin(i, m).wait_recv()
        load_weight(i).start()

    def first_norm(b):
        if b == 0:
            load_x.wait()
        rows = rows_of(b)
        unit, _ = unit_of(b0[rows, :].astype(f32))
        low = (unit * vector_full[0:1, :] + vector_full[1:2, :]).astype(bf16)
        b1[rows, :] = low
        b2[rows, :] = dot_nn(low, value_full[...]).astype(bf16)
        if b == tokens // block - 1:
            keep_normed.start()

    twin_rows = pl.ds(pl.multiple_of((1 - core) * (SEQ // 2), SEQ // 2), SEQ // 2)

    def load_pair(p):
        return pltpu.make_async_copy(
            mixing_full.at[pl.ds(2 * p, 2), twin_rows], raised.at[p % 2, :, twin_rows], pair_sem.at[p % 2]
        )

    def keep_pair(p):
        return pltpu.make_async_copy(raised.at[p % 2], mixing_full.at[pl.ds(2 * p, 2)], back_sem.at[p % 2])

    def mix(p):
        early_own("mx%d" % p).wait()
        load_pair(p).wait()
        if p + 1 < HEADS // 2:
            early_copy("mx%d" % (p + 1)).wait_recv()
            if p >= 1:
                keep_pair(p - 1).wait()
            early_own("mx%d" % (p + 1)).start()
            load_pair(p + 1).start()
        lanes = slice(p * 128, (p + 1) * 128)
        low_lanes = lane_ids(block) < HEAD
        pair_raised = raised.at[p % 2]
        for half in range(2):
            for i in range(0, SEQ, block):
                part = pair_raised[half, i : i + block].astype(f32)
                pair_raised[half, i : i + block] = jnp.exp(part).astype(bf16)
        keep_pair(p).start()

        def mix_row(r, _):
            pair = b2[pl.ds(pl.multiple_of(r * SEQ, SEQ), SEQ), lanes]
            left_half = lane_ids(SEQ) < HEAD
            ones = jnp.ones_like(pair)
            first = jnp.where(left_half, pair, ones)
            second = jnp.where(left_half, ones, pair)
            for i in range(0, SEQ, block):
                keep = mask[r, i : i + block]
                one = dot_nn(pair_raised[0, i : i + block] * keep, first)
                two = dot_nn(pair_raised[1, i : i + block] * keep, second)
                part = 1.0 / pltpu.roll(jnp.where(low_lanes, two, one), HEAD, 1)
                done = pl.ds(pl.multiple_of(r * SEQ + i, block), block)
                slope[done, lanes] = part
                b3[done, lanes] = (jnp.where(low_lanes, one, two) * part).astype(bf16)
            return 0

        lax.fori_loop(0, rows_count, mix_row, 0)
        if p == HEADS // 2 - 1:
            keep_share.start()
            keep_normed.wait()
            load_cotangent.start()

    def early_ready(name):
        if name in ("vw", "ow"):
            early_own(name).wait()
        early_copy(name).wait_recv()
        if name == "mx0":
            early_own("mx0").start()
            load_pair(0).start()

    def project(b):
        rows = rows_of(b)
        middle = b0[rows, :].astype(f32) + dot_nn(b3[rows, :], output_full[...])
        total[rows, :] = middle
        unit, _ = unit_of(middle)
        b0[rows, :] = (unit * vector_full[2:3, :] + vector_full[3:4, :]).astype(bf16)
        if b == tokens // block - 1:
            keep_middle.start()
            keep_share.wait()
            sums[...] = jnp.zeros_like(sums)

    def dense_units(i, u):
        k = ks[i]
        if u == 0:
            load_weight(i).wait()
        if i == 0 and u == 0:
            load_cotangent.wait()
        units = slice(u * 256, (u + 1) * 256)
        lanes = pl.ds(pl.multiple_of(lax.div(k, 2) * HALF, 128), HALF)
        row = 5 + 2 * lax.rem(k, 2)
        bias = jnp.concatenate(
            [vector_full[pl.ds(row, 1), lanes], vector_full[pl.ds(row + 1, 1), lanes]], axis=1
        )[:, units]
        hidden = dot_nt(b0[...], weight[i % 2, 0, units, :]) + bias
        pulled = dot_nt(b1[...], weight[i % 2, 1, units, :])
        act, pull = gelu_and_slope(hidden)
        turned = (pulled * pull).astype(bf16)
        b4[:, units] = act.astype(bf16)
        b5[:, units] = turned
        sums[pl.ds(3 + k, 1), units] = jnp.sum(turned.astype(f32), axis=0, keepdims=True)

    def dense_grad(i, m):
        left, right = ((b5, b0), (b4, b1))[m]
        grads[...] = dot_tn(left[...], right[...])

    def dense_back(i, m):
        if m == 1:
            if i == 0:
                keep_middle.wait()
            total[...] += dot_nn(b4[...], weight[i % 2, 1])
        elif i == 0:
            slope[...] = dot_nn(b5[...], weight[i % 2, 0])
        else:
            slope[...] += dot_nn(b5[...], weight[i % 2, 0])
        if i == 3 and m == 0:
            for b in range(3):
                load_middle(b).start()

    def dense_twin(i, m):
        return remote(
            to_twin.at[m], from_twin.at[i % 2, m], twin_sent.at[i, m], twin_recv.at[i, m], twin
        )

    def swap_dense(i, m):
        if i >= 1:
            dense_twin(i - 1, m).wait_send()
        to_twin[m] = grads[:, other].astype(bf16)
        dense_part[ks[i], m] = grads[:, mine].astype(bf16).reshape((2, 2) + DENSE_PIECE)
        if i >= 2:
            pl.semaphore_wait(twin_credit.at[i % 2, m], 1)
        dense_twin(i, m).start()

    def swapped_dense(i, m):
        dense_twin(i, m).wait_recv()
        k = ks[i]
        both = dense_part[k, m].astype(f32) + from_twin[i % 2, m].reshape((2, 2) + DENSE_PIECE).astype(f32)
        dense_part[k, m] = both.astype(bf16)
        if i < 2:
            pl.semaphore_signal(twin_credit.at[i % 2, m], inc=1, device_id=twin, device_id_type=MESH)

    def second_finish(b):
        load_middle(b).wait()
        rows = rows_of(b)
        unit, reciprocal = unit_of(grads[pl.ds((b % 3) * block, block), :])
        if b == 0:
            load_middle(3).start()
        raw = slope[rows, :]
        cot = b1[rows, :].astype(f32)
        sums[0:1, :] += jnp.sum(cot, axis=0, keepdims=True)
        sums[1:2, :] += jnp.sum(raw * unit, axis=0, keepdims=True)
        sums[2:3, :] += jnp.sum(raw, axis=0, keepdims=True)
        moved = cot + norm_slope(raw, unit, reciprocal, vector_full[2:3, :])
        slope[rows, :] = moved
        low = moved.astype(bf16)
        b4[rows, :] = low
        b5[rows, :] = dot_nt(low, output_full[...]).astype(bf16)
        b1[rows, :] = (total[rows, :] + vector_full[4:5, :]).astype(bf16)
        if b == tokens // block - 1:
            keep_result.start()
            load_share.start()
            load_normed.start()

    def output_grad():
        grads[...] = dot_tn(b3[...], b4[...])
        keep_result.wait()
        load_x_again.start()

    def scale_pair(p, _):
        lanes = pl.ds(pl.multiple_of(p * 128, 128), 128)
        for r in range(rows_count):
            rows = pl.ds(r * SEQ, SEQ)
            low = (b5[rows, lanes].astype(f32) * total[rows, lanes]).astype(bf16)
            b5[rows, lanes] = low
            weight[r, 0, lanes, 0:SEQ] = low.T
        return 0

    def load_head(n):
        h = ORDER[n // TRIPLE] * TRIPLE + n % TRIPLE
        return pltpu.make_async_copy(mixing_full.at[h], raised.at[n // 2 % 2, n % 2], head_sem.at[n % 4])

    def prepare():
        load_share.wait()
        for p in range(HEADS // 2 - 2, HEADS // 2):
            keep_pair(p).wait()
        for n in range(3):
            load_head(n).start()
        lax.fori_loop(0, HEADS // 2, scale_pair, 0)

    def head(i, n):
        k, step = ORDER[i], i * TRIPLE + n
        load_head(step).wait()
        if step + 3 < HEADS:
            load_head(step + 3).start()
        if n == 0 and i >= 2:
            mix_twin(i - 2).wait_send()
        h = k * TRIPLE + n
        lanes = slice((h // 2) * 128, (h // 2 + 1) * 128)
        side = h % 2
        lane = lane_ids(block)
        inside = lane < HEAD if side == 0 else lane >= HEAD
        inside_all = lane_ids(SEQ) < HEAD if side == 0 else lane_ids(SEQ) >= HEAD
        spot = lane - HEAD * (1 - side)
        for where in range(2):
            half = core if where == 0 else 1 - core
            start = pl.multiple_of(half * block, block)
            here = pl.ds(start, block)
            sum_rows = None
            for r in range(rows_count):
                rows = pl.ds(pl.multiple_of(r * SEQ + start, block), block)
                low = b5[rows, lanes].astype(f32)
                delta = jnp.sum(
                    jnp.where(inside, low * b3[rows, lanes].astype(f32), 0.0), axis=-1, keepdims=True
                )
                coarse = delta.astype(bf16).astype(f32)
                extra = jnp.where(spot == 0, -coarse, jnp.where(spot == 1, coarse - delta, 0.0))
                left = jnp.where(inside, low, extra).astype(bf16)
                pair = b2[r * SEQ : (r + 1) * SEQ, lanes].astype(f32)
                right = jnp.where(inside_all, pair, 1.0).astype(bf16)
                part = raised[step // 2 % 2, step % 2, here] * mask[r, here]
                chance[r, here] = part
                term = part.astype(f32) * dot_nt(left, right)
                sum_rows = term if sum_rows is None else sum_rows + term
            block_t[...] = sum_rows.astype(bf16)
            spots = []
            for row, column in BLOCKS + FOLDED:
                top, side_lanes = corner(half, row, column)
                spots.append((top, side_lanes))
            first, second = (block_t[pl.ds(top, 128), on].astype(f32) for top, on in spots[-2:])
            shared = (first + second.T).astype(bf16)
            for p in range(len(BLOCKS) + 1):
                top, side_lanes = spots[p]
                for q in range(8):
                    if p < len(BLOCKS):
                        strip = block_t[pl.ds(pl.multiple_of(top + q * 16, 16), 16), side_lanes]
                    else:
                        strip = shared[q * 16 : q * 16 + 16]
                    spot_of = (q % 2, q // 4, (q // 2) % 2, n, p)
                    if where == 0:
                        mix_part[(k,) + spot_of] = strip
                    else:
                        mix_to[(i % 2,) + spot_of] = strip
        heads_rows = slice(h * HEAD, (h + 1) * HEAD)
        for r in range(rows_count):
            weight[r, 1, heads_rows, 0:SEQ] = dot_nn(
                weight[r, 0, heads_rows, 0:SEQ], chance[r]
            ).astype(bf16)

    def turn():
        def turn_pair(p, _):
            lanes = pl.ds(pl.multiple_of(p * 128, 128), 128)
            for r in range(rows_count):
                b4[r * SEQ : (r + 1) * SEQ, lanes] = weight[r, 1, lanes, 0:SEQ].T
            return 0

        lax.fori_loop(0, D // 128, turn_pair, 0)

    def value_grad():
        load_normed.wait()
        grads[...] = dot_tn(b0[...], b4[...])

    def first_finish(b):
        if b == 0:
            load_x_again.wait()
            small[0] = jnp.zeros_like(small[0])
            small[0, 0:8] = sums[...]
        rows = rows_of(b)
        back = dot_nt(b4[rows, :], value_full[...])
        unit, reciprocal = unit_of(b1[rows, :].astype(f32))
        small[0, 7:8, :] += jnp.sum(back * unit, axis=0, keepdims=True)
        small[0, 8:9, :] += jnp.sum(back, axis=0, keepdims=True)
        moved = slope[rows, :] + norm_slope(back, unit, reciprocal, vector_full[0:1, :])
        b0[rows, :] = moved.astype(bf16)
        if b == tokens // block - 1:
            keep_inputs.start()

    other_rows = pl.ds(pl.multiple_of((1 - core) * HALF, HALF), HALF)
    share_rows = D // 4

    def weights_twin(m):
        return remote(to_twin.at[m], weights_from.at[m], weights_sent.at[m], weights_recv.at[m], twin)

    def mix_twin(i):
        return remote(mix_to.at[i % 2], mix_from.at[i % 2], mix_sent.at[i], mix_recv.at[i], twin)

    def swap(what):
        if what == "vg" or what == "og":
            m = 0 if what == "vg" else 1
            dense_twin(3, m).wait_send()
            if m == 0:
                to_twin[0] = grads[:, other].astype(bf16)
            else:
                for side in range(2):
                    to_twin[1, side * HALF : (side + 1) * HALF] = grads[
                        other_rows, side * HALF : (side + 1) * HALF
                    ].astype(bf16)
            for k in range(4):
                rows = slice(k * share_rows, (k + 1) * share_rows)
                own_rows = pl.ds(pl.multiple_of(core * HALF + (k % 2) * share_rows, 64), share_rows)
                side = slice((k // 2) * HALF, (k // 2 + 1) * HALF)
                part = grads[rows, mine] if m == 0 else grads[own_rows, side]
                weights_part[k, m] = part.astype(bf16).reshape((2, 2) + WEIGHT_PIECE)
            weights_twin(m).start()
        else:
            if what >= 2:
                pl.semaphore_wait(mix_credit.at[what % 2], 1)
            mix_twin(what).start()

    def swapped(what):
        if what == "vg" or what == "og":
            m = 0 if what == "vg" else 1
            weights_twin(m).wait_recv()
            for k in range(4):
                got = weights_from[m, k * share_rows : (k + 1) * share_rows].astype(f32)
                both = weights_part[k, m].astype(f32) + got.reshape((2, 2) + WEIGHT_PIECE)
                weights_part[k, m] = both.astype(bf16)
        else:
            mix_twin(what).wait_recv()
            k = ORDER[what]
            for m in range(2):
                for y_of in range(2):
                    for x_of in range(2):
                        families["m"][0].add_in(k, m, y_of, x_of, mix_from[what % 2, m, y_of, x_of])
            if what < 2:
                pl.semaphore_signal(mix_credit.at[what % 2], inc=1, device_id=twin, device_id_type=MESH)

    def small_copy(n):
        return remote(small.at[n], small_in.at[n], small_sent.at[n], small_recv.at[n], rounds[n])

    def small_round(n):
        if n > 0:
            small_copy(n - 1).wait_recv()
            small[n] = small[n - 1] + small_in[n - 1]
        if n < len(rounds):
            small_copy(n).start()

    def dense_reduce(step, *rest):
        if step == "hop":
            dense.hop(*rest)
        else:
            i, m = rest
            getattr(dense, step)(ks[i], m)

    load_x.start()
    shard[0] = hidden_ref[...]
    shard[1] = down_ref[...]
    vector_own[...] = jnp.zeros_like(vector_own)
    singles = (first_gain_ref, first_shift_ref, second_gain_ref, second_shift_ref, down_bias_ref)
    for n, ref in enumerate(singles):
        vector_own[n : n + 1, :] = ref[...].astype(f32).reshape(1, HALF)
    for n in range(4):
        piece = hidden_bias_ref[n * HALF : (n + 1) * HALF]
        vector_own[5 + n : 6 + n, :] = piece.astype(f32).reshape(1, HALF)
    vector_full[:, mine] = vector_own[...]
    greet(core, x, y, z, (pairs[1],))
    for m in range(2):
        own_copy(m).start()
    for name in ("vw", "ow"):
        early_own(name).start()

    local_steps = {
        "early": lambda name: early_copy(name).start(), "ready": early_ready, "gs": gather,
        "pass": pass_full, "fetch": fetch, "norm": first_norm,
        "mask": lambda: fill_mask(docs_ref, mask, rows_count), "mix": mix, "proj": project,
        "dense": dense_units, "grad": dense_grad, "acc": dense_back, "swapF": swap_dense,
        "swappedF": swapped_dense, "Fs": dense_reduce, "fin2": second_finish, "og": output_grad,
        "scale": prepare, "head": head, "turn": turn, "vg": value_grad, "fin1": first_finish,
        "swap": swap, "swapped": swapped, "small": small_round,
    }
    for name, *rest in SCHEDULE:
        if name in local_steps:
            local_steps[name](*rest)
            continue
        reduce, spread, part = families[name]
        step, *rest = rest
        if step == "at":
            spread.at(*rest, part)
        elif step in ("two", "cross", "rest"):
            getattr(spread, step)(*rest)
        else:
            getattr(reduce, step)(*rest)
            if step == "line":
                reduce.hop(*rest, 0)

    def out_copy(n, src, dst):
        return pltpu.make_async_copy(src, dst, out_sem.at[n])

    outs = [out_copy(0, mix_whole, mixing_out), out_copy(1, weights_whole, weights_out)]
    for copy in outs:
        copy.start()
    for k in range(4):

        @pl.when(z == k)
        def _():
            for m, out in enumerate((hidden_out, down_out)):
                out[...] = dense_part[k, m, y, x].astype(f32)

    for n, row in enumerate((0, 1, 2, 7, 8)):
        sums_out[n : n + 1, :] = small[5, row : row + 1, mine]
    for n in range(4):
        line = pl.ds(3 + 2 * core + n // 2, 1)
        sums_out[5 + n : 6 + n, :] = small[5, line, (n % 2) * HALF : (n % 2 + 1) * HALF]
    sums_out[9:16, :] = jnp.zeros((7, HALF), f32)
    for name in names:
        early_copy(name).wait_send()
    for n in range(5):
        small_copy(n).wait_send()
    for m in range(2):
        weights_twin(m).wait_send()
        for i in range(4):
            full_twin(i, m).wait_send()
    for i in (2, 3):
        mix_twin(i).wait_send()

    def settle_line(k, _):
        line = chunk_of(k, y, x)
        for m in range(2):
            full_copy(m, line, full_x, near_x).wait_send()
            full_copy(m, line, full_y, near_y).wait_send()

            @pl.when(jnp.logical_and(k <= z, z < 3))
            def _():
                full_copy(m, line, full_up, above).wait_send()

            @pl.when(jnp.logical_and(k >= z, z > 0))
            def _():
                full_copy(m, line, full_down, below).wait_send()

        full_copy(0, chunk_of(k, y, 1 - x), full_y, near_y).wait_send()
        full_copy(1, chunk_of(k, 1 - y, x), full_x, near_x).wait_send()
        return 0

    lax.fori_loop(0, 4, settle_line, 0)
    for k in range(4):
        dense.settle(k)
        for reduce, spread, _ in families.values():
            reduce.settle(k)
            spread.settle(k)
    keep_inputs.wait()
    for copy in outs:
        copy.wait()


def layer_call(
    x, documents, mixing, value_weight, output_weight, hidden_weight, down_weight, cotangent, *vectors
):
    tokens = x.shape[0]
    rows = tokens // SEQ
    any_spec = pl.BlockSpec(memory_space=pl.ANY)
    vmem = pl.BlockSpec(memory_space=pltpu.VMEM)
    shape = jax.ShapeDtypeStruct
    dma = pltpu.SemaphoreType.DMA
    credit = pltpu.SemaphoreType.REGULAR
    token_rows = pltpu.VMEM((tokens, D), bf16)
    half_grads = (2, D, HALF)
    quads = (2, 2, 2)
    return pl.pallas_call(
        layer_kernel,
        out_shape=(
            shape((tokens, D), bf16), shape((tokens, D), bf16), shape((4,) + quads + MIX_PIECE, bf16),
            shape((4,) + quads + WEIGHT_PIECE, bf16), shape(DENSE_PIECE, f32), shape(DENSE_PIECE, f32),
            shape((16, HALF), f32),
            shape((2, FF, D), bf16), shape((HEADS, SEQ, SEQ), bf16), shape((tokens, D), bf16),
            shape((tokens, D), f32), shape((tokens, D), f32),
        ),
        in_specs=[any_spec, vmem, any_spec, any_spec, any_spec, vmem, vmem, any_spec] + [vmem] * 6,
        out_specs=[any_spec] * 4 + [vmem] * 3 + [any_spec] * 5,
        scratch_shapes=[
            *[token_rows] * 6,
            pltpu.VMEM((D, D), bf16), pltpu.VMEM((D, D), bf16), pltpu.VMEM((16, D), f32),
            pltpu.VMEM((16, HALF), f32), pltpu.VMEM((2,) + DENSE_PIECE, bf16), pltpu.VMEM((rows, SEQ, SEQ), bf16),
            pltpu.VMEM((2, 2, SEQ, SEQ), bf16),
            pltpu.VMEM((tokens, D), f32), pltpu.VMEM((tokens, D), f32),
            pltpu.VMEM((2, 2, GROUP, D), bf16), pltpu.VMEM((D, D), f32), pltpu.VMEM(half_grads, bf16),
            pltpu.VMEM((2,) + half_grads, bf16), pltpu.VMEM((4,) + quads + DENSE_PIECE, bf16),
            pltpu.VMEM((rows, SEQ, SEQ), bf16), pltpu.VMEM((SEQ // 2, SEQ), bf16),
            pltpu.VMEM((4,) + quads + MIX_PIECE, bf16), pltpu.VMEM((2,) + quads + MIX_PIECE, bf16),
            pltpu.VMEM((2,) + quads + MIX_PIECE, bf16), pltpu.VMEM(half_grads, bf16),
            pltpu.VMEM((4,) + quads + WEIGHT_PIECE, bf16),
            pltpu.VMEM((6, 16, D), f32), pltpu.VMEM((5, 16, D), f32), pltpu.VMEM((8, D), f32),
            *Reduce.scratch(DENSE_PIECE), *Reduce.scratch(MIX_PIECE), *Reduce.scratch(WEIGHT_PIECE),
            *Gather.scratch(MIX_PIECE), *Gather.scratch(WEIGHT_PIECE),
            dma((9,)), dma((9,)), dma((9,)), dma((2,)),
            dma((2, 16)), dma((2, 4)), dma((2, 16)), dma((2, 16)), dma((2, 16)), dma((2, 16)), dma((2, 4)),
            dma((2,)), dma((2,)), dma((4,)), dma((2,)), dma((14,)), dma((2,)),
            dma((4, 2)), dma((4, 2)), credit((2, 2)), dma((4,)), dma((4,)), credit((2,)),
            dma((2,)), dma((2,)), dma((5,)), dma((5,)),
        ],
        compiler_params=pltpu.CompilerParams(
            collective_id=0, has_side_effects=True, vmem_limit_bytes=64 << 20
        ),
    )(x, documents, mixing, value_weight, output_weight, hidden_weight, down_weight, cotangent, *vectors)


def unpack_kernel(
    mixing_ref, weights_ref, sums_ref, hidden_ref, down_ref, result_ref, inputs_ref,
    result_out, inputs_out, mixing_out, value_out, output_out, first_gain_out, first_shift_out,
    second_gain_out, second_shift_out, hidden_out, hidden_bias_out, down_out, down_bias_out,
):
    half = lax.axis_index("narrow")
    below = lax.broadcasted_iota(jnp.int32, (128, 128), 0) - lane_ids(128)
    below = jnp.where(half == 0, below, -below)
    for h in range(TRIPLE):
        top, lanes = corner(half, 0, 3)
        mixing_out[h, pl.ds(top, 128), lanes] = jnp.zeros((128, 128), f32)
        strips = []
        for p in range(len(BLOCKS) + 1):
            for q in range(8):
                strip = mixing_ref[0, q % 2, q // 4, (q // 2) % 2, h, p].astype(f32)
                if p == len(BLOCKS):
                    strips.append(strip)
                    continue
                top, lanes = corner(half, *BLOCKS[p])
                mixing_out[h, pl.ds(pl.multiple_of(top + q * 16, 16), 16), lanes] = strip
        shared = jnp.concatenate(strips, axis=0)
        top, lanes = corner(half, *FOLDED[0])
        mixing_out[h, pl.ds(top, 128), lanes] = jnp.where(below > 0, shared, 0.0)
        top, lanes = corner(half, *FOLDED[1])
        mixing_out[h, pl.ds(top, 128), lanes] = jnp.where(below < 0, shared, 0.0).T
    value_out[...] = weights_ref[0, 0].astype(f32).reshape(D // 4, HALF)
    output_out[...] = weights_ref[0, 1].astype(f32).reshape(D // 4, HALF)
    result_out[...] = result_ref[...]
    inputs_out[...] = inputs_ref[...]

    @pl.when(pl.program_id(0) == 0)
    def _():
        hidden_out[...] = hidden_ref[...]
        down_out[...] = down_ref[...]
        singles = (down_bias_out, second_gain_out, second_shift_out, first_gain_out, first_shift_out)
        for n, out in enumerate(singles):
            out[...] = sums_ref[n]
        for n in range(4):
            hidden_bias_out[n * HALF : (n + 1) * HALF] = sums_ref[5 + n]


def unpack_call(mixing_packed, weights_packed, sums, hidden_share, down_share, result, inputs_slope):
    tokens = result.shape[0]
    shape = jax.ShapeDtypeStruct
    rows = pl.BlockSpec((tokens // 4, D), lambda k: (k, 0))
    piece = pl.BlockSpec(DENSE_PIECE, lambda k: (0, 0))
    single = pl.BlockSpec((HALF,), lambda k: (0,))
    quads = (1, 2, 2, 2)
    return pl.pallas_call(
        unpack_kernel,
        grid=(4,),
        out_shape=(
            shape((tokens, D), bf16), shape((tokens, D), bf16), shape((HEADS, SEQ // 2, SEQ), f32),
            shape((D, HALF), f32), shape((HALF, D), f32), *[shape((HALF,), f32)] * 4,
            shape(DENSE_PIECE, f32), shape((4 * HALF,), f32), shape(DENSE_PIECE, f32), shape((HALF,), f32),
        ),
        in_specs=[
            pl.BlockSpec(quads + MIX_PIECE, lambda k: (k,) + (0,) * 7),
            pl.BlockSpec(quads + WEIGHT_PIECE, lambda k: (k,) + (0,) * 5),
            pl.BlockSpec((16, HALF), lambda k: (0, 0)), piece, piece, rows, rows,
        ],
        out_specs=(
            rows, rows, pl.BlockSpec((TRIPLE, SEQ // 2, SEQ), lambda k: (k, 0, 0)),
            pl.BlockSpec((D // 4, HALF), lambda k: (k, 0)),
            pl.BlockSpec((D // 4, HALF), lambda k: (lax.rem(k, 2), lax.div(k, 2))),
            *[single] * 4, piece, pl.BlockSpec((4 * HALF,), lambda k: (0,)), piece, single,
        ),
        compiler_params=pltpu.CompilerParams(vmem_limit_bytes=62 << 20),
    )(mixing_packed, weights_packed, sums, hidden_share, down_share, result, inputs_slope)


def local(
    inputs, documents, mixing, value_weight, output_weight, mixer_gain, mixer_shift, dense_gain,
    dense_shift, hidden_weight, hidden_bias, down_weight, down_bias, cotangent,
):
    tokens = inputs.shape[0] * SEQ
    result, inputs_slope, mixing_packed, weights_packed, hidden_share, down_share, sums, *_ = layer_call(
        inputs.reshape(tokens, D), documents, mixing, value_weight, output_weight, hidden_weight.T,
        down_weight, cotangent.reshape(tokens, D), mixer_gain, mixer_shift, dense_gain, dense_shift,
        down_bias, hidden_bias,
    )
    outs = list(unpack_call(
        mixing_packed, weights_packed, sums, hidden_share, down_share, result, inputs_slope
    ))
    outs[0] = outs[0].reshape(inputs.shape)
    outs[1] = outs[1].reshape(inputs.shape)
    outs[9] = outs[9].T
    return tuple(outs)


SCHEDULE = (
    ("early", "vec"), ("early", "vw"), ("early", "mx0"), ("early", "mx1"), ("gs", "at", 0, 0),
    ("gs", "at", 0, 1), ("early", "mx2"), ("early", "mx3"), ("early", "mx4"), ("early", "mx5"),
    ("early", "ow"), ("gs", "two", 0, 0), ("gs", "two", 0, 1), ("ready", "vec"), ("ready", "vw"), ("norm", 0),
    ("norm", 1), ("norm", 2), ("gs", "at", 1, 0), ("ready", "mx0"), ("norm", 3), ("gs", "cross", 0, 0),
    ("gs", "cross", 0, 1), ("mask",), ("gs", "at", 1, 1), ("gs", "at", 2, 0), ("gs", "two", 1, 0),
    ("gs", "two", 2, 0), ("gs", "two", 1, 1), ("mix", 0), ("mix", 1), ("mix", 2), ("gs", "cross", 1, 0),
    ("gs", "rest", 0, 0), ("gs", "at", 2, 1), ("pass", 0, 0), ("gs", "two", 2, 1), ("mix", 3), ("mix", 4),
    ("gs", "at", 3, 0), ("gs", "rest", 0, 1), ("pass", 0, 1), ("mix", 5), ("ready", "ow"), ("proj", 0),
    ("proj", 1), ("gs", "at", 3, 1), ("gs", "two", 3, 1), ("gs", "two", 3, 0), ("fetch", 0), ("proj", 2),
    ("gs", "cross", 2, 0), ("proj", 3), ("gs", "cross", 1, 1), ("dense", 0, 0), ("dense", 0, 1),
    ("dense", 0, 2), ("gs", "rest", 1, 0), ("pass", 1, 0), ("grad", 0, 0), ("swapF", 0, 0), ("grad", 0, 1),
    ("swapF", 0, 1), ("gs", "cross", 2, 1), ("gs", "cross", 3, 1), ("gs", "cross", 3, 0), ("acc", 0, 0),
    ("gs", "rest", 1, 1), ("pass", 1, 1), ("acc", 0, 1), ("gs", "rest", 2, 0), ("swappedF", 0, 0),
    ("Fs", "first", 0, 0), ("swappedF", 0, 1), ("Fs", "first", 0, 1), ("fetch", 1), ("gs", "rest", 2, 1),
    ("pass", 2, 1), ("pass", 2, 0), ("dense", 1, 0), ("dense", 1, 1), ("dense", 1, 2), ("gs", "rest", 3, 0),
    ("pass", 3, 0), ("grad", 1, 0), ("gs", "rest", 3, 1), ("pass", 3, 1), ("Fs", "second", 0, 0),
    ("swapF", 1, 0), ("grad", 1, 1), ("fetch", 2), ("swapF", 1, 1), ("acc", 1, 0), ("Fs", "second", 0, 1),
    ("acc", 1, 1), ("swappedF", 1, 0), ("swappedF", 1, 1), ("Fs", "first", 1, 1), ("Fs", "first", 1, 0),
    ("fetch", 3), ("dense", 2, 0), ("dense", 2, 1), ("dense", 2, 2), ("grad", 2, 0), ("swapF", 2, 0),
    ("grad", 2, 1), ("swapF", 2, 1), ("acc", 2, 0), ("swappedF", 2, 0), ("acc", 2, 1), ("Fs", "second", 1, 1),
    ("Fs", "second", 1, 0), ("swappedF", 2, 1), ("Fs", "first", 2, 1), ("dense", 3, 0), ("Fs", "first", 2, 0),
    ("dense", 3, 1), ("dense", 3, 2), ("Fs", "line", 0, 0), ("Fs", "line", 1, 1), ("grad", 3, 0),
    ("Fs", "line", 1, 0), ("swapF", 3, 0), ("grad", 3, 1), ("Fs", "line", 0, 1), ("swapF", 3, 1),
    ("acc", 3, 0), ("acc", 3, 1), ("swappedF", 3, 0), ("Fs", "second", 2, 0), ("Fs", "second", 2, 1),
    ("fin2", 0), ("swappedF", 3, 1), ("Fs", "first", 3, 0), ("Fs", "first", 3, 1), ("fin2", 1),
    ("Fs", "line", 2, 0), ("Fs", "hop", 1, 0, 0), ("Fs", "hop", 2, 0, 0), ("Fs", "line", 2, 1),
    ("Fs", "hop", 1, 1, 0), ("fin2", 2), ("fin2", 3), ("og",), ("Fs", "hop", 2, 1, 0), ("swap", "og"),
    ("Fs", "hop", 1, 0, 1), ("Fs", "second", 3, 0), ("scale",), ("Fs", "second", 3, 1), ("swapped", "og"),
    ("w", "first", 0, 1), ("w", "first", 1, 1), ("Fs", "hop", 2, 0, 1), ("head", 0, 0), ("head", 0, 1),
    ("head", 0, 2), ("w", "first", 2, 1), ("swap", 0), ("head", 1, 0), ("Fs", "hop", 1, 1, 1),
    ("Fs", "line", 3, 0), ("Fs", "hop", 0, 0, 0), ("w", "first", 3, 1), ("Fs", "hop", 1, 0, 2),
    ("Fs", "hop", 3, 0, 0), ("Fs", "line", 3, 1), ("Fs", "hop", 0, 1, 0), ("Fs", "hop", 3, 1, 0),
    ("w", "second", 0, 1), ("head", 1, 1), ("head", 1, 2), ("Fs", "hop", 2, 1, 1), ("w", "second", 1, 1),
    ("swapped", 0), ("m", "first", 0, 0), ("w", "second", 2, 1), ("swap", 1), ("head", 2, 0),
    ("w", "line", 0, 1), ("m", "first", 0, 1), ("head", 2, 1), ("head", 2, 2), ("w", "second", 3, 1),
    ("Fs", "hop", 0, 0, 1), ("Fs", "hop", 3, 0, 1), ("swap", 2), ("swapped", 1), ("m", "first", 3, 0),
    ("head", 3, 0), ("Fs", "hop", 2, 1, 2), ("m", "first", 3, 1), ("head", 3, 1), ("m", "second", 0, 0),
    ("Fs", "hop", 3, 1, 1), ("w", "line", 2, 1), ("Fs", "hop", 0, 1, 1), ("Fs", "hop", 2, 0, 2),
    ("m", "second", 0, 1), ("swapped", 2), ("m", "first", 1, 0), ("w", "hop", 0, 1, 1),
    ("Fs", "hop", 3, 0, 2), ("Fs", "hop", 1, 1, 2), ("w", "line", 3, 1), ("Fs", "hop", 0, 0, 2),
    ("w", "line", 1, 1), ("head", 3, 2), ("m", "first", 1, 1), ("w", "hop", 2, 1, 1), ("swap", 3), ("turn",),
    ("vg",), ("m", "second", 3, 1), ("m", "second", 3, 0), ("w", "hop", 3, 1, 1), ("swapped", 3),
    ("m", "first", 2, 0), ("w", "hop", 1, 1, 1), ("m", "line", 0, 0), ("Fs", "hop", 3, 1, 2),
    ("w", "hop", 0, 1, 2), ("m", "first", 2, 1), ("Fs", "hop", 0, 1, 2), ("swap", "vg"),
    ("Fs", "hop", 0, 0, 3), ("fin1", 0), ("w", "hop", 3, 1, 2), ("m", "line", 0, 1), ("w", "hop", 1, 1, 2),
    ("Fs", "hop", 3, 0, 3), ("w", "hop", 2, 1, 2), ("w", "hop", 0, 1, 3), ("m", "hop", 0, 0, 1),
    ("w", "at", 1, 1, 0), ("w", "at", 2, 1, 0), ("m", "second", 1, 1), ("swapped", "vg"),
    ("w", "first", 0, 0), ("w", "first", 3, 0), ("w", "first", 1, 0), ("w", "first", 2, 0), ("fin1", 1),
    ("m", "second", 1, 0), ("m", "line", 3, 0), ("w", "two", 1, 1, 0), ("w", "at", 1, 1, 1),
    ("m", "line", 3, 1), ("m", "hop", 0, 0, 2), ("Fs", "hop", 3, 1, 3), ("w", "at", 0, 1, 0),
    ("m", "hop", 0, 1, 1), ("fin1", 2), ("w", "cross", 2, 1, 0), ("w", "hop", 3, 1, 3), ("w", "at", 2, 1, 1),
    ("m", "second", 2, 0), ("w", "at", 3, 1, 0), ("w", "two", 0, 1, 0), ("w", "two", 3, 1, 0),
    ("m", "hop", 0, 0, 3), ("m", "at", 0, 0, 0), ("w", "at", 1, 1, 2), ("m", "hop", 3, 0, 1), ("fin1", 3),
    ("m", "second", 2, 1), ("m", "line", 1, 0), ("w", "two", 2, 1, 0), ("w", "two", 2, 1, 1),
    ("w", "at", 2, 1, 2), ("m", "hop", 3, 0, 2), ("w", "two", 1, 1, 1), ("m", "hop", 3, 1, 1),
    ("w", "at", 3, 1, 1), ("m", "line", 1, 1), ("w", "at", 0, 1, 1), ("m", "two", 0, 0, 0),
    ("m", "hop", 0, 1, 2), ("w", "second", 0, 0), ("small", 0), ("w", "two", 2, 1, 2), ("small", 1),
    ("m", "line", 2, 0), ("m", "hop", 1, 0, 1), ("w", "second", 1, 0), ("m", "cross", 0, 0, 0),
    ("w", "two", 1, 1, 2), ("Fs", "hop", 0, 1, 3), ("w", "at", 3, 1, 2), ("w", "two", 3, 1, 1),
    ("m", "hop", 3, 1, 2), ("m", "hop", 0, 1, 3), ("m", "at", 0, 0, 1), ("m", "at", 0, 1, 0),
    ("m", "two", 0, 1, 0), ("w", "cross", 1, 1, 0), ("w", "two", 3, 1, 2), ("w", "two", 0, 1, 1),
    ("w", "at", 0, 1, 2), ("w", "two", 0, 1, 2), ("w", "at", 3, 1, 3), ("w", "line", 0, 0),
    ("m", "hop", 1, 1, 1), ("w", "second", 2, 0), ("m", "two", 0, 0, 1), ("w", "hop", 0, 0, 1),
    ("m", "hop", 3, 0, 3), ("m", "at", 3, 0, 0), ("m", "hop", 1, 0, 2), ("w", "two", 3, 1, 3),
    ("m", "two", 3, 0, 0), ("m", "at", 1, 0, 0), ("w", "line", 1, 0), ("w", "second", 3, 0),
    ("m", "cross", 0, 0, 1), ("m", "hop", 1, 1, 2), ("small", 2), ("m", "hop", 2, 0, 1), ("m", "at", 0, 0, 2),
    ("m", "two", 0, 0, 2), ("m", "at", 1, 0, 1), ("m", "at", 1, 1, 0), ("m", "hop", 3, 1, 3),
    ("w", "line", 2, 0), ("w", "at", 0, 1, 3), ("w", "cross", 3, 1, 0), ("w", "two", 0, 1, 3),
    ("m", "at", 3, 1, 0), ("m", "at", 0, 1, 1), ("m", "two", 3, 1, 0), ("m", "cross", 3, 0, 0),
    ("m", "two", 1, 0, 0), ("w", "hop", 1, 0, 1), ("m", "at", 3, 0, 1), ("m", "two", 0, 1, 1),
    ("m", "two", 3, 0, 1), ("m", "line", 2, 1), ("w", "cross", 1, 1, 1), ("w", "cross", 1, 1, 2),
    ("w", "hop", 0, 0, 2), ("w", "cross", 2, 1, 1), ("w", "hop", 1, 0, 2), ("w", "at", 1, 0, 0),
    ("m", "two", 1, 1, 0), ("m", "two", 1, 0, 1), ("w", "cross", 2, 1, 2), ("w", "cross", 0, 1, 0),
    ("w", "cross", 0, 1, 1), ("w", "cross", 0, 1, 2), ("w", "hop", 2, 0, 1), ("w", "two", 1, 0, 0),
    ("w", "cross", 3, 1, 1), ("m", "at", 0, 0, 3), ("w", "line", 3, 0), ("m", "hop", 2, 0, 2),
    ("m", "hop", 2, 1, 1), ("m", "at", 2, 0, 0), ("m", "at", 1, 1, 1), ("m", "two", 2, 0, 0),
    ("w", "hop", 0, 0, 3), ("w", "at", 0, 0, 0), ("w", "two", 0, 0, 0), ("m", "cross", 0, 0, 2),
    ("m", "at", 3, 1, 1), ("w", "rest", 1, 1), ("m", "at", 3, 0, 2), ("m", "at", 1, 0, 2),
    ("m", "two", 3, 0, 2), ("m", "two", 3, 1, 1), ("m", "two", 1, 0, 2), ("w", "rest", 2, 1),
    ("w", "cross", 0, 1, 3), ("w", "at", 1, 0, 1), ("w", "hop", 3, 0, 1), ("m", "two", 0, 0, 3),
    ("m", "at", 0, 1, 2), ("m", "cross", 3, 1, 0), ("w", "hop", 2, 0, 2), ("m", "at", 2, 0, 1),
    ("m", "cross", 0, 0, 3), ("m", "two", 2, 0, 1), ("w", "cross", 3, 1, 2), ("w", "at", 2, 0, 0),
    ("w", "at", 0, 0, 1), ("m", "cross", 1, 0, 0), ("m", "cross", 1, 0, 1), ("m", "cross", 3, 0, 1),
    ("w", "cross", 3, 1, 3), ("m", "two", 1, 1, 1), ("w", "rest", 0, 1), ("w", "two", 0, 0, 1),
    ("m", "at", 2, 0, 2), ("m", "at", 3, 0, 3), ("m", "two", 3, 0, 3), ("small", 3), ("m", "cross", 1, 1, 0),
    ("m", "at", 1, 1, 2), ("m", "two", 1, 1, 2), ("m", "hop", 2, 1, 2), ("m", "at", 3, 1, 2),
    ("w", "cross", 1, 0, 0), ("m", "at", 2, 1, 0), ("m", "cross", 3, 0, 2), ("m", "cross", 0, 1, 0),
    ("m", "cross", 1, 0, 2), ("m", "at", 0, 1, 3), ("m", "two", 0, 1, 2), ("m", "two", 0, 1, 3),
    ("m", "two", 2, 0, 2), ("m", "at", 3, 1, 3), ("w", "cross", 0, 0, 0), ("w", "hop", 3, 0, 2),
    ("m", "cross", 3, 1, 1), ("w", "at", 1, 0, 2), ("w", "two", 1, 0, 1), ("w", "two", 1, 0, 2),
    ("w", "at", 2, 0, 1), ("w", "at", 0, 0, 2), ("w", "two", 0, 0, 2), ("w", "rest", 3, 1),
    ("m", "rest", 0, 0), ("m", "two", 2, 1, 0), ("m", "two", 3, 1, 2), ("m", "two", 3, 1, 3),
    ("m", "at", 2, 1, 1), ("m", "cross", 2, 0, 0), ("m", "two", 2, 1, 1), ("w", "cross", 1, 0, 1),
    ("m", "cross", 2, 0, 1), ("w", "cross", 0, 0, 1), ("small", 4), ("w", "two", 2, 0, 0),
    ("w", "two", 2, 0, 1), ("w", "cross", 2, 0, 0), ("m", "cross", 3, 0, 3), ("w", "hop", 3, 0, 3),
    ("w", "at", 3, 0, 0), ("w", "at", 0, 0, 3), ("w", "two", 0, 0, 3), ("w", "two", 3, 0, 0),
    ("m", "cross", 0, 1, 1), ("m", "at", 2, 1, 2), ("m", "two", 2, 1, 2), ("w", "cross", 1, 0, 2),
    ("w", "cross", 2, 0, 1), ("m", "cross", 1, 1, 1), ("m", "cross", 1, 1, 2), ("m", "cross", 3, 1, 2),
    ("m", "cross", 2, 0, 2), ("m", "cross", 0, 1, 2), ("w", "at", 3, 0, 1), ("w", "at", 3, 0, 2),
    ("m", "rest", 3, 0), ("w", "at", 2, 0, 2), ("w", "two", 2, 0, 2), ("small", 5), ("m", "cross", 2, 1, 0),
    ("w", "two", 3, 0, 1), ("w", "at", 3, 0, 3), ("w", "two", 3, 0, 2), ("w", "cross", 3, 0, 0),
    ("m", "cross", 3, 1, 3), ("m", "cross", 0, 1, 3), ("m", "rest", 0, 1), ("m", "rest", 1, 0),
    ("w", "two", 3, 0, 3), ("w", "cross", 0, 0, 2), ("w", "cross", 2, 0, 2), ("w", "cross", 0, 0, 3),
    ("w", "cross", 3, 0, 1), ("m", "rest", 2, 0), ("w", "cross", 3, 0, 2), ("m", "cross", 2, 1, 1),
    ("m", "cross", 2, 1, 2), ("m", "rest", 1, 1), ("w", "cross", 3, 0, 3), ("w", "rest", 1, 0),
    ("w", "rest", 2, 0), ("m", "rest", 3, 1), ("w", "rest", 3, 0), ("m", "rest", 2, 1), ("w", "rest", 0, 0),
)


def normalize(matrix, norm_gain, norm_shift):
    average = jnp.mean(matrix, axis=-1, keepdims=True)
    center = matrix - average
    reciprocal = lax.rsqrt(jnp.mean(center * center, axis=-1, keepdims=True) + epsilon)
    unit_rows = center * reciprocal
    return (unit_rows * norm_gain + norm_shift, unit_rows, reciprocal)


def plain_norm_back(slope_rows, unit_rows, reciprocal, norm_gain):
    tilted = slope_rows * norm_gain
    centered_slope = tilted - jnp.mean(tilted, axis=-1, keepdims=True)
    centered_slope = centered_slope - unit_rows * jnp.mean(
        tilted * unit_rows, axis=-1, keepdims=True
    )
    return (
        centered_slope * reciprocal,
        jnp.sum(slope_rows * unit_rows, axis=0),
        jnp.sum(slope_rows, axis=0),
    )


def plain_contract(left_side, right_side):
    return lax.dot_general(
        left_side, right_side, (((0,), (0,)), ((), ())), preferred_element_type=jnp.float32
    )


def times_transpose(left_side, right_side):
    return lax.dot_general(
        left_side, right_side, (((1,), (1,)), ((), ())), preferred_element_type=jnp.float32
    )


def row_chances(mixing_full, row_docs):
    same_doc = row_docs[:, None] == row_docs[None, :]
    scores = jnp.where(same_doc[None, :, :], mixing_full.astype(jnp.float32), -1e30)
    row_top = jnp.max(scores, axis=-1, keepdims=True)
    raised = jnp.exp(scores - row_top)
    return raised / jnp.sum(raised, axis=-1, keepdims=True)


def plain(
    inputs,
    documents,
    mixing,
    value_weight,
    output_weight,
    mixer_gain,
    mixer_shift,
    dense_gain,
    dense_shift,
    hidden_weight,
    hidden_bias,
    down_weight,
    down_bias,
    cotangent,
):
    gathered = (
        lax.all_gather(mixing, "narrow", axis=1, tiled=True),
        lax.all_gather(value_weight, "narrow", axis=1, tiled=True),
        lax.all_gather(output_weight, "narrow", axis=0, tiled=True),
        lax.all_gather(mixer_gain, "narrow", axis=0, tiled=True),
        lax.all_gather(mixer_shift, "narrow", axis=0, tiled=True),
        lax.all_gather(dense_gain, "narrow", axis=0, tiled=True),
        lax.all_gather(dense_shift, "narrow", axis=0, tiled=True),
        lax.all_gather(hidden_bias, "narrow", axis=0, tiled=True),
        lax.all_gather(down_bias, "narrow", axis=0, tiled=True),
    )
    mixing_full, value_full, output_full = (gathered[0], gathered[1], gathered[2])
    gain_first = gathered[3].astype(jnp.float32)
    shift_first = gathered[4].astype(jnp.float32)
    gain_second = gathered[5].astype(jnp.float32)
    shift_second = gathered[6].astype(jnp.float32)
    bias_hidden = gathered[7].astype(jnp.float32)
    bias_down = gathered[8].astype(jnp.float32)
    halfway = (
        lax.all_gather(hidden_weight, "narrow", axis=0, tiled=True),
        lax.all_gather(down_weight, "narrow", axis=1, tiled=True),
    )
    hidden_full, down_full = (
        lax.all_gather(halfway[0], "wide", axis=1, tiled=True),
        lax.all_gather(halfway[1], "wide", axis=0, tiled=True),
    )
    row_count = inputs.shape[0]
    stream = inputs.reshape(row_count * SEQ, D).astype(jnp.float32)
    normed, unit_first, recip_first = normalize(stream, gain_first, shift_first)
    normed_low = normed.astype(jnp.bfloat16)
    values = jnp.dot(normed_low, value_full, preferred_element_type=jnp.float32).astype(
        jnp.bfloat16
    )
    value_rows = values.reshape(row_count, SEQ, D)

    def mix_one(bundle):
        row_values, row_docs = bundle
        chances_low = row_chances(mixing_full, row_docs).astype(jnp.bfloat16)
        per_head = row_values.reshape(SEQ, HEADS, HEAD)
        blended_row = jnp.einsum(
            "hij,jhd->ihd", chances_low, per_head, preferred_element_type=jnp.float32
        )
        return blended_row.reshape(SEQ, D).astype(jnp.bfloat16)

    blended = lax.map(mix_one, (value_rows, documents)).reshape(row_count * SEQ, D)
    middle = stream + jnp.dot(blended, output_full, preferred_element_type=jnp.float32)
    normed_two, unit_second, recip_second = normalize(middle, gain_second, shift_second)
    normed_two_low = normed_two.astype(jnp.bfloat16)
    hidden = jnp.dot(normed_two_low, hidden_full, preferred_element_type=jnp.float32) + bias_hidden
    activated, gelu_pull = jax.vjp(jax.nn.gelu, hidden)
    active = activated.astype(jnp.bfloat16)
    result = middle + jnp.dot(active, down_full, preferred_element_type=jnp.float32) + bias_down
    slope_low = cotangent.reshape(row_count * SEQ, D)
    slope_wide = slope_low.astype(jnp.float32)
    down_bias_sum = jnp.sum(slope_wide, axis=0)
    down_grad = plain_contract(active, slope_low)
    active_slope = times_transpose(slope_low, down_full)
    hidden_slope_wide = gelu_pull(active_slope)[0]
    hidden_slope = hidden_slope_wide.astype(jnp.bfloat16)
    hidden_bias_sum = jnp.sum(hidden_slope.astype(jnp.float32), axis=0)
    hidden_grad = plain_contract(normed_two_low, hidden_slope)
    normed_two_slope = times_transpose(hidden_slope, hidden_full)
    back_second, gain_second_sum, shift_second_sum = plain_norm_back(
        normed_two_slope, unit_second, recip_second, gain_second
    )
    middle_slope = slope_wide + back_second
    attended_slope = middle_slope.astype(jnp.bfloat16)
    output_grad = plain_contract(blended, attended_slope)
    blended_slope = times_transpose(attended_slope, output_full).astype(jnp.bfloat16)

    def mix_back(running, bundle):
        row_values, row_docs, row_slope = bundle
        chances = row_chances(mixing_full, row_docs)
        per_head = row_values.reshape(SEQ, HEADS, HEAD)
        head_slope = row_slope.reshape(SEQ, HEADS, HEAD)
        chance_slope = jnp.einsum(
            "ihd,jhd->hij", head_slope, per_head, preferred_element_type=jnp.float32
        )
        score_slope = chances * (
            chance_slope - jnp.sum(chances * chance_slope, axis=-1, keepdims=True)
        )
        value_part = jnp.einsum(
            "hij,ihd->jhd",
            chances.astype(jnp.bfloat16),
            head_slope,
            preferred_element_type=jnp.float32,
        )
        return (running + score_slope, value_part.reshape(SEQ, D).astype(jnp.bfloat16))

    mixing_start = jnp.zeros((HEADS, SEQ, SEQ), jnp.float32)
    mixing_grad, value_slopes = lax.scan(
        mix_back, mixing_start, (value_rows, documents, blended_slope.reshape(row_count, SEQ, D))
    )
    value_slope = value_slopes.reshape(row_count * SEQ, D)
    value_grad = plain_contract(normed_low, value_slope)
    normed_slope = times_transpose(value_slope, value_full)
    back_first, gain_first_sum, shift_first_sum = plain_norm_back(
        normed_slope, unit_first, recip_first, gain_first
    )
    inputs_slope = (middle_slope + back_first).astype(jnp.bfloat16)
    sums_half = (
        lax.psum_scatter(
            hidden_grad.astype(jnp.bfloat16), "wide", scatter_dimension=1, tiled=True
        ).astype(jnp.float32),
        lax.psum_scatter(
            down_grad.astype(jnp.bfloat16), "wide", scatter_dimension=0, tiled=True
        ).astype(jnp.float32),
    )
    hidden_share, down_share = (
        lax.psum_scatter(
            sums_half[0].astype(jnp.bfloat16), "narrow", scatter_dimension=0, tiled=True
        ).astype(jnp.float32),
        lax.psum_scatter(
            sums_half[1].astype(jnp.bfloat16), "narrow", scatter_dimension=1, tiled=True
        ).astype(jnp.float32),
    )
    shares = (
        lax.psum_scatter(
            mixing_grad.astype(jnp.bfloat16), "narrow", scatter_dimension=1, tiled=True
        ).astype(jnp.float32),
        lax.psum_scatter(
            value_grad.astype(jnp.bfloat16), "narrow", scatter_dimension=1, tiled=True
        ).astype(jnp.float32),
        lax.psum_scatter(
            output_grad.astype(jnp.bfloat16), "narrow", scatter_dimension=0, tiled=True
        ).astype(jnp.float32),
        lax.psum_scatter(
            gain_first_sum.astype(jnp.bfloat16), "narrow", scatter_dimension=0, tiled=True
        ).astype(jnp.float32),
        lax.psum_scatter(
            shift_first_sum.astype(jnp.bfloat16), "narrow", scatter_dimension=0, tiled=True
        ).astype(jnp.float32),
        lax.psum_scatter(
            gain_second_sum.astype(jnp.bfloat16), "narrow", scatter_dimension=0, tiled=True
        ).astype(jnp.float32),
        lax.psum_scatter(
            shift_second_sum.astype(jnp.bfloat16), "narrow", scatter_dimension=0, tiled=True
        ).astype(jnp.float32),
        lax.psum_scatter(
            hidden_bias_sum.astype(jnp.bfloat16), "narrow", scatter_dimension=0, tiled=True
        ).astype(jnp.float32),
        lax.psum_scatter(
            down_bias_sum.astype(jnp.bfloat16), "narrow", scatter_dimension=0, tiled=True
        ).astype(jnp.float32),
    )
    totals = (
        lax.psum(shares[0].astype(jnp.bfloat16), "wide").astype(jnp.float32),
        lax.psum(shares[1].astype(jnp.bfloat16), "wide").astype(jnp.float32),
        lax.psum(shares[2].astype(jnp.bfloat16), "wide").astype(jnp.float32),
        lax.psum(shares[3].astype(jnp.bfloat16), "wide").astype(jnp.float32),
        lax.psum(shares[4].astype(jnp.bfloat16), "wide").astype(jnp.float32),
        lax.psum(shares[5].astype(jnp.bfloat16), "wide").astype(jnp.float32),
        lax.psum(shares[6].astype(jnp.bfloat16), "wide").astype(jnp.float32),
        lax.psum(shares[7].astype(jnp.bfloat16), "wide").astype(jnp.float32),
        lax.psum(shares[8].astype(jnp.bfloat16), "wide").astype(jnp.float32),
    )
    return (
        result.reshape(row_count, SEQ, D).astype(jnp.bfloat16),
        inputs_slope.reshape(row_count, SEQ, D),
        totals[0],
        totals[1],
        totals[2],
        totals[3],
        totals[4],
        totals[5],
        totals[6],
        hidden_share,
        totals[7],
        down_share,
        totals[8],
    )


def solution(mesh):
    inner = local if dict(mesh.shape) == {"narrow": 2, "wide": 16} else plain
    return jax.shard_map(
        inner,
        mesh=mesh,
        in_specs=(
            P(("narrow", "wide"), None, None),
            P(("narrow", "wide"), None),
            P(None, "narrow", None),
            P(None, "narrow"),
            P("narrow", None),
            P("narrow"),
            P("narrow"),
            P("narrow"),
            P("narrow"),
            P("narrow", "wide"),
            P("narrow"),
            P("wide", "narrow"),
            P("narrow"),
            P(("narrow", "wide"), None, None),
        ),
        out_specs=(
            P(("narrow", "wide"), None, None),
            P(("narrow", "wide"), None, None),
            P(None, "narrow", None),
            P(None, "narrow"),
            P("narrow", None),
            P("narrow"),
            P("narrow"),
            P("narrow"),
            P("narrow"),
            P("narrow", "wide"),
            P("narrow"),
            P("wide", "narrow"),
            P("narrow"),
        ),
        check_vma=False,
    )
```

```python
import functools

import jax
import jax.numpy as jnp
from jax import lax
from jax.experimental import pallas as pl
from jax.experimental.pallas import tpu as pltpu
from jax.sharding import PartitionSpec as P

D = 768
HEADS = 12
HEAD = 64
SEQ = 512
FF = 3072
HALF = D // 2
CHUNK = 192
GROUP = 4 * CHUNK
epsilon = 1e-05

MESH = pl.DeviceIdType.MESH
f32 = jnp.float32
bf16 = jnp.bfloat16


def place():
    core = lax.axis_index("narrow")
    wide = lax.axis_index("wide")
    return core, lax.rem(wide, 2), lax.rem(lax.div(wide, 2), 2), lax.div(wide, 4)


def seat(core, x, y, z):
    return (core, z * 4 + y * 2 + x)


def remote(src, dst, send_sem, recv_sem, device):
    return pltpu.make_async_remote_copy(
        src_ref=src,
        dst_ref=dst,
        send_sem=send_sem,
        recv_sem=recv_sem,
        device_id=device,
        device_id_type=MESH,
    )


def greet(core, x, y, z, more=()):
    barrier = pltpu.get_barrier_semaphore()
    near = (seat(1 - core, x, y, z), seat(core, 1 - x, y, z), seat(core, x, 1 - y, z)) + more
    for device in near:
        pl.semaphore_signal(barrier, inc=1, device_id=device, device_id_type=MESH)

    @pl.when(z < 3)
    def _():
        pl.semaphore_signal(
            barrier, inc=1, device_id=seat(core, x, y, z + 1), device_id_type=MESH
        )

    @pl.when(z > 0)
    def _():
        pl.semaphore_signal(
            barrier, inc=1, device_id=seat(core, x, y, z - 1), device_id_type=MESH
        )

    above, below = jnp.where(z < 3, 1, 0), jnp.where(z > 0, 1, 0)
    pl.semaphore_wait(barrier, len(near) + above + below)


def halves(core):
    mine = pl.ds(pl.multiple_of(core * HALF, 128), HALF)
    other = pl.ds(pl.multiple_of((1 - core) * HALF, 128), HALF)
    return mine, other


def line_order(z, step):
    table = ((0, 1, 2, 3), (1, 0, 2, 3), (2, 1, 3, 0), (3, 2, 1, 0))
    return jnp.where(
        z == 0,
        table[0][step],
        jnp.where(z == 1, table[1][step], jnp.where(z == 2, table[2][step], table[3][step])),
    )


def unit_of(rows):
    center = rows - jnp.mean(rows, axis=-1, keepdims=True)
    reciprocal = lax.rsqrt(jnp.mean(center * center, axis=-1, keepdims=True) + epsilon)
    return center * reciprocal, reciprocal


def dot_nn(left, right):
    return lax.dot_general(left, right, (((1,), (0,)), ((), ())), preferred_element_type=f32)


def dot_nt(left, right):
    return lax.dot_general(left, right, (((1,), (1,)), ((), ())), preferred_element_type=f32)


def dot_tn(left, right):
    return lax.dot_general(left, right, (((0,), (0,)), ((), ())), preferred_element_type=f32)


def corner(half, row, column):
    return (
        pl.multiple_of((row + half * (1 - 2 * row)) * 128, 128),
        pl.ds(pl.multiple_of((column + half * (3 - 2 * column)) * 128, 128), 128),
    )


def lane_ids(rows):
    return lax.broadcasted_iota(jnp.int32, (rows, 128), 1)


def fill_mask(docs_ref, mask, rows):
    for r in range(rows):
        flat = docs_ref[r : r + 1, :].astype(f32)
        for i in range(0, SEQ, 128):
            tall = jnp.broadcast_to(flat[:, i : i + 128], (128, 128)).T
            for j in range(0, SEQ, 128):
                wide = jnp.broadcast_to(flat[:, j : j + 128], (128, 128))
                mask[r, i : i + 128, j : j + 128] = jnp.where(tall == wide, 1.0, 0.0).astype(bf16)


def gelu_and_slope(v):
    scale = 0.7978845608028654
    square = v * v
    t = jnp.tanh(scale * v * (1.0 + 0.044715 * square))
    rise = 0.5 * (1.0 + t)
    slope = rise + 0.5 * scale * v * (1.0 - t * t) * (1.0 + 3.0 * 0.044715 * square)
    return v * rise, slope


def norm_slope(slope, unit, reciprocal, gain):
    tilted = slope * gain
    centered = tilted - jnp.mean(tilted, axis=-1, keepdims=True)
    centered = centered - unit * jnp.mean(tilted * unit, axis=-1, keepdims=True)
    return centered * reciprocal


class Reduce:
    def __init__(self, part, refs):
        self.part = part
        (
            self.first_y, self.first_x, self.second_x, self.second_y, self.line_in,
            self.first_sent, self.first_recv, self.second_sent, self.second_recv,
            self.line_sent, self.line_recv,
        ) = refs
        core, x, y, z = place()
        self.x, self.y, self.z = x, y, z
        self.near_x, self.near_y = seat(core, 1 - x, y, z), seat(core, x, 1 - y, z)
        self.above, self.below = seat(core, x, y, z + 1), seat(core, x, y, z - 1)

    @staticmethod
    def scratch(piece):
        dma = pltpu.SemaphoreType.DMA
        return [
            pltpu.VMEM((4, 2) + piece, bf16), pltpu.VMEM((4, 2) + piece, bf16),
            pltpu.VMEM((4,) + piece, bf16), pltpu.VMEM((4,) + piece, bf16),
            pltpu.VMEM((2, 4, 2) + piece, bf16),
            dma((4, 2)), dma((4, 2)), dma((4, 2)), dma((4, 2)), dma((2, 4, 2)), dma((2, 4, 2)),
        ]

    def first_copy(self, k, m):
        sems = self.first_sent.at[k, m], self.first_recv.at[k, m]
        if m == 0:
            return remote(self.part.at[k, 0, 1 - self.y], self.first_y.at[k], *sems, self.near_y)
        return remote(self.part.at[k, 1, :, 1 - self.x], self.first_x.at[k], *sems, self.near_x)

    def second_copy(self, k, m):
        x, y = self.x, self.y
        sems = self.second_sent.at[k, m], self.second_recv.at[k, m]
        if m == 0:
            return remote(self.part.at[k, 0, y, 1 - x], self.second_x.at[k], *sems, self.near_x)
        return remote(self.part.at[k, 1, 1 - y, x], self.second_y.at[k], *sems, self.near_y)

    def line_copy(self, k, m, down):
        return remote(
            self.part.at[k, m, self.y, self.x], self.line_in.at[down, k, m],
            self.line_sent.at[down, k, m], self.line_recv.at[down, k, m],
            self.below if down else self.above,
        )

    def add_in(self, k, m, y_of, x_of, got):
        old = self.part[k, m, y_of, x_of].astype(f32)
        self.part[k, m, y_of, x_of] = (old + got.astype(f32)).astype(bf16)

    def first(self, k, m):
        self.first_copy(k, m).start()

    def second(self, k, m):
        x, y = self.x, self.y
        self.first_copy(k, m).wait_recv()
        if m == 0:
            self.add_in(k, 0, y, 1 - x, self.first_y[k, 1 - x])
            self.second_copy(k, 0).start()
            self.add_in(k, 0, y, x, self.first_y[k, x])
        else:
            self.add_in(k, 1, 1 - y, x, self.first_x[k, 1 - y])
            self.second_copy(k, 1).start()
            self.add_in(k, 1, y, x, self.first_x[k, y])

    def line(self, k, m):
        self.second_copy(k, m).wait_recv()
        self.add_in(k, m, self.y, self.x, (self.second_x, self.second_y)[m][k])

    def hop(self, k, m, hop):
        x, y, z = self.x, self.y, self.z
        for down, length, seat_z in ((0, k, hop), (1, 3 - k, 3 - hop)):
            if hop < length:

                @pl.when(z == seat_z)
                def _():
                    if hop > 0:
                        self.line_copy(k, m, down).wait_recv()
                        self.add_in(k, m, y, x, self.line_in[down, k, m])
                    self.line_copy(k, m, down).start()

        if hop == max(k, 3 - k):

            @pl.when(z == k)
            def _():
                for down, length in ((0, k), (1, 3 - k)):
                    if length > 0:
                        self.line_copy(k, m, down).wait_recv()
                        self.add_in(k, m, y, x, self.line_in[down, k, m])

    def settle(self, k):
        for m in range(2):
            self.first_copy(k, m).wait_send()
            self.second_copy(k, m).wait_send()
            if k > 0:

                @pl.when(self.z < k)
                def _():
                    self.line_copy(k, m, 0).wait_send()

            if k < 3:

                @pl.when(self.z > k)
                def _():
                    self.line_copy(k, m, 1).wait_send()


class Gather:
    def __init__(self, whole, refs):
        self.whole = whole
        self.recv, self.sent_x, self.sent_y, self.sent_z = refs
        core, x, y, z = place()
        self.x, self.y, self.z = x, y, z
        self.near_x, self.near_y = seat(core, 1 - x, y, z), seat(core, x, 1 - y, z)
        self.above, self.below = seat(core, x, y, z + 1), seat(core, x, y, z - 1)

    @staticmethod
    def scratch(piece):
        dma = pltpu.SemaphoreType.DMA
        return [
            pltpu.VMEM((4, 2, 2, 2) + piece, bf16),
            dma((4, 2, 2, 2)), dma((4, 2, 2)), dma((4, 2, 2)), dma((2, 4, 2)),
        ]

    def send(self, k, m, y_of, x_of, sem, device):
        src = self.whole.at[k, m, y_of, x_of]
        return remote(src, src, sem, self.recv.at[k, m, y_of, x_of], device)

    def to_x(self, k, m, y_of):
        return self.send(k, m, y_of, self.x, self.sent_x.at[k, m, y_of], self.near_x)

    def to_y(self, k, m, x_of):
        return self.send(k, m, self.y, x_of, self.sent_y.at[k, m, x_of], self.near_y)

    def along(self, k, m, down):
        device = self.below if down else self.above
        return self.send(k, m, self.y, self.x, self.sent_z.at[down, k, m], device)

    def arrived(self, k, m, y_of, x_of):
        self.send(k, m, y_of, x_of, self.sent_x.at[k, m, 0], self.near_x).wait_recv()

    def at(self, k, m, distance, part=None):
        x, y, z = self.x, self.y, self.z
        up, down = k + distance, k - distance
        for seat_z in sorted({up, down}):
            if 0 <= seat_z < 4:

                @pl.when(z == seat_z)
                def _():
                    if distance:
                        self.arrived(k, m, y, x)
                    elif part is not None:
                        self.whole[k, m, y, x] = part[k, m, y, x]
                    if k <= seat_z < 3:
                        self.along(k, m, 0).start()
                    if k >= seat_z > 0:
                        self.along(k, m, 1).start()
                    if m == 0:
                        self.to_x(k, 0, y).start()
                    else:
                        self.to_y(k, 1, x).start()

    def two(self, k, m, distance):
        x, y, z = self.x, self.y, self.z
        for seat_z in sorted({k + distance, k - distance}):
            if 0 <= seat_z < 4:

                @pl.when(z == seat_z)
                def _():
                    if m == 0:
                        self.to_y(k, 0, x).start()
                    else:
                        self.to_x(k, 1, y).start()

    def cross(self, k, m, distance):
        x, y, z = self.x, self.y, self.z
        up, down = k + distance, k - distance
        for seat_z in sorted({up, down}):
            if 0 <= seat_z < 4:

                @pl.when(z == seat_z)
                def _():
                    if m == 0:
                        self.arrived(k, 0, y, 1 - x)
                        self.to_y(k, 0, 1 - x).start()
                    else:
                        self.arrived(k, 1, 1 - y, x)
                        self.to_x(k, 1, 1 - y).start()

    def rest(self, k, m):
        x, y = self.x, self.y
        if m == 0:
            self.arrived(k, 0, 1 - y, x)
        else:
            self.arrived(k, 1, y, 1 - x)
        self.arrived(k, m, 1 - y, 1 - x)

    def settle(self, k):
        x, y, z = self.x, self.y, self.z
        for m in range(2):
            self.to_x(k, m, y).wait_send()
            self.to_y(k, m, x).wait_send()
            if k < 3:

                @pl.when(jnp.logical_and(z >= k, z < 3))
                def _():
                    self.along(k, m, 0).wait_send()

            if k > 0:

                @pl.when(jnp.logical_and(z <= k, z > 0))
                def _():
                    self.along(k, m, 1).wait_send()

        self.to_y(k, 0, 1 - x).wait_send()
        self.to_x(k, 1, 1 - y).wait_send()


BLOCKS = ((0, 0), (0, 1), (1, 0), (1, 1), (1, 2))
FOLDED = ((0, 2), (1, 3))
TRIPLE = HEADS // 4
MIX_PIECE = (TRIPLE, 6, 16, 128)
WEIGHT_PIECE = (48, HALF)
DENSE_PIECE = (CHUNK, HALF)
ORDER = (0, 3, 1, 2)


def layer_kernel(
    x_hbm, docs_ref, mixing_ref, value_ref, output_ref, hidden_ref, down_ref, cotangent_hbm,
    first_gain_ref, first_shift_ref, second_gain_ref, second_shift_ref, down_bias_ref, hidden_bias_ref,
    result_out, inputs_out, mixing_out, weights_out, hidden_out, down_out, sums_out,
    full_ref, mixing_full, normed_hbm, share_hbm, middle_hbm,
    *scratch,
):
    scratch = list(scratch)

    def take(n):
        got = scratch[:n]
        del scratch[:n]
        return got

    b0, b1, b2, b3, b4, b5 = take(6)
    value_full, output_full, vector_full, vector_own, shard, mask, raised = take(7)
    total, slope, weight, grads, to_twin, from_twin, dense_part = take(7)
    chance, block_t, mix_part, mix_to, mix_from, weights_from, weights_part = take(7)
    small, small_in, sums = take(3)
    dense_refs = take(11)
    mix_reduce_refs = take(11)
    weights_reduce_refs = take(11)
    mix_whole, *mix_gather_refs = take(5)
    weights_whole, *weights_gather_refs = take(5)
    early_send, early_recv, early_local, shard_sem = take(4)
    full_recv, full_core_recv, full_x, full_y, full_up, full_down, full_core = take(7)
    pair_sem, back_sem, head_sem, weight_sem, move_sem, out_sem = take(6)
    twin_sent, twin_recv, twin_credit, mix_sent, mix_recv, mix_credit = take(6)
    weights_sent, weights_recv, small_sent, small_recv = take(4)

    core, x, y, z = place()
    mine, other = halves(core)
    near_x, near_y = seat(core, 1 - x, y, z), seat(core, x, 1 - y, z)
    above, below = seat(core, x, y, z + 1), seat(core, x, y, z - 1)
    twin = seat(1 - core, x, y, z)
    tokens = b0.shape[0]
    rows_count = tokens // SEQ
    block = 256
    dense = Reduce(dense_part, dense_refs)
    families = {
        "m": (Reduce(mix_part, mix_reduce_refs), Gather(mix_whole, mix_gather_refs), mix_part),
        "w": (Reduce(weights_part, weights_reduce_refs), Gather(weights_whole, weights_gather_refs), weights_part),
    }
    pairs = (seat(core, x, y, z + 1 - 2 * lax.rem(z, 2)), seat(core, x, y, lax.rem(z + 2, 4)))
    rounds = (twin, near_x, near_y) + pairs
    ks = [line_order(z, i) for i in range(4)]

    def rows_of(b):
        return pl.ds(pl.multiple_of(b * block, block), block)

    def move(n, src, dst):
        return pltpu.make_async_copy(src, dst, move_sem.at[n])

    load_x = move(0, x_hbm, b0)
    keep_normed = move(1, b1, normed_hbm)
    load_cotangent = move(2, cotangent_hbm, b1)
    keep_share = move(3, slope, share_hbm)
    keep_middle = move(4, total, middle_hbm)
    load_share = move(5, share_hbm, total)
    load_normed = move(6, normed_hbm, b0)
    keep_result = move(7, b1, result_out)
    load_x_again = move(8, x_hbm, b1)
    keep_inputs = move(9, b0, inputs_out)

    def load_middle(b):
        return move(10 + b, middle_hbm.at[rows_of(b)], grads.at[pl.ds((b % 3) * block, block)])

    my_rows = pl.ds(pl.multiple_of(core * (SEQ // 2), SEQ // 2), SEQ // 2)
    early = {"vec": (vector_own, vector_full.at[:, mine]), "vw": (value_ref, value_full.at[:, mine])}
    for p in range(HEADS // 2):
        heads_of = pl.ds(2 * p, 2)
        early["mx%d" % p] = (mixing_ref.at[heads_of], mixing_full.at[heads_of, my_rows])
    early["ow"] = (output_ref, output_full.at[mine, :])
    names = list(early)

    def early_copy(name):
        n = names.index(name)
        return remote(*early[name], early_send.at[n], early_recv.at[n], twin)

    def early_own(name):
        src, dst = early[name]
        if name.startswith("mx"):
            dst = raised.at[int(name[2:]) % 2, :, my_rows]
        return pltpu.make_async_copy(src, dst, early_local.at[names.index(name)])

    def chunk_of(k, y_of, x_of):
        return k * 4 + y_of * 2 + x_of

    own = chunk_of(z, y, x)

    def slot(m, chunk):
        return full_ref.at[m, pl.ds(pl.multiple_of(chunk * CHUNK, CHUNK), CHUNK), mine]

    def full_copy(m, chunk, sems, device, src=None):
        dst = slot(m, chunk)
        return remote(dst if src is None else src, dst, sems.at[m, chunk], full_recv.at[m, chunk], device)

    def full_arrived(m, chunk):
        full_copy(m, chunk, full_x, near_x).wait_recv()

    def own_copy(m):
        return pltpu.make_async_copy(shard.at[m], slot(m, own), shard_sem.at[m])

    def gather(step, i, m):
        k = ks[i]
        if step == "at":
            chunk = chunk_of(k, y, x)
            src = shard.at[m] if i == 0 else None
            if i > 0:
                full_arrived(m, chunk)

            @pl.when(jnp.logical_and(k <= z, z < 3))
            def _():
                full_copy(m, chunk, full_up, above, src).start()

            @pl.when(jnp.logical_and(k >= z, z > 0))
            def _():
                full_copy(m, chunk, full_down, below, src).start()

            sems, device = ((full_x, near_x), (full_y, near_y))[m]
            full_copy(m, chunk, sems, device, src).start()
        elif step == "two":
            sems, device = ((full_y, near_y), (full_x, near_x))[m]
            full_copy(m, chunk_of(k, y, x), sems, device, shard.at[m] if i == 0 else None).start()
        elif step == "cross":
            if m == 0:
                full_arrived(0, chunk_of(k, y, 1 - x))
                full_copy(0, chunk_of(k, y, 1 - x), full_y, near_y).start()
            else:
                full_arrived(1, chunk_of(k, 1 - y, x))
                full_copy(1, chunk_of(k, 1 - y, x), full_x, near_x).start()
        else:
            full_arrived(m, chunk_of(k, 1 - y, x) if m == 0 else chunk_of(k, y, 1 - x))
            full_arrived(m, chunk_of(k, 1 - y, 1 - x))

    def full_twin(i, m):
        src = full_ref.at[m, pl.ds(pl.multiple_of(ks[i] * GROUP, GROUP), GROUP), mine]
        return remote(src, src, full_core.at[m, i], full_core_recv.at[m, i], twin)

    def pass_full(i, m):
        if i == 0:
            own_copy(m).wait()
        full_twin(i, m).start()

    def load_weight(i):
        rows = pl.ds(pl.multiple_of(ks[i] * GROUP, GROUP), GROUP)
        return pltpu.make_async_copy(full_ref.at[:, rows], weight.at[i % 2], weight_sem.at[i % 2])

    def fetch(i):
        for m in range(2):
            full_twin(i, m).wait_recv()
        load_weight(i).start()

    def first_norm(b):
        if b == 0:
            load_x.wait()
        rows = rows_of(b)
        unit, _ = unit_of(b0[rows, :].astype(f32))
        low = (unit * vector_full[0:1, :] + vector_full[1:2, :]).astype(bf16)
        b1[rows, :] = low
        b2[rows, :] = dot_nn(low, value_full[...]).astype(bf16)
        if b == tokens // block - 1:
            keep_normed.start()

    twin_rows = pl.ds(pl.multiple_of((1 - core) * (SEQ // 2), SEQ // 2), SEQ // 2)

    def load_pair(p):
        return pltpu.make_async_copy(
            mixing_full.at[pl.ds(2 * p, 2), twin_rows], raised.at[p % 2, :, twin_rows], pair_sem.at[p % 2]
        )

    def keep_pair(p):
        return pltpu.make_async_copy(raised.at[p % 2], mixing_full.at[pl.ds(2 * p, 2)], back_sem.at[p % 2])

    def mix(p):
        early_own("mx%d" % p).wait()
        load_pair(p).wait()
        if p + 1 < HEADS // 2:
            early_copy("mx%d" % (p + 1)).wait_recv()
            if p >= 1:
                keep_pair(p - 1).wait()
            early_own("mx%d" % (p + 1)).start()
            load_pair(p + 1).start()
        lanes = slice(p * 128, (p + 1) * 128)
        low_lanes = lane_ids(block) < HEAD
        pair_raised = raised.at[p % 2]
        for half in range(2):
            for i in range(0, SEQ, block):
                part = pair_raised[half, i : i + block].astype(f32)
                pair_raised[half, i : i + block] = jnp.exp(part).astype(bf16)
        keep_pair(p).start()

        def mix_row(r, _):
            pair = b2[pl.ds(pl.multiple_of(r * SEQ, SEQ), SEQ), lanes]
            left_half = lane_ids(SEQ) < HEAD
            ones = jnp.ones_like(pair)
            first = jnp.where(left_half, pair, ones)
            second = jnp.where(left_half, ones, pair)
            for i in range(0, SEQ, block):
                keep = mask[r, i : i + block]
                one = dot_nn(pair_raised[0, i : i + block] * keep, first)
                two = dot_nn(pair_raised[1, i : i + block] * keep, second)
                part = 1.0 / pltpu.roll(jnp.where(low_lanes, two, one), HEAD, 1)
                done = pl.ds(pl.multiple_of(r * SEQ + i, block), block)
                slope[done, lanes] = part
                b3[done, lanes] = (jnp.where(low_lanes, one, two) * part).astype(bf16)
            return 0

        lax.fori_loop(0, rows_count, mix_row, 0)
        if p == HEADS // 2 - 1:
            keep_share.start()
            keep_normed.wait()
            load_cotangent.start()

    def early_ready(name):
        if name in ("vw", "ow"):
            early_own(name).wait()
        early_copy(name).wait_recv()
        if name == "mx0":
            early_own("mx0").start()
            load_pair(0).start()

    def project(b):
        rows = rows_of(b)
        middle = b0[rows, :].astype(f32) + dot_nn(b3[rows, :], output_full[...])
        total[rows, :] = middle
        unit, _ = unit_of(middle)
        b0[rows, :] = (unit * vector_full[2:3, :] + vector_full[3:4, :]).astype(bf16)
        if b == tokens // block - 1:
            keep_middle.start()
            keep_share.wait()
            sums[...] = jnp.zeros_like(sums)

    def dense_units(i, u):
        k = ks[i]
        if u == 0:
            load_weight(i).wait()
        if i == 0 and u == 0:
            load_cotangent.wait()
        units = slice(u * 256, (u + 1) * 256)
        lanes = pl.ds(pl.multiple_of(lax.div(k, 2) * HALF, 128), HALF)
        row = 5 + 2 * lax.rem(k, 2)
        bias = jnp.concatenate(
            [vector_full[pl.ds(row, 1), lanes], vector_full[pl.ds(row + 1, 1), lanes]], axis=1
        )[:, units]
        hidden = dot_nt(b0[...], weight[i % 2, 0, units, :]) + bias
        pulled = dot_nt(b1[...], weight[i % 2, 1, units, :])
        act, pull = gelu_and_slope(hidden)
        turned = (pulled * pull).astype(bf16)
        b4[:, units] = act.astype(bf16)
        b5[:, units] = turned
        sums[pl.ds(3 + k, 1), units] = jnp.sum(turned.astype(f32), axis=0, keepdims=True)

    def dense_grad(i, m):
        left, right = ((b5, b0), (b4, b1))[m]
        grads[...] = dot_tn(left[...], right[...])

    def dense_back(i, m):
        if m == 1:
            if i == 0:
                keep_middle.wait()
            total[...] += dot_nn(b4[...], weight[i % 2, 1])
        elif i == 0:
            slope[...] = dot_nn(b5[...], weight[i % 2, 0])
        else:
            slope[...] += dot_nn(b5[...], weight[i % 2, 0])
        if i == 3 and m == 0:
            for b in range(3):
                load_middle(b).start()

    def dense_twin(i, m):
        return remote(
            to_twin.at[m], from_twin.at[i % 2, m], twin_sent.at[i, m], twin_recv.at[i, m], twin
        )

    def swap_dense(i, m):
        if i >= 1:
            dense_twin(i - 1, m).wait_send()
        to_twin[m] = grads[:, other].astype(bf16)
        dense_part[ks[i], m] = grads[:, mine].astype(bf16).reshape((2, 2) + DENSE_PIECE)
        if i >= 2:
            pl.semaphore_wait(twin_credit.at[i % 2, m], 1)
        dense_twin(i, m).start()

    def swapped_dense(i, m):
        dense_twin(i, m).wait_recv()
        k = ks[i]
        both = dense_part[k, m].astype(f32) + from_twin[i % 2, m].reshape((2, 2) + DENSE_PIECE).astype(f32)
        dense_part[k, m] = both.astype(bf16)
        if i < 2:
            pl.semaphore_signal(twin_credit.at[i % 2, m], inc=1, device_id=twin, device_id_type=MESH)

    def second_finish(b):
        load_middle(b).wait()
        rows = rows_of(b)
        unit, reciprocal = unit_of(grads[pl.ds((b % 3) * block, block), :])
        if b == 0:
            load_middle(3).start()
        raw = slope[rows, :]
        cot = b1[rows, :].astype(f32)
        sums[0:1, :] += jnp.sum(cot, axis=0, keepdims=True)
        sums[1:2, :] += jnp.sum(raw * unit, axis=0, keepdims=True)
        sums[2:3, :] += jnp.sum(raw, axis=0, keepdims=True)
        moved = cot + norm_slope(raw, unit, reciprocal, vector_full[2:3, :])
        slope[rows, :] = moved
        low = moved.astype(bf16)
        b4[rows, :] = low
        b5[rows, :] = dot_nt(low, output_full[...]).astype(bf16)
        b1[rows, :] = (total[rows, :] + vector_full[4:5, :]).astype(bf16)
        if b == tokens // block - 1:
            keep_result.start()
            load_share.start()
            load_normed.start()

    def output_grad():
        grads[...] = dot_tn(b3[...], b4[...])
        keep_result.wait()
        load_x_again.start()

    def scale_pair(p, _):
        lanes = pl.ds(pl.multiple_of(p * 128, 128), 128)
        for r in range(rows_count):
            rows = pl.ds(r * SEQ, SEQ)
            low = (b5[rows, lanes].astype(f32) * total[rows, lanes]).astype(bf16)
            b5[rows, lanes] = low
            weight[r, 0, lanes, 0:SEQ] = low.T
        return 0

    def load_head(n):
        h = ORDER[n // TRIPLE] * TRIPLE + n % TRIPLE
        return pltpu.make_async_copy(mixing_full.at[h], raised.at[n // 2 % 2, n % 2], head_sem.at[n % 4])

    def prepare():
        load_share.wait()
        for p in range(HEADS // 2 - 2, HEADS // 2):
            keep_pair(p).wait()
        for n in range(3):
            load_head(n).start()
        lax.fori_loop(0, HEADS // 2, scale_pair, 0)

    def head(i, n):
        k, step = ORDER[i], i * TRIPLE + n
        load_head(step).wait()
        if step + 3 < HEADS:
            load_head(step + 3).start()
        if n == 0 and i >= 2:
            mix_twin(i - 2).wait_send()
        h = k * TRIPLE + n
        lanes = slice((h // 2) * 128, (h // 2 + 1) * 128)
        side = h % 2
        lane = lane_ids(block)
        inside = lane < HEAD if side == 0 else lane >= HEAD
        inside_all = lane_ids(SEQ) < HEAD if side == 0 else lane_ids(SEQ) >= HEAD
        spot = lane - HEAD * (1 - side)
        for where in range(2):
            half = core if where == 0 else 1 - core
            start = pl.multiple_of(half * block, block)
            here = pl.ds(start, block)
            sum_rows = None
            for r in range(rows_count):
                rows = pl.ds(pl.multiple_of(r * SEQ + start, block), block)
                low = b5[rows, lanes].astype(f32)
                delta = jnp.sum(
                    jnp.where(inside, low * b3[rows, lanes].astype(f32), 0.0), axis=-1, keepdims=True
                )
                coarse = delta.astype(bf16).astype(f32)
                extra = jnp.where(spot == 0, -coarse, jnp.where(spot == 1, coarse - delta, 0.0))
                left = jnp.where(inside, low, extra).astype(bf16)
                pair = b2[r * SEQ : (r + 1) * SEQ, lanes].astype(f32)
                right = jnp.where(inside_all, pair, 1.0).astype(bf16)
                part = raised[step // 2 % 2, step % 2, here] * mask[r, here]
                chance[r, here] = part
                term = part.astype(f32) * dot_nt(left, right)
                sum_rows = term if sum_rows is None else sum_rows + term
            block_t[...] = sum_rows.astype(bf16)
            spots = []
            for row, column in BLOCKS + FOLDED:
                top, side_lanes = corner(half, row, column)
                spots.append((top, side_lanes))
            first, second = (block_t[pl.ds(top, 128), on].astype(f32) for top, on in spots[-2:])
            shared = (first + second.T).astype(bf16)
            for p in range(len(BLOCKS) + 1):
                top, side_lanes = spots[p]
                for q in range(8):
                    if p < len(BLOCKS):
                        strip = block_t[pl.ds(pl.multiple_of(top + q * 16, 16), 16), side_lanes]
                    else:
                        strip = shared[q * 16 : q * 16 + 16]
                    spot_of = (q % 2, q // 4, (q // 2) % 2, n, p)
                    if where == 0:
                        mix_part[(k,) + spot_of] = strip
                    else:
                        mix_to[(i % 2,) + spot_of] = strip
        heads_rows = slice(h * HEAD, (h + 1) * HEAD)
        for r in range(rows_count):
            weight[r, 1, heads_rows, 0:SEQ] = dot_nn(
                weight[r, 0, heads_rows, 0:SEQ], chance[r]
            ).astype(bf16)

    def turn():
        def turn_pair(p, _):
            lanes = pl.ds(pl.multiple_of(p * 128, 128), 128)
            for r in range(rows_count):
                b4[r * SEQ : (r + 1) * SEQ, lanes] = weight[r, 1, lanes, 0:SEQ].T
            return 0

        lax.fori_loop(0, D // 128, turn_pair, 0)

    def value_grad():
        load_normed.wait()
        grads[...] = dot_tn(b0[...], b4[...])

    def first_finish(b):
        if b == 0:
            load_x_again.wait()
            small[0] = jnp.zeros_like(small[0])
            small[0, 0:8] = sums[...]
        rows = rows_of(b)
        back = dot_nt(b4[rows, :], value_full[...])
        unit, reciprocal = unit_of(b1[rows, :].astype(f32))
        small[0, 7:8, :] += jnp.sum(back * unit, axis=0, keepdims=True)
        small[0, 8:9, :] += jnp.sum(back, axis=0, keepdims=True)
        moved = slope[rows, :] + norm_slope(back, unit, reciprocal, vector_full[0:1, :])
        b0[rows, :] = moved.astype(bf16)
        if b == tokens // block - 1:
            keep_inputs.start()

    other_rows = pl.ds(pl.multiple_of((1 - core) * HALF, HALF), HALF)
    share_rows = D // 4

    def weights_twin(m):
        return remote(to_twin.at[m], weights_from.at[m], weights_sent.at[m], weights_recv.at[m], twin)

    def mix_twin(i):
        return remote(mix_to.at[i % 2], mix_from.at[i % 2], mix_sent.at[i], mix_recv.at[i], twin)

    def swap(what):
        if what == "vg" or what == "og":
            m = 0 if what == "vg" else 1
            dense_twin(3, m).wait_send()
            if m == 0:
                to_twin[0] = grads[:, other].astype(bf16)
            else:
                for side in range(2):
                    to_twin[1, side * HALF : (side + 1) * HALF] = grads[
                        other_rows, side * HALF : (side + 1) * HALF
                    ].astype(bf16)
            for k in range(4):
                rows = slice(k * share_rows, (k + 1) * share_rows)
                own_rows = pl.ds(pl.multiple_of(core * HALF + (k % 2) * share_rows, 64), share_rows)
                side = slice((k // 2) * HALF, (k // 2 + 1) * HALF)
                part = grads[rows, mine] if m == 0 else grads[own_rows, side]
                weights_part[k, m] = part.astype(bf16).reshape((2, 2) + WEIGHT_PIECE)
            weights_twin(m).start()
        else:
            if what >= 2:
                pl.semaphore_wait(mix_credit.at[what % 2], 1)
            mix_twin(what).start()

    def swapped(what):
        if what == "vg" or what == "og":
            m = 0 if what == "vg" else 1
            weights_twin(m).wait_recv()
            for k in range(4):
                got = weights_from[m, k * share_rows : (k + 1) * share_rows].astype(f32)
                both = weights_part[k, m].astype(f32) + got.reshape((2, 2) + WEIGHT_PIECE)
                weights_part[k, m] = both.astype(bf16)
        else:
            mix_twin(what).wait_recv()
            k = ORDER[what]
            for m in range(2):
                for y_of in range(2):
                    for x_of in range(2):
                        families["m"][0].add_in(k, m, y_of, x_of, mix_from[what % 2, m, y_of, x_of])
            if what < 2:
                pl.semaphore_signal(mix_credit.at[what % 2], inc=1, device_id=twin, device_id_type=MESH)

    def small_copy(n):
        return remote(small.at[n], small_in.at[n], small_sent.at[n], small_recv.at[n], rounds[n])

    def small_round(n):
        if n > 0:
            small_copy(n - 1).wait_recv()
            small[n] = small[n - 1] + small_in[n - 1]
        if n < len(rounds):
            small_copy(n).start()

    def dense_reduce(step, *rest):
        if step == "hop":
            dense.hop(*rest)
        else:
            i, m = rest
            getattr(dense, step)(ks[i], m)

    load_x.start()
    shard[0] = hidden_ref[...]
    shard[1] = down_ref[...]
    vector_own[...] = jnp.zeros_like(vector_own)
    singles = (first_gain_ref, first_shift_ref, second_gain_ref, second_shift_ref, down_bias_ref)
    for n, ref in enumerate(singles):
        vector_own[n : n + 1, :] = ref[...].astype(f32).reshape(1, HALF)
    for n in range(4):
        piece = hidden_bias_ref[n * HALF : (n + 1) * HALF]
        vector_own[5 + n : 6 + n, :] = piece.astype(f32).reshape(1, HALF)
    vector_full[:, mine] = vector_own[...]
    greet(core, x, y, z, (pairs[1],))
    for m in range(2):
        own_copy(m).start()
    for name in ("vw", "ow"):
        early_own(name).start()

    local_steps = {
        "early": lambda name: early_copy(name).start(), "ready": early_ready, "gs": gather,
        "pass": pass_full, "fetch": fetch, "norm": first_norm,
        "mask": lambda: fill_mask(docs_ref, mask, rows_count), "mix": mix, "proj": project,
        "dense": dense_units, "grad": dense_grad, "acc": dense_back, "swapF": swap_dense,
        "swappedF": swapped_dense, "Fs": dense_reduce, "fin2": second_finish, "og": output_grad,
        "scale": prepare, "head": head, "turn": turn, "vg": value_grad, "fin1": first_finish,
        "swap": swap, "swapped": swapped, "small": small_round,
    }
    def out_copy(n, src, dst, k):
        return pltpu.make_async_copy(src.at[k], dst.at[k], out_sem.at[n, k])

    outs, whole_parts = [], set()
    for name, *rest in SCHEDULE:
        if name in local_steps:
            local_steps[name](*rest)
            continue
        reduce, spread, part = families[name]
        step, *rest = rest
        if step == "at":
            spread.at(*rest, part)
        elif step in ("two", "cross", "rest"):
            getattr(spread, step)(*rest)
            if step == "rest":
                k, m = rest
                whole_parts.add((name, k, m))
                if (name, k, 1 - m) in whole_parts:
                    outs.append((0, mix_whole, mixing_out, k) if name == "m" else (1, weights_whole, weights_out, k))
                    out_copy(*outs[-1]).start()
        else:
            getattr(reduce, step)(*rest)
            if step == "line":
                reduce.hop(*rest, 0)

    for k in range(4):

        @pl.when(z == k)
        def _():
            for m, out in enumerate((hidden_out, down_out)):
                out[...] = dense_part[k, m, y, x].astype(f32)

    for n, row in enumerate((0, 1, 2, 7, 8)):
        sums_out[n : n + 1, :] = small[5, row : row + 1, mine]
    for n in range(4):
        line = pl.ds(3 + 2 * core + n // 2, 1)
        sums_out[5 + n : 6 + n, :] = small[5, line, (n % 2) * HALF : (n % 2 + 1) * HALF]
    sums_out[9:16, :] = jnp.zeros((7, HALF), f32)
    for name in names:
        early_copy(name).wait_send()
    for n in range(5):
        small_copy(n).wait_send()
    for m in range(2):
        weights_twin(m).wait_send()
        for i in range(4):
            full_twin(i, m).wait_send()
    for i in (2, 3):
        mix_twin(i).wait_send()

    def settle_line(k, _):
        line = chunk_of(k, y, x)
        for m in range(2):
            full_copy(m, line, full_x, near_x).wait_send()
            full_copy(m, line, full_y, near_y).wait_send()

            @pl.when(jnp.logical_and(k <= z, z < 3))
            def _():
                full_copy(m, line, full_up, above).wait_send()

            @pl.when(jnp.logical_and(k >= z, z > 0))
            def _():
                full_copy(m, line, full_down, below).wait_send()

        full_copy(0, chunk_of(k, y, 1 - x), full_y, near_y).wait_send()
        full_copy(1, chunk_of(k, 1 - y, x), full_x, near_x).wait_send()
        return 0

    lax.fori_loop(0, 4, settle_line, 0)
    for k in range(4):
        dense.settle(k)
        for reduce, spread, _ in families.values():
            reduce.settle(k)
            spread.settle(k)
    keep_inputs.wait()
    for out in outs:
        out_copy(*out).wait()


def layer_call(
    x, documents, mixing, value_weight, output_weight, hidden_weight, down_weight, cotangent, *vectors
):
    tokens = x.shape[0]
    rows = tokens // SEQ
    any_spec = pl.BlockSpec(memory_space=pl.ANY)
    vmem = pl.BlockSpec(memory_space=pltpu.VMEM)
    shape = jax.ShapeDtypeStruct
    dma = pltpu.SemaphoreType.DMA
    credit = pltpu.SemaphoreType.REGULAR
    token_rows = pltpu.VMEM((tokens, D), bf16)
    half_grads = (2, D, HALF)
    quads = (2, 2, 2)
    return pl.pallas_call(
        layer_kernel,
        out_shape=(
            shape((tokens, D), bf16), shape((tokens, D), bf16), shape((4,) + quads + MIX_PIECE, bf16),
            shape((4,) + quads + WEIGHT_PIECE, bf16), shape(DENSE_PIECE, f32), shape(DENSE_PIECE, f32),
            shape((16, HALF), f32),
            shape((2, FF, D), bf16), shape((HEADS, SEQ, SEQ), bf16), shape((tokens, D), bf16),
            shape((tokens, D), f32), shape((tokens, D), f32),
        ),
        in_specs=[any_spec, vmem, any_spec, any_spec, any_spec, vmem, vmem, any_spec] + [vmem] * 6,
        out_specs=[any_spec] * 4 + [vmem] * 3 + [any_spec] * 5,
        scratch_shapes=[
            *[token_rows] * 6,
            pltpu.VMEM((D, D), bf16), pltpu.VMEM((D, D), bf16), pltpu.VMEM((16, D), f32),
            pltpu.VMEM((16, HALF), f32), pltpu.VMEM((2,) + DENSE_PIECE, bf16), pltpu.VMEM((rows, SEQ, SEQ), bf16),
            pltpu.VMEM((2, 2, SEQ, SEQ), bf16),
            pltpu.VMEM((tokens, D), f32), pltpu.VMEM((tokens, D), f32),
            pltpu.VMEM((2, 2, GROUP, D), bf16), pltpu.VMEM((D, D), f32), pltpu.VMEM(half_grads, bf16),
            pltpu.VMEM((2,) + half_grads, bf16), pltpu.VMEM((4,) + quads + DENSE_PIECE, bf16),
            pltpu.VMEM((rows, SEQ, SEQ), bf16), pltpu.VMEM((SEQ // 2, SEQ), bf16),
            pltpu.VMEM((4,) + quads + MIX_PIECE, bf16), pltpu.VMEM((2,) + quads + MIX_PIECE, bf16),
            pltpu.VMEM((2,) + quads + MIX_PIECE, bf16), pltpu.VMEM(half_grads, bf16),
            pltpu.VMEM((4,) + quads + WEIGHT_PIECE, bf16),
            pltpu.VMEM((6, 16, D), f32), pltpu.VMEM((5, 16, D), f32), pltpu.VMEM((8, D), f32),
            *Reduce.scratch(DENSE_PIECE), *Reduce.scratch(MIX_PIECE), *Reduce.scratch(WEIGHT_PIECE),
            *Gather.scratch(MIX_PIECE), *Gather.scratch(WEIGHT_PIECE),
            dma((9,)), dma((9,)), dma((9,)), dma((2,)),
            dma((2, 16)), dma((2, 4)), dma((2, 16)), dma((2, 16)), dma((2, 16)), dma((2, 16)), dma((2, 4)),
            dma((2,)), dma((2,)), dma((4,)), dma((2,)), dma((14,)), dma((2, 4)),
            dma((4, 2)), dma((4, 2)), credit((2, 2)), dma((4,)), dma((4,)), credit((2,)),
            dma((2,)), dma((2,)), dma((5,)), dma((5,)),
        ],
        compiler_params=pltpu.CompilerParams(
            collective_id=0, has_side_effects=True, vmem_limit_bytes=64 << 20
        ),
    )(x, documents, mixing, value_weight, output_weight, hidden_weight, down_weight, cotangent, *vectors)


def unpack_kernel(
    mixing_ref, weights_ref, sums_ref, hidden_ref, down_ref, result_ref, inputs_ref,
    result_out, inputs_out, mixing_out, value_out, output_out, first_gain_out, first_shift_out,
    second_gain_out, second_shift_out, hidden_out, hidden_bias_out, down_out, down_bias_out,
):
    half = lax.axis_index("narrow")
    below = lax.broadcasted_iota(jnp.int32, (128, 128), 0) - lane_ids(128)
    below = jnp.where(half == 0, below, -below)
    top, lanes = corner(half, 0, 3)
    mixing_out[0, pl.ds(top, 128), lanes] = jnp.zeros((128, 128), f32)
    strips = []
    for p in range(len(BLOCKS) + 1):
        for q in range(8):
            strip = mixing_ref[0, q % 2, q // 4, (q // 2) % 2, 0, p].astype(f32)
            if p == len(BLOCKS):
                strips.append(strip)
                continue
            top, lanes = corner(half, *BLOCKS[p])
            mixing_out[0, pl.ds(pl.multiple_of(top + q * 16, 16), 16), lanes] = strip
    shared = jnp.concatenate(strips, axis=0)
    top, lanes = corner(half, *FOLDED[0])
    mixing_out[0, pl.ds(top, 128), lanes] = jnp.where(below > 0, shared, 0.0)
    top, lanes = corner(half, *FOLDED[1])
    mixing_out[0, pl.ds(top, 128), lanes] = jnp.where(below < 0, shared, 0.0).T

    @pl.when(pl.program_id(1) == 0)
    def _():
        value_out[...] = weights_ref[0, 0].astype(f32).reshape(D // 4, HALF)
        output_out[...] = weights_ref[0, 1].astype(f32).reshape(D // 4, HALF)
        result_out[...] = result_ref[...]
        inputs_out[...] = inputs_ref[...]

    @pl.when(jnp.logical_and(pl.program_id(0) == 0, pl.program_id(1) == 0))
    def _():
        hidden_out[...] = hidden_ref[...]
        down_out[...] = down_ref[...]
        singles = (down_bias_out, second_gain_out, second_shift_out, first_gain_out, first_shift_out)
        for n, out in enumerate(singles):
            out[...] = sums_ref[n]
        for n in range(4):
            hidden_bias_out[n * HALF : (n + 1) * HALF] = sums_ref[5 + n]


def unpack_call(mixing_packed, weights_packed, sums, hidden_share, down_share, result, inputs_slope):
    tokens = result.shape[0]
    shape = jax.ShapeDtypeStruct
    rows = pl.BlockSpec((tokens // 4, D), lambda k, h: (k, 0))
    piece = pl.BlockSpec(DENSE_PIECE, lambda k, h: (0, 0))
    single = pl.BlockSpec((HALF,), lambda k, h: (0,))
    quads = (1, 2, 2, 2)
    return pl.pallas_call(
        unpack_kernel,
        grid=(4, TRIPLE),
        out_shape=(
            shape((tokens, D), bf16), shape((tokens, D), bf16), shape((HEADS, SEQ // 2, SEQ), f32),
            shape((D, HALF), f32), shape((HALF, D), f32), *[shape((HALF,), f32)] * 4,
            shape(DENSE_PIECE, f32), shape((4 * HALF,), f32), shape(DENSE_PIECE, f32), shape((HALF,), f32),
        ),
        in_specs=[
            pl.BlockSpec(quads + (1,) + MIX_PIECE[1:], lambda k, h: (k, 0, 0, 0, h, 0, 0, 0)),
            pl.BlockSpec(quads + WEIGHT_PIECE, lambda k, h: (k,) + (0,) * 5),
            pl.BlockSpec((16, HALF), lambda k, h: (0, 0)), piece, piece, rows, rows,
        ],
        out_specs=(
            rows, rows, pl.BlockSpec((1, SEQ // 2, SEQ), lambda k, h: (k * TRIPLE + h, 0, 0)),
            pl.BlockSpec((D // 4, HALF), lambda k, h: (k, 0)),
            pl.BlockSpec((D // 4, HALF), lambda k, h: (lax.rem(k, 2), lax.div(k, 2))),
            *[single] * 4, piece, pl.BlockSpec((4 * HALF,), lambda k, h: (0,)), piece, single,
        ),
        compiler_params=pltpu.CompilerParams(vmem_limit_bytes=62 << 20),
    )(mixing_packed, weights_packed, sums, hidden_share, down_share, result, inputs_slope)


def local(
    inputs, documents, mixing, value_weight, output_weight, mixer_gain, mixer_shift, dense_gain,
    dense_shift, hidden_weight, hidden_bias, down_weight, down_bias, cotangent,
):
    tokens = inputs.shape[0] * SEQ
    result, inputs_slope, mixing_packed, weights_packed, hidden_share, down_share, sums, *_ = layer_call(
        inputs.reshape(tokens, D), documents, mixing, value_weight, output_weight, hidden_weight.T,
        down_weight, cotangent.reshape(tokens, D), mixer_gain, mixer_shift, dense_gain, dense_shift,
        down_bias, hidden_bias,
    )
    outs = list(unpack_call(
        mixing_packed, weights_packed, sums, hidden_share, down_share, result, inputs_slope
    ))
    outs[0] = outs[0].reshape(inputs.shape)
    outs[1] = outs[1].reshape(inputs.shape)
    outs[9] = outs[9].T
    return tuple(outs)


SCHEDULE = (
    ("early", "vec"), ("early", "vw"), ("early", "mx0"), ("early", "mx1"), ("gs", "at", 0, 0),
    ("gs", "at", 0, 1), ("early", "mx2"), ("early", "mx3"), ("early", "mx4"), ("early", "mx5"),
    ("early", "ow"), ("gs", "two", 0, 0), ("gs", "two", 0, 1), ("mask",), ("ready", "vec"), ("ready", "vw"), ("norm", 0),
    ("norm", 1), ("norm", 2), ("gs", "at", 1, 0), ("ready", "mx0"), ("norm", 3), ("gs", "cross", 0, 0),
    ("gs", "cross", 0, 1), ("gs", "at", 1, 1), ("gs", "at", 2, 0), ("gs", "two", 1, 0),
    ("gs", "two", 2, 0), ("gs", "two", 1, 1), ("mix", 0), ("mix", 1), ("mix", 2), ("gs", "cross", 1, 0),
    ("gs", "rest", 0, 0), ("gs", "at", 2, 1), ("pass", 0, 0), ("gs", "two", 2, 1), ("mix", 3), ("mix", 4),
    ("gs", "at", 3, 0), ("gs", "rest", 0, 1), ("pass", 0, 1), ("mix", 5), ("ready", "ow"), ("proj", 0),
    ("proj", 1), ("gs", "at", 3, 1), ("gs", "two", 3, 1), ("gs", "two", 3, 0), ("fetch", 0), ("proj", 2),
    ("gs", "cross", 2, 0), ("proj", 3), ("gs", "cross", 1, 1), ("dense", 0, 0), ("dense", 0, 1),
    ("dense", 0, 2), ("gs", "rest", 1, 0), ("pass", 1, 0), ("grad", 0, 0), ("swapF", 0, 0), ("grad", 0, 1),
    ("swapF", 0, 1), ("gs", "cross", 2, 1), ("gs", "cross", 3, 1), ("gs", "cross", 3, 0), ("acc", 0, 0),
    ("gs", "rest", 1, 1), ("pass", 1, 1), ("acc", 0, 1), ("gs", "rest", 2, 0), ("swappedF", 0, 0),
    ("Fs", "first", 0, 0), ("swappedF", 0, 1), ("Fs", "first", 0, 1), ("fetch", 1), ("gs", "rest", 2, 1),
    ("pass", 2, 1), ("pass", 2, 0), ("dense", 1, 0), ("dense", 1, 1), ("dense", 1, 2), ("gs", "rest", 3, 0),
    ("pass", 3, 0), ("grad", 1, 0), ("gs", "rest", 3, 1), ("pass", 3, 1), ("Fs", "second", 0, 0),
    ("swapF", 1, 0), ("grad", 1, 1), ("fetch", 2), ("swapF", 1, 1), ("acc", 1, 0), ("Fs", "second", 0, 1),
    ("acc", 1, 1), ("swappedF", 1, 0), ("swappedF", 1, 1), ("Fs", "first", 1, 1), ("Fs", "first", 1, 0),
    ("fetch", 3), ("dense", 2, 0), ("dense", 2, 1), ("dense", 2, 2), ("grad", 2, 0), ("swapF", 2, 0),
    ("grad", 2, 1), ("swapF", 2, 1), ("acc", 2, 0), ("swappedF", 2, 0), ("acc", 2, 1), ("Fs", "second", 1, 1),
    ("Fs", "second", 1, 0), ("swappedF", 2, 1), ("Fs", "first", 2, 1), ("dense", 3, 0), ("Fs", "first", 2, 0),
    ("dense", 3, 1), ("dense", 3, 2), ("Fs", "line", 0, 0), ("Fs", "line", 1, 1), ("grad", 3, 0),
    ("Fs", "line", 1, 0), ("swapF", 3, 0), ("grad", 3, 1), ("Fs", "line", 0, 1), ("swapF", 3, 1),
    ("acc", 3, 0), ("acc", 3, 1), ("swappedF", 3, 0), ("Fs", "second", 2, 0), ("Fs", "second", 2, 1),
    ("fin2", 0), ("swappedF", 3, 1), ("Fs", "first", 3, 0), ("Fs", "first", 3, 1), ("fin2", 1),
    ("Fs", "line", 2, 0), ("Fs", "hop", 1, 0, 0), ("Fs", "hop", 2, 0, 0), ("Fs", "line", 2, 1),
    ("Fs", "hop", 1, 1, 0), ("fin2", 2), ("fin2", 3), ("og",), ("Fs", "hop", 2, 1, 0), ("swap", "og"),
    ("Fs", "hop", 1, 0, 1), ("Fs", "second", 3, 0), ("scale",), ("Fs", "second", 3, 1), ("swapped", "og"),
    ("w", "first", 0, 1), ("w", "first", 1, 1), ("Fs", "hop", 2, 0, 1), ("head", 0, 0), ("head", 0, 1),
    ("head", 0, 2), ("w", "first", 2, 1), ("swap", 0), ("head", 1, 0), ("Fs", "hop", 1, 1, 1),
    ("Fs", "line", 3, 0), ("Fs", "hop", 0, 0, 0), ("w", "first", 3, 1), ("Fs", "hop", 1, 0, 2),
    ("Fs", "hop", 3, 0, 0), ("Fs", "line", 3, 1), ("Fs", "hop", 0, 1, 0), ("Fs", "hop", 3, 1, 0),
    ("w", "second", 0, 1), ("head", 1, 1), ("head", 1, 2), ("Fs", "hop", 2, 1, 1), ("w", "second", 1, 1),
    ("swapped", 0), ("m", "first", 0, 0), ("w", "second", 2, 1), ("swap", 1), ("head", 2, 0),
    ("w", "line", 0, 1), ("m", "first", 0, 1), ("head", 2, 1), ("head", 2, 2), ("w", "second", 3, 1),
    ("Fs", "hop", 0, 0, 1), ("Fs", "hop", 3, 0, 1), ("swap", 2), ("swapped", 1), ("m", "first", 3, 0),
    ("head", 3, 0), ("Fs", "hop", 2, 1, 2), ("m", "first", 3, 1), ("head", 3, 1), ("m", "second", 0, 0),
    ("Fs", "hop", 3, 1, 1), ("w", "line", 2, 1), ("Fs", "hop", 0, 1, 1), ("Fs", "hop", 2, 0, 2),
    ("m", "second", 0, 1), ("swapped", 2), ("m", "first", 1, 0), ("w", "hop", 0, 1, 1),
    ("Fs", "hop", 3, 0, 2), ("Fs", "hop", 1, 1, 2), ("w", "line", 3, 1), ("Fs", "hop", 0, 0, 2),
    ("w", "line", 1, 1), ("head", 3, 2), ("m", "first", 1, 1), ("w", "hop", 2, 1, 1), ("swap", 3), ("turn",),
    ("vg",), ("m", "second", 3, 1), ("m", "second", 3, 0), ("w", "hop", 3, 1, 1), ("swapped", 3),
    ("m", "first", 2, 0), ("w", "hop", 1, 1, 1), ("m", "line", 0, 0), ("Fs", "hop", 3, 1, 2),
    ("w", "hop", 0, 1, 2), ("m", "first", 2, 1), ("Fs", "hop", 0, 1, 2), ("swap", "vg"),
    ("Fs", "hop", 0, 0, 3), ("fin1", 0), ("w", "hop", 3, 1, 2), ("m", "line", 0, 1), ("w", "hop", 1, 1, 2),
    ("Fs", "hop", 3, 0, 3), ("w", "hop", 2, 1, 2), ("w", "hop", 0, 1, 3), ("m", "hop", 0, 0, 1),
    ("w", "at", 1, 1, 0), ("w", "at", 2, 1, 0), ("m", "second", 1, 1), ("swapped", "vg"),
    ("w", "first", 0, 0), ("w", "first", 3, 0), ("w", "first", 1, 0), ("w", "first", 2, 0), ("fin1", 1),
    ("m", "second", 1, 0), ("m", "line", 3, 0), ("w", "two", 1, 1, 0), ("w", "at", 1, 1, 1),
    ("m", "line", 3, 1), ("m", "hop", 0, 0, 2), ("Fs", "hop", 3, 1, 3), ("w", "at", 0, 1, 0),
    ("m", "hop", 0, 1, 1), ("fin1", 2), ("w", "cross", 2, 1, 0), ("w", "hop", 3, 1, 3), ("w", "at", 2, 1, 1),
    ("m", "second", 2, 0), ("w", "at", 3, 1, 0), ("w", "two", 0, 1, 0), ("w", "two", 3, 1, 0),
    ("m", "hop", 0, 0, 3), ("m", "at", 0, 0, 0), ("w", "at", 1, 1, 2), ("m", "hop", 3, 0, 1), ("fin1", 3),
    ("m", "second", 2, 1), ("m", "line", 1, 0), ("w", "two", 2, 1, 0), ("w", "two", 2, 1, 1),
    ("w", "at", 2, 1, 2), ("m", "hop", 3, 0, 2), ("w", "two", 1, 1, 1), ("m", "hop", 3, 1, 1),
    ("w", "at", 3, 1, 1), ("m", "line", 1, 1), ("w", "at", 0, 1, 1), ("m", "two", 0, 0, 0),
    ("m", "hop", 0, 1, 2), ("w", "second", 0, 0), ("small", 0), ("w", "two", 2, 1, 2), ("small", 1),
    ("m", "line", 2, 0), ("m", "hop", 1, 0, 1), ("w", "second", 1, 0), ("m", "cross", 0, 0, 0),
    ("w", "two", 1, 1, 2), ("Fs", "hop", 0, 1, 3), ("w", "at", 3, 1, 2), ("w", "two", 3, 1, 1),
    ("m", "hop", 3, 1, 2), ("m", "hop", 0, 1, 3), ("m", "at", 0, 0, 1), ("m", "at", 0, 1, 0),
    ("m", "two", 0, 1, 0), ("w", "cross", 1, 1, 0), ("w", "two", 3, 1, 2), ("w", "two", 0, 1, 1),
    ("w", "at", 0, 1, 2), ("w", "two", 0, 1, 2), ("w", "at", 3, 1, 3), ("w", "line", 0, 0),
    ("m", "hop", 1, 1, 1), ("w", "second", 2, 0), ("m", "two", 0, 0, 1), ("w", "hop", 0, 0, 1),
    ("m", "hop", 3, 0, 3), ("m", "at", 3, 0, 0), ("m", "hop", 1, 0, 2), ("w", "two", 3, 1, 3),
    ("m", "two", 3, 0, 0), ("m", "at", 1, 0, 0), ("w", "line", 1, 0), ("w", "second", 3, 0),
    ("m", "cross", 0, 0, 1), ("m", "hop", 1, 1, 2), ("small", 2), ("m", "hop", 2, 0, 1), ("m", "at", 0, 0, 2),
    ("m", "two", 0, 0, 2), ("m", "at", 1, 0, 1), ("m", "at", 1, 1, 0), ("m", "hop", 3, 1, 3),
    ("w", "line", 2, 0), ("w", "at", 0, 1, 3), ("w", "cross", 3, 1, 0), ("w", "two", 0, 1, 3),
    ("m", "at", 3, 1, 0), ("m", "at", 0, 1, 1), ("m", "two", 3, 1, 0), ("m", "cross", 3, 0, 0),
    ("m", "two", 1, 0, 0), ("w", "hop", 1, 0, 1), ("m", "at", 3, 0, 1), ("m", "two", 0, 1, 1),
    ("m", "two", 3, 0, 1), ("m", "line", 2, 1), ("w", "cross", 1, 1, 1), ("w", "cross", 1, 1, 2),
    ("w", "hop", 0, 0, 2), ("w", "cross", 2, 1, 1), ("w", "hop", 1, 0, 2), ("w", "at", 1, 0, 0),
    ("m", "two", 1, 1, 0), ("m", "two", 1, 0, 1), ("w", "cross", 2, 1, 2), ("w", "cross", 0, 1, 0),
    ("w", "cross", 0, 1, 1), ("w", "cross", 0, 1, 2), ("w", "hop", 2, 0, 1), ("w", "two", 1, 0, 0),
    ("w", "cross", 3, 1, 1), ("m", "at", 0, 0, 3), ("w", "line", 3, 0), ("m", "hop", 2, 0, 2),
    ("m", "hop", 2, 1, 1), ("m", "at", 2, 0, 0), ("m", "at", 1, 1, 1), ("m", "two", 2, 0, 0),
    ("w", "hop", 0, 0, 3), ("w", "at", 0, 0, 0), ("w", "two", 0, 0, 0), ("m", "cross", 0, 0, 2),
    ("m", "at", 3, 1, 1), ("w", "rest", 1, 1), ("m", "at", 3, 0, 2), ("m", "at", 1, 0, 2),
    ("m", "two", 3, 0, 2), ("m", "two", 3, 1, 1), ("m", "two", 1, 0, 2), ("w", "rest", 2, 1),
    ("w", "cross", 0, 1, 3), ("w", "at", 1, 0, 1), ("w", "hop", 3, 0, 1), ("m", "two", 0, 0, 3),
    ("m", "at", 0, 1, 2), ("m", "cross", 3, 1, 0), ("w", "hop", 2, 0, 2), ("m", "at", 2, 0, 1),
    ("m", "cross", 0, 0, 3), ("m", "two", 2, 0, 1), ("w", "cross", 3, 1, 2), ("w", "at", 2, 0, 0),
    ("w", "at", 0, 0, 1), ("m", "cross", 1, 0, 0), ("m", "cross", 1, 0, 1), ("m", "cross", 3, 0, 1),
    ("w", "cross", 3, 1, 3), ("m", "two", 1, 1, 1), ("w", "rest", 0, 1), ("w", "two", 0, 0, 1),
    ("m", "at", 2, 0, 2), ("m", "at", 3, 0, 3), ("m", "two", 3, 0, 3), ("small", 3), ("m", "cross", 1, 1, 0),
    ("m", "at", 1, 1, 2), ("m", "two", 1, 1, 2), ("m", "hop", 2, 1, 2), ("m", "at", 3, 1, 2),
    ("w", "cross", 1, 0, 0), ("m", "at", 2, 1, 0), ("m", "cross", 3, 0, 2), ("m", "cross", 0, 1, 0),
    ("m", "cross", 1, 0, 2), ("m", "at", 0, 1, 3), ("m", "two", 0, 1, 2), ("m", "two", 0, 1, 3),
    ("m", "two", 2, 0, 2), ("m", "at", 3, 1, 3), ("w", "cross", 0, 0, 0), ("w", "hop", 3, 0, 2),
    ("m", "cross", 3, 1, 1), ("w", "at", 1, 0, 2), ("w", "two", 1, 0, 1), ("w", "two", 1, 0, 2),
    ("w", "at", 2, 0, 1), ("w", "at", 0, 0, 2), ("w", "two", 0, 0, 2), ("w", "rest", 3, 1),
    ("m", "rest", 0, 0), ("m", "two", 2, 1, 0), ("m", "two", 3, 1, 2), ("m", "two", 3, 1, 3),
    ("m", "at", 2, 1, 1), ("m", "cross", 2, 0, 0), ("m", "two", 2, 1, 1), ("w", "cross", 1, 0, 1),
    ("m", "cross", 2, 0, 1), ("w", "cross", 0, 0, 1), ("small", 4), ("w", "two", 2, 0, 0),
    ("w", "two", 2, 0, 1), ("w", "cross", 2, 0, 0), ("m", "cross", 3, 0, 3), ("w", "hop", 3, 0, 3),
    ("w", "at", 3, 0, 0), ("w", "at", 0, 0, 3), ("w", "two", 0, 0, 3), ("w", "two", 3, 0, 0),
    ("m", "cross", 0, 1, 1), ("m", "at", 2, 1, 2), ("m", "two", 2, 1, 2), ("w", "cross", 1, 0, 2),
    ("w", "cross", 2, 0, 1), ("m", "cross", 1, 1, 1), ("m", "cross", 1, 1, 2), ("m", "cross", 3, 1, 2),
    ("m", "cross", 2, 0, 2), ("m", "cross", 0, 1, 2), ("w", "at", 3, 0, 1), ("w", "at", 3, 0, 2),
    ("m", "rest", 3, 0), ("w", "at", 2, 0, 2), ("w", "two", 2, 0, 2), ("small", 5), ("m", "cross", 2, 1, 0),
    ("w", "two", 3, 0, 1), ("w", "at", 3, 0, 3), ("w", "two", 3, 0, 2), ("w", "cross", 3, 0, 0),
    ("m", "cross", 3, 1, 3), ("m", "cross", 0, 1, 3), ("m", "rest", 0, 1), ("m", "rest", 1, 0),
    ("w", "two", 3, 0, 3), ("w", "cross", 0, 0, 2), ("w", "cross", 2, 0, 2), ("w", "cross", 0, 0, 3),
    ("w", "cross", 3, 0, 1), ("m", "rest", 2, 0), ("w", "cross", 3, 0, 2), ("m", "cross", 2, 1, 1),
    ("m", "cross", 2, 1, 2), ("m", "rest", 1, 1), ("w", "cross", 3, 0, 3), ("w", "rest", 1, 0),
    ("w", "rest", 2, 0), ("m", "rest", 3, 1), ("w", "rest", 3, 0), ("m", "rest", 2, 1), ("w", "rest", 0, 0),
)


def normalize(matrix, norm_gain, norm_shift):
    average = jnp.mean(matrix, axis=-1, keepdims=True)
    center = matrix - average
    reciprocal = lax.rsqrt(jnp.mean(center * center, axis=-1, keepdims=True) + epsilon)
    unit_rows = center * reciprocal
    return (unit_rows * norm_gain + norm_shift, unit_rows, reciprocal)


def plain_norm_back(slope_rows, unit_rows, reciprocal, norm_gain):
    tilted = slope_rows * norm_gain
    centered_slope = tilted - jnp.mean(tilted, axis=-1, keepdims=True)
    centered_slope = centered_slope - unit_rows * jnp.mean(
        tilted * unit_rows, axis=-1, keepdims=True
    )
    return (
        centered_slope * reciprocal,
        jnp.sum(slope_rows * unit_rows, axis=0),
        jnp.sum(slope_rows, axis=0),
    )


def plain_contract(left_side, right_side):
    return lax.dot_general(
        left_side, right_side, (((0,), (0,)), ((), ())), preferred_element_type=jnp.float32
    )


def times_transpose(left_side, right_side):
    return lax.dot_general(
        left_side, right_side, (((1,), (1,)), ((), ())), preferred_element_type=jnp.float32
    )


def row_chances(mixing_full, row_docs):
    same_doc = row_docs[:, None] == row_docs[None, :]
    scores = jnp.where(same_doc[None, :, :], mixing_full.astype(jnp.float32), -1e30)
    row_top = jnp.max(scores, axis=-1, keepdims=True)
    raised = jnp.exp(scores - row_top)
    return raised / jnp.sum(raised, axis=-1, keepdims=True)


def plain(
    inputs,
    documents,
    mixing,
    value_weight,
    output_weight,
    mixer_gain,
    mixer_shift,
    dense_gain,
    dense_shift,
    hidden_weight,
    hidden_bias,
    down_weight,
    down_bias,
    cotangent,
):
    gathered = (
        lax.all_gather(mixing, "narrow", axis=1, tiled=True),
        lax.all_gather(value_weight, "narrow", axis=1, tiled=True),
        lax.all_gather(output_weight, "narrow", axis=0, tiled=True),
        lax.all_gather(mixer_gain, "narrow", axis=0, tiled=True),
        lax.all_gather(mixer_shift, "narrow", axis=0, tiled=True),
        lax.all_gather(dense_gain, "narrow", axis=0, tiled=True),
        lax.all_gather(dense_shift, "narrow", axis=0, tiled=True),
        lax.all_gather(hidden_bias, "narrow", axis=0, tiled=True),
        lax.all_gather(down_bias, "narrow", axis=0, tiled=True),
    )
    mixing_full, value_full, output_full = (gathered[0], gathered[1], gathered[2])
    gain_first = gathered[3].astype(jnp.float32)
    shift_first = gathered[4].astype(jnp.float32)
    gain_second = gathered[5].astype(jnp.float32)
    shift_second = gathered[6].astype(jnp.float32)
    bias_hidden = gathered[7].astype(jnp.float32)
    bias_down = gathered[8].astype(jnp.float32)
    halfway = (
        lax.all_gather(hidden_weight, "narrow", axis=0, tiled=True),
        lax.all_gather(down_weight, "narrow", axis=1, tiled=True),
    )
    hidden_full, down_full = (
        lax.all_gather(halfway[0], "wide", axis=1, tiled=True),
        lax.all_gather(halfway[1], "wide", axis=0, tiled=True),
    )
    row_count = inputs.shape[0]
    stream = inputs.reshape(row_count * SEQ, D).astype(jnp.float32)
    normed, unit_first, recip_first = normalize(stream, gain_first, shift_first)
    normed_low = normed.astype(jnp.bfloat16)
    values = jnp.dot(normed_low, value_full, preferred_element_type=jnp.float32).astype(
        jnp.bfloat16
    )
    value_rows = values.reshape(row_count, SEQ, D)

    def mix_one(bundle):
        row_values, row_docs = bundle
        chances_low = row_chances(mixing_full, row_docs).astype(jnp.bfloat16)
        per_head = row_values.reshape(SEQ, HEADS, HEAD)
        blended_row = jnp.einsum(
            "hij,jhd->ihd", chances_low, per_head, preferred_element_type=jnp.float32
        )
        return blended_row.reshape(SEQ, D).astype(jnp.bfloat16)

    blended = lax.map(mix_one, (value_rows, documents)).reshape(row_count * SEQ, D)
    middle = stream + jnp.dot(blended, output_full, preferred_element_type=jnp.float32)
    normed_two, unit_second, recip_second = normalize(middle, gain_second, shift_second)
    normed_two_low = normed_two.astype(jnp.bfloat16)
    hidden = jnp.dot(normed_two_low, hidden_full, preferred_element_type=jnp.float32) + bias_hidden
    activated, gelu_pull = jax.vjp(jax.nn.gelu, hidden)
    active = activated.astype(jnp.bfloat16)
    result = middle + jnp.dot(active, down_full, preferred_element_type=jnp.float32) + bias_down
    slope_low = cotangent.reshape(row_count * SEQ, D)
    slope_wide = slope_low.astype(jnp.float32)
    down_bias_sum = jnp.sum(slope_wide, axis=0)
    down_grad = plain_contract(active, slope_low)
    active_slope = times_transpose(slope_low, down_full)
    hidden_slope_wide = gelu_pull(active_slope)[0]
    hidden_slope = hidden_slope_wide.astype(jnp.bfloat16)
    hidden_bias_sum = jnp.sum(hidden_slope.astype(jnp.float32), axis=0)
    hidden_grad = plain_contract(normed_two_low, hidden_slope)
    normed_two_slope = times_transpose(hidden_slope, hidden_full)
    back_second, gain_second_sum, shift_second_sum = plain_norm_back(
        normed_two_slope, unit_second, recip_second, gain_second
    )
    middle_slope = slope_wide + back_second
    attended_slope = middle_slope.astype(jnp.bfloat16)
    output_grad = plain_contract(blended, attended_slope)
    blended_slope = times_transpose(attended_slope, output_full).astype(jnp.bfloat16)

    def mix_back(running, bundle):
        row_values, row_docs, row_slope = bundle
        chances = row_chances(mixing_full, row_docs)
        per_head = row_values.reshape(SEQ, HEADS, HEAD)
        head_slope = row_slope.reshape(SEQ, HEADS, HEAD)
        chance_slope = jnp.einsum(
            "ihd,jhd->hij", head_slope, per_head, preferred_element_type=jnp.float32
        )
        score_slope = chances * (
            chance_slope - jnp.sum(chances * chance_slope, axis=-1, keepdims=True)
        )
        value_part = jnp.einsum(
            "hij,ihd->jhd",
            chances.astype(jnp.bfloat16),
            head_slope,
            preferred_element_type=jnp.float32,
        )
        return (running + score_slope, value_part.reshape(SEQ, D).astype(jnp.bfloat16))

    mixing_start = jnp.zeros((HEADS, SEQ, SEQ), jnp.float32)
    mixing_grad, value_slopes = lax.scan(
        mix_back, mixing_start, (value_rows, documents, blended_slope.reshape(row_count, SEQ, D))
    )
    value_slope = value_slopes.reshape(row_count * SEQ, D)
    value_grad = plain_contract(normed_low, value_slope)
    normed_slope = times_transpose(value_slope, value_full)
    back_first, gain_first_sum, shift_first_sum = plain_norm_back(
        normed_slope, unit_first, recip_first, gain_first
    )
    inputs_slope = (middle_slope + back_first).astype(jnp.bfloat16)
    sums_half = (
        lax.psum_scatter(
            hidden_grad.astype(jnp.bfloat16), "wide", scatter_dimension=1, tiled=True
        ).astype(jnp.float32),
        lax.psum_scatter(
            down_grad.astype(jnp.bfloat16), "wide", scatter_dimension=0, tiled=True
        ).astype(jnp.float32),
    )
    hidden_share, down_share = (
        lax.psum_scatter(
            sums_half[0].astype(jnp.bfloat16), "narrow", scatter_dimension=0, tiled=True
        ).astype(jnp.float32),
        lax.psum_scatter(
            sums_half[1].astype(jnp.bfloat16), "narrow", scatter_dimension=1, tiled=True
        ).astype(jnp.float32),
    )
    shares = (
        lax.psum_scatter(
            mixing_grad.astype(jnp.bfloat16), "narrow", scatter_dimension=1, tiled=True
        ).astype(jnp.float32),
        lax.psum_scatter(
            value_grad.astype(jnp.bfloat16), "narrow", scatter_dimension=1, tiled=True
        ).astype(jnp.float32),
        lax.psum_scatter(
            output_grad.astype(jnp.bfloat16), "narrow", scatter_dimension=0, tiled=True
        ).astype(jnp.float32),
        lax.psum_scatter(
            gain_first_sum.astype(jnp.bfloat16), "narrow", scatter_dimension=0, tiled=True
        ).astype(jnp.float32),
        lax.psum_scatter(
            shift_first_sum.astype(jnp.bfloat16), "narrow", scatter_dimension=0, tiled=True
        ).astype(jnp.float32),
        lax.psum_scatter(
            gain_second_sum.astype(jnp.bfloat16), "narrow", scatter_dimension=0, tiled=True
        ).astype(jnp.float32),
        lax.psum_scatter(
            shift_second_sum.astype(jnp.bfloat16), "narrow", scatter_dimension=0, tiled=True
        ).astype(jnp.float32),
        lax.psum_scatter(
            hidden_bias_sum.astype(jnp.bfloat16), "narrow", scatter_dimension=0, tiled=True
        ).astype(jnp.float32),
        lax.psum_scatter(
            down_bias_sum.astype(jnp.bfloat16), "narrow", scatter_dimension=0, tiled=True
        ).astype(jnp.float32),
    )
    totals = (
        lax.psum(shares[0].astype(jnp.bfloat16), "wide").astype(jnp.float32),
        lax.psum(shares[1].astype(jnp.bfloat16), "wide").astype(jnp.float32),
        lax.psum(shares[2].astype(jnp.bfloat16), "wide").astype(jnp.float32),
        lax.psum(shares[3].astype(jnp.bfloat16), "wide").astype(jnp.float32),
        lax.psum(shares[4].astype(jnp.bfloat16), "wide").astype(jnp.float32),
        lax.psum(shares[5].astype(jnp.bfloat16), "wide").astype(jnp.float32),
        lax.psum(shares[6].astype(jnp.bfloat16), "wide").astype(jnp.float32),
        lax.psum(shares[7].astype(jnp.bfloat16), "wide").astype(jnp.float32),
        lax.psum(shares[8].astype(jnp.bfloat16), "wide").astype(jnp.float32),
    )
    return (
        result.reshape(row_count, SEQ, D).astype(jnp.bfloat16),
        inputs_slope.reshape(row_count, SEQ, D),
        totals[0],
        totals[1],
        totals[2],
        totals[3],
        totals[4],
        totals[5],
        totals[6],
        hidden_share,
        totals[7],
        down_share,
        totals[8],
    )


def solution(mesh):
    inner = local if dict(mesh.shape) == {"narrow": 2, "wide": 16} else plain
    return jax.shard_map(
        inner,
        mesh=mesh,
        in_specs=(
            P(("narrow", "wide"), None, None),
            P(("narrow", "wide"), None),
            P(None, "narrow", None),
            P(None, "narrow"),
            P("narrow", None),
            P("narrow"),
            P("narrow"),
            P("narrow"),
            P("narrow"),
            P("narrow", "wide"),
            P("narrow"),
            P("wide", "narrow"),
            P("narrow"),
            P(("narrow", "wide"), None, None),
        ),
        out_specs=(
            P(("narrow", "wide"), None, None),
            P(("narrow", "wide"), None, None),
            P(None, "narrow", None),
            P(None, "narrow"),
            P("narrow", None),
            P("narrow"),
            P("narrow"),
            P("narrow"),
            P("narrow"),
            P("narrow", "wide"),
            P("narrow"),
            P("wide", "narrow"),
            P("narrow"),
        ),
        check_vma=False,
    )
```
